128 devices in a mesh: sub: 8 (over x, core), band: 16 (over z, y).
Axes of the slice: x: 4, y: 4, z: 4, core: 2. Of those that a mesh axis runs over, the one named last changes fastest.
Arguments:
- coeffs_in: float32 [32, 128, 1024], P('sub'), may hold values from -6 to 6
- basis: bfloat16 [224, 32], P('band'), may hold values from -0.375 to 0.375
- kernels: float32 [224, 9, 9], P('band'), may hold values from -0.625 to 0.625
- response: bfloat16 [8, 224], P(None, 'band'), may hold values from -1.5 to 1.5
- hs_image: bfloat16 [224, 32, 256], P('band', 'sub'), may hold values from -6 to 6
- ms_image: bfloat16 [8, 128, 1024], P(None, 'sub'), may hold values from -6 to 6
Outputs:
- coeffs: float32 [32, 128, 1024], P('sub')
The draws below stay inside these ranges and needn't reach their ends.
All inputs are finite; a program needn't handle non-finite values.
Results may differ from the reference program's by a relative error of at most 0.0003.
The reference program's roundings to bfloat16 on the way (of `combined`, `rounded`, `mixed`, `back` and `ms_misfit`) count: a program that leaves them out, or rounds other values in their place, can miss the bound.
Values may be sent and summed in bfloat16 or wider, within the bound.
No kernel may reach another device: no remote copies, remote signals or barrier semaphores. Data moves between devices by JAX's collectives and lax.ppermute only.
A program may use at most 128 MiB of HBM per device.

```python
import jax
import jax.numpy as jnp
from jax import lax

K = 32
L = 224
M = 8
TAPS = 9
ITERS = 2
H = 128
W = 1024


def level_of(stream_key, shape, cuts, low, high):
    factor_of = 1.0
    for axis_at, shards_of in cuts:
        draws = jax.random.uniform(jax.random.fold_in(jax.random.fold_in(stream_key, 6), axis_at), (shards_of,), jnp.float32, low / len(cuts), high / len(cuts))
        factor_of = factor_of * jnp.repeat(jnp.exp(draws), shape[axis_at] // shards_of).reshape((-1,) + (1,) * (len(shape) - 1 - axis_at))
    return factor_of


def centred(own_key, extent, deviation, limit, pieces=(), dtype=jnp.bfloat16):
    factor_of = level_of(own_key, extent, pieces, -0.22, 0.18) if pieces else 1.0
    drawn = jax.random.normal(own_key, extent, jnp.float32) * deviation * factor_of
    return jnp.minimum(jnp.maximum(drawn, -limit), limit).astype(dtype)


def setup_inputs(seed: int = 0) -> dict:
    key_of = jax.random.split(jax.random.key(seed), 7)
    return {
        "coeffs_in": centred(key_of[0], (K, H, W), 1.0, 6.0, ((0, 8),), jnp.float32),
        "basis": centred(key_of[1], (L, K), L ** -0.5, 0.375, ((0, 16),)),
        "kernels": centred(key_of[2], (L, TAPS, TAPS), (TAPS * TAPS) ** -0.5, 0.625, ((0, 16),), jnp.float32),
        "response": centred(key_of[3], (M, L), (L // 16) ** -0.5, 1.5, ((1, 16),)),
        "hs_image": centred(key_of[4], (L, H // 4, W // 4), 1.0, 6.0, ((0, 16), (1, 8))),
        "ms_image": centred(key_of[5], (M, H, W), 1.0, 6.0, ((1, 8),)),
    }


step_scale = 0.15

def blur(field, kernels):
    return lax.conv_general_dilated(field[None], kernels[:, None], (4, 4), ((4, 4), (4, 4)), dimension_numbers=('NCHW', 'OIHW', 'NCHW'), feature_group_count=field.shape[0], precision=lax.Precision.HIGHEST)[0]

def reference(coeffs_in, basis, kernels, response, hs_image, ms_image):
    height = coeffs_in.shape[1]
    width = coeffs_in.shape[2]
    combined = jnp.dot(response, basis, preferred_element_type=jnp.float32).astype(jnp.bfloat16)
    coeffs = coeffs_in
    for turn in range(ITERS):
        rounded = coeffs.astype(jnp.bfloat16).reshape(K, -1)
        mixed = jnp.dot(basis, rounded, preferred_element_type=jnp.float32).astype(jnp.bfloat16)
        field = mixed.reshape(L, height, width).astype(jnp.float32)
        blurred, adjoint = jax.vjp(lambda value: blur(value, kernels), field)
        misfit = hs_image.astype(jnp.float32) - blurred
        back = adjoint(misfit)[0].astype(jnp.bfloat16).reshape(L, -1)
        hs_grad = jnp.dot(basis.T, back, preferred_element_type=jnp.float32)
        predicted = jnp.dot(combined, rounded, preferred_element_type=jnp.float32)
        ms_misfit = (ms_image.reshape(M, -1).astype(jnp.float32) - predicted).astype(jnp.bfloat16)
        ms_grad = jnp.dot(combined.T, ms_misfit, preferred_element_type=jnp.float32)
        coeffs = coeffs + step_scale * (hs_grad + ms_grad).reshape(K, height, width)
    return coeffs
```

```python
import functools

import jax
import jax.numpy as jnp
from jax import lax
from jax.experimental import pallas as pl
from jax.experimental.pallas import tpu as pltpu
from jax.sharding import PartitionSpec as P

STEP = 0.15
TR, TC = 16, 64
TAPS = 9
LANES = 128
CROWS = 48
MROWS = 32
IROWS = 10
JCOLS = 24
ROWS_LO, COLS_LO = 32, 256
f32 = jnp.float32
bf16 = jnp.bfloat16


def rounded(value):
    return value.astype(bf16).astype(f32)


def refine_kernel(pos_ref, c_ref, hp_ref, ms_ref, out_ref, m0, m1, f0, f1, b0, b1, c1_ref, hs0, hs1, w0, w1):
    s = pos_ref[0]
    b = pos_ref[1]
    m = (m0, m1)
    f = (f0, f1)
    bk = (b0, b1)
    hst = (hs0, hs1)
    w = (w0, w1)
    for h in range(2):
        part = hp_ref[h * 128 : h * 128 + 128, :]
        for piece in range(2):
            hst[h][piece * 128 : piece * 128 + 128, :] = part[:, piece * 128 : piece * 128 + 128].T
        w[h][...] = part[:, 256:384].T
    basis = jnp.concatenate([w0[81:113, :], w1[81:113, :]], axis=1).astype(bf16)
    response = jnp.concatenate([w0[113:121, :], w1[113:121, :]], axis=1).astype(bf16)
    combined = lax.dot_general(response, basis, (((1,), (1,)), ((), ())), preferred_element_type=f32).astype(bf16)
    lane = lax.broadcasted_iota(jnp.int32, (1, LANES), 1)
    column = 64 * b - 16 + lane
    in_columns = (column >= 0) & (column < 1024) & (lane >= 8) & (lane < 88)

    def mix(row, value):
        mixed = lax.dot_general(
            value.astype(bf16), basis, (((0,), (0,)), ((), ())), preferred_element_type=f32
        )
        mixed = rounded(mixed)
        for h in range(2):
            m[h][pl.ds(pl.multiple_of(row * LANES, LANES), LANES), :] = mixed[:, h * 128 : h * 128 + 128]

    def blur_row(n, lane0, i_off, j_off):
        jj = lax.broadcasted_iota(jnp.int32, (JCOLS, LANES), 0) + j_off
        i_at = 4 * s + n + i_off - 3
        j_at = 16 * b + jj - 3
        inside = (i_at >= 0) & (i_at < ROWS_LO) & (j_at >= 0) & (j_at < COLS_LO)
        for h in range(2):
            acc = [None, None, None]
            for a in range(TAPS):
                for q in range(4):
                    x = m[h][pl.ds((4 * n + a) * LANES + lane0 + q, JCOLS, stride=4), :]
                    for d in range(3):
                        if 4 * d + q > 8:
                            continue
                        term = w[h][a * 9 + 4 * d + q : a * 9 + 4 * d + q + 1, :] * x
                        acc[d] = term if acc[d] is None else acc[d] + term
            blurred = (
                acc[0]
                + pltpu.roll(acc[1], JCOLS - 1, 0)
                + pltpu.roll(acc[2], JCOLS - 2, 0)
            )
            seen = hst[h][pl.ds((n + i_off) * JCOLS + j_off, JCOLS), :]
            f[h][pl.ds(pl.multiple_of(n * JCOLS, 8), JCOLS), :] = jnp.where(inside, seen - blurred, 0.0)

    def back_rows(u, lane0, width):
        for h in range(2):
            win = [
                [f[h][pl.ds((u + 2 - t) * JCOLS + 2 - tt, width), :] for tt in range(3)]
                for t in range(3)
            ]
            for p in range(4):
                for q in range(4):
                    total = None
                    for t in range(3):
                        for tt in range(3):
                            if p + 4 * t > 8 or q + 4 * tt > 8:
                                continue
                            tap = (p + 4 * t) * 9 + q + 4 * tt
                            term = w[h][tap : tap + 1, :] * win[t][tt]
                            total = term if total is None else total + term
                    bk[h][pl.ds((4 * u + p) * LANES + lane0 + q, width, stride=4), :] = rounded(total)

    def gradient(row, ms_row, now):
        at = pl.ds(pl.multiple_of(row * LANES, LANES), LANES)
        back = jnp.concatenate([b0[at, :], b1[at, :]], axis=1).astype(bf16)
        hs_grad = lax.dot_general(basis, back, (((1,), (1,)), ((), ())), preferred_element_type=f32)
        near = now.astype(bf16)
        predicted = jnp.dot(combined, near, preferred_element_type=f32)
        ms_misfit = (ms_ref[pl.ds(ms_row, 8, stride=MROWS), :] - predicted).astype(bf16)
        ms_grad = lax.dot_general(combined, ms_misfit, (((0,), (0,)), ((), ())), preferred_element_type=f32)
        return now + STEP * (hs_grad + ms_grad)

    def start_row(row):
        return c_ref[pl.ds(row, 32, stride=CROWS), :]

    def loop(count, body):
        def step(n, _):
            body(n)
            return 0

        lax.fori_loop(0, count, step, 0)

    loop(CROWS, lambda r: mix(r, start_row(r)))
    loop(IROWS, lambda n: blur_row(n, 0, 0, 0))
    loop(MROWS // 4, lambda u: back_rows(u, 8, 24))

    def first(r):
        row_at = 16 * s - 8 + r
        value = gradient(r, r, start_row(r + 8))
        value = jnp.where(in_columns & (row_at >= 0) & (row_at < 128), value, 0.0)
        c1_ref[pl.ds(pl.multiple_of(r * 32, 32), 32), :] = value
        mix(r, value)

    loop(MROWS, first)
    loop(6, lambda n: blur_row(n, 8, 2, 2))
    loop(TR // 4, lambda u: back_rows(u, 16, 16))

    def last(r):
        halves = []
        for half in range(2):
            row = r + 8 * half
            now = c1_ref[pl.ds(pl.multiple_of((row + 8) * 32, 32), 32), :]
            value = gradient(row, row + 8, now)
            halves.append(pltpu.roll(value, LANES - 16 if half == 0 else 48, 1))
        out_ref[pl.ds(r, 32, stride=8), :] = jnp.where(lane < 64, halves[0], halves[1])

    loop(8, last)


def refine(pos, c, hp, ms):
    vmem = pl.BlockSpec(memory_space=pltpu.VMEM)
    return pl.pallas_call(
        refine_kernel,
        out_shape=jax.ShapeDtypeStruct((32 * 8, LANES), f32),
        in_specs=[pl.BlockSpec(memory_space=pltpu.SMEM), vmem, vmem, vmem],
        out_specs=vmem,
        scratch_shapes=[
            pltpu.VMEM((CROWS * LANES, LANES), f32),
            pltpu.VMEM((CROWS * LANES, LANES), f32),
            pltpu.VMEM((256, LANES), f32),
            pltpu.VMEM((256, LANES), f32),
            pltpu.VMEM((MROWS * LANES, LANES), f32),
            pltpu.VMEM((MROWS * LANES, LANES), f32),
            pltpu.VMEM((MROWS * 32, LANES), f32),
            pltpu.VMEM((256, LANES), f32),
            pltpu.VMEM((256, LANES), f32),
            pltpu.VMEM((LANES, LANES), f32),
            pltpu.VMEM((LANES, LANES), f32),
        ],
        compiler_params=pltpu.CompilerParams(vmem_limit_bytes=40 * 2**20),
        cost_estimate=pl.CostEstimate(flops=400_000_000, bytes_accessed=2_000_000, transcendentals=0),
        name="refine",
    )(pos, c, hp, ms)


def place_kernel(g_ref, out_ref):
    lane = lax.broadcasted_iota(jnp.int32, (1, LANES), 1)
    low = lane < 64
    for s in range(8):
        for j in range(8):
            even = g_ref[2 * j, s, 0]
            odd = g_ref[2 * j + 1, s, 0]
            at = slice(j * 128, j * 128 + 128)
            out_ref[0, 16 * s : 16 * s + 8, at] = jnp.where(low, even, pltpu.roll(odd, 64, 1))
            out_ref[0, 16 * s + 8 : 16 * s + 16, at] = jnp.where(low, pltpu.roll(even, 64, 1), odd)


def place(gathered):
    return pl.pallas_call(
        place_kernel,
        out_shape=jax.ShapeDtypeStruct((4, 128, 1024), f32),
        grid=(4,),
        in_specs=[pl.BlockSpec((16, 8, 1, 8, LANES), lambda k: (0, 0, k, 0, 0))],
        out_specs=pl.BlockSpec((1, 128, 1024), lambda k: (k, 0, 0)),
        compiler_params=pltpu.CompilerParams(vmem_limit_bytes=32 * 2**20),
        name="place",
    )(gathered)


def per_device(coeffs_in, basis, kernels, response, hs_image, ms_image):
    s = lax.axis_index("sub")
    b = lax.axis_index("band")
    up = [(i, i + 1) for i in range(7)]
    down = [(i + 1, i) for i in range(7)]
    ms_wide = jnp.pad(ms_image, ((0, 0), (0, 0), (16, 48)))
    ms_tile = lax.dynamic_slice(ms_wide, (0, 0, 64 * b), (8, TR, LANES))
    hs_above = lax.ppermute(hs_image[:, 1:, :], "sub", up)
    hs_below = lax.ppermute(hs_image[:, :3, :], "sub", down)
    ms_above = lax.ppermute(ms_tile[:, 8:, :], "sub", up)
    ms_below = lax.ppermute(ms_tile[:, :8, :], "sub", down)
    hs = jnp.concatenate([hs_above, hs_image, hs_below], axis=1)
    ms = jnp.concatenate([ms_above, ms_tile, ms_below], axis=1).astype(f32)
    hs = jnp.pad(hs, ((0, 2), (0, 0), (3, 5))).astype(f32)
    windows = jnp.stack([hs[:, :, 16 * t : 16 * t + JCOLS] for t in range(16)])
    windows = jnp.pad(windows.reshape(16, 16, IROWS * JCOLS), ((0, 0), (0, 0), (0, 16)))
    params = jnp.concatenate(
        [kernels.reshape(14, 81), basis.astype(f32), response.T.astype(f32)], axis=1
    )
    params = jnp.pad(params, ((0, 2), (0, 7)))
    sent = jnp.concatenate([windows, jnp.broadcast_to(params, (16, 16, 128))], axis=2)
    hp = lax.all_to_all(sent, "band", split_axis=0, concat_axis=0, tiled=True).reshape(256, 384)
    wide = jnp.pad(coeffs_in, ((0, 0), (16, 16), (16, 48)))
    wide = lax.dynamic_slice(wide, (0, 0, 64 * b), (4, 160, LANES))
    tiles = jnp.stack([wide[:, 16 * t : 16 * t + CROWS] for t in range(8)])
    c = lax.all_to_all(tiles, "sub", split_axis=0, concat_axis=0, tiled=True).reshape(32 * CROWS, LANES)
    pos = jnp.stack([s, b]).astype(jnp.int32)
    new = refine(pos, c, hp, ms.reshape(8 * MROWS, LANES))
    owned = lax.all_to_all(new.reshape(8, 4, 8, LANES), "sub", split_axis=0, concat_axis=0, tiled=True)
    copies = jnp.broadcast_to(owned[None], (16,) + owned.shape)
    gathered = lax.all_to_all(copies, "band", split_axis=0, concat_axis=0, tiled=True)
    return place(gathered)


def solution(mesh):
    return jax.shard_map(
        per_device,
        mesh=mesh,
        in_specs=(
            P("sub", None, None),
            P("band", None),
            P("band", None, None),
            P(None, "band"),
            P("band", "sub", None),
            P(None, "sub", None),
        ),
        out_specs=P("sub", None, None),
        check_vma=False,
    )
```

```python
import functools

import jax
import jax.numpy as jnp
from jax import lax
from jax.experimental import pallas as pl
from jax.experimental.pallas import tpu as pltpu
from jax.sharding import PartitionSpec as P

STEP = 0.15
TR, TC = 16, 64
TAPS = 9
LANES = 128
CROWS = 48
MROWS = 32
IROWS = 10
JCOLS = 24
ROWS_LO, COLS_LO = 32, 256
f32 = jnp.float32
bf16 = jnp.bfloat16


def rounded(value):
    return value.astype(bf16).astype(f32)


def refine_kernel(pos_ref, c_ref, hp_ref, ms_ref, out_ref, m0, m1, f0, f1, b0, b1, c1_ref, g_ref, hs0, hs1, w0, w1):
    s = pos_ref[0]
    b = pos_ref[1]
    m = (m0, m1)
    f = (f0, f1)
    bk = (b0, b1)
    hst = (hs0, hs1)
    w = (w0, w1)
    for h in range(2):
        part = hp_ref[h * 128 : h * 128 + 128, :]
        for piece in range(2):
            hst[h][piece * 128 : piece * 128 + 128, :] = part[:, piece * 128 : piece * 128 + 128].T
        w[h][...] = part[:, 256:384].T
    basis = jnp.concatenate([w0[81:113, :], w1[81:113, :]], axis=1).astype(bf16)
    response = jnp.concatenate([w0[113:121, :], w1[113:121, :]], axis=1).astype(bf16)
    combined = lax.dot_general(response, basis, (((1,), (1,)), ((), ())), preferred_element_type=f32).astype(bf16)
    lane = lax.broadcasted_iota(jnp.int32, (1, LANES), 1)
    group = lane % 32
    column = 64 * b - 16 + 4 * group + lane // 32
    in_columns = (column >= 0) & (column < 1024) & (group >= 2) & (group < 22)

    def mix(row, value, rows):
        mixed = lax.dot_general(value.astype(bf16), basis, (((0,), (0,)), ((), ())), preferred_element_type=f32)
        mixed = rounded(mixed)
        at = pl.ds(pl.multiple_of(row * LANES, LANES), rows * LANES)
        for h in range(2):
            m[h][at, :] = mixed[:, h * 128 : h * 128 + 128]

    def ms_gradient(row, block):
        predicted = jnp.dot(combined, block.astype(bf16), preferred_element_type=f32)
        seen = jnp.concatenate([ms_ref[pl.ds(row - 8 + r, 8, stride=MROWS), :] for r in range(8)], axis=1)
        misfit = (seen - predicted).astype(bf16)
        grad = lax.dot_general(combined, misfit, (((0,), (0,)), ((), ())), preferred_element_type=f32)
        for r in range(8):
            g_ref[pl.ds((row - 8 + r) * 32, 32), :] = grad[:, r * 128 : r * 128 + 128]

    def blur_row(n):
        g = lax.broadcasted_iota(jnp.int32, (JCOLS, LANES), 0)
        i_at = 4 * s + n - 3
        j_at = 16 * b + g - 3
        inside = (i_at >= 0) & (i_at < ROWS_LO) & (j_at >= 0) & (j_at < COLS_LO)
        for h in range(2):
            acc = [None, None, None]
            for a in range(TAPS):
                for q in range(4):
                    at = pl.multiple_of((4 * n + a) * LANES + 32 * q, 32)
                    x = m[h][pl.ds(at, JCOLS), :]
                    for d in range(3):
                        if 4 * d + q > 8:
                            continue
                        tap = a * 9 + 4 * d + q
                        term = w[h][tap : tap + 1, :] * x
                        acc[d] = term if acc[d] is None else acc[d] + term
            blurred = acc[0] + pltpu.roll(acc[1], JCOLS - 1, 0) + pltpu.roll(acc[2], JCOLS - 2, 0)
            seen = hst[h][pl.ds(pl.multiple_of(n * JCOLS, 8), JCOLS), :]
            f[h][pl.ds(pl.multiple_of(8 + n * JCOLS, 8), JCOLS), :] = jnp.where(inside, seen - blurred, 0.0)

    def back_rows(u):
        for h in range(2):
            win = [[f[h][pl.ds(8 + (u - t) * JCOLS - tt, JCOLS), :] for tt in range(3)] for t in range(3)]
            for p in range(4):
                for q in range(4):
                    total = None
                    for t in range(3):
                        for tt in range(3):
                            if p + 4 * t > 8 or q + 4 * tt > 8:
                                continue
                            tap = (p + 4 * t) * 9 + q + 4 * tt
                            term = w[h][tap : tap + 1, :] * win[t][tt]
                            total = term if total is None else total + term
                    at = pl.multiple_of((4 * u - 8 + p) * LANES + 32 * q, 32)
                    bk[h][pl.ds(at, JCOLS), :] = rounded(total)

    def hs_gradient(row, rows):
        at = pl.ds((row - 8) * LANES, rows * LANES)
        back = jnp.concatenate([b0[at, :].astype(bf16), b1[at, :].astype(bf16)], axis=1)
        return lax.dot_general(basis, back, (((1,), (1,)), ((), ())), preferred_element_type=f32)

    def start_row(row):
        return c_ref[pl.ds(row, 32, stride=CROWS), :]

    def loop(low, high, body):
        def step(n, _):
            body(n)
            return 0

        lax.fori_loop(low, high, step, 0)

    for block in range(CROWS // 8):
        value = jnp.concatenate([start_row(block * 8 + r) for r in range(8)], axis=1)
        mix(block * 8, value, 8)
        if 1 <= block < 5:
            ms_gradient(block * 8, value)
    loop(0, IROWS, blur_row)
    loop(2, 10, back_rows)
    for block in range(1, 5):
        grad = hs_gradient(block * 8, 8)
        values = []
        for r in range(8):
            row = block * 8 + r
            now = start_row(row)
            new = now + STEP * (grad[:, r * 128 : r * 128 + 128] + g_ref[pl.ds((row - 8) * 32, 32), :])
            row_at = 16 * s - 16 + row
            new = jnp.where(in_columns & (row_at >= 0) & (row_at < 128), new, 0.0)
            c1_ref[pl.ds((row - 8) * 32, 32), :] = new
            values.append(new)
        value = jnp.concatenate(values, axis=1)
        mix(block * 8, value, 8)
        if 2 <= block < 4:
            ms_gradient(block * 8, value)
    loop(2, 8, blur_row)
    loop(4, 8, back_rows)
    place_at = lax.broadcasted_iota(jnp.int32, (LANES, LANES), 1)
    take = lax.broadcasted_iota(jnp.int32, (LANES, LANES), 0)
    shift = 4 * (take % 32) + take // 32 - 16
    order = [(place_at == shift + 64 * half) & (shift >= 0) & (shift < 64) for half in range(2)]
    order = [jnp.where(o, 1.0, 0.0).astype(bf16) for o in order]
    grads = [hs_gradient(16, 8), hs_gradient(24, 8)]
    for r in range(8):
        total = None
        for half in range(2):
            row = 8 + r + 8 * half
            at = pl.ds(row * 32, 32)
            value = c1_ref[at, :] + STEP * (grads[half][:, r * 128 : r * 128 + 128] + g_ref[at, :])
            rest = jnp.where((group >= 4) & (group < 20), value, 0.0)
            for _ in range(3):
                piece = rest.astype(bf16)
                rest = rest - piece.astype(f32)
                moved = jnp.dot(piece, order[half], preferred_element_type=f32)
                total = moved if total is None else total + moved
        out_ref[pl.ds(r, 32, stride=8), :] = total


def refine(pos, c, hp, ms):
    vmem = pl.BlockSpec(memory_space=pltpu.VMEM)
    return pl.pallas_call(
        refine_kernel,
        out_shape=jax.ShapeDtypeStruct((32 * 8, LANES), f32),
        in_specs=[pl.BlockSpec(memory_space=pltpu.SMEM), vmem, vmem, vmem],
        out_specs=vmem,
        scratch_shapes=[
            pltpu.VMEM((CROWS * LANES, LANES), f32),
            pltpu.VMEM((CROWS * LANES, LANES), f32),
            pltpu.VMEM((256, LANES), f32),
            pltpu.VMEM((256, LANES), f32),
            pltpu.VMEM((MROWS * LANES, LANES), f32),
            pltpu.VMEM((MROWS * LANES, LANES), f32),
            pltpu.VMEM((MROWS * 32, LANES), f32),
            pltpu.VMEM((MROWS * 32, LANES), f32),
            pltpu.VMEM((256, LANES), f32),
            pltpu.VMEM((256, LANES), f32),
            pltpu.VMEM((LANES, LANES), f32),
            pltpu.VMEM((LANES, LANES), f32),
        ],
        compiler_params=pltpu.CompilerParams(vmem_limit_bytes=40 * 2**20),
        cost_estimate=pl.CostEstimate(flops=400_000_000, bytes_accessed=2_000_000, transcendentals=0),
        name="refine",
    )(pos, c, hp, ms)


def pack_kernel(pos_ref, ca_ref, cb_ref, ma_ref, mb_ref, hs_ref, tiles_ref, near_ref):
    b = pos_ref[1]
    off = pos_ref[4]
    lane = lax.broadcasted_iota(jnp.int32, (1, LANES), 1)
    first = lane >= off
    block = (b + 1) // 2 - jnp.where(first, 1, 0)
    keep = (block >= 0) & (block < 8)
    source = lax.broadcasted_iota(jnp.int32, (LANES, LANES), 0)
    target = lax.broadcasted_iota(jnp.int32, (LANES, LANES), 1)
    order = jnp.where(source == (4 * (target % 32) + target // 32 + off) % LANES, 1.0, 0.0).astype(bf16)
    ms = jnp.where(first, ma_ref[...].reshape(128, LANES).astype(f32), mb_ref[...].reshape(128, LANES).astype(f32))
    ms = jnp.where(keep, ms, 0.0).astype(bf16)
    near_ref[0:128, :] = jnp.dot(ms, order, preferred_element_type=f32).astype(bf16)
    near_ref[128:192, :] = hs_ref[:, 0:128]
    near_ref[192:256, :] = hs_ref[:, 128:256]
    edge = jnp.zeros((16, LANES), f32)
    for k in range(4):
        rest = jnp.where(keep, jnp.where(first, ca_ref[k], cb_ref[k]), 0.0)
        total = None
        for _ in range(3):
            piece = rest.astype(bf16)
            rest = rest - piece.astype(f32)
            moved = jnp.dot(piece, order, preferred_element_type=f32)
            total = moved if total is None else total + moved
        for t in range(8):
            low = 16 * t - 16
            tiles_ref[t, k, 16:32] = total[low + 16 : low + 32]
            tiles_ref[t, k, 0:16] = edge if t == 0 else total[low : low + 16]
            tiles_ref[t, k, 32:48] = edge if t == 7 else total[low + 32 : low + 48]


def pack(pos, coeffs_in, ms_image, hs_rows):
    return pl.pallas_call(
        pack_kernel,
        out_shape=(
            jax.ShapeDtypeStruct((8, 4, CROWS, LANES), f32),
            jax.ShapeDtypeStruct((256, LANES), bf16),
        ),
        grid_spec=pltpu.PrefetchScalarGridSpec(
            num_scalar_prefetch=1,
            grid=(1,),
            in_specs=[
                pl.BlockSpec((4, 128, LANES), lambda i, p: (0, 0, p[2])),
                pl.BlockSpec((4, 128, LANES), lambda i, p: (0, 0, p[3])),
                pl.BlockSpec((8, 16, LANES), lambda i, p: (0, 0, p[2])),
                pl.BlockSpec((8, 16, LANES), lambda i, p: (0, 0, p[3])),
                pl.BlockSpec((64, 256), lambda i, p: (0, 0)),
            ],
            out_specs=(
                pl.BlockSpec((8, 4, CROWS, LANES), lambda i, p: (0, 0, 0, 0)),
                pl.BlockSpec((256, LANES), lambda i, p: (0, 0)),
            ),
        ),
        compiler_params=pltpu.CompilerParams(vmem_limit_bytes=32 * 2**20),
        cost_estimate=pl.CostEstimate(flops=100_000_000, bytes_accessed=1_600_000, transcendentals=0),
        name="pack",
    )(pos, coeffs_in, coeffs_in, ms_image, ms_image, hs_rows)


def spread_kernel(above_ref, own_ref, below_ref, k_ref, basis_ref, response_ref, sent_ref, ms_ref):
    for m in range(8):
        at = slice(16 * m, 16 * m + 16)
        ms_ref[32 * m : 32 * m + 8, :] = above_ref[at, :].astype(f32)[8:16]
        ms_ref[32 * m + 8 : 32 * m + 24, :] = own_ref[at, :].astype(f32)
        ms_ref[32 * m + 24 : 32 * m + 32, :] = below_ref[at, :].astype(f32)[0:8]
    lane = lax.broadcasted_iota(jnp.int32, (1, 256), 1)
    rows = []
    for i in range(IROWS):
        ref, r = (above_ref, i + 1) if i < 3 else (own_ref, i - 3) if i < 7 else (below_ref, i - 7)
        row = [ref[128 + 64 * h + 16 * r : 144 + 64 * h + 16 * r, :].astype(f32) for h in range(2)]
        rows.append(jnp.concatenate(row, axis=1))
    sent_ref[:, :, 256:384] = jnp.zeros((16, 16, 128), f32)
    for a in range(9):
        sent_ref[0, 0:14, 256 + 9 * a : 265 + 9 * a] = k_ref[:, a, :]
    sent_ref[0, 0:14, 337:369] = basis_ref[...].astype(f32)
    sent_ref[0, 0:14, 369:377] = response_ref[...].astype(f32).T
    params = sent_ref[0, :, 256:384]
    for t in range(16):
        total = jnp.zeros((16, 256), f32)
        for i in range(IROWS):
            moved = pltpu.roll(rows[i], (24 * i + 3 - 16 * t) % 256, 1)
            total = jnp.where((lane >= 24 * i) & (lane < 24 * i + 24), moved, total)
        sent_ref[t, :, 0:256] = total
        if t:
            sent_ref[t, :, 256:384] = params


def spread(above, own, below, kernels, basis, response):
    vmem = pl.BlockSpec(memory_space=pltpu.VMEM)
    return pl.pallas_call(
        spread_kernel,
        out_shape=(
            jax.ShapeDtypeStruct((16, 16, 384), f32),
            jax.ShapeDtypeStruct((8 * MROWS, LANES), f32),
        ),
        in_specs=[vmem] * 6,
        out_specs=(vmem, vmem),
        compiler_params=pltpu.CompilerParams(vmem_limit_bytes=16 * 2**20),
        cost_estimate=pl.CostEstimate(flops=1_000_000, bytes_accessed=1_000_000, transcendentals=0),
        name="spread",
    )(above, own, below, kernels, basis, response)


def place_kernel(g_ref, out_ref):
    lane = lax.broadcasted_iota(jnp.int32, (1, LANES), 1)
    low = lane < 64
    for s in range(8):
        for j in range(8):
            even = g_ref[2 * j, s, 0]
            odd = g_ref[2 * j + 1, s, 0]
            at = slice(j * 128, j * 128 + 128)
            out_ref[0, 16 * s : 16 * s + 8, at] = jnp.where(low, even, pltpu.roll(odd, 64, 1))
            out_ref[0, 16 * s + 8 : 16 * s + 16, at] = jnp.where(low, pltpu.roll(even, 64, 1), odd)


def place(gathered):
    return pl.pallas_call(
        place_kernel,
        out_shape=jax.ShapeDtypeStruct((4, 128, 1024), f32),
        grid=(4,),
        in_specs=[pl.BlockSpec((16, 8, 1, 8, LANES), lambda k: (0, 0, k, 0, 0))],
        out_specs=pl.BlockSpec((1, 128, 1024), lambda k: (k, 0, 0)),
        compiler_params=pltpu.CompilerParams(vmem_limit_bytes=32 * 2**20),
        name="place",
    )(gathered)


def per_device(coeffs_in, basis, kernels, response, hs_image, ms_image):
    s = lax.axis_index("sub").astype(jnp.int32)
    b = lax.axis_index("band").astype(jnp.int32)
    at = (b + 1) // 2 - 1
    off = jnp.where(b % 2 == 0, 112, 48)
    pos = jnp.stack([s, b, jnp.maximum(at, 0), jnp.minimum(at + 1, 7), off]).astype(jnp.int32)
    hs_rows = jnp.pad(hs_image.transpose(1, 0, 2), ((0, 0), (0, 2), (0, 0))).reshape(64, 256)
    tiles, own = pack(pos, coeffs_in, ms_image, hs_rows)
    above = lax.ppermute(own, "sub", [(i, i + 1) for i in range(7)])
    below = lax.ppermute(own, "sub", [(i + 1, i) for i in range(7)])
    sent, ms = spread(above, own, below, kernels, basis, response)
    hp = lax.all_to_all(sent, "band", split_axis=0, concat_axis=0, tiled=True).reshape(256, 384)
    c = lax.all_to_all(tiles, "sub", split_axis=0, concat_axis=0, tiled=True).reshape(32 * CROWS, LANES)
    new = refine(pos, c, hp, ms)
    owned = lax.all_to_all(new.reshape(8, 4, 8, LANES), "sub", split_axis=0, concat_axis=0, tiled=True)
    copies = jnp.broadcast_to(owned[None], (16,) + owned.shape)
    gathered = lax.all_to_all(copies, "band", split_axis=0, concat_axis=0, tiled=True)
    return place(gathered)


def solution(mesh):
    return jax.shard_map(
        per_device,
        mesh=mesh,
        in_specs=(
            P("sub", None, None),
            P("band", None),
            P("band", None, None),
            P(None, "band"),
            P("band", "sub", None),
            P(None, "sub", None),
        ),
        out_specs=P("sub", None, None),
        check_vma=False,
    )
```

```python
import functools

import jax
import jax.numpy as jnp
from jax import lax
from jax.experimental import pallas as pl
from jax.experimental.pallas import tpu as pltpu
from jax.sharding import PartitionSpec as P

STEP = 0.15
TR, TC = 16, 64
TAPS = 9
LANES = 128
CROWS = 48
MROWS = 32
IROWS = 10
JCOLS = 24
ROWS_LO, COLS_LO = 32, 256
f32 = jnp.float32
bf16 = jnp.bfloat16


def rounded(value):
    return value.astype(bf16).astype(f32)


def refine_kernel(pos_ref, c_ref, hp_ref, ms_ref, out_ref, m0, m1, f0, f1, b0, b1, c1_ref, g_ref, hs0, hs1, w0, w1):
    s = pos_ref[0]
    b = pos_ref[1]
    m = (m0, m1)
    f = (f0, f1)
    bk = (b0, b1)
    hst = (hs0, hs1)
    w = (w0, w1)
    for h in range(2):
        part = hp_ref[h * 128 : h * 128 + 128, :]
        for piece in range(2):
            hst[h][piece * 128 : piece * 128 + 128, :] = part[:, piece * 128 : piece * 128 + 128].T
        w[h][...] = part[:, 256:384].T
    basis = jnp.concatenate([w0[81:113, :], w1[81:113, :]], axis=1).astype(bf16)
    response = jnp.concatenate([w0[113:121, :], w1[113:121, :]], axis=1).astype(bf16)
    combined = lax.dot_general(response, basis, (((1,), (1,)), ((), ())), preferred_element_type=f32).astype(bf16)
    lane = lax.broadcasted_iota(jnp.int32, (1, LANES), 1)
    group = lane % 32
    column = 64 * b - 16 + 4 * group + lane // 32
    in_columns = (column >= 0) & (column < 1024) & (group >= 2) & (group < 22)

    def mix(row, value, rows):
        mixed = lax.dot_general(value.astype(bf16), basis, (((0,), (0,)), ((), ())), preferred_element_type=f32)
        mixed = rounded(mixed)
        at = pl.ds(pl.multiple_of(row * LANES, LANES), rows * LANES)
        for h in range(2):
            m[h][at, :] = mixed[:, h * 128 : h * 128 + 128]

    def ms_gradient(row, block):
        predicted = jnp.dot(combined, block.astype(bf16), preferred_element_type=f32)
        seen = jnp.concatenate([ms_ref[pl.ds(row - 8 + r, 8, stride=MROWS), :] for r in range(8)], axis=1)
        misfit = (seen - predicted).astype(bf16)
        grad = lax.dot_general(combined, misfit, (((0,), (0,)), ((), ())), preferred_element_type=f32)
        for r in range(8):
            g_ref[pl.ds((row - 8 + r) * 32, 32), :] = grad[:, r * 128 : r * 128 + 128]

    def blur_row(n):
        g = lax.broadcasted_iota(jnp.int32, (JCOLS, LANES), 0)
        i_at = 4 * s + n - 3
        j_at = 16 * b + g - 3
        inside = (i_at >= 0) & (i_at < ROWS_LO) & (j_at >= 0) & (j_at < COLS_LO)
        for h in range(2):
            acc = [None, None, None]
            for a in range(TAPS):
                for q in range(4):
                    at = pl.multiple_of((4 * n + a) * LANES + 32 * q, 32)
                    x = m[h][pl.ds(at, JCOLS), :]
                    for d in range(3):
                        if 4 * d + q > 8:
                            continue
                        tap = a * 9 + 4 * d + q
                        term = w[h][tap : tap + 1, :] * x
                        acc[d] = term if acc[d] is None else acc[d] + term
            blurred = acc[0] + pltpu.roll(acc[1], JCOLS - 1, 0) + pltpu.roll(acc[2], JCOLS - 2, 0)
            seen = hst[h][pl.ds(pl.multiple_of(n * JCOLS, 8), JCOLS), :]
            f[h][pl.ds(pl.multiple_of(8 + n * JCOLS, 8), JCOLS), :] = jnp.where(inside, seen - blurred, 0.0)

    def back_rows(u):
        for h in range(2):
            win = [[f[h][pl.ds(8 + (u - t) * JCOLS - tt, JCOLS), :] for tt in range(3)] for t in range(3)]
            for p in range(4):
                for q in range(4):
                    total = None
                    for t in range(3):
                        for tt in range(3):
                            if p + 4 * t > 8 or q + 4 * tt > 8:
                                continue
                            tap = (p + 4 * t) * 9 + q + 4 * tt
                            term = w[h][tap : tap + 1, :] * win[t][tt]
                            total = term if total is None else total + term
                    at = pl.multiple_of((4 * u - 8 + p) * LANES + 32 * q, 32)
                    bk[h][pl.ds(at, JCOLS), :] = rounded(total)

    def hs_gradient(row, rows):
        at = pl.ds((row - 8) * LANES, rows * LANES)
        back = jnp.concatenate([b0[at, :].astype(bf16), b1[at, :].astype(bf16)], axis=1)
        return lax.dot_general(basis, back, (((1,), (1,)), ((), ())), preferred_element_type=f32)

    def start_row(row):
        return c_ref[pl.ds(row, 32, stride=CROWS), :]

    def loop(low, high, body):
        def step(n, _):
            body(n)
            return 0

        lax.fori_loop(low, high, step, 0)

    for block in range(CROWS // 8):
        value = jnp.concatenate([start_row(block * 8 + r) for r in range(8)], axis=1)
        mix(block * 8, value, 8)
        if 1 <= block < 5:
            ms_gradient(block * 8, value)
    loop(0, IROWS, blur_row)
    loop(2, 10, back_rows)
    for block in range(1, 5):
        grad = hs_gradient(block * 8, 8)
        values = []
        for r in range(8):
            row = block * 8 + r
            now = start_row(row)
            new = now + STEP * (grad[:, r * 128 : r * 128 + 128] + g_ref[pl.ds((row - 8) * 32, 32), :])
            row_at = 16 * s - 16 + row
            new = jnp.where(in_columns & (row_at >= 0) & (row_at < 128), new, 0.0)
            c1_ref[pl.ds((row - 8) * 32, 32), :] = new
            values.append(new)
        value = jnp.concatenate(values, axis=1)
        mix(block * 8, value, 8)
        if 2 <= block < 4:
            ms_gradient(block * 8, value)
    loop(2, 8, blur_row)
    loop(4, 8, back_rows)
    place_at = lax.broadcasted_iota(jnp.int32, (LANES, LANES), 1)
    take = lax.broadcasted_iota(jnp.int32, (LANES, LANES), 0)
    shift = 4 * (take % 32) + take // 32 - 16
    order = [(place_at == shift + 64 * half) & (shift >= 0) & (shift < 64) for half in range(2)]
    order = [jnp.where(o, 1.0, 0.0).astype(bf16) for o in order]
    grads = [hs_gradient(16, 8), hs_gradient(24, 8)]
    for r in range(8):
        total = None
        for half in range(2):
            row = 8 + r + 8 * half
            at = pl.ds(row * 32, 32)
            value = c1_ref[at, :] + STEP * (grads[half][:, r * 128 : r * 128 + 128] + g_ref[at, :])
            rest = jnp.where((group >= 4) & (group < 20), value, 0.0)
            for _ in range(3):
                piece = rest.astype(bf16)
                rest = rest - piece.astype(f32)
                moved = jnp.dot(piece, order[half], preferred_element_type=f32)
                total = moved if total is None else total + moved
        out_ref[pl.ds(r, 32, stride=8), :] = total


def refine(pos, c, hp, ms):
    vmem = pl.BlockSpec(memory_space=pltpu.VMEM)
    return pl.pallas_call(
        refine_kernel,
        out_shape=jax.ShapeDtypeStruct((32 * 8, LANES), f32),
        in_specs=[pl.BlockSpec(memory_space=pltpu.SMEM), vmem, vmem, vmem],
        out_specs=vmem,
        scratch_shapes=[
            pltpu.VMEM((CROWS * LANES, LANES), f32),
            pltpu.VMEM((CROWS * LANES, LANES), f32),
            pltpu.VMEM((256, LANES), f32),
            pltpu.VMEM((256, LANES), f32),
            pltpu.VMEM((MROWS * LANES, LANES), f32),
            pltpu.VMEM((MROWS * LANES, LANES), f32),
            pltpu.VMEM((MROWS * 32, LANES), f32),
            pltpu.VMEM((MROWS * 32, LANES), f32),
            pltpu.VMEM((256, LANES), f32),
            pltpu.VMEM((256, LANES), f32),
            pltpu.VMEM((LANES, LANES), f32),
            pltpu.VMEM((LANES, LANES), f32),
        ],
        compiler_params=pltpu.CompilerParams(vmem_limit_bytes=40 * 2**20),
        cost_estimate=pl.CostEstimate(flops=400_000_000, bytes_accessed=2_000_000, transcendentals=0),
        name="refine",
    )(pos, c, hp, ms)


def pack_kernel(pos_ref, ca_ref, cb_ref, ma_ref, mb_ref, hs_ref, tiles_ref, near_ref):
    b = pos_ref[1]
    off = pos_ref[4]
    lane = lax.broadcasted_iota(jnp.int32, (1, LANES), 1)
    first = lane >= off
    block = (b + 1) // 2 - jnp.where(first, 1, 0)
    keep = (block >= 0) & (block < 8)
    source = lax.broadcasted_iota(jnp.int32, (LANES, LANES), 0)
    target = lax.broadcasted_iota(jnp.int32, (LANES, LANES), 1)
    order = jnp.where(source == (4 * (target % 32) + target // 32 + off) % LANES, 1.0, 0.0).astype(bf16)
    ms = jnp.where(first, ma_ref[...].reshape(128, LANES).astype(f32), mb_ref[...].reshape(128, LANES).astype(f32))
    ms = jnp.where(keep, ms, 0.0).astype(bf16)
    near_ref[0:128, :] = jnp.dot(ms, order, preferred_element_type=f32).astype(bf16)
    near_ref[128:192, :] = hs_ref[:, 0:128]
    near_ref[192:256, :] = hs_ref[:, 128:256]
    edge = jnp.zeros((16, LANES), f32)
    for k in range(4):
        rest = jnp.where(keep, jnp.where(first, ca_ref[k], cb_ref[k]), 0.0)
        total = None
        for _ in range(3):
            piece = rest.astype(bf16)
            rest = rest - piece.astype(f32)
            moved = jnp.dot(piece, order, preferred_element_type=f32)
            total = moved if total is None else total + moved
        for t in range(8):
            low = 16 * t - 16
            tiles_ref[t, k, 16:32] = total[low + 16 : low + 32]
            tiles_ref[t, k, 0:16] = edge if t == 0 else total[low : low + 16]
            tiles_ref[t, k, 32:48] = edge if t == 7 else total[low + 32 : low + 48]


def pack(pos, coeffs_in, ms_image, hs_rows):
    return pl.pallas_call(
        pack_kernel,
        out_shape=(
            jax.ShapeDtypeStruct((8, 4, CROWS, LANES), f32),
            jax.ShapeDtypeStruct((256, LANES), bf16),
        ),
        grid_spec=pltpu.PrefetchScalarGridSpec(
            num_scalar_prefetch=1,
            grid=(1,),
            in_specs=[
                pl.BlockSpec((4, 128, LANES), lambda i, p: (0, 0, p[2])),
                pl.BlockSpec((4, 128, LANES), lambda i, p: (0, 0, p[3])),
                pl.BlockSpec((8, 16, LANES), lambda i, p: (0, 0, p[2])),
                pl.BlockSpec((8, 16, LANES), lambda i, p: (0, 0, p[3])),
                pl.BlockSpec((64, 256), lambda i, p: (0, 0)),
            ],
            out_specs=(
                pl.BlockSpec((8, 4, CROWS, LANES), lambda i, p: (0, 0, 0, 0)),
                pl.BlockSpec((256, LANES), lambda i, p: (0, 0)),
            ),
        ),
        compiler_params=pltpu.CompilerParams(vmem_limit_bytes=60 * 2**20),
        cost_estimate=pl.CostEstimate(flops=100_000_000, bytes_accessed=1_600_000, transcendentals=0),
        name="pack",
    )(pos, coeffs_in, coeffs_in, ms_image, ms_image, hs_rows)


def spread_kernel(above_ref, own_ref, below_ref, k_ref, basis_ref, response_ref, sent_ref, ms_ref):
    for m in range(8):
        at = slice(16 * m, 16 * m + 16)
        ms_ref[32 * m : 32 * m + 8, :] = above_ref[at, :].astype(f32)[8:16]
        ms_ref[32 * m + 8 : 32 * m + 24, :] = own_ref[at, :].astype(f32)
        ms_ref[32 * m + 24 : 32 * m + 32, :] = below_ref[at, :].astype(f32)[0:8]
    lane = lax.broadcasted_iota(jnp.int32, (1, 256), 1)
    rows = []
    for i in range(IROWS):
        ref, r = (above_ref, i + 1) if i < 3 else (own_ref, i - 3) if i < 7 else (below_ref, i - 7)
        row = [ref[128 + 64 * h + 16 * r : 144 + 64 * h + 16 * r, :].astype(f32) for h in range(2)]
        rows.append(jnp.concatenate(row, axis=1))
    sent_ref[:, :, 256:384] = jnp.zeros((16, 16, 128), f32)
    for a in range(9):
        sent_ref[0, 0:14, 256 + 9 * a : 265 + 9 * a] = k_ref[:, a, :]
    sent_ref[0, 0:14, 337:369] = basis_ref[...].astype(f32)
    sent_ref[0, 0:14, 369:377] = response_ref[...].astype(f32).T
    params = sent_ref[0, :, 256:384]
    for t in range(16):
        total = jnp.zeros((16, 256), f32)
        for i in range(IROWS):
            moved = pltpu.roll(rows[i], (24 * i + 3 - 16 * t) % 256, 1)
            total = jnp.where((lane >= 24 * i) & (lane < 24 * i + 24), moved, total)
        sent_ref[t, :, 0:256] = total
        if t:
            sent_ref[t, :, 256:384] = params


def spread(above, own, below, kernels, basis, response):
    vmem = pl.BlockSpec(memory_space=pltpu.VMEM)
    return pl.pallas_call(
        spread_kernel,
        out_shape=(
            jax.ShapeDtypeStruct((16, 16, 384), f32),
            jax.ShapeDtypeStruct((8 * MROWS, LANES), f32),
        ),
        in_specs=[vmem] * 6,
        out_specs=(vmem, vmem),
        compiler_params=pltpu.CompilerParams(vmem_limit_bytes=16 * 2**20),
        cost_estimate=pl.CostEstimate(flops=1_000_000, bytes_accessed=1_000_000, transcendentals=0),
        name="spread",
    )(above, own, below, kernels, basis, response)


def place_kernel(g_ref, out_ref):
    lane = lax.broadcasted_iota(jnp.int32, (1, LANES), 1)
    low = lane < 64
    for s in range(8):
        for j in range(8):
            even = g_ref[2 * j, s, 0]
            odd = g_ref[2 * j + 1, s, 0]
            at = slice(j * 128, j * 128 + 128)
            out_ref[0, 16 * s : 16 * s + 8, at] = jnp.where(low, even, pltpu.roll(odd, 64, 1))
            out_ref[0, 16 * s + 8 : 16 * s + 16, at] = jnp.where(low, pltpu.roll(even, 64, 1), odd)


def place(gathered):
    return pl.pallas_call(
        place_kernel,
        out_shape=jax.ShapeDtypeStruct((4, 128, 1024), f32),
        grid=(4,),
        in_specs=[pl.BlockSpec((16, 8, 1, 8, LANES), lambda k: (0, 0, k, 0, 0))],
        out_specs=pl.BlockSpec((1, 128, 1024), lambda k: (k, 0, 0)),
        compiler_params=pltpu.CompilerParams(vmem_limit_bytes=32 * 2**20),
        name="place",
    )(gathered)


def per_device(coeffs_in, basis, kernels, response, hs_image, ms_image):
    s = lax.axis_index("sub").astype(jnp.int32)
    b = lax.axis_index("band").astype(jnp.int32)
    at = (b + 1) // 2 - 1
    off = jnp.where(b % 2 == 0, 112, 48)
    pos = jnp.stack([s, b, jnp.maximum(at, 0), jnp.minimum(at + 1, 7), off]).astype(jnp.int32)
    hs_rows = jnp.pad(hs_image.transpose(1, 0, 2), ((0, 0), (0, 2), (0, 0))).reshape(64, 256)
    tiles, own = pack(pos, coeffs_in, ms_image, hs_rows)
    c = lax.all_to_all(tiles, "sub", split_axis=0, concat_axis=0, tiled=True).reshape(32 * CROWS, LANES)
    above = lax.ppermute(own, "sub", [(i, i + 1) for i in range(7)])
    below = lax.ppermute(own, "sub", [(i + 1, i) for i in range(7)])
    sent, ms = spread(above, own, below, kernels, basis, response)
    sent, c = lax.optimization_barrier((sent, c))
    hp = lax.all_to_all(sent, "band", split_axis=0, concat_axis=0, tiled=True).reshape(256, 384)
    new = refine(pos, c, hp, ms)
    owned = lax.all_to_all(new.reshape(8, 4, 8, LANES), "sub", split_axis=0, concat_axis=0, tiled=True)
    copies = jnp.broadcast_to(owned[None], (16,) + owned.shape)
    gathered = lax.all_to_all(copies, "band", split_axis=0, concat_axis=0, tiled=True)
    return place(gathered)


def solution(mesh):
    return jax.shard_map(
        per_device,
        mesh=mesh,
        in_specs=(
            P("sub", None, None),
            P("band", None),
            P("band", None, None),
            P(None, "band"),
            P("band", "sub", None),
            P(None, "sub", None),
        ),
        out_specs=P("sub", None, None),
        check_vma=False,
    )
```

```python
import functools

import jax
import jax.numpy as jnp
from jax import lax
from jax.experimental import pallas as pl
from jax.experimental.pallas import tpu as pltpu
from jax.sharding import PartitionSpec as P

STEP = 0.15
TR, TC = 16, 64
TAPS = 9
LANES = 128
CROWS = 48
MROWS = 32
IROWS = 10
JCOLS = 24
ROWS_LO, COLS_LO = 32, 256
f32 = jnp.float32
bf16 = jnp.bfloat16


def rounded(value):
    return value.astype(bf16).astype(f32)


def refine_kernel(pos_ref, *refs):
    tiles = refs[:8]
    hp_ref, ms_ref, out_ref, c_ref, m0, m1, f0, f1, b0, b1, c1_ref, g_ref, hs0, hs1, w0, w1 = refs[8:]
    s = pos_ref[0] // 16
    b = pos_ref[0] % 16
    for d in range(8):
        at = pl.multiple_of((s + 8 - d) % 8 * (4 * CROWS), 4 * CROWS)
        c_ref[pl.ds(at, 4 * CROWS), :] = tiles[d][...].reshape(4 * CROWS, LANES)
    m = (m0, m1)
    f = (f0, f1)
    bk = (b0, b1)
    hst = (hs0, hs1)
    w = (w0, w1)
    for h in range(2):
        part = hp_ref[h * 128 : h * 128 + 128, :]
        for piece in range(2):
            hst[h][piece * 128 : piece * 128 + 128, :] = part[:, piece * 128 : piece * 128 + 128].T
        w[h][...] = part[:, 256:384].T
    basis = jnp.concatenate([w0[81:113, :], w1[81:113, :]], axis=1).astype(bf16)
    response = jnp.concatenate([w0[113:121, :], w1[113:121, :]], axis=1).astype(bf16)
    combined = lax.dot_general(response, basis, (((1,), (1,)), ((), ())), preferred_element_type=f32).astype(bf16)
    lane = lax.broadcasted_iota(jnp.int32, (1, LANES), 1)
    group = lane % 32
    column = 64 * b - 16 + 4 * group + lane // 32
    in_columns = (column >= 0) & (column < 1024) & (group >= 2) & (group < 22)

    def mix(row, value, rows):
        mixed = lax.dot_general(value.astype(bf16), basis, (((0,), (0,)), ((), ())), preferred_element_type=f32)
        mixed = rounded(mixed)
        at = pl.ds(pl.multiple_of(row * LANES, LANES), rows * LANES)
        for h in range(2):
            m[h][at, :] = mixed[:, h * 128 : h * 128 + 128]

    def ms_gradient(row, block):
        predicted = jnp.dot(combined, block.astype(bf16), preferred_element_type=f32)
        seen = jnp.concatenate([ms_ref[pl.ds(row - 8 + r, 8, stride=MROWS), :] for r in range(8)], axis=1)
        misfit = (seen - predicted).astype(bf16)
        grad = lax.dot_general(combined, misfit, (((0,), (0,)), ((), ())), preferred_element_type=f32)
        for r in range(8):
            g_ref[pl.ds((row - 8 + r) * 32, 32), :] = grad[:, r * 128 : r * 128 + 128]

    def blur_row(n):
        g = lax.broadcasted_iota(jnp.int32, (JCOLS, LANES), 0)
        i_at = 4 * s + n - 3
        j_at = 16 * b + g - 3
        inside = (i_at >= 0) & (i_at < ROWS_LO) & (j_at >= 0) & (j_at < COLS_LO)
        for h in range(2):
            acc = [None, None, None]
            for a in range(TAPS):
                for q in range(4):
                    at = pl.multiple_of((4 * n + a) * LANES + 32 * q, 32)
                    x = m[h][pl.ds(at, JCOLS), :]
                    for d in range(3):
                        if 4 * d + q > 8:
                            continue
                        tap = a * 9 + 4 * d + q
                        term = w[h][tap : tap + 1, :] * x
                        acc[d] = term if acc[d] is None else acc[d] + term
            blurred = acc[0] + pltpu.roll(acc[1], JCOLS - 1, 0) + pltpu.roll(acc[2], JCOLS - 2, 0)
            seen = hst[h][pl.ds(pl.multiple_of(n * JCOLS, 8), JCOLS), :]
            f[h][pl.ds(pl.multiple_of(8 + n * JCOLS, 8), JCOLS), :] = jnp.where(inside, seen - blurred, 0.0)

    def back_rows(u):
        for h in range(2):
            win = [[f[h][pl.ds(8 + (u - t) * JCOLS - tt, JCOLS), :] for tt in range(3)] for t in range(3)]
            for p in range(4):
                for q in range(4):
                    total = None
                    for t in range(3):
                        for tt in range(3):
                            if p + 4 * t > 8 or q + 4 * tt > 8:
                                continue
                            tap = (p + 4 * t) * 9 + q + 4 * tt
                            term = w[h][tap : tap + 1, :] * win[t][tt]
                            total = term if total is None else total + term
                    at = pl.multiple_of((4 * u - 8 + p) * LANES + 32 * q, 32)
                    bk[h][pl.ds(at, JCOLS), :] = rounded(total)

    def hs_gradient(row, rows):
        at = pl.ds((row - 8) * LANES, rows * LANES)
        back = jnp.concatenate([b0[at, :].astype(bf16), b1[at, :].astype(bf16)], axis=1)
        return lax.dot_general(basis, back, (((1,), (1,)), ((), ())), preferred_element_type=f32)

    def start_row(row):
        return c_ref[pl.ds(row, 32, stride=CROWS), :]

    def loop(low, high, body):
        def step(n, _):
            body(n)
            return 0

        lax.fori_loop(low, high, step, 0)

    for block in range(CROWS // 8):
        value = jnp.concatenate([start_row(block * 8 + r) for r in range(8)], axis=1)
        mix(block * 8, value, 8)
        if 1 <= block < 5:
            ms_gradient(block * 8, value)
    loop(0, IROWS, blur_row)
    loop(2, 10, back_rows)
    for block in range(1, 5):
        grad = hs_gradient(block * 8, 8)
        values = []
        for r in range(8):
            row = block * 8 + r
            now = start_row(row)
            new = now + STEP * (grad[:, r * 128 : r * 128 + 128] + g_ref[pl.ds((row - 8) * 32, 32), :])
            row_at = 16 * s - 16 + row
            new = jnp.where(in_columns & (row_at >= 0) & (row_at < 128), new, 0.0)
            c1_ref[pl.ds((row - 8) * 32, 32), :] = new
            values.append(new)
        value = jnp.concatenate(values, axis=1)
        mix(block * 8, value, 8)
        if 2 <= block < 4:
            ms_gradient(block * 8, value)
    loop(2, 8, blur_row)
    loop(4, 8, back_rows)
    place_at = lax.broadcasted_iota(jnp.int32, (LANES, LANES), 1)
    take = lax.broadcasted_iota(jnp.int32, (LANES, LANES), 0)
    shift = 4 * (take % 32) + take // 32 - 16
    order = [(place_at == shift + 64 * half) & (shift >= 0) & (shift < 64) for half in range(2)]
    order = [jnp.where(o, 1.0, 0.0).astype(bf16) for o in order]
    grads = [hs_gradient(16, 8), hs_gradient(24, 8)]
    for r in range(8):
        total = None
        for half in range(2):
            row = 8 + r + 8 * half
            at = pl.ds(row * 32, 32)
            value = c1_ref[at, :] + STEP * (grads[half][:, r * 128 : r * 128 + 128] + g_ref[at, :])
            rest = jnp.where((group >= 4) & (group < 20), value, 0.0)
            for _ in range(3):
                piece = rest.astype(bf16)
                rest = rest - piece.astype(f32)
                moved = jnp.dot(piece, order[half], preferred_element_type=f32)
                total = moved if total is None else total + moved
        out_ref[pl.ds(r, 32, stride=8), :] = total


def refine(pos, tiles, hp, ms):
    vmem = pl.BlockSpec(memory_space=pltpu.VMEM)
    return pl.pallas_call(
        refine_kernel,
        out_shape=jax.ShapeDtypeStruct((32 * 8, LANES), f32),
        in_specs=[pl.BlockSpec(memory_space=pltpu.SMEM)] + [vmem] * 10,
        out_specs=vmem,
        scratch_shapes=[
            pltpu.VMEM((32 * CROWS, LANES), f32),
            pltpu.VMEM((CROWS * LANES, LANES), f32),
            pltpu.VMEM((CROWS * LANES, LANES), f32),
            pltpu.VMEM((256, LANES), f32),
            pltpu.VMEM((256, LANES), f32),
            pltpu.VMEM((MROWS * LANES, LANES), f32),
            pltpu.VMEM((MROWS * LANES, LANES), f32),
            pltpu.VMEM((MROWS * 32, LANES), f32),
            pltpu.VMEM((MROWS * 32, LANES), f32),
            pltpu.VMEM((256, LANES), f32),
            pltpu.VMEM((256, LANES), f32),
            pltpu.VMEM((LANES, LANES), f32),
            pltpu.VMEM((LANES, LANES), f32),
        ],
        compiler_params=pltpu.CompilerParams(vmem_limit_bytes=40 * 2**20),
        cost_estimate=pl.CostEstimate(flops=400_000_000, bytes_accessed=2_000_000, transcendentals=0),
        name="refine",
    )(pos, *tiles, hp, ms)


def pack_kernel(pos_ref, ca_ref, cb_ref, ma_ref, mb_ref, hs_ref, near_ref, *rest_refs):
    tile_refs = rest_refs[:8]
    wide_ref = rest_refs[8]
    s = pos_ref[0] // 16
    b = pos_ref[0] % 16
    off = jnp.where(b % 2 == 0, 112, 48)
    lane = lax.broadcasted_iota(jnp.int32, (1, LANES), 1)
    first = lane >= off
    block = (b + 1) // 2 - jnp.where(first, 1, 0)
    keep = (block >= 0) & (block < 8)
    source = lax.broadcasted_iota(jnp.int32, (LANES, LANES), 0)
    target = lax.broadcasted_iota(jnp.int32, (LANES, LANES), 1)
    order = jnp.where(source == (4 * (target % 32) + target // 32 + off) % LANES, 1.0, 0.0).astype(bf16)
    ms = jnp.where(first, ma_ref[...].reshape(128, LANES).astype(f32), mb_ref[...].reshape(128, LANES).astype(f32))
    ms = jnp.where(keep, ms, 0.0).astype(bf16)
    near_ref[0:128, :] = jnp.dot(ms, order, preferred_element_type=f32).astype(bf16)
    hs = hs_ref[...].astype(f32)
    for i in range(4):
        row = jnp.concatenate([hs[:, i, :], jnp.zeros((2, 256), f32)], axis=0).astype(bf16)
        near_ref[128 + 16 * i : 144 + 16 * i, :] = row[:, 0:128]
        near_ref[192 + 16 * i : 208 + 16 * i, :] = row[:, 128:256]
    edge = jnp.zeros((16, LANES), f32)
    for k in range(4):
        rest = jnp.where(keep, jnp.where(first, ca_ref[k], cb_ref[k]), 0.0)
        total = None
        for _ in range(3):
            piece = rest.astype(bf16)
            rest = rest - piece.astype(f32)
            moved = jnp.dot(piece, order, preferred_element_type=f32)
            total = moved if total is None else total + moved
        wide_ref[k, 0:16] = edge
        wide_ref[k, 16:144] = total
        wide_ref[k, 144:160] = edge
    for d in range(8):
        t = (s + d) % 8
        at = pl.ds(pl.multiple_of(16 * t, 16), CROWS)
        for k in range(4):
            tile_refs[d][k] = wide_ref[k, at, :]


def pack(pos, coeffs_in, ms_image, hs_image):
    def low(i, p):
        return (0, 0, jnp.maximum((p[0] % 16 + 1) // 2 - 1, 0))

    def high(i, p):
        return (0, 0, jnp.minimum((p[0] % 16 + 1) // 2, 7))

    tile = jax.ShapeDtypeStruct((4, CROWS, LANES), f32)
    return pl.pallas_call(
        pack_kernel,
        out_shape=(jax.ShapeDtypeStruct((256, LANES), bf16),) + (tile,) * 8,
        grid_spec=pltpu.PrefetchScalarGridSpec(
            num_scalar_prefetch=1,
            grid=(1,),
            in_specs=[
                pl.BlockSpec((4, 128, LANES), low),
                pl.BlockSpec((4, 128, LANES), high),
                pl.BlockSpec((8, 16, LANES), low),
                pl.BlockSpec((8, 16, LANES), high),
                pl.BlockSpec((14, 4, 256), lambda i, p: (0, 0, 0)),
            ],
            out_specs=(pl.BlockSpec((256, LANES), lambda i, p: (0, 0)),)
            + (pl.BlockSpec((4, CROWS, LANES), lambda i, p: (0, 0, 0)),) * 8,
            scratch_shapes=[pltpu.VMEM((4, 160, LANES), f32)],
        ),
        compiler_params=pltpu.CompilerParams(vmem_limit_bytes=60 * 2**20),
        cost_estimate=pl.CostEstimate(flops=100_000_000, bytes_accessed=1_600_000, transcendentals=0),
        name="pack",
    )(pos, coeffs_in, coeffs_in, ms_image, ms_image, hs_image)


def spread_kernel(above_ref, own_ref, below_ref, k_ref, basis_ref, response_ref, sent_ref, ms_ref):
    for m in range(8):
        at = slice(16 * m, 16 * m + 16)
        ms_ref[32 * m : 32 * m + 8, :] = above_ref[at, :].astype(f32)[8:16]
        ms_ref[32 * m + 8 : 32 * m + 24, :] = own_ref[at, :].astype(f32)
        ms_ref[32 * m + 24 : 32 * m + 32, :] = below_ref[at, :].astype(f32)[0:8]
    lane = lax.broadcasted_iota(jnp.int32, (1, 256), 1)
    rows = []
    for i in range(IROWS):
        ref, r = (above_ref, i + 1) if i < 3 else (own_ref, i - 3) if i < 7 else (below_ref, i - 7)
        row = [ref[128 + 64 * h + 16 * r : 144 + 64 * h + 16 * r, :].astype(f32) for h in range(2)]
        rows.append(jnp.concatenate(row, axis=1))
    sent_ref[:, :, 256:384] = jnp.zeros((16, 16, 128), f32)
    for a in range(9):
        sent_ref[0, 0:14, 256 + 9 * a : 265 + 9 * a] = k_ref[:, a, :]
    sent_ref[0, 0:14, 337:369] = basis_ref[...].astype(f32)
    sent_ref[0, 0:14, 369:377] = response_ref[...].astype(f32).T
    params = sent_ref[0, :, 256:384]
    for t in range(16):
        total = jnp.zeros((16, 256), f32)
        for i in range(IROWS):
            moved = pltpu.roll(rows[i], (24 * i + 3 - 16 * t) % 256, 1)
            total = jnp.where((lane >= 24 * i) & (lane < 24 * i + 24), moved, total)
        sent_ref[t, :, 0:256] = total
        if t:
            sent_ref[t, :, 256:384] = params


def spread(above, own, below, kernels, basis, response):
    vmem = pl.BlockSpec(memory_space=pltpu.VMEM)
    return pl.pallas_call(
        spread_kernel,
        out_shape=(
            jax.ShapeDtypeStruct((16, 16, 384), f32),
            jax.ShapeDtypeStruct((8 * MROWS, LANES), f32),
        ),
        in_specs=[vmem] * 6,
        out_specs=(vmem, vmem),
        compiler_params=pltpu.CompilerParams(vmem_limit_bytes=16 * 2**20),
        cost_estimate=pl.CostEstimate(flops=1_000_000, bytes_accessed=1_000_000, transcendentals=0),
        name="spread",
    )(above, own, below, kernels, basis, response)


def place_kernel(g_ref, out_ref):
    lane = lax.broadcasted_iota(jnp.int32, (1, LANES), 1)
    low = lane < 64
    for s in range(8):
        for j in range(8):
            even = g_ref[2 * j, s, 0]
            odd = g_ref[2 * j + 1, s, 0]
            at = slice(j * 128, j * 128 + 128)
            out_ref[0, 16 * s : 16 * s + 8, at] = jnp.where(low, even, pltpu.roll(odd, 64, 1))
            out_ref[0, 16 * s + 8 : 16 * s + 16, at] = jnp.where(low, pltpu.roll(even, 64, 1), odd)


def place(gathered):
    return pl.pallas_call(
        place_kernel,
        out_shape=jax.ShapeDtypeStruct((4, 128, 1024), f32),
        grid=(4,),
        in_specs=[pl.BlockSpec((16, 8, 1, 8, LANES), lambda k: (0, 0, k, 0, 0))],
        out_specs=pl.BlockSpec((1, 128, 1024), lambda k: (k, 0, 0)),
        compiler_params=pltpu.CompilerParams(vmem_limit_bytes=32 * 2**20),
        name="place",
    )(gathered)


def per_device(coeffs_in, basis, kernels, response, hs_image, ms_image):
    pos = (lax.axis_index("sub") * 16 + lax.axis_index("band")).astype(jnp.int32).reshape(1)
    own, *tiles = pack(pos, coeffs_in, ms_image, hs_image)
    above = lax.ppermute(own, "sub", [(i, i + 1) for i in range(7)])
    below = lax.ppermute(own, "sub", [(i + 1, i) for i in range(7)])
    sent, ms = spread(above, own, below, kernels, basis, response)
    hp = lax.all_to_all(sent, "band", split_axis=0, concat_axis=0, tiled=True).reshape(256, 384)
    tiles = [tiles[0]] + [
        lax.ppermute(tiles[d], "sub", [(i, (i + d) % 8) for i in range(8)]) for d in range(1, 8)
    ]
    new = refine(pos, tiles, hp, ms)
    owned = lax.all_to_all(new.reshape(8, 4, 8, LANES), "sub", split_axis=0, concat_axis=0, tiled=True)
    copies = jnp.broadcast_to(owned[None], (16,) + owned.shape)
    gathered = lax.all_to_all(copies, "band", split_axis=0, concat_axis=0, tiled=True)
    return place(gathered)


def solution(mesh):
    return jax.shard_map(
        per_device,
        mesh=mesh,
        in_specs=(
            P("sub", None, None),
            P("band", None),
            P("band", None, None),
            P(None, "band"),
            P("band", "sub", None),
            P(None, "sub", None),
        ),
        out_specs=P("sub", None, None),
        check_vma=False,
    )
```

```python
import functools

import jax
import jax.numpy as jnp
from jax import lax
from jax.experimental import pallas as pl
from jax.experimental.pallas import tpu as pltpu
from jax.sharding import PartitionSpec as P

STEP = 0.15
TR, TC = 16, 64
TAPS = 9
SPAN = 250.0
LANES = 128
CROWS = 48
MROWS = 32
IROWS = 10
JCOLS = 24
ROWS_LO, COLS_LO = 32, 256
f32 = jnp.float32
bf16 = jnp.bfloat16


def rounded(value):
    return value.astype(bf16).astype(f32)


def refine_kernel(pos_ref, *refs):
    tiles = refs[:8]
    hp_ref, ms_ref, out_ref, c_ref, m0, m1, f0, f1, b0, b1, c1_ref, g_ref, hs0, hs1, w0, w1 = refs[8:]
    s = pos_ref[0] // 16
    b = pos_ref[0] % 16
    for d in range(8):
        at = pl.multiple_of((s + 8 - d) % 8 * (4 * CROWS), 4 * CROWS)
        c_ref[pl.ds(at, 4 * CROWS), :] = tiles[d][...].reshape(4 * CROWS, LANES)
    m = (m0, m1)
    f = (f0, f1)
    bk = (b0, b1)
    hst = (hs0, hs1)
    w = (w0, w1)
    for h in range(2):
        part = hp_ref[h * 128 : h * 128 + 128, :]
        for piece in range(2):
            hst[h][piece * 128 : piece * 128 + 128, :] = part[:, piece * 128 : piece * 128 + 128].T
        w[h][...] = part[:, 256:384].T
    basis = jnp.concatenate([w0[81:113, :], w1[81:113, :]], axis=1).astype(bf16)
    response = jnp.concatenate([w0[113:121, :], w1[113:121, :]], axis=1).astype(bf16)
    combined = lax.dot_general(response, basis, (((1,), (1,)), ((), ())), preferred_element_type=f32).astype(bf16)
    lane = lax.broadcasted_iota(jnp.int32, (1, LANES), 1)
    group = lane % 32
    column = 64 * b - 16 + 4 * group + lane // 32
    in_columns = (column >= 0) & (column < 1024) & (group >= 2) & (group < 22)

    def mix(row, value, rows):
        mixed = lax.dot_general(value.astype(bf16), basis, (((0,), (0,)), ((), ())), preferred_element_type=f32)
        mixed = rounded(mixed)
        at = pl.ds(pl.multiple_of(row * LANES, LANES), rows * LANES)
        for h in range(2):
            m[h][at, :] = mixed[:, h * 128 : h * 128 + 128]

    def ms_gradient(row, block):
        predicted = jnp.dot(combined, block.astype(bf16), preferred_element_type=f32)
        seen = jnp.concatenate([ms_ref[pl.ds(row - 8 + r, 8, stride=MROWS), :] for r in range(8)], axis=1)
        misfit = (seen - predicted).astype(bf16)
        grad = lax.dot_general(combined, misfit, (((0,), (0,)), ((), ())), preferred_element_type=f32)
        for r in range(8):
            g_ref[pl.ds((row - 8 + r) * 32, 32), :] = grad[:, r * 128 : r * 128 + 128]

    def blur_row(n):
        g = lax.broadcasted_iota(jnp.int32, (JCOLS, LANES), 0)
        i_at = 4 * s + n - 3
        j_at = 16 * b + g - 3
        inside = (i_at >= 0) & (i_at < ROWS_LO) & (j_at >= 0) & (j_at < COLS_LO)
        for h in range(2):
            acc = [None, None, None]
            for a in range(TAPS):
                for q in range(4):
                    at = pl.multiple_of((4 * n + a) * LANES + 32 * q, 32)
                    x = m[h][pl.ds(at, JCOLS), :]
                    for d in range(3):
                        if 4 * d + q > 8:
                            continue
                        tap = a * 9 + 4 * d + q
                        term = w[h][tap : tap + 1, :] * x
                        acc[d] = term if acc[d] is None else acc[d] + term
            blurred = acc[0] + pltpu.roll(acc[1], JCOLS - 1, 0) + pltpu.roll(acc[2], JCOLS - 2, 0)
            seen = hst[h][pl.ds(pl.multiple_of(n * JCOLS, 8), JCOLS), :]
            f[h][pl.ds(pl.multiple_of(8 + n * JCOLS, 8), JCOLS), :] = jnp.where(inside, seen - blurred, 0.0)

    def back_rows(u):
        for h in range(2):
            win = [[f[h][pl.ds(8 + (u - t) * JCOLS - tt, JCOLS), :] for tt in range(3)] for t in range(3)]
            for p in range(4):
                for q in range(4):
                    total = None
                    for t in range(3):
                        for tt in range(3):
                            if p + 4 * t > 8 or q + 4 * tt > 8:
                                continue
                            tap = (p + 4 * t) * 9 + q + 4 * tt
                            term = w[h][tap : tap + 1, :] * win[t][tt]
                            total = term if total is None else total + term
                    at = pl.multiple_of((4 * u - 8 + p) * LANES + 32 * q, 32)
                    bk[h][pl.ds(at, JCOLS), :] = rounded(total)

    def hs_gradient(row, rows):
        at = pl.ds((row - 8) * LANES, rows * LANES)
        back = jnp.concatenate([b0[at, :].astype(bf16), b1[at, :].astype(bf16)], axis=1)
        return lax.dot_general(basis, back, (((1,), (1,)), ((), ())), preferred_element_type=f32)

    def start_row(row):
        return c_ref[pl.ds(row, 32, stride=CROWS), :]

    def loop(low, high, body):
        def step(n, _):
            body(n)
            return 0

        lax.fori_loop(low, high, step, 0)

    for block in range(CROWS // 8):
        value = jnp.concatenate([start_row(block * 8 + r) for r in range(8)], axis=1)
        mix(block * 8, value, 8)
        if 1 <= block < 5:
            ms_gradient(block * 8, value)
    loop(0, IROWS, blur_row)
    loop(2, 10, back_rows)
    for block in range(1, 5):
        grad = hs_gradient(block * 8, 8)
        values = []
        for r in range(8):
            row = block * 8 + r
            now = start_row(row)
            new = now + STEP * (grad[:, r * 128 : r * 128 + 128] + g_ref[pl.ds((row - 8) * 32, 32), :])
            row_at = 16 * s - 16 + row
            new = jnp.where(in_columns & (row_at >= 0) & (row_at < 128), new, 0.0)
            c1_ref[pl.ds((row - 8) * 32, 32), :] = new
            values.append(new)
        value = jnp.concatenate(values, axis=1)
        mix(block * 8, value, 8)
        if 2 <= block < 4:
            ms_gradient(block * 8, value)
    loop(2, 8, blur_row)
    loop(4, 8, back_rows)
    place_at = lax.broadcasted_iota(jnp.int32, (LANES, LANES), 1)
    take = lax.broadcasted_iota(jnp.int32, (LANES, LANES), 0)
    shift = 4 * (take % 32) + take // 32 - 16
    order = [(place_at == shift + 64 * half) & (shift >= 0) & (shift < 64) for half in range(2)]
    order = [jnp.where(o, 1.0, 0.0).astype(bf16) for o in order]
    grads = [hs_gradient(16, 8), hs_gradient(24, 8)]
    for r in range(8):
        total = None
        for half in range(2):
            row = 8 + r + 8 * half
            at = pl.ds(row * 32, 32)
            value = STEP * (grads[half][:, r * 128 : r * 128 + 128] + g_ref[at, :])
            value = value + (c1_ref[at, :] - start_row(row + 8))
            rest = jnp.where((group >= 4) & (group < 20), value, 0.0)
            for _ in range(3):
                piece = rest.astype(bf16)
                rest = rest - piece.astype(f32)
                moved = jnp.dot(piece, order[half], preferred_element_type=f32)
                total = moved if total is None else total + moved
        out_ref[pl.ds(r, 32, stride=8), :] = total


def refine(pos, tiles, hp, ms):
    vmem = pl.BlockSpec(memory_space=pltpu.VMEM)
    return pl.pallas_call(
        refine_kernel,
        out_shape=jax.ShapeDtypeStruct((32 * 8, LANES), f32),
        in_specs=[pl.BlockSpec(memory_space=pltpu.SMEM)] + [vmem] * 10,
        out_specs=vmem,
        scratch_shapes=[
            pltpu.VMEM((32 * CROWS, LANES), f32),
            pltpu.VMEM((CROWS * LANES, LANES), f32),
            pltpu.VMEM((CROWS * LANES, LANES), f32),
            pltpu.VMEM((256, LANES), f32),
            pltpu.VMEM((256, LANES), f32),
            pltpu.VMEM((MROWS * LANES, LANES), f32),
            pltpu.VMEM((MROWS * LANES, LANES), f32),
            pltpu.VMEM((MROWS * 32, LANES), f32),
            pltpu.VMEM((MROWS * 32, LANES), f32),
            pltpu.VMEM((256, LANES), f32),
            pltpu.VMEM((256, LANES), f32),
            pltpu.VMEM((LANES, LANES), f32),
            pltpu.VMEM((LANES, LANES), f32),
        ],
        compiler_params=pltpu.CompilerParams(vmem_limit_bytes=40 * 2**20),
        cost_estimate=pl.CostEstimate(flops=400_000_000, bytes_accessed=2_000_000, transcendentals=0),
        name="refine",
    )(pos, *tiles, hp, ms)


def pack_kernel(pos_ref, ca_ref, cb_ref, ma_ref, mb_ref, hs_ref, near_ref, *rest_refs):
    tile_refs = rest_refs[:8]
    wide_ref = rest_refs[8]
    s = pos_ref[0] // 16
    b = pos_ref[0] % 16
    off = jnp.where(b % 2 == 0, 112, 48)
    lane = lax.broadcasted_iota(jnp.int32, (1, LANES), 1)
    first = lane >= off
    block = (b + 1) // 2 - jnp.where(first, 1, 0)
    keep = (block >= 0) & (block < 8)
    source = lax.broadcasted_iota(jnp.int32, (LANES, LANES), 0)
    target = lax.broadcasted_iota(jnp.int32, (LANES, LANES), 1)
    order = jnp.where(source == (4 * (target % 32) + target // 32 + off) % LANES, 1.0, 0.0).astype(bf16)
    ms = jnp.where(first, ma_ref[...].reshape(128, LANES).astype(f32), mb_ref[...].reshape(128, LANES).astype(f32))
    ms = jnp.where(keep, ms, 0.0).astype(bf16)
    near_ref[0:128, :] = jnp.dot(ms, order, preferred_element_type=f32).astype(bf16)
    hs = hs_ref[...].astype(f32)
    for i in range(4):
        row = jnp.concatenate([hs[:, i, :], jnp.zeros((2, 256), f32)], axis=0).astype(bf16)
        near_ref[128 + 16 * i : 144 + 16 * i, :] = row[:, 0:128]
        near_ref[192 + 16 * i : 208 + 16 * i, :] = row[:, 128:256]
    edge = jnp.zeros((16, LANES), f32)
    for k in range(4):
        rest = jnp.where(keep, jnp.where(first, ca_ref[k], cb_ref[k]), 0.0)
        total = None
        for _ in range(3):
            piece = rest.astype(bf16)
            rest = rest - piece.astype(f32)
            moved = jnp.dot(piece, order, preferred_element_type=f32)
            total = moved if total is None else total + moved
        wide_ref[k, 0:16] = edge
        wide_ref[k, 16:144] = total
        wide_ref[k, 144:160] = edge
    for d in range(8):
        t = (s + d) % 8
        at = pl.ds(pl.multiple_of(16 * t, 16), CROWS)
        for k in range(4):
            tile_refs[d][k] = wide_ref[k, at, :]


def pack(pos, coeffs_in, ms_image, hs_image):
    def low(i, p):
        return (0, 0, jnp.maximum((p[0] % 16 + 1) // 2 - 1, 0))

    def high(i, p):
        return (0, 0, jnp.minimum((p[0] % 16 + 1) // 2, 7))

    tile = jax.ShapeDtypeStruct((4, CROWS, LANES), f32)
    return pl.pallas_call(
        pack_kernel,
        out_shape=(jax.ShapeDtypeStruct((256, LANES), bf16),) + (tile,) * 8,
        grid_spec=pltpu.PrefetchScalarGridSpec(
            num_scalar_prefetch=1,
            grid=(1,),
            in_specs=[
                pl.BlockSpec((4, 128, LANES), low),
                pl.BlockSpec((4, 128, LANES), high),
                pl.BlockSpec((8, 16, LANES), low),
                pl.BlockSpec((8, 16, LANES), high),
                pl.BlockSpec((14, 4, 256), lambda i, p: (0, 0, 0)),
            ],
            out_specs=(pl.BlockSpec((256, LANES), lambda i, p: (0, 0)),)
            + (pl.BlockSpec((4, CROWS, LANES), lambda i, p: (0, 0, 0)),) * 8,
            scratch_shapes=[pltpu.VMEM((4, 160, LANES), f32)],
        ),
        compiler_params=pltpu.CompilerParams(vmem_limit_bytes=60 * 2**20),
        cost_estimate=pl.CostEstimate(flops=100_000_000, bytes_accessed=1_600_000, transcendentals=0),
        name="pack",
    )(pos, coeffs_in, coeffs_in, ms_image, ms_image, hs_image)


def spread_kernel(above_ref, own_ref, below_ref, k_ref, basis_ref, response_ref, sent_ref, ms_ref):
    for m in range(8):
        at = slice(16 * m, 16 * m + 16)
        ms_ref[32 * m : 32 * m + 8, :] = above_ref[at, :].astype(f32)[8:16]
        ms_ref[32 * m + 8 : 32 * m + 24, :] = own_ref[at, :].astype(f32)
        ms_ref[32 * m + 24 : 32 * m + 32, :] = below_ref[at, :].astype(f32)[0:8]
    lane = lax.broadcasted_iota(jnp.int32, (1, 256), 1)
    rows = []
    for i in range(IROWS):
        ref, r = (above_ref, i + 1) if i < 3 else (own_ref, i - 3) if i < 7 else (below_ref, i - 7)
        row = [ref[128 + 64 * h + 16 * r : 144 + 64 * h + 16 * r, :].astype(f32) for h in range(2)]
        rows.append(jnp.concatenate(row, axis=1))
    sent_ref[:, :, 256:384] = jnp.zeros((16, 16, 128), f32)
    for a in range(9):
        sent_ref[0, 0:14, 256 + 9 * a : 265 + 9 * a] = k_ref[:, a, :]
    sent_ref[0, 0:14, 337:369] = basis_ref[...].astype(f32)
    sent_ref[0, 0:14, 369:377] = response_ref[...].astype(f32).T
    params = sent_ref[0, :, 256:384]
    for t in range(16):
        total = jnp.zeros((16, 256), f32)
        for i in range(IROWS):
            moved = pltpu.roll(rows[i], (24 * i + 3 - 16 * t) % 256, 1)
            total = jnp.where((lane >= 24 * i) & (lane < 24 * i + 24), moved, total)
        sent_ref[t, :, 0:256] = total
        if t:
            sent_ref[t, :, 256:384] = params


def spread(above, own, below, kernels, basis, response):
    vmem = pl.BlockSpec(memory_space=pltpu.VMEM)
    return pl.pallas_call(
        spread_kernel,
        out_shape=(
            jax.ShapeDtypeStruct((16, 16, 384), f32),
            jax.ShapeDtypeStruct((8 * MROWS, LANES), f32),
        ),
        in_specs=[vmem] * 6,
        out_specs=(vmem, vmem),
        compiler_params=pltpu.CompilerParams(vmem_limit_bytes=16 * 2**20),
        cost_estimate=pl.CostEstimate(flops=1_000_000, bytes_accessed=1_000_000, transcendentals=0),
        name="spread",
    )(above, own, below, kernels, basis, response)


def encode_kernel(d_ref, out_ref):
    scales = []
    codes = []
    for k in range(4):
        part = d_ref[:, k]
        size = jnp.abs(part)
        top = jnp.max(size, axis=(0, 1, 2), keepdims=True)
        scale = rounded(jnp.maximum(top * (1 + 2**-7), 1e-30))
        code = jnp.exp2(size * (SPAN / scale) - SPAN / 2)
        codes.append(jnp.where(part < 0, -code, code))
        scales.append(jnp.broadcast_to(scale[0], (1, LANES)))
    scales = jnp.concatenate(scales + [jnp.zeros((12, LANES), f32)], axis=0).astype(bf16)
    for s in range(8):
        row = jnp.concatenate([codes[k][s] for k in range(4)], axis=0).astype(bf16)
        for t in range(16):
            out_ref[t, 32 * s : 32 * s + 32] = row
    for t in range(16):
        out_ref[t, 256:272] = scales


def encode(owned):
    vmem = pl.BlockSpec(memory_space=pltpu.VMEM)
    return pl.pallas_call(
        encode_kernel,
        out_shape=jax.ShapeDtypeStruct((16, 272, LANES), bf16),
        in_specs=[vmem],
        out_specs=vmem,
        compiler_params=pltpu.CompilerParams(vmem_limit_bytes=16 * 2**20),
        name="encode",
    )(owned)


def place_kernel(g_ref, c_ref, out_ref):
    lane = lax.broadcasted_iota(jnp.int32, (1, LANES), 1)
    low = lane < 64
    scales = [g_ref[e, 256:272].astype(f32) * (1 / SPAN) for e in range(2)]
    for s in range(8):
        pair = []
        for e in range(2):
            code = g_ref[e, 32 * s : 32 * s + 32].astype(f32)
            size = jnp.log2(jnp.abs(code)) + SPAN / 2
            pair.append(jnp.where(code < 0, -size, size))
        for k in range(4):
            even, odd = [pair[e][8 * k : 8 * k + 8] * scales[e][k : k + 1] for e in range(2)]
            for half, value in enumerate(
                [jnp.where(low, even, pltpu.roll(odd, 64, 1)), jnp.where(low, pltpu.roll(even, 64, 1), odd)]
            ):
                at = slice(16 * s + 8 * half, 16 * s + 8 * half + 8)
                out_ref[k, at] = c_ref[k, at] + value


def place(gathered, coeffs_in):
    block = pl.BlockSpec((4, 128, LANES), lambda j: (0, 0, j))
    return pl.pallas_call(
        place_kernel,
        out_shape=jax.ShapeDtypeStruct((4, 128, 1024), f32),
        grid=(8,),
        in_specs=[pl.BlockSpec((2, 272, LANES), lambda j: (j, 0, 0)), block],
        out_specs=block,
        compiler_params=pltpu.CompilerParams(vmem_limit_bytes=32 * 2**20),
        name="place",
    )(gathered, coeffs_in)


def per_device(coeffs_in, basis, kernels, response, hs_image, ms_image):
    pos = (lax.axis_index("sub") * 16 + lax.axis_index("band")).astype(jnp.int32).reshape(1)
    own, *tiles = pack(pos, coeffs_in, ms_image, hs_image)
    above = lax.ppermute(own, "sub", [(i, i + 1) for i in range(7)])
    below = lax.ppermute(own, "sub", [(i + 1, i) for i in range(7)])
    sent, ms = spread(above, own, below, kernels, basis, response)
    hp = lax.all_to_all(sent, "band", split_axis=0, concat_axis=0, tiled=True).reshape(256, 384)
    tiles = [tiles[0]] + [
        lax.ppermute(tiles[d], "sub", [(i, (i + d) % 8) for i in range(8)]) for d in range(1, 8)
    ]
    new = refine(pos, tiles, hp, ms)
    owned = lax.all_to_all(new.reshape(8, 4, 8, LANES), "sub", split_axis=0, concat_axis=0, tiled=True)
    gathered = lax.all_to_all(encode(owned), "band", split_axis=0, concat_axis=0, tiled=True)
    return place(gathered, coeffs_in)


def solution(mesh):
    return jax.shard_map(
        per_device,
        mesh=mesh,
        in_specs=(
            P("sub", None, None),
            P("band", None),
            P("band", None, None),
            P(None, "band"),
            P("band", "sub", None),
            P(None, "sub", None),
        ),
        out_specs=P("sub", None, None),
        check_vma=False,
    )
```

```python
import functools

import jax
import jax.numpy as jnp
from jax import lax
from jax.experimental import pallas as pl
from jax.experimental.pallas import tpu as pltpu
from jax.sharding import PartitionSpec as P

STEP = 0.15
TR, TC = 16, 64
TAPS = 9
SPAN = 250.0
LANES = 128
CROWS = 48
MROWS = 32
IROWS = 10
JCOLS = 24
ROWS_LO, COLS_LO = 32, 256
f32 = jnp.float32
bf16 = jnp.bfloat16


def rounded(value):
    return value.astype(bf16).astype(f32)


def refine_kernel(pos_ref, *refs):
    tiles = refs[:8]
    ms_own_ref, hp_ref, above_ref, below_ref, out_ref, c_ref, ms_ref, m0, m1, f0, f1, b0, b1, c1_ref, g_ref, hs0, hs1, w0, w1 = refs[8:]
    s = pos_ref[0] // 16
    b = pos_ref[0] % 16
    for d in range(8):
        at = pl.multiple_of((s + 8 - d) % 8 * (4 * CROWS), 4 * CROWS)
        c_ref[pl.ds(at, 4 * CROWS), :] = tiles[d][0 : 4 * CROWS]
    for k in range(8):
        ms_ref[32 * k : 32 * k + 8, :] = tiles[1][4 * CROWS + 8 * k : 4 * CROWS + 8 * k + 8]
        ms_ref[32 * k + 8 : 32 * k + 24, :] = ms_own_ref[16 * k : 16 * k + 16, :]
        ms_ref[32 * k + 24 : 32 * k + 32, :] = tiles[7][4 * CROWS + 8 * k : 4 * CROWS + 8 * k + 8]
    bk = (b0, b1)
    m = (m0, m1)
    f = (f0, f1)
    hst = (hs0, hs1)
    w = (w0, w1)
    for h in range(2):
        at = slice(h * 128, h * 128 + 128)
        hst[h][0:72, :] = above_ref[at, :].astype(f32).T[24:96]
        hst[h][72:168, :] = hp_ref[at, 0:128].T[0:96]
        hst[h][168:240, :] = below_ref[at, :].astype(f32).T[0:72]
        w[h][...] = hp_ref[at, 128:256].T
    basis = jnp.concatenate([w0[81:113, :], w1[81:113, :]], axis=1).astype(bf16)
    response = jnp.concatenate([w0[113:121, :], w1[113:121, :]], axis=1).astype(bf16)
    combined = lax.dot_general(response, basis, (((1,), (1,)), ((), ())), preferred_element_type=f32).astype(bf16)
    lane = lax.broadcasted_iota(jnp.int32, (1, LANES), 1)
    group = lane % 32
    column = 64 * b - 16 + 4 * group + lane // 32
    in_columns = (column >= 0) & (column < 1024) & (group >= 2) & (group < 22)

    def mix(row, value, rows):
        mixed = lax.dot_general(value.astype(bf16), basis, (((0,), (0,)), ((), ())), preferred_element_type=f32)
        mixed = rounded(mixed)
        at = pl.ds(pl.multiple_of(row * LANES, LANES), rows * LANES)
        for h in range(2):
            m[h][at, :] = mixed[:, h * 128 : h * 128 + 128]

    def ms_gradient(row, block):
        predicted = jnp.dot(combined, block.astype(bf16), preferred_element_type=f32)
        seen = jnp.concatenate([ms_ref[pl.ds(row - 8 + r, 8, stride=MROWS), :] for r in range(8)], axis=1)
        misfit = (seen - predicted).astype(bf16)
        grad = lax.dot_general(combined, misfit, (((0,), (0,)), ((), ())), preferred_element_type=f32)
        for r in range(8):
            g_ref[pl.ds((row - 8 + r) * 32, 32), :] = grad[:, r * 128 : r * 128 + 128]

    def blur_row(n):
        g = lax.broadcasted_iota(jnp.int32, (JCOLS, LANES), 0)
        i_at = 4 * s + n - 3
        j_at = 16 * b + g - 3
        inside = (i_at >= 0) & (i_at < ROWS_LO) & (j_at >= 0) & (j_at < COLS_LO)
        for h in range(2):
            acc = [None, None, None]
            for a in range(TAPS):
                for q in range(4):
                    at = pl.multiple_of((4 * n + a) * LANES + 32 * q, 32)
                    x = m[h][pl.ds(at, JCOLS), :]
                    for d in range(3):
                        if 4 * d + q > 8:
                            continue
                        tap = a * 9 + 4 * d + q
                        term = w[h][tap : tap + 1, :] * x
                        acc[d] = term if acc[d] is None else acc[d] + term
            blurred = acc[0] + pltpu.roll(acc[1], JCOLS - 1, 0) + pltpu.roll(acc[2], JCOLS - 2, 0)
            seen = hst[h][pl.ds(pl.multiple_of(n * JCOLS, 8), JCOLS), :]
            f[h][pl.ds(pl.multiple_of(8 + n * JCOLS, 8), JCOLS), :] = jnp.where(inside, seen - blurred, 0.0)

    def back_rows(u):
        for h in range(2):
            win = [[f[h][pl.ds(8 + (u - t) * JCOLS - tt, JCOLS), :] for tt in range(3)] for t in range(3)]
            for p in range(4):
                for q in range(4):
                    total = None
                    for t in range(3):
                        for tt in range(3):
                            if p + 4 * t > 8 or q + 4 * tt > 8:
                                continue
                            tap = (p + 4 * t) * 9 + q + 4 * tt
                            term = w[h][tap : tap + 1, :] * win[t][tt]
                            total = term if total is None else total + term
                    at = pl.multiple_of((4 * u - 8 + p) * LANES + 32 * q, 32)
                    bk[h][pl.ds(at, JCOLS), :] = rounded(total)

    def hs_gradient(row, rows):
        at = pl.ds((row - 8) * LANES, rows * LANES)
        back = jnp.concatenate([b0[at, :].astype(bf16), b1[at, :].astype(bf16)], axis=1)
        return lax.dot_general(basis, back, (((1,), (1,)), ((), ())), preferred_element_type=f32)

    def start_row(row):
        return c_ref[pl.ds(row, 32, stride=CROWS), :]

    def loop(low, high, body):
        def step(n, _):
            body(n)
            return 0

        lax.fori_loop(low, high, step, 0)

    for block in range(CROWS // 8):
        value = jnp.concatenate([start_row(block * 8 + r) for r in range(8)], axis=1)
        mix(block * 8, value, 8)
        if 1 <= block < 5:
            ms_gradient(block * 8, value)
    loop(0, IROWS, blur_row)
    loop(2, 10, back_rows)
    for block in range(1, 5):
        grad = hs_gradient(block * 8, 8)
        values = []
        for r in range(8):
            row = block * 8 + r
            now = start_row(row)
            new = now + STEP * (grad[:, r * 128 : r * 128 + 128] + g_ref[pl.ds((row - 8) * 32, 32), :])
            row_at = 16 * s - 16 + row
            new = jnp.where(in_columns & (row_at >= 0) & (row_at < 128), new, 0.0)
            c1_ref[pl.ds((row - 8) * 32, 32), :] = new
            values.append(new)
        value = jnp.concatenate(values, axis=1)
        mix(block * 8, value, 8)
        if 2 <= block < 4:
            ms_gradient(block * 8, value)
    loop(2, 8, blur_row)
    loop(4, 8, back_rows)
    place_at = lax.broadcasted_iota(jnp.int32, (LANES, LANES), 1)
    take = lax.broadcasted_iota(jnp.int32, (LANES, LANES), 0)
    shift = 4 * (take % 32) + take // 32 - 16
    order = [(place_at == shift + 64 * half) & (shift >= 0) & (shift < 64) for half in range(2)]
    order = [jnp.where(o, 1.0, 0.0).astype(bf16) for o in order]
    grads = [hs_gradient(16, 8), hs_gradient(24, 8)]
    for r in range(8):
        total = None
        for half in range(2):
            row = 8 + r + 8 * half
            at = pl.ds(row * 32, 32)
            value = STEP * (grads[half][:, r * 128 : r * 128 + 128] + g_ref[at, :])
            value = value + (c1_ref[at, :] - start_row(row + 8))
            rest = jnp.where((group >= 4) & (group < 20), value, 0.0)
            for _ in range(3):
                piece = rest.astype(bf16)
                rest = rest - piece.astype(f32)
                moved = jnp.dot(piece, order[half], preferred_element_type=f32)
                total = moved if total is None else total + moved
        out_ref[pl.ds(r, 32, stride=8), :] = total


def refine(pos, tiles, ms, hp, above, below):
    vmem = pl.BlockSpec(memory_space=pltpu.VMEM)
    return pl.pallas_call(
        refine_kernel,
        out_shape=jax.ShapeDtypeStruct((32 * 8, LANES), f32),
        in_specs=[pl.BlockSpec(memory_space=pltpu.SMEM)] + [vmem] * 12,
        out_specs=vmem,
        scratch_shapes=[
            pltpu.VMEM((32 * CROWS, LANES), f32),
            pltpu.VMEM((8 * MROWS, LANES), f32),
            pltpu.VMEM((CROWS * LANES, LANES), f32),
            pltpu.VMEM((CROWS * LANES, LANES), f32),
            pltpu.VMEM((256, LANES), f32),
            pltpu.VMEM((256, LANES), f32),
            pltpu.VMEM((MROWS * LANES, LANES), f32),
            pltpu.VMEM((MROWS * LANES, LANES), f32),
            pltpu.VMEM((MROWS * 32, LANES), f32),
            pltpu.VMEM((MROWS * 32, LANES), f32),
            pltpu.VMEM((256, LANES), f32),
            pltpu.VMEM((256, LANES), f32),
            pltpu.VMEM((LANES, LANES), f32),
            pltpu.VMEM((LANES, LANES), f32),
        ],
        compiler_params=pltpu.CompilerParams(vmem_limit_bytes=40 * 2**20),
        cost_estimate=pl.CostEstimate(flops=400_000_000, bytes_accessed=2_000_000, transcendentals=0),
        name="refine",
    )(pos, *tiles, ms, hp, above, below)


def pack_kernel(pos_ref, ca_ref, cb_ref, ma_ref, mb_ref, ms_ref, *rest_refs):
    tile_refs = rest_refs[:8]
    wide_ref = rest_refs[8]
    s = pos_ref[0] // 16
    b = pos_ref[0] % 16
    off = jnp.where(b % 2 == 0, 112, 48)
    lane = lax.broadcasted_iota(jnp.int32, (1, LANES), 1)
    first = lane >= off
    block = (b + 1) // 2 - jnp.where(first, 1, 0)
    keep = (block >= 0) & (block < 8)
    source = lax.broadcasted_iota(jnp.int32, (LANES, LANES), 0)
    target = lax.broadcasted_iota(jnp.int32, (LANES, LANES), 1)
    order = jnp.where(source == (4 * (target % 32) + target // 32 + off) % LANES, 1.0, 0.0).astype(bf16)
    ms = jnp.where(first, ma_ref[...].reshape(128, LANES).astype(f32), mb_ref[...].reshape(128, LANES).astype(f32))
    ms = jnp.where(keep, ms, 0.0).astype(bf16)
    ms = jnp.dot(ms, order, preferred_element_type=f32)
    ms_ref[...] = ms
    for k in range(8):
        at = slice(4 * CROWS + 8 * k, 4 * CROWS + 8 * k + 8)
        tile_refs[1][at] = ms[16 * k + 8 : 16 * k + 16]
        tile_refs[7][at] = ms[16 * k : 16 * k + 8]
    edge = jnp.zeros((16, LANES), f32)
    for k in range(4):
        rest = jnp.where(keep, jnp.where(first, ca_ref[k], cb_ref[k]), 0.0)
        total = None
        for _ in range(3):
            piece = rest.astype(bf16)
            rest = rest - piece.astype(f32)
            moved = jnp.dot(piece, order, preferred_element_type=f32)
            total = moved if total is None else total + moved
        wide_ref[k, 0:16] = edge
        wide_ref[k, 16:144] = total
        wide_ref[k, 144:160] = edge
    for d in range(8):
        t = (s + d) % 8
        at = pl.ds(pl.multiple_of(16 * t, 16), CROWS)
        for k in range(4):
            tile_refs[d][k * CROWS : k * CROWS + CROWS] = wide_ref[k, at, :]


def pack(pos, coeffs_in, ms_image):
    def low(i, p):
        return (0, 0, jnp.maximum((p[0] % 16 + 1) // 2 - 1, 0))

    def high(i, p):
        return (0, 0, jnp.minimum((p[0] % 16 + 1) // 2, 7))

    rows = [128] + [4 * CROWS + (64 if d in (1, 7) else 0) for d in range(8)]
    return pl.pallas_call(
        pack_kernel,
        out_shape=tuple(jax.ShapeDtypeStruct((count, LANES), f32) for count in rows),
        grid_spec=pltpu.PrefetchScalarGridSpec(
            num_scalar_prefetch=1,
            grid=(1,),
            in_specs=[
                pl.BlockSpec((4, 128, LANES), low),
                pl.BlockSpec((4, 128, LANES), high),
                pl.BlockSpec((8, 16, LANES), low),
                pl.BlockSpec((8, 16, LANES), high),
            ],
            out_specs=tuple(pl.BlockSpec((count, LANES), lambda i, p: (0, 0)) for count in rows),
            scratch_shapes=[pltpu.VMEM((4, 160, LANES), f32)],
        ),
        compiler_params=pltpu.CompilerParams(vmem_limit_bytes=60 * 2**20),
        cost_estimate=pl.CostEstimate(flops=100_000_000, bytes_accessed=1_600_000, transcendentals=0),
        name="pack",
    )(pos, coeffs_in, coeffs_in, ms_image, ms_image)


def spread_kernel(hs_ref, k_ref, basis_ref, response_ref, sent_ref):
    lane = lax.broadcasted_iota(jnp.int32, (1, LANES), 1)
    hs = hs_ref[...].astype(f32)
    rows = [jnp.concatenate([hs[:, i, :], jnp.zeros((2, 256), f32)], axis=0) for i in range(4)]
    sent_ref[0, :, 128:256] = jnp.zeros((16, 128), f32)
    for a in range(9):
        sent_ref[0, 0:14, 128 + 9 * a : 137 + 9 * a] = k_ref[:, a, :]
    sent_ref[0, 0:14, 209:241] = basis_ref[...].astype(f32)
    sent_ref[0, 0:14, 241:249] = response_ref[...].astype(f32).T
    params = sent_ref[0, :, 128:256]
    for t in range(16):
        total = jnp.zeros((16, LANES), f32)
        for i in range(4):
            moved = pltpu.roll(rows[i], (24 * i + 3 - 16 * t) % 256, 1)[:, 0:128]
            total = jnp.where((lane >= 24 * i) & (lane < 24 * i + 24), moved, total)
        sent_ref[t, :, 0:128] = total
        if t:
            sent_ref[t, :, 128:256] = params


def spread(hs_image, kernels, basis, response):
    vmem = pl.BlockSpec(memory_space=pltpu.VMEM)
    return pl.pallas_call(
        spread_kernel,
        out_shape=jax.ShapeDtypeStruct((16, 16, 256), f32),
        in_specs=[vmem] * 4,
        out_specs=vmem,
        compiler_params=pltpu.CompilerParams(vmem_limit_bytes=16 * 2**20),
        cost_estimate=pl.CostEstimate(flops=1_000_000, bytes_accessed=1_000_000, transcendentals=0),
        name="spread",
    )(hs_image, kernels, basis, response)


def encode_kernel(d_ref, out_ref):
    scales = []
    codes = []
    for k in range(4):
        part = d_ref[:, k]
        size = jnp.abs(part)
        top = jnp.max(size, axis=(0, 1, 2), keepdims=True)
        scale = rounded(jnp.maximum(top * (1 + 2**-7), 1e-30))
        code = jnp.exp2(size * (SPAN / scale) - SPAN / 2)
        codes.append(jnp.where(part < 0, -code, code))
        scales.append(jnp.broadcast_to(scale[0], (1, LANES)))
    scales = jnp.concatenate(scales + [jnp.zeros((12, LANES), f32)], axis=0).astype(bf16)
    for s in range(8):
        row = jnp.concatenate([codes[k][s] for k in range(4)], axis=0).astype(bf16)
        for t in range(16):
            out_ref[t, 32 * s : 32 * s + 32] = row
    for t in range(16):
        out_ref[t, 256:272] = scales


def encode(owned):
    vmem = pl.BlockSpec(memory_space=pltpu.VMEM)
    return pl.pallas_call(
        encode_kernel,
        out_shape=jax.ShapeDtypeStruct((16, 272, LANES), bf16),
        in_specs=[vmem],
        out_specs=vmem,
        compiler_params=pltpu.CompilerParams(vmem_limit_bytes=16 * 2**20),
        name="encode",
    )(owned)


def place_kernel(g_ref, c_ref, out_ref):
    lane = lax.broadcasted_iota(jnp.int32, (1, LANES), 1)
    low = lane < 64
    scales = [g_ref[e, 256:272].astype(f32) * (1 / SPAN) for e in range(2)]
    for s in range(8):
        pair = []
        for e in range(2):
            code = g_ref[e, 32 * s : 32 * s + 32].astype(f32)
            size = jnp.log2(jnp.abs(code)) + SPAN / 2
            pair.append(jnp.where(code < 0, -size, size))
        for k in range(4):
            even, odd = [pair[e][8 * k : 8 * k + 8] * scales[e][k : k + 1] for e in range(2)]
            for half, value in enumerate(
                [jnp.where(low, even, pltpu.roll(odd, 64, 1)), jnp.where(low, pltpu.roll(even, 64, 1), odd)]
            ):
                at = slice(16 * s + 8 * half, 16 * s + 8 * half + 8)
                out_ref[k, at] = c_ref[k, at] + value


def place(gathered, coeffs_in):
    block = pl.BlockSpec((4, 128, LANES), lambda j: (0, 0, j))
    return pl.pallas_call(
        place_kernel,
        out_shape=jax.ShapeDtypeStruct((4, 128, 1024), f32),
        grid=(8,),
        in_specs=[pl.BlockSpec((2, 272, LANES), lambda j: (j, 0, 0)), block],
        out_specs=block,
        compiler_params=pltpu.CompilerParams(vmem_limit_bytes=32 * 2**20),
        name="place",
    )(gathered, coeffs_in)


def per_device(coeffs_in, basis, kernels, response, hs_image, ms_image):
    pos = (lax.axis_index("sub") * 16 + lax.axis_index("band")).astype(jnp.int32).reshape(1)
    sent = spread(hs_image, kernels, basis, response)
    hp = lax.all_to_all(sent, "band", split_axis=0, concat_axis=0, tiled=True).reshape(256, 256)
    ms, *tiles = pack(pos, coeffs_in, ms_image)
    tiles = [tiles[0]] + [
        lax.ppermute(tiles[d], "sub", [(i, (i + d) % 8) for i in range(8)]) for d in range(1, 8)
    ]
    seen = hp[:, 0:128].astype(bf16)
    above = lax.ppermute(seen, "sub", [(i, i + 1) for i in range(7)])
    below = lax.ppermute(seen, "sub", [(i + 1, i) for i in range(7)])
    new = refine(pos, tiles, ms, hp, above, below)
    owned = lax.all_to_all(new.reshape(8, 4, 8, LANES), "sub", split_axis=0, concat_axis=0, tiled=True)
    gathered = lax.all_to_all(encode(owned), "band", split_axis=0, concat_axis=0, tiled=True)
    return place(gathered, coeffs_in)


def solution(mesh):
    return jax.shard_map(
        per_device,
        mesh=mesh,
        in_specs=(
            P("sub", None, None),
            P("band", None),
            P("band", None, None),
            P(None, "band"),
            P("band", "sub", None),
            P(None, "sub", None),
        ),
        out_specs=P("sub", None, None),
        check_vma=False,
    )
```

```python
import functools

import jax
import jax.numpy as jnp
from jax import lax
from jax.experimental import pallas as pl
from jax.experimental.pallas import tpu as pltpu
from jax.sharding import PartitionSpec as P

STEP = 0.15
TR, TC = 16, 64
TAPS = 9
SPAN = 250.0
LANES = 128
CROWS = 48
MROWS = 32
IROWS = 10
JCOLS = 24
ROWS_LO, COLS_LO = 32, 256
f32 = jnp.float32
bf16 = jnp.bfloat16


def rounded(value):
    return value.astype(bf16).astype(f32)


def refine_kernel(pos_ref, *refs):
    tiles = refs[:8]
    hp_ref, above_ref, below_ref, out_ref, c_ref, ms_ref, m0, m1, f0, f1, b0, b1, c1_ref, g_ref, hs0, hs1, w0, w1 = refs[8:]
    s = pos_ref[0] // 16
    b = pos_ref[0] % 16
    for d in range(8):
        at = pl.multiple_of((s + 8 - d) % 8 * (4 * CROWS), 4 * CROWS)
        c_ref[pl.ds(at, 4 * CROWS), :] = tiles[d][0 : 4 * CROWS]
    for k in range(8):
        ms_ref[32 * k : 32 * k + 8, :] = tiles[1][4 * CROWS + 8 * k : 4 * CROWS + 8 * k + 8]
        ms_ref[32 * k + 8 : 32 * k + 24, :] = tiles[0][4 * CROWS + 16 * k : 4 * CROWS + 16 * k + 16]
        ms_ref[32 * k + 24 : 32 * k + 32, :] = tiles[7][4 * CROWS + 8 * k : 4 * CROWS + 8 * k + 8]
    bk = (b0, b1)
    m = (m0, m1)
    f = (f0, f1)
    hst = (hs0, hs1)
    w = (w0, w1)
    for h in range(2):
        at = slice(h * 128, h * 128 + 128)
        hst[h][0:72, :] = above_ref[at, :].astype(f32).T[24:96]
        hst[h][72:168, :] = hp_ref[at, 0:128].T[0:96]
        hst[h][168:240, :] = below_ref[at, :].astype(f32).T[0:72]
        w[h][...] = hp_ref[at, 128:256].T
    basis = jnp.concatenate([w0[81:113, :], w1[81:113, :]], axis=1).astype(bf16)
    response = jnp.concatenate([w0[113:121, :], w1[113:121, :]], axis=1).astype(bf16)
    combined = lax.dot_general(response, basis, (((1,), (1,)), ((), ())), preferred_element_type=f32).astype(bf16)
    lane = lax.broadcasted_iota(jnp.int32, (1, LANES), 1)
    group = lane % 32
    column = 64 * b - 16 + 4 * group + lane // 32
    in_columns = (column >= 0) & (column < 1024) & (group >= 2) & (group < 22)

    def mix(row, value, rows):
        mixed = lax.dot_general(value.astype(bf16), basis, (((0,), (0,)), ((), ())), preferred_element_type=f32)
        mixed = rounded(mixed)
        at = pl.ds(pl.multiple_of(row * LANES, LANES), rows * LANES)
        for h in range(2):
            m[h][at, :] = mixed[:, h * 128 : h * 128 + 128]

    def ms_gradient(row, block):
        predicted = jnp.dot(combined, block.astype(bf16), preferred_element_type=f32)
        seen = jnp.concatenate([ms_ref[pl.ds(row - 8 + r, 8, stride=MROWS), :] for r in range(8)], axis=1)
        misfit = (seen - predicted).astype(bf16)
        grad = lax.dot_general(combined, misfit, (((0,), (0,)), ((), ())), preferred_element_type=f32)
        for r in range(8):
            g_ref[pl.ds((row - 8 + r) * 32, 32), :] = grad[:, r * 128 : r * 128 + 128]

    def blur_row(n):
        g = lax.broadcasted_iota(jnp.int32, (JCOLS, LANES), 0)
        i_at = 4 * s + n - 3
        j_at = 16 * b + g - 3
        inside = (i_at >= 0) & (i_at < ROWS_LO) & (j_at >= 0) & (j_at < COLS_LO)
        for h in range(2):
            acc = [None, None, None]
            for a in range(TAPS):
                for q in range(4):
                    at = pl.multiple_of((4 * n + a) * LANES + 32 * q, 32)
                    x = m[h][pl.ds(at, JCOLS), :]
                    for d in range(3):
                        if 4 * d + q > 8:
                            continue
                        tap = a * 9 + 4 * d + q
                        term = w[h][tap : tap + 1, :] * x
                        acc[d] = term if acc[d] is None else acc[d] + term
            blurred = acc[0] + pltpu.roll(acc[1], JCOLS - 1, 0) + pltpu.roll(acc[2], JCOLS - 2, 0)
            seen = hst[h][pl.ds(pl.multiple_of(n * JCOLS, 8), JCOLS), :]
            f[h][pl.ds(pl.multiple_of(8 + n * JCOLS, 8), JCOLS), :] = jnp.where(inside, seen - blurred, 0.0)

    def back_rows(u):
        for h in range(2):
            win = [[f[h][pl.ds(8 + (u - t) * JCOLS - tt, JCOLS), :] for tt in range(3)] for t in range(3)]
            for p in range(4):
                for q in range(4):
                    total = None
                    for t in range(3):
                        for tt in range(3):
                            if p + 4 * t > 8 or q + 4 * tt > 8:
                                continue
                            tap = (p + 4 * t) * 9 + q + 4 * tt
                            term = w[h][tap : tap + 1, :] * win[t][tt]
                            total = term if total is None else total + term
                    at = pl.multiple_of((4 * u - 8 + p) * LANES + 32 * q, 32)
                    bk[h][pl.ds(at, JCOLS), :] = rounded(total)

    def hs_gradient(row, rows):
        at = pl.ds((row - 8) * LANES, rows * LANES)
        back = jnp.concatenate([b0[at, :].astype(bf16), b1[at, :].astype(bf16)], axis=1)
        return lax.dot_general(basis, back, (((1,), (1,)), ((), ())), preferred_element_type=f32)

    def start_row(row):
        return c_ref[pl.ds(row, 32, stride=CROWS), :]

    def loop(low, high, body):
        def step(n, _):
            body(n)
            return 0

        lax.fori_loop(low, high, step, 0)

    for block in range(CROWS // 8):
        value = jnp.concatenate([start_row(block * 8 + r) for r in range(8)], axis=1)
        mix(block * 8, value, 8)
        if 1 <= block < 5:
            ms_gradient(block * 8, value)
    loop(0, IROWS, blur_row)
    loop(2, 10, back_rows)
    for block in range(1, 5):
        grad = hs_gradient(block * 8, 8)
        values = []
        for r in range(8):
            row = block * 8 + r
            now = start_row(row)
            new = now + STEP * (grad[:, r * 128 : r * 128 + 128] + g_ref[pl.ds((row - 8) * 32, 32), :])
            row_at = 16 * s - 16 + row
            new = jnp.where(in_columns & (row_at >= 0) & (row_at < 128), new, 0.0)
            c1_ref[pl.ds((row - 8) * 32, 32), :] = new
            values.append(new)
        value = jnp.concatenate(values, axis=1)
        mix(block * 8, value, 8)
        if 2 <= block < 4:
            ms_gradient(block * 8, value)
    loop(2, 8, blur_row)
    loop(4, 8, back_rows)
    place_at = lax.broadcasted_iota(jnp.int32, (LANES, LANES), 1)
    take = lax.broadcasted_iota(jnp.int32, (LANES, LANES), 0)
    shift = 4 * (take % 32) + take // 32 - 16
    order = [(place_at == shift + 64 * half) & (shift >= 0) & (shift < 64) for half in range(2)]
    order = [jnp.where(o, 1.0, 0.0).astype(bf16) for o in order]
    grads = [hs_gradient(16, 8), hs_gradient(24, 8)]
    for r in range(8):
        total = None
        for half in range(2):
            row = 8 + r + 8 * half
            at = pl.ds(row * 32, 32)
            value = STEP * (grads[half][:, r * 128 : r * 128 + 128] + g_ref[at, :])
            value = value + (c1_ref[at, :] - start_row(row + 8))
            rest = jnp.where((group >= 4) & (group < 20), value, 0.0)
            for _ in range(3):
                piece = rest.astype(bf16)
                rest = rest - piece.astype(f32)
                moved = jnp.dot(piece, order[half], preferred_element_type=f32)
                total = moved if total is None else total + moved
        out_ref[pl.ds(r, 32, stride=8), :] = total


def refine(pos, tiles, hp, above, below):
    vmem = pl.BlockSpec(memory_space=pltpu.VMEM)
    return pl.pallas_call(
        refine_kernel,
        out_shape=jax.ShapeDtypeStruct((32 * 8, LANES), f32),
        in_specs=[pl.BlockSpec(memory_space=pltpu.SMEM)] + [vmem] * 11,
        out_specs=vmem,
        scratch_shapes=[
            pltpu.VMEM((32 * CROWS, LANES), f32),
            pltpu.VMEM((8 * MROWS, LANES), f32),
            pltpu.VMEM((CROWS * LANES, LANES), f32),
            pltpu.VMEM((CROWS * LANES, LANES), f32),
            pltpu.VMEM((256, LANES), f32),
            pltpu.VMEM((256, LANES), f32),
            pltpu.VMEM((MROWS * LANES, LANES), f32),
            pltpu.VMEM((MROWS * LANES, LANES), f32),
            pltpu.VMEM((MROWS * 32, LANES), f32),
            pltpu.VMEM((MROWS * 32, LANES), f32),
            pltpu.VMEM((256, LANES), f32),
            pltpu.VMEM((256, LANES), f32),
            pltpu.VMEM((LANES, LANES), f32),
            pltpu.VMEM((LANES, LANES), f32),
        ],
        compiler_params=pltpu.CompilerParams(vmem_limit_bytes=40 * 2**20),
        cost_estimate=pl.CostEstimate(flops=400_000_000, bytes_accessed=2_000_000, transcendentals=0),
        name="refine",
    )(pos, *tiles, hp, above, below)


def pack_kernel(pos_ref, ca_ref, cb_ref, ma_ref, mb_ref, *rest_refs):
    tile_refs = rest_refs[:8]
    wide_ref = rest_refs[8]
    s = pos_ref[0] // 16
    b = pos_ref[0] % 16
    off = jnp.where(b % 2 == 0, 112, 48)
    lane = lax.broadcasted_iota(jnp.int32, (1, LANES), 1)
    first = lane >= off
    block = (b + 1) // 2 - jnp.where(first, 1, 0)
    keep = (block >= 0) & (block < 8)
    source = lax.broadcasted_iota(jnp.int32, (LANES, LANES), 0)
    target = lax.broadcasted_iota(jnp.int32, (LANES, LANES), 1)
    order = jnp.where(source == (4 * (target % 32) + target // 32 + off) % LANES, 1.0, 0.0).astype(bf16)
    ms = jnp.where(first, ma_ref[...].reshape(128, LANES).astype(f32), mb_ref[...].reshape(128, LANES).astype(f32))
    ms = jnp.where(keep, ms, 0.0).astype(bf16)
    ms = jnp.dot(ms, order, preferred_element_type=f32)
    tile_refs[0][4 * CROWS : 4 * CROWS + 128] = ms
    for k in range(8):
        at = slice(4 * CROWS + 8 * k, 4 * CROWS + 8 * k + 8)
        tile_refs[1][at] = ms[16 * k + 8 : 16 * k + 16]
        tile_refs[7][at] = ms[16 * k : 16 * k + 8]
    edge = jnp.zeros((16, LANES), f32)
    for k in range(4):
        rest = jnp.where(keep, jnp.where(first, ca_ref[k], cb_ref[k]), 0.0)
        total = None
        for _ in range(3):
            piece = rest.astype(bf16)
            rest = rest - piece.astype(f32)
            moved = jnp.dot(piece, order, preferred_element_type=f32)
            total = moved if total is None else total + moved
        wide_ref[k, 0:16] = edge
        wide_ref[k, 16:144] = total
        wide_ref[k, 144:160] = edge
    for d in range(8):
        t = (s + d) % 8
        at = pl.ds(pl.multiple_of(16 * t, 16), CROWS)
        for k in range(4):
            tile_refs[d][k * CROWS : k * CROWS + CROWS] = wide_ref[k, at, :]


def pack(pos, coeffs_in, ms_image):
    def low(i, p):
        return (0, 0, jnp.maximum((p[0] % 16 + 1) // 2 - 1, 0))

    def high(i, p):
        return (0, 0, jnp.minimum((p[0] % 16 + 1) // 2, 7))

    rows = [4 * CROWS + {0: 128, 1: 64, 7: 64}.get(d, 0) for d in range(8)]
    return pl.pallas_call(
        pack_kernel,
        out_shape=tuple(jax.ShapeDtypeStruct((count, LANES), f32) for count in rows),
        grid_spec=pltpu.PrefetchScalarGridSpec(
            num_scalar_prefetch=1,
            grid=(1,),
            in_specs=[
                pl.BlockSpec((4, 128, LANES), low),
                pl.BlockSpec((4, 128, LANES), high),
                pl.BlockSpec((8, 16, LANES), low),
                pl.BlockSpec((8, 16, LANES), high),
            ],
            out_specs=tuple(pl.BlockSpec((count, LANES), lambda i, p: (0, 0)) for count in rows),
            scratch_shapes=[pltpu.VMEM((4, 160, LANES), f32)],
        ),
        compiler_params=pltpu.CompilerParams(vmem_limit_bytes=60 * 2**20),
        cost_estimate=pl.CostEstimate(flops=100_000_000, bytes_accessed=1_600_000, transcendentals=0),
        name="pack",
    )(pos, coeffs_in, coeffs_in, ms_image, ms_image)


def spread_kernel(hs_ref, k_ref, basis_ref, response_ref, sent_ref):
    lane = lax.broadcasted_iota(jnp.int32, (1, LANES), 1)
    hs = hs_ref[...].astype(f32)
    rows = [jnp.concatenate([hs[:, i, :], jnp.zeros((2, 256), f32)], axis=0) for i in range(4)]
    sent_ref[0, :, 128:256] = jnp.zeros((16, 128), f32)
    for a in range(9):
        sent_ref[0, 0:14, 128 + 9 * a : 137 + 9 * a] = k_ref[a]
    sent_ref[0, 0:14, 209:241] = basis_ref[...].astype(f32)
    sent_ref[0, 0:14, 241:249] = response_ref[...].astype(f32).T
    params = sent_ref[0, :, 128:256]
    for t in range(16):
        total = jnp.zeros((16, LANES), f32)
        for i in range(4):
            moved = pltpu.roll(rows[i], (24 * i + 3 - 16 * t) % 256, 1)[:, 0:128]
            total = jnp.where((lane >= 24 * i) & (lane < 24 * i + 24), moved, total)
        sent_ref[t, :, 0:128] = total
        if t:
            sent_ref[t, :, 128:256] = params


def spread(hs_image, kernels, basis, response):
    vmem = pl.BlockSpec(memory_space=pltpu.VMEM)
    return pl.pallas_call(
        spread_kernel,
        out_shape=jax.ShapeDtypeStruct((16, 16, 256), f32),
        in_specs=[vmem] * 4,
        out_specs=vmem,
        compiler_params=pltpu.CompilerParams(vmem_limit_bytes=60 * 2**20),
        cost_estimate=pl.CostEstimate(flops=1_000_000, bytes_accessed=1_000_000, transcendentals=0),
        name="spread",
    )(hs_image, kernels, basis, response)


def encode_kernel(d_ref, out_ref):
    scales = []
    codes = []
    for k in range(4):
        part = d_ref[:, k]
        size = jnp.abs(part)
        top = jnp.max(size, axis=(0, 1, 2), keepdims=True)
        scale = rounded(jnp.maximum(top * (1 + 2**-7), 1e-30))
        code = jnp.exp2(size * (SPAN / scale) - SPAN / 2)
        codes.append(jnp.where(part < 0, -code, code))
        scales.append(jnp.broadcast_to(scale[0], (1, LANES)))
    scales = jnp.concatenate(scales + [jnp.zeros((12, LANES), f32)], axis=0).astype(bf16)
    for s in range(8):
        row = jnp.concatenate([codes[k][s] for k in range(4)], axis=0).astype(bf16)
        for t in range(16):
            out_ref[t, 32 * s : 32 * s + 32] = row
    for t in range(16):
        out_ref[t, 256:272] = scales


def encode(owned):
    vmem = pl.BlockSpec(memory_space=pltpu.VMEM)
    return pl.pallas_call(
        encode_kernel,
        out_shape=jax.ShapeDtypeStruct((16, 272, LANES), bf16),
        in_specs=[vmem],
        out_specs=vmem,
        compiler_params=pltpu.CompilerParams(vmem_limit_bytes=16 * 2**20),
        name="encode",
    )(owned)


def place_kernel(g_ref, c_ref, out_ref):
    lane = lax.broadcasted_iota(jnp.int32, (1, LANES), 1)
    low = lane < 64
    scales = [g_ref[e, 256:272].astype(f32) * (1 / SPAN) for e in range(2)]
    for s in range(8):
        pair = []
        for e in range(2):
            code = g_ref[e, 32 * s : 32 * s + 32].astype(f32)
            size = jnp.log2(jnp.abs(code)) + SPAN / 2
            pair.append(jnp.where(code < 0, -size, size))
        for k in range(4):
            even, odd = [pair[e][8 * k : 8 * k + 8] * scales[e][k : k + 1] for e in range(2)]
            for half, value in enumerate(
                [jnp.where(low, even, pltpu.roll(odd, 64, 1)), jnp.where(low, pltpu.roll(even, 64, 1), odd)]
            ):
                at = slice(16 * s + 8 * half, 16 * s + 8 * half + 8)
                out_ref[k, at] = c_ref[k, at] + value


def place(gathered, coeffs_in):
    block = pl.BlockSpec((4, 128, LANES), lambda j: (0, 0, j))
    return pl.pallas_call(
        place_kernel,
        out_shape=jax.ShapeDtypeStruct((4, 128, 1024), f32),
        grid=(8,),
        in_specs=[pl.BlockSpec((2, 272, LANES), lambda j: (j, 0, 0)), block],
        out_specs=block,
        compiler_params=pltpu.CompilerParams(vmem_limit_bytes=32 * 2**20),
        name="place",
    )(gathered, coeffs_in)


def per_device(coeffs_in, basis, kernels, response, hs_image, ms_image):
    pos = (lax.axis_index("sub") * 16 + lax.axis_index("band")).astype(jnp.int32).reshape(1)
    sent = spread(hs_image, kernels.transpose(1, 0, 2), basis, response)
    hp = lax.all_to_all(sent, "band", split_axis=0, concat_axis=0, tiled=True).reshape(256, 256)
    tiles = pack(pos, coeffs_in, ms_image)
    tiles = [tiles[0]] + [
        lax.ppermute(tiles[d], "sub", [(i, (i + d) % 8) for i in range(8)]) for d in range(1, 8)
    ]
    seen = hp[:, 0:128].astype(bf16)
    above = lax.ppermute(seen, "sub", [(i, i + 1) for i in range(7)])
    below = lax.ppermute(seen, "sub", [(i + 1, i) for i in range(7)])
    new = refine(pos, tiles, hp, above, below)
    owned = lax.all_to_all(new.reshape(8, 4, 8, LANES), "sub", split_axis=0, concat_axis=0, tiled=True)
    gathered = lax.all_to_all(encode(owned), "band", split_axis=0, concat_axis=0, tiled=True)
    return place(gathered, coeffs_in)


def solution(mesh):
    return jax.shard_map(
        per_device,
        mesh=mesh,
        in_specs=(
            P("sub", None, None),
            P("band", None),
            P("band", None, None),
            P(None, "band"),
            P("band", "sub", None),
            P(None, "sub", None),
        ),
        out_specs=P("sub", None, None),
        check_vma=False,
    )
```

```python
import functools

import jax
import jax.numpy as jnp
from jax import lax
from jax.experimental import pallas as pl
from jax.experimental.pallas import tpu as pltpu
from jax.sharding import PartitionSpec as P

STEP = 0.15
TR, TC = 16, 64
TAPS = 9
SPAN = 250.0
LANES = 128
CROWS = 48
MROWS = 32
IROWS = 10
JCOLS = 24
ROWS_LO, COLS_LO = 32, 256
f32 = jnp.float32
bf16 = jnp.bfloat16


def rounded(value):
    return value.astype(bf16).astype(f32)


def refine_kernel(pos_ref, *refs):
    tiles = refs[:8]
    hp_ref, above_ref, below_ref, out_ref, c_ref, ms_ref, m0, m1, f0, f1, b0, b1, c1_ref, g_ref, hs0, hs1, w0, w1 = refs[8:]
    s = pos_ref[0] // 16
    b = pos_ref[0] % 16
    for d in range(8):
        at = pl.multiple_of((s + 8 - d) % 8 * (4 * CROWS), 4 * CROWS)
        c_ref[pl.ds(at, 4 * CROWS), :] = tiles[d][0 : 4 * CROWS]
    for k in range(8):
        ms_ref[32 * k : 32 * k + 8, :] = tiles[1][4 * CROWS + 8 * k : 4 * CROWS + 8 * k + 8]
        ms_ref[32 * k + 8 : 32 * k + 24, :] = tiles[0][4 * CROWS + 16 * k : 4 * CROWS + 16 * k + 16]
        ms_ref[32 * k + 24 : 32 * k + 32, :] = tiles[7][4 * CROWS + 8 * k : 4 * CROWS + 8 * k + 8]
    bk = (b0, b1)
    m = (m0, m1)
    f = (f0, f1)
    hst = (hs0, hs1)
    w = (w0, w1)
    for h in range(2):
        at = slice(h * 128, h * 128 + 128)
        hst[h][0:72, :] = above_ref[at, :].astype(f32).T[24:96]
        hst[h][72:168, :] = hp_ref[at, 0:128].T[0:96]
        hst[h][168:240, :] = below_ref[at, :].astype(f32).T[0:72]
        w[h][...] = hp_ref[at, 128:256].T
    basis = jnp.concatenate([w0[81:113, :], w1[81:113, :]], axis=1).astype(bf16)
    response = jnp.concatenate([w0[113:121, :], w1[113:121, :]], axis=1).astype(bf16)
    combined = lax.dot_general(response, basis, (((1,), (1,)), ((), ())), preferred_element_type=f32).astype(bf16)
    lane = lax.broadcasted_iota(jnp.int32, (1, LANES), 1)
    group = lane % 32
    column = 64 * b - 16 + 4 * group + lane // 32
    in_columns = (column >= 0) & (column < 1024) & (group >= 2) & (group < 22)

    def mix(row, value, rows):
        mixed = lax.dot_general(value.astype(bf16), basis, (((0,), (0,)), ((), ())), preferred_element_type=f32)
        mixed = rounded(mixed)
        at = pl.ds(pl.multiple_of(row * LANES, LANES), rows * LANES)
        for h in range(2):
            m[h][at, :] = mixed[:, h * 128 : h * 128 + 128]

    def ms_gradient(row, block):
        predicted = jnp.dot(combined, block.astype(bf16), preferred_element_type=f32)
        seen = jnp.concatenate([ms_ref[pl.ds(row - 8 + r, 8, stride=MROWS), :] for r in range(8)], axis=1)
        misfit = (seen - predicted).astype(bf16)
        grad = lax.dot_general(combined, misfit, (((0,), (0,)), ((), ())), preferred_element_type=f32)
        for r in range(8):
            g_ref[pl.ds((row - 8 + r) * 32, 32), :] = grad[:, r * 128 : r * 128 + 128]

    def blur_row(n):
        g = lax.broadcasted_iota(jnp.int32, (JCOLS, LANES), 0)
        i_at = 4 * s + n - 3
        j_at = 16 * b + g - 3
        inside = (i_at >= 0) & (i_at < ROWS_LO) & (j_at >= 0) & (j_at < COLS_LO)
        for h in range(2):
            acc = [None, None, None]
            for a in range(TAPS):
                for q in range(4):
                    at = pl.multiple_of((4 * n + a) * LANES + 32 * q, 32)
                    x = m[h][pl.ds(at, JCOLS), :]
                    for d in range(3):
                        if 4 * d + q > 8:
                            continue
                        tap = a * 9 + 4 * d + q
                        term = w[h][tap : tap + 1, :] * x
                        acc[d] = term if acc[d] is None else acc[d] + term
            blurred = acc[0] + pltpu.roll(acc[1], JCOLS - 1, 0) + pltpu.roll(acc[2], JCOLS - 2, 0)
            seen = hst[h][pl.ds(pl.multiple_of(n * JCOLS, 8), JCOLS), :]
            f[h][pl.ds(pl.multiple_of(8 + n * JCOLS, 8), JCOLS), :] = jnp.where(inside, seen - blurred, 0.0)

    def back_rows(u):
        for h in range(2):
            win = [[f[h][pl.ds(8 + (u - t) * JCOLS - tt, JCOLS), :] for tt in range(3)] for t in range(3)]
            for p in range(4):
                for q in range(4):
                    total = None
                    for t in range(3):
                        for tt in range(3):
                            if p + 4 * t > 8 or q + 4 * tt > 8:
                                continue
                            tap = (p + 4 * t) * 9 + q + 4 * tt
                            term = w[h][tap : tap + 1, :] * win[t][tt]
                            total = term if total is None else total + term
                    at = pl.multiple_of((4 * u - 8 + p) * LANES + 32 * q, 32)
                    bk[h][pl.ds(at, JCOLS), :] = rounded(total)

    def hs_gradient(row, rows):
        at = pl.ds((row - 8) * LANES, rows * LANES)
        back = jnp.concatenate([b0[at, :].astype(bf16), b1[at, :].astype(bf16)], axis=1)
        return lax.dot_general(basis, back, (((1,), (1,)), ((), ())), preferred_element_type=f32)

    def start_row(row):
        return c_ref[pl.ds(row, 32, stride=CROWS), :]

    def loop(low, high, body):
        def step(n, _):
            body(n)
            return 0

        lax.fori_loop(low, high, step, 0)

    for block in range(CROWS // 8):
        value = jnp.concatenate([start_row(block * 8 + r) for r in range(8)], axis=1)
        mix(block * 8, value, 8)
        if 1 <= block < 5:
            ms_gradient(block * 8, value)
    loop(0, IROWS, blur_row)
    loop(2, 10, back_rows)
    for block in range(1, 5):
        grad = hs_gradient(block * 8, 8)
        values = []
        for r in range(8):
            row = block * 8 + r
            now = start_row(row)
            new = now + STEP * (grad[:, r * 128 : r * 128 + 128] + g_ref[pl.ds((row - 8) * 32, 32), :])
            row_at = 16 * s - 16 + row
            new = jnp.where(in_columns & (row_at >= 0) & (row_at < 128), new, 0.0)
            c1_ref[pl.ds((row - 8) * 32, 32), :] = new
            values.append(new)
        value = jnp.concatenate(values, axis=1)
        mix(block * 8, value, 8)
        if 2 <= block < 4:
            ms_gradient(block * 8, value)
    loop(2, 8, blur_row)
    loop(4, 8, back_rows)
    place_at = lax.broadcasted_iota(jnp.int32, (LANES, LANES), 1)
    take = lax.broadcasted_iota(jnp.int32, (LANES, LANES), 0)
    shift = 4 * (take % 32) + take // 32 - 16
    order = [(place_at == shift + 64 * ((half + b) % 2)) & (shift >= 0) & (shift < 64) for half in range(2)]
    order = [jnp.where(o, 1.0, 0.0).astype(bf16) for o in order]
    grads = [hs_gradient(16, 8), hs_gradient(24, 8)]
    for r in range(8):
        total = None
        for half in range(2):
            row = 8 + r + 8 * half
            at = pl.ds(row * 32, 32)
            value = STEP * (grads[half][:, r * 128 : r * 128 + 128] + g_ref[at, :])
            value = value + (c1_ref[at, :] - start_row(row + 8))
            rest = jnp.where((group >= 4) & (group < 20), value, 0.0)
            for _ in range(3):
                piece = rest.astype(bf16)
                rest = rest - piece.astype(f32)
                moved = jnp.dot(piece, order[half], preferred_element_type=f32)
                total = moved if total is None else total + moved
        out_ref[pl.ds(r, 32, stride=8), :] = total


def refine(pos, tiles, hp, above, below):
    vmem = pl.BlockSpec(memory_space=pltpu.VMEM)
    return pl.pallas_call(
        refine_kernel,
        out_shape=jax.ShapeDtypeStruct((32 * 8, LANES), f32),
        in_specs=[pl.BlockSpec(memory_space=pltpu.SMEM)] + [vmem] * 11,
        out_specs=vmem,
        scratch_shapes=[
            pltpu.VMEM((32 * CROWS, LANES), f32),
            pltpu.VMEM((8 * MROWS, LANES), f32),
            pltpu.VMEM((CROWS * LANES, LANES), f32),
            pltpu.VMEM((CROWS * LANES, LANES), f32),
            pltpu.VMEM((256, LANES), f32),
            pltpu.VMEM((256, LANES), f32),
            pltpu.VMEM((MROWS * LANES, LANES), f32),
            pltpu.VMEM((MROWS * LANES, LANES), f32),
            pltpu.VMEM((MROWS * 32, LANES), f32),
            pltpu.VMEM((MROWS * 32, LANES), f32),
            pltpu.VMEM((256, LANES), f32),
            pltpu.VMEM((256, LANES), f32),
            pltpu.VMEM((LANES, LANES), f32),
            pltpu.VMEM((LANES, LANES), f32),
        ],
        compiler_params=pltpu.CompilerParams(vmem_limit_bytes=40 * 2**20),
        cost_estimate=pl.CostEstimate(flops=400_000_000, bytes_accessed=2_000_000, transcendentals=0),
        name="refine",
    )(pos, *tiles, hp, above, below)


def pack_kernel(pos_ref, ca_ref, cb_ref, ma_ref, mb_ref, *rest_refs):
    tile_refs = rest_refs[:8]
    wide_ref = rest_refs[8]
    s = pos_ref[0] // 16
    b = pos_ref[0] % 16
    off = jnp.where(b % 2 == 0, 112, 48)
    lane = lax.broadcasted_iota(jnp.int32, (1, LANES), 1)
    first = lane >= off
    block = (b + 1) // 2 - jnp.where(first, 1, 0)
    keep = (block >= 0) & (block < 8)
    source = lax.broadcasted_iota(jnp.int32, (LANES, LANES), 0)
    target = lax.broadcasted_iota(jnp.int32, (LANES, LANES), 1)
    order = jnp.where(source == (4 * (target % 32) + target // 32 + off) % LANES, 1.0, 0.0).astype(bf16)
    ms = jnp.where(first, ma_ref[...].reshape(128, LANES).astype(f32), mb_ref[...].reshape(128, LANES).astype(f32))
    ms = jnp.where(keep, ms, 0.0).astype(bf16)
    ms = jnp.dot(ms, order, preferred_element_type=f32)
    tile_refs[0][4 * CROWS : 4 * CROWS + 128] = ms
    for k in range(8):
        at = slice(4 * CROWS + 8 * k, 4 * CROWS + 8 * k + 8)
        tile_refs[1][at] = ms[16 * k + 8 : 16 * k + 16]
        tile_refs[7][at] = ms[16 * k : 16 * k + 8]
    edge = jnp.zeros((16, LANES), f32)
    for k in range(4):
        rest = jnp.where(keep, jnp.where(first, ca_ref[k], cb_ref[k]), 0.0)
        total = None
        for _ in range(3):
            piece = rest.astype(bf16)
            rest = rest - piece.astype(f32)
            moved = jnp.dot(piece, order, preferred_element_type=f32)
            total = moved if total is None else total + moved
        wide_ref[k, 0:16] = edge
        wide_ref[k, 16:144] = total
        wide_ref[k, 144:160] = edge
    for d in range(8):
        t = (s + d) % 8
        at = pl.ds(pl.multiple_of(16 * t, 16), CROWS)
        for k in range(4):
            tile_refs[d][k * CROWS : k * CROWS + CROWS] = wide_ref[k, at, :]


def pack(pos, coeffs_in, ms_image):
    def low(i, p):
        return (0, 0, jnp.maximum((p[0] % 16 + 1) // 2 - 1, 0))

    def high(i, p):
        return (0, 0, jnp.minimum((p[0] % 16 + 1) // 2, 7))

    rows = [4 * CROWS + {0: 128, 1: 64, 7: 64}.get(d, 0) for d in range(8)]
    return pl.pallas_call(
        pack_kernel,
        out_shape=tuple(jax.ShapeDtypeStruct((count, LANES), f32) for count in rows),
        grid_spec=pltpu.PrefetchScalarGridSpec(
            num_scalar_prefetch=1,
            grid=(1,),
            in_specs=[
                pl.BlockSpec((4, 128, LANES), low),
                pl.BlockSpec((4, 128, LANES), high),
                pl.BlockSpec((8, 16, LANES), low),
                pl.BlockSpec((8, 16, LANES), high),
            ],
            out_specs=tuple(pl.BlockSpec((count, LANES), lambda i, p: (0, 0)) for count in rows),
            scratch_shapes=[pltpu.VMEM((4, 160, LANES), f32)],
        ),
        compiler_params=pltpu.CompilerParams(vmem_limit_bytes=60 * 2**20),
        cost_estimate=pl.CostEstimate(flops=100_000_000, bytes_accessed=1_600_000, transcendentals=0),
        name="pack",
    )(pos, coeffs_in, coeffs_in, ms_image, ms_image)


def spread_kernel(hs_ref, k_ref, basis_ref, response_ref, sent_ref):
    lane = lax.broadcasted_iota(jnp.int32, (1, LANES), 1)
    hs = hs_ref[...].astype(f32)
    rows = [jnp.concatenate([hs[:, i, :], jnp.zeros((2, 256), f32)], axis=0) for i in range(4)]
    sent_ref[0, :, 128:256] = jnp.zeros((16, 128), f32)
    for a in range(9):
        sent_ref[0, 0:14, 128 + 9 * a : 137 + 9 * a] = k_ref[a]
    sent_ref[0, 0:14, 209:241] = basis_ref[...].astype(f32)
    sent_ref[0, 0:14, 241:249] = response_ref[...].astype(f32).T
    params = sent_ref[0, :, 128:256]
    for t in range(16):
        total = jnp.zeros((16, LANES), f32)
        for i in range(4):
            moved = pltpu.roll(rows[i], (24 * i + 3 - 16 * t) % 256, 1)[:, 0:128]
            total = jnp.where((lane >= 24 * i) & (lane < 24 * i + 24), moved, total)
        sent_ref[t, :, 0:128] = total
        if t:
            sent_ref[t, :, 128:256] = params


def spread(hs_image, kernels, basis, response):
    vmem = pl.BlockSpec(memory_space=pltpu.VMEM)
    return pl.pallas_call(
        spread_kernel,
        out_shape=jax.ShapeDtypeStruct((16, 16, 256), f32),
        in_specs=[vmem] * 4,
        out_specs=vmem,
        compiler_params=pltpu.CompilerParams(vmem_limit_bytes=60 * 2**20),
        cost_estimate=pl.CostEstimate(flops=1_000_000, bytes_accessed=1_000_000, transcendentals=0),
        name="spread",
    )(hs_image, kernels, basis, response)


def encode_kernel(d_ref, out_ref):
    scales = []
    codes = []
    for k in range(4):
        part = d_ref[:, k]
        size = jnp.abs(part)
        top = jnp.max(size, axis=(0, 1, 2), keepdims=True)
        scale = rounded(jnp.maximum(top * (1 + 2**-7), 1e-30))
        code = jnp.exp2(size * (SPAN / scale) - SPAN / 2)
        codes.append(jnp.where(part < 0, -code, code))
        scales.append(jnp.broadcast_to(scale[0], (1, LANES)))
    scales = jnp.concatenate(scales + [jnp.zeros((12, LANES), f32)], axis=0).astype(bf16)
    for s in range(8):
        row = jnp.concatenate([codes[k][s] for k in range(4)], axis=0).astype(bf16)
        for t in range(16):
            out_ref[t, 32 * s : 32 * s + 32] = row
    for t in range(16):
        out_ref[t, 256:272] = scales


def encode(owned):
    vmem = pl.BlockSpec(memory_space=pltpu.VMEM)
    return pl.pallas_call(
        encode_kernel,
        out_shape=jax.ShapeDtypeStruct((16, 272, LANES), bf16),
        in_specs=[vmem],
        out_specs=vmem,
        compiler_params=pltpu.CompilerParams(vmem_limit_bytes=16 * 2**20),
        name="encode",
    )(owned)


def place_kernel(g_ref, c_ref, out_ref):
    lane = lax.broadcasted_iota(jnp.int32, (1, LANES), 1)
    low = lane < 64
    count = g_ref.shape[0] // 2
    for j in range(count):
        even, odd = [g_ref[2 * j + e, 256:272].astype(f32) * (1 / SPAN) for e in range(2)]
        scales = (jnp.where(low, even, odd), jnp.where(low, odd, even))
        columns = slice(j * LANES, j * LANES + LANES)
        for s in range(8):
            even, odd = [g_ref[2 * j + e, 32 * s : 32 * s + 32].astype(f32) for e in range(2)]
            for half, code in enumerate((jnp.where(low, even, odd), jnp.where(low, odd, even))):
                size = jnp.log2(jnp.abs(code)) + SPAN / 2
                value = jnp.where(code < 0, -size, size)
                for k in range(4):
                    part = value[8 * k : 8 * k + 8] * scales[half][k : k + 1]
                    if half:
                        part = pltpu.roll(part, 64, 1)
                    at = slice(16 * s + 8 * half, 16 * s + 8 * half + 8)
                    out_ref[k, at, columns] = c_ref[k, at, columns] + part


def place(gathered, coeffs_in):
    block = pl.BlockSpec((4, 128, 4 * LANES), lambda j: (0, 0, j))
    return pl.pallas_call(
        place_kernel,
        out_shape=jax.ShapeDtypeStruct((4, 128, 1024), f32),
        grid=(2,),
        in_specs=[pl.BlockSpec((8, 272, LANES), lambda j: (j, 0, 0)), block],
        out_specs=block,
        compiler_params=pltpu.CompilerParams(vmem_limit_bytes=32 * 2**20),
        name="place",
    )(gathered, coeffs_in)


def per_device(coeffs_in, basis, kernels, response, hs_image, ms_image):
    pos = (lax.axis_index("sub") * 16 + lax.axis_index("band")).astype(jnp.int32).reshape(1)
    sent = spread(hs_image, kernels.transpose(1, 0, 2), basis, response)
    hp = lax.all_to_all(sent, "band", split_axis=0, concat_axis=0, tiled=True).reshape(256, 256)
    tiles = pack(pos, coeffs_in, ms_image)
    tiles = [tiles[0]] + [
        lax.ppermute(tiles[d], "sub", [(i, (i + d) % 8) for i in range(8)]) for d in range(1, 8)
    ]
    seen = hp[:, 0:128].astype(bf16)
    above = lax.ppermute(seen, "sub", [(i, i + 1) for i in range(7)])
    below = lax.ppermute(seen, "sub", [(i + 1, i) for i in range(7)])
    new = refine(pos, tiles, hp, above, below)
    owned = lax.all_to_all(new.reshape(8, 4, 8, LANES), "sub", split_axis=0, concat_axis=0, tiled=True)
    gathered = lax.all_to_all(encode(owned), "band", split_axis=0, concat_axis=0, tiled=True)
    return place(gathered, coeffs_in)


def solution(mesh):
    return jax.shard_map(
        per_device,
        mesh=mesh,
        in_specs=(
            P("sub", None, None),
            P("band", None),
            P("band", None, None),
            P(None, "band"),
            P("band", "sub", None),
            P(None, "sub", None),
        ),
        out_specs=P("sub", None, None),
        check_vma=False,
    )
```

```python
import functools

import jax
import jax.numpy as jnp
from jax import lax
from jax.experimental import pallas as pl
from jax.experimental.pallas import tpu as pltpu
from jax.sharding import PartitionSpec as P

STEP = 0.15
TR, TC = 16, 64
TAPS = 9
SPAN = 250.0
LANES = 128
CROWS = 48
MROWS = 32
IROWS = 10
JCOLS = 24
ROWS_LO, COLS_LO = 32, 256
f32 = jnp.float32
bf16 = jnp.bfloat16


def rounded(value):
    return value.astype(bf16).astype(f32)


def refine_kernel(pos_ref, *refs):
    mine_ref, other_ref, hp_ref, seen_ref, above_ref, below_ref, out_ref, c_ref, ms_ref, m0, m1, f0, f1, b0, b1, c1_ref, g_ref, hs0, hs1, w0, w1 = refs
    s = pos_ref[0] // 16
    b = pos_ref[0] % 16
    core = s % 2
    for d in range(4):
        chip = (s // 2 + 4 - d) % 4
        mine = pl.multiple_of((2 * chip + core) * (4 * CROWS), 4 * CROWS)
        theirs = pl.multiple_of((2 * chip + 1 - core) * (4 * CROWS), 4 * CROWS)
        c_ref[pl.ds(mine, 4 * CROWS), :] = mine_ref[d * 4 * CROWS : (d + 1) * 4 * CROWS]
        c_ref[pl.ds(theirs, 4 * CROWS), :] = other_ref[d * 4 * CROWS : (d + 1) * 4 * CROWS]
    for k in range(8):
        at = slice(256 + 16 * k, 272 + 16 * k)
        ms_ref[32 * k : 32 * k + 8, :] = above_ref[at, :].astype(f32)[8:16]
        ms_ref[32 * k + 8 : 32 * k + 24, :] = seen_ref[at, :].astype(f32)
        ms_ref[32 * k + 24 : 32 * k + 32, :] = below_ref[at, :].astype(f32)[0:8]
    bk = (b0, b1)
    m = (m0, m1)
    f = (f0, f1)
    hst = (hs0, hs1)
    w = (w0, w1)
    for h in range(2):
        at = slice(h * 128, h * 128 + 128)
        hst[h][0:72, :] = above_ref[at, :].astype(f32).T[24:96]
        hst[h][72:168, :] = hp_ref[at, 0:128].T[0:96]
        hst[h][168:240, :] = below_ref[at, :].astype(f32).T[0:72]
        w[h][...] = hp_ref[at, 128:256].T
    basis = jnp.concatenate([w0[81:113, :], w1[81:113, :]], axis=1).astype(bf16)
    response = jnp.concatenate([w0[113:121, :], w1[113:121, :]], axis=1).astype(bf16)
    combined = lax.dot_general(response, basis, (((1,), (1,)), ((), ())), preferred_element_type=f32).astype(bf16)
    lane = lax.broadcasted_iota(jnp.int32, (1, LANES), 1)
    group = lane % 32
    column = 64 * b - 16 + 4 * group + lane // 32
    in_columns = (column >= 0) & (column < 1024) & (group >= 2) & (group < 22)

    def mix(row, value, rows):
        mixed = lax.dot_general(value.astype(bf16), basis, (((0,), (0,)), ((), ())), preferred_element_type=f32)
        mixed = rounded(mixed)
        at = pl.ds(pl.multiple_of(row * LANES, LANES), rows * LANES)
        for h in range(2):
            m[h][at, :] = mixed[:, h * 128 : h * 128 + 128]

    def ms_gradient(row, block):
        predicted = jnp.dot(combined, block.astype(bf16), preferred_element_type=f32)
        seen = jnp.concatenate([ms_ref[pl.ds(row - 8 + r, 8, stride=MROWS), :] for r in range(8)], axis=1)
        misfit = (seen - predicted).astype(bf16)
        grad = lax.dot_general(combined, misfit, (((0,), (0,)), ((), ())), preferred_element_type=f32)
        for r in range(8):
            g_ref[pl.ds((row - 8 + r) * 32, 32), :] = grad[:, r * 128 : r * 128 + 128]

    def blur_row(n):
        g = lax.broadcasted_iota(jnp.int32, (JCOLS, LANES), 0)
        i_at = 4 * s + n - 3
        j_at = 16 * b + g - 3
        inside = (i_at >= 0) & (i_at < ROWS_LO) & (j_at >= 0) & (j_at < COLS_LO)
        for h in range(2):
            acc = [None, None, None]
            for a in range(TAPS):
                for q in range(4):
                    at = pl.multiple_of((4 * n + a) * LANES + 32 * q, 32)
                    x = m[h][pl.ds(at, JCOLS), :]
                    for d in range(3):
                        if 4 * d + q > 8:
                            continue
                        tap = a * 9 + 4 * d + q
                        term = w[h][tap : tap + 1, :] * x
                        acc[d] = term if acc[d] is None else acc[d] + term
            blurred = acc[0] + pltpu.roll(acc[1], JCOLS - 1, 0) + pltpu.roll(acc[2], JCOLS - 2, 0)
            seen = hst[h][pl.ds(pl.multiple_of(n * JCOLS, 8), JCOLS), :]
            f[h][pl.ds(pl.multiple_of(8 + n * JCOLS, 8), JCOLS), :] = jnp.where(inside, seen - blurred, 0.0)

    def back_rows(u):
        for h in range(2):
            win = [[f[h][pl.ds(8 + (u - t) * JCOLS - tt, JCOLS), :] for tt in range(3)] for t in range(3)]
            for p in range(4):
                for q in range(4):
                    total = None
                    for t in range(3):
                        for tt in range(3):
                            if p + 4 * t > 8 or q + 4 * tt > 8:
                                continue
                            tap = (p + 4 * t) * 9 + q + 4 * tt
                            term = w[h][tap : tap + 1, :] * win[t][tt]
                            total = term if total is None else total + term
                    at = pl.multiple_of((4 * u - 8 + p) * LANES + 32 * q, 32)
                    bk[h][pl.ds(at, JCOLS), :] = rounded(total)

    def hs_gradient(row, rows):
        at = pl.ds((row - 8) * LANES, rows * LANES)
        back = jnp.concatenate([b0[at, :].astype(bf16), b1[at, :].astype(bf16)], axis=1)
        return lax.dot_general(basis, back, (((1,), (1,)), ((), ())), preferred_element_type=f32)

    def start_row(row):
        return c_ref[pl.ds(row, 32, stride=CROWS), :]

    def loop(low, high, body):
        def step(n, _):
            body(n)
            return 0

        lax.fori_loop(low, high, step, 0)

    for block in range(CROWS // 8):
        value = jnp.concatenate([start_row(block * 8 + r) for r in range(8)], axis=1)
        mix(block * 8, value, 8)
        if 1 <= block < 5:
            ms_gradient(block * 8, value)
    loop(0, IROWS, blur_row)
    loop(2, 10, back_rows)
    for block in range(1, 5):
        grad = hs_gradient(block * 8, 8)
        values = []
        for r in range(8):
            row = block * 8 + r
            now = start_row(row)
            new = now + STEP * (grad[:, r * 128 : r * 128 + 128] + g_ref[pl.ds((row - 8) * 32, 32), :])
            row_at = 16 * s - 16 + row
            new = jnp.where(in_columns & (row_at >= 0) & (row_at < 128), new, 0.0)
            c1_ref[pl.ds((row - 8) * 32, 32), :] = new
            values.append(new)
        value = jnp.concatenate(values, axis=1)
        mix(block * 8, value, 8)
        if 2 <= block < 4:
            ms_gradient(block * 8, value)
    loop(2, 8, blur_row)
    loop(4, 8, back_rows)
    place_at = lax.broadcasted_iota(jnp.int32, (LANES, LANES), 1)
    take = lax.broadcasted_iota(jnp.int32, (LANES, LANES), 0)
    shift = 4 * (take % 32) + take // 32 - 16
    order = [(place_at == shift + 64 * ((half + b) % 2)) & (shift >= 0) & (shift < 64) for half in range(2)]
    order = [jnp.where(o, 1.0, 0.0).astype(bf16) for o in order]
    grads = [hs_gradient(16, 8), hs_gradient(24, 8)]
    for r in range(8):
        total = None
        for half in range(2):
            row = 8 + r + 8 * half
            at = pl.ds(row * 32, 32)
            value = STEP * (grads[half][:, r * 128 : r * 128 + 128] + g_ref[at, :])
            value = value + (c1_ref[at, :] - start_row(row + 8))
            rest = jnp.where((group >= 4) & (group < 20), value, 0.0)
            for _ in range(3):
                piece = rest.astype(bf16)
                rest = rest - piece.astype(f32)
                moved = jnp.dot(piece, order[half], preferred_element_type=f32)
                total = moved if total is None else total + moved
        out_ref[pl.ds(r, 32, stride=8), :] = total


def refine(pos, mine, other, hp, seen, above, below):
    vmem = pl.BlockSpec(memory_space=pltpu.VMEM)
    return pl.pallas_call(
        refine_kernel,
        out_shape=jax.ShapeDtypeStruct((32 * 8, LANES), f32),
        in_specs=[pl.BlockSpec(memory_space=pltpu.SMEM)] + [vmem] * 6,
        out_specs=vmem,
        scratch_shapes=[
            pltpu.VMEM((32 * CROWS, LANES), f32),
            pltpu.VMEM((8 * MROWS, LANES), f32),
            pltpu.VMEM((CROWS * LANES, LANES), f32),
            pltpu.VMEM((CROWS * LANES, LANES), f32),
            pltpu.VMEM((256, LANES), f32),
            pltpu.VMEM((256, LANES), f32),
            pltpu.VMEM((MROWS * LANES, LANES), f32),
            pltpu.VMEM((MROWS * LANES, LANES), f32),
            pltpu.VMEM((MROWS * 32, LANES), f32),
            pltpu.VMEM((MROWS * 32, LANES), f32),
            pltpu.VMEM((256, LANES), f32),
            pltpu.VMEM((256, LANES), f32),
            pltpu.VMEM((LANES, LANES), f32),
            pltpu.VMEM((LANES, LANES), f32),
        ],
        compiler_params=pltpu.CompilerParams(vmem_limit_bytes=40 * 2**20),
        cost_estimate=pl.CostEstimate(flops=400_000_000, bytes_accessed=2_000_000, transcendentals=0),
        name="refine",
    )(pos, mine, other, hp, seen, above, below)


def pack_kernel(pos_ref, ca_ref, cb_ref, ma_ref, mb_ref, *rest_refs):
    near_ref, wide_ref = rest_refs[4:]
    s = pos_ref[0] // 16
    b = pos_ref[0] % 16
    off = jnp.where(b % 2 == 0, 112, 48)
    lane = lax.broadcasted_iota(jnp.int32, (1, LANES), 1)
    first = lane >= off
    block = (b + 1) // 2 - jnp.where(first, 1, 0)
    keep = (block >= 0) & (block < 8)
    source = lax.broadcasted_iota(jnp.int32, (LANES, LANES), 0)
    target = lax.broadcasted_iota(jnp.int32, (LANES, LANES), 1)
    order = jnp.where(source == (4 * (target % 32) + target // 32 + off) % LANES, 1.0, 0.0).astype(bf16)
    ms = jnp.where(first, ma_ref[...].reshape(128, LANES).astype(f32), mb_ref[...].reshape(128, LANES).astype(f32))
    ms = jnp.where(keep, ms, 0.0).astype(bf16)
    ms = jnp.dot(ms, order, preferred_element_type=f32)
    near_ref[...] = ms.astype(bf16)
    edge = jnp.zeros((16, LANES), f32)
    for k in range(4):
        rest = jnp.where(keep, jnp.where(first, ca_ref[k], cb_ref[k]), 0.0)
        total = None
        for _ in range(3):
            piece = rest.astype(bf16)
            rest = rest - piece.astype(f32)
            moved = jnp.dot(piece, order, preferred_element_type=f32)
            total = moved if total is None else total + moved
        wide_ref[k, 0:16] = edge
        wide_ref[k, 16:144] = total
        wide_ref[k, 144:160] = edge
    for d in range(4):
        at = pl.ds(pl.multiple_of(32 * ((s // 2 + d) % 4), 32), 64)
        for k in range(4):
            rest_refs[d][64 * k : 64 * k + 64] = wide_ref[k, at, :]


def pack(pos, coeffs_in, ms_image):
    def low(i, p):
        return (0, 0, jnp.maximum((p[0] % 16 + 1) // 2 - 1, 0))

    def high(i, p):
        return (0, 0, jnp.minimum((p[0] % 16 + 1) // 2, 7))

    return pl.pallas_call(
        pack_kernel,
        out_shape=(jax.ShapeDtypeStruct((256, LANES), f32),) * 4 + (jax.ShapeDtypeStruct((128, LANES), bf16),),
        grid_spec=pltpu.PrefetchScalarGridSpec(
            num_scalar_prefetch=1,
            grid=(1,),
            in_specs=[
                pl.BlockSpec((4, 128, LANES), low),
                pl.BlockSpec((4, 128, LANES), high),
                pl.BlockSpec((8, 16, LANES), low),
                pl.BlockSpec((8, 16, LANES), high),
            ],
            out_specs=(pl.BlockSpec((256, LANES), lambda i, p: (0, 0)),) * 4
            + (pl.BlockSpec((128, LANES), lambda i, p: (0, 0)),),
            scratch_shapes=[pltpu.VMEM((4, 160, LANES), f32)],
        ),
        compiler_params=pltpu.CompilerParams(vmem_limit_bytes=60 * 2**20),
        cost_estimate=pl.CostEstimate(flops=100_000_000, bytes_accessed=1_600_000, transcendentals=0),
        name="pack",
    )(pos, coeffs_in, coeffs_in, ms_image, ms_image)


def spread_kernel(hs_ref, k_ref, basis_ref, response_ref, sent_ref):
    lane = lax.broadcasted_iota(jnp.int32, (1, LANES), 1)
    hs = hs_ref[...].astype(f32)
    rows = [jnp.concatenate([hs[:, i, :], jnp.zeros((2, 256), f32)], axis=0) for i in range(4)]
    sent_ref[0, :, 128:256] = jnp.zeros((16, 128), f32)
    for a in range(9):
        sent_ref[0, 0:14, 128 + 9 * a : 137 + 9 * a] = k_ref[a]
    sent_ref[0, 0:14, 209:241] = basis_ref[...].astype(f32)
    sent_ref[0, 0:14, 241:249] = response_ref[...].astype(f32).T
    params = sent_ref[0, :, 128:256]
    for t in range(16):
        total = jnp.zeros((16, LANES), f32)
        for i in range(4):
            moved = pltpu.roll(rows[i], (24 * i + 3 - 16 * t) % 256, 1)[:, 0:128]
            total = jnp.where((lane >= 24 * i) & (lane < 24 * i + 24), moved, total)
        sent_ref[t, :, 0:128] = total
        if t:
            sent_ref[t, :, 128:256] = params


def spread(hs_image, kernels, basis, response):
    vmem = pl.BlockSpec(memory_space=pltpu.VMEM)
    return pl.pallas_call(
        spread_kernel,
        out_shape=jax.ShapeDtypeStruct((16, 16, 256), f32),
        in_specs=[vmem] * 4,
        out_specs=vmem,
        compiler_params=pltpu.CompilerParams(vmem_limit_bytes=60 * 2**20),
        cost_estimate=pl.CostEstimate(flops=1_000_000, bytes_accessed=1_000_000, transcendentals=0),
        name="spread",
    )(hs_image, kernels, basis, response)


def hand_kernel(pos_ref, r0, r1, r2, r3, mine_ref, other_ref):
    skip = 16 * (pos_ref[0] // 16 % 2)
    for d, region in enumerate((r0, r1, r2, r3)):
        for k in range(4):
            at = CROWS * (4 * d + k)
            mine_ref[at : at + CROWS] = region[pl.ds(pl.multiple_of(64 * k + skip, 16), CROWS), :]
            other_ref[at : at + CROWS] = region[pl.ds(pl.multiple_of(64 * k + 16 - skip, 16), CROWS), :]


def hand(pos, tiles):
    vmem = pl.BlockSpec(memory_space=pltpu.VMEM)
    return pl.pallas_call(
        hand_kernel,
        out_shape=(jax.ShapeDtypeStruct((16 * CROWS, LANES), f32),) * 2,
        in_specs=[pl.BlockSpec(memory_space=pltpu.SMEM)] + [vmem] * 4,
        out_specs=(vmem, vmem),
        compiler_params=pltpu.CompilerParams(vmem_limit_bytes=16 * 2**20),
        cost_estimate=pl.CostEstimate(flops=1_000_000, bytes_accessed=800_000, transcendentals=0),
        name="hand",
    )(pos, *tiles)


def encode_kernel(d_ref, out_ref):
    scales = []
    codes = []
    for k in range(4):
        part = d_ref[:, k]
        size = jnp.abs(part)
        top = jnp.max(size, axis=(0, 1, 2), keepdims=True)
        scale = rounded(jnp.maximum(top * (1 + 2**-7), 1e-30))
        code = jnp.exp2(size * (SPAN / scale) - SPAN / 2)
        codes.append(jnp.where(part < 0, -code, code))
        scales.append(jnp.broadcast_to(scale[0], (1, LANES)))
    scales = jnp.concatenate(scales + [jnp.zeros((12, LANES), f32)], axis=0).astype(bf16)
    for s in range(8):
        row = jnp.concatenate([codes[k][s] for k in range(4)], axis=0).astype(bf16)
        for t in range(16):
            out_ref[t, 32 * s : 32 * s + 32] = row
    for t in range(16):
        out_ref[t, 256:272] = scales


def encode(owned):
    vmem = pl.BlockSpec(memory_space=pltpu.VMEM)
    return pl.pallas_call(
        encode_kernel,
        out_shape=jax.ShapeDtypeStruct((16, 272, LANES), bf16),
        in_specs=[vmem],
        out_specs=vmem,
        compiler_params=pltpu.CompilerParams(vmem_limit_bytes=16 * 2**20),
        name="encode",
    )(owned)


def place_kernel(g_ref, c_ref, out_ref):
    lane = lax.broadcasted_iota(jnp.int32, (1, LANES), 1)
    low = lane < 64
    count = g_ref.shape[0] // 2
    for j in range(count):
        even, odd = [g_ref[2 * j + e, 256:272].astype(f32) * (1 / SPAN) for e in range(2)]
        scales = (jnp.where(low, even, odd), jnp.where(low, odd, even))
        columns = slice(j * LANES, j * LANES + LANES)
        for s in range(8):
            even, odd = [g_ref[2 * j + e, 32 * s : 32 * s + 32].astype(f32) for e in range(2)]
            for half, code in enumerate((jnp.where(low, even, odd), jnp.where(low, odd, even))):
                size = jnp.log2(jnp.abs(code)) + SPAN / 2
                value = jnp.where(code < 0, -size, size)
                for k in range(4):
                    part = value[8 * k : 8 * k + 8] * scales[half][k : k + 1]
                    if half:
                        part = pltpu.roll(part, 64, 1)
                    at = slice(16 * s + 8 * half, 16 * s + 8 * half + 8)
                    out_ref[k, at, columns] = c_ref[k, at, columns] + part


def place(gathered, coeffs_in):
    block = pl.BlockSpec((4, 128, 4 * LANES), lambda j: (0, 0, j))
    return pl.pallas_call(
        place_kernel,
        out_shape=jax.ShapeDtypeStruct((4, 128, 1024), f32),
        grid=(2,),
        in_specs=[pl.BlockSpec((8, 272, LANES), lambda j: (j, 0, 0)), block],
        out_specs=block,
        compiler_params=pltpu.CompilerParams(vmem_limit_bytes=32 * 2**20),
        name="place",
    )(gathered, coeffs_in)


def per_device(coeffs_in, basis, kernels, response, hs_image, ms_image):
    pos = (lax.axis_index("sub") * 16 + lax.axis_index("band")).astype(jnp.int32).reshape(1)
    sent = spread(hs_image, kernels.transpose(1, 0, 2), basis, response)
    hp = lax.all_to_all(sent, "band", split_axis=0, concat_axis=0, tiled=True).reshape(256, 256)
    *tiles, near = pack(pos, coeffs_in, ms_image)
    tiles = [tiles[0]] + [
        lax.ppermute(tiles[d], "sub", [(i, (i + 2 * d) % 8) for i in range(8)]) for d in range(1, 4)
    ]
    mine, other = hand(pos, tiles)
    other = lax.ppermute(other, "sub", [(i, i ^ 1) for i in range(8)])
    seen = jnp.concatenate([hp[:, 0:128].astype(bf16), near], axis=0)
    above = lax.ppermute(seen, "sub", [(i, i + 1) for i in range(7)])
    below = lax.ppermute(seen, "sub", [(i + 1, i) for i in range(7)])
    new = refine(pos, mine, other, hp, seen, above, below)
    owned = lax.all_to_all(new.reshape(8, 4, 8, LANES), "sub", split_axis=0, concat_axis=0, tiled=True)
    gathered = lax.all_to_all(encode(owned), "band", split_axis=0, concat_axis=0, tiled=True)
    return place(gathered, coeffs_in)


def solution(mesh):
    return jax.shard_map(
        per_device,
        mesh=mesh,
        in_specs=(
            P("sub", None, None),
            P("band", None),
            P("band", None, None),
            P(None, "band"),
            P("band", "sub", None),
            P(None, "sub", None),
        ),
        out_specs=P("sub", None, None),
        check_vma=False,
    )
```

```python
import functools

import jax
import jax.numpy as jnp
from jax import lax
from jax.experimental import pallas as pl
from jax.experimental.pallas import tpu as pltpu
from jax.sharding import PartitionSpec as P

STEP = 0.15
TR, TC = 16, 64
TAPS = 9
SPAN = 250.0
LANES = 128
CROWS = 48
MROWS = 32
IROWS = 10
JCOLS = 24
ROWS_LO, COLS_LO = 32, 256
f32 = jnp.float32
bf16 = jnp.bfloat16


def rounded(value):
    return value.astype(bf16).astype(f32)


def refine_kernel(pos_ref, *refs):
    mine_ref, other_ref, hp_ref, seen_ref, above_ref, below_ref, out_ref, c_ref, ms_ref, m0, m1, f0, f1, b0, b1, c1_ref, g_ref, hs0, hs1, w0, w1 = refs
    s = pos_ref[0] // 16
    b = pos_ref[0] % 16
    core = s % 2
    for d in range(4):
        chip = (s // 2 + 4 - d) % 4
        mine = pl.multiple_of((2 * chip + core) * (4 * CROWS), 4 * CROWS)
        theirs = pl.multiple_of((2 * chip + 1 - core) * (4 * CROWS), 4 * CROWS)
        c_ref[pl.ds(mine, 4 * CROWS), :] = mine_ref[d * 4 * CROWS : (d + 1) * 4 * CROWS]
        c_ref[pl.ds(theirs, 4 * CROWS), :] = other_ref[d * 4 * CROWS : (d + 1) * 4 * CROWS]
    for k in range(8):
        at = slice(256 + 16 * k, 272 + 16 * k)
        ms_ref[32 * k : 32 * k + 8, :] = above_ref[at, :].astype(f32)[8:16]
        ms_ref[32 * k + 8 : 32 * k + 24, :] = seen_ref[at, :].astype(f32)
        ms_ref[32 * k + 24 : 32 * k + 32, :] = below_ref[at, :].astype(f32)[0:8]
    bk = (b0, b1)
    m = (m0, m1)
    f = (f0, f1)
    hst = (hs0, hs1)
    w = (w0, w1)
    for h in range(2):
        at = slice(h * 128, h * 128 + 128)
        hst[h][0:72, :] = above_ref[at, :].astype(f32).T[24:96]
        hst[h][72:168, :] = hp_ref[at, 0:128].T[0:96]
        hst[h][168:240, :] = below_ref[at, :].astype(f32).T[0:72]
        w[h][...] = hp_ref[at, 128:256].T
    basis = jnp.concatenate([w0[81:113, :], w1[81:113, :]], axis=1).astype(bf16)
    response = jnp.concatenate([w0[113:121, :], w1[113:121, :]], axis=1).astype(bf16)
    combined = lax.dot_general(response, basis, (((1,), (1,)), ((), ())), preferred_element_type=f32).astype(bf16)
    lane = lax.broadcasted_iota(jnp.int32, (1, LANES), 1)
    group = lane % 32
    column = 64 * b - 16 + 4 * group + lane // 32
    in_columns = (column >= 0) & (column < 1024) & (group >= 2) & (group < 22)

    def mix(row, value, rows):
        mixed = lax.dot_general(value.astype(bf16), basis, (((0,), (0,)), ((), ())), preferred_element_type=f32)
        mixed = rounded(mixed)
        at = pl.ds(pl.multiple_of(row * LANES, LANES), rows * LANES)
        for h in range(2):
            m[h][at, :] = mixed[:, h * 128 : h * 128 + 128]

    def ms_gradient(row, block):
        predicted = jnp.dot(combined, block.astype(bf16), preferred_element_type=f32)
        seen = jnp.concatenate([ms_ref[pl.ds(row - 8 + r, 8, stride=MROWS), :] for r in range(8)], axis=1)
        misfit = (seen - predicted).astype(bf16)
        grad = lax.dot_general(combined, misfit, (((0,), (0,)), ((), ())), preferred_element_type=f32)
        for r in range(8):
            g_ref[pl.ds((row - 8 + r) * 32, 32), :] = grad[:, r * 128 : r * 128 + 128]

    def blur_row(n):
        g = lax.broadcasted_iota(jnp.int32, (JCOLS, LANES), 0)
        i_at = 4 * s + n - 3
        j_at = 16 * b + g - 3
        inside = (i_at >= 0) & (i_at < ROWS_LO) & (j_at >= 0) & (j_at < COLS_LO)
        for h in range(2):
            acc = [None, None, None]
            for a in range(TAPS):
                for q in range(4):
                    at = pl.multiple_of((4 * n + a) * LANES + 32 * q, 32)
                    x = m[h][pl.ds(at, JCOLS), :]
                    for d in range(3):
                        if 4 * d + q > 8:
                            continue
                        tap = a * 9 + 4 * d + q
                        term = w[h][tap : tap + 1, :] * x
                        acc[d] = term if acc[d] is None else acc[d] + term
            blurred = acc[0] + pltpu.roll(acc[1], JCOLS - 1, 0) + pltpu.roll(acc[2], JCOLS - 2, 0)
            seen = hst[h][pl.ds(pl.multiple_of(n * JCOLS, 8), JCOLS), :]
            f[h][pl.ds(pl.multiple_of(8 + n * JCOLS, 8), JCOLS), :] = jnp.where(inside, seen - blurred, 0.0)

    def back_rows(u):
        for h in range(2):
            win = [[f[h][pl.ds(8 + (u - t) * JCOLS - tt, JCOLS), :] for tt in range(3)] for t in range(3)]
            for p in range(4):
                for q in range(4):
                    total = None
                    for t in range(3):
                        for tt in range(3):
                            if p + 4 * t > 8 or q + 4 * tt > 8:
                                continue
                            tap = (p + 4 * t) * 9 + q + 4 * tt
                            term = w[h][tap : tap + 1, :] * win[t][tt]
                            total = term if total is None else total + term
                    at = pl.multiple_of((4 * u - 8 + p) * LANES + 32 * q, 32)
                    bk[h][pl.ds(at, JCOLS), :] = rounded(total)

    def hs_gradient(row, rows):
        at = pl.ds((row - 8) * LANES, rows * LANES)
        back = jnp.concatenate([b0[at, :].astype(bf16), b1[at, :].astype(bf16)], axis=1)
        return lax.dot_general(basis, back, (((1,), (1,)), ((), ())), preferred_element_type=f32)

    def start_row(row):
        return c_ref[pl.ds(row, 32, stride=CROWS), :]

    def loop(low, high, body):
        def step(n, _):
            body(n)
            return 0

        lax.fori_loop(low, high, step, 0)

    for block in range(CROWS // 8):
        value = jnp.concatenate([start_row(block * 8 + r) for r in range(8)], axis=1)
        mix(block * 8, value, 8)
        if 1 <= block < 5:
            ms_gradient(block * 8, value)
    loop(0, IROWS, blur_row)
    loop(2, 10, back_rows)
    for block in range(1, 5):
        grad = hs_gradient(block * 8, 8)
        values = []
        for r in range(8):
            row = block * 8 + r
            now = start_row(row)
            new = now + STEP * (grad[:, r * 128 : r * 128 + 128] + g_ref[pl.ds((row - 8) * 32, 32), :])
            row_at = 16 * s - 16 + row
            new = jnp.where(in_columns & (row_at >= 0) & (row_at < 128), new, 0.0)
            c1_ref[pl.ds((row - 8) * 32, 32), :] = new
            values.append(new)
        value = jnp.concatenate(values, axis=1)
        mix(block * 8, value, 8)
        if 2 <= block < 4:
            ms_gradient(block * 8, value)
    loop(2, 8, blur_row)
    loop(4, 8, back_rows)
    place_at = lax.broadcasted_iota(jnp.int32, (LANES, LANES), 1)
    take = lax.broadcasted_iota(jnp.int32, (LANES, LANES), 0)
    shift = 4 * (take % 32) + take // 32 - 16
    order = [(place_at == shift + 64 * ((half + b) % 2)) & (shift >= 0) & (shift < 64) for half in range(2)]
    order = [jnp.where(o, 1.0, 0.0).astype(bf16) for o in order]
    grads = [hs_gradient(16, 8), hs_gradient(24, 8)]
    for r in range(8):
        total = None
        for half in range(2):
            row = 8 + r + 8 * half
            at = pl.ds(row * 32, 32)
            value = STEP * (grads[half][:, r * 128 : r * 128 + 128] + g_ref[at, :])
            value = value + (c1_ref[at, :] - start_row(row + 8))
            rest = jnp.where((group >= 4) & (group < 20), value, 0.0)
            for _ in range(3):
                piece = rest.astype(bf16)
                rest = rest - piece.astype(f32)
                moved = jnp.dot(piece, order[half], preferred_element_type=f32)
                total = moved if total is None else total + moved
        out_ref[pl.ds(r, 32, stride=8), :] = total


def refine(pos, mine, other, hp, seen, above, below):
    vmem = pl.BlockSpec(memory_space=pltpu.VMEM)
    return pl.pallas_call(
        refine_kernel,
        out_shape=jax.ShapeDtypeStruct((32 * 8, LANES), f32),
        in_specs=[pl.BlockSpec(memory_space=pltpu.SMEM)] + [vmem] * 6,
        out_specs=vmem,
        scratch_shapes=[
            pltpu.VMEM((32 * CROWS, LANES), f32),
            pltpu.VMEM((8 * MROWS, LANES), f32),
            pltpu.VMEM((CROWS * LANES, LANES), f32),
            pltpu.VMEM((CROWS * LANES, LANES), f32),
            pltpu.VMEM((256, LANES), f32),
            pltpu.VMEM((256, LANES), f32),
            pltpu.VMEM((MROWS * LANES, LANES), f32),
            pltpu.VMEM((MROWS * LANES, LANES), f32),
            pltpu.VMEM((MROWS * 32, LANES), f32),
            pltpu.VMEM((MROWS * 32, LANES), f32),
            pltpu.VMEM((256, LANES), f32),
            pltpu.VMEM((256, LANES), f32),
            pltpu.VMEM((LANES, LANES), f32),
            pltpu.VMEM((LANES, LANES), f32),
        ],
        compiler_params=pltpu.CompilerParams(vmem_limit_bytes=40 * 2**20),
        cost_estimate=pl.CostEstimate(flops=400_000_000, bytes_accessed=2_000_000, transcendentals=0),
        name="refine",
    )(pos, mine, other, hp, seen, above, below)


def pack_kernel(pos_ref, ca_ref, cb_ref, ma_ref, mb_ref, *rest_refs):
    near_ref, wide_ref = rest_refs[4:]
    s = pos_ref[0] // 16
    b = pos_ref[0] % 16
    off = jnp.where(b % 2 == 0, 112, 48)
    lane = lax.broadcasted_iota(jnp.int32, (1, LANES), 1)
    first = lane >= off
    block = (b + 1) // 2 - jnp.where(first, 1, 0)
    keep = (block >= 0) & (block < 8)
    source = lax.broadcasted_iota(jnp.int32, (LANES, LANES), 0)
    target = lax.broadcasted_iota(jnp.int32, (LANES, LANES), 1)
    order = jnp.where(source == (4 * (target % 32) + target // 32 + off) % LANES, 1.0, 0.0).astype(bf16)
    ms = jnp.where(first, ma_ref[...].reshape(128, LANES).astype(f32), mb_ref[...].reshape(128, LANES).astype(f32))
    ms = jnp.where(keep, ms, 0.0).astype(bf16)
    ms = jnp.dot(ms, order, preferred_element_type=f32)
    near_ref[...] = ms.astype(bf16)
    edge = jnp.zeros((16, LANES), f32)
    for k in range(4):
        rest = jnp.where(keep, jnp.where(first, ca_ref[k], cb_ref[k]), 0.0)
        total = None
        for _ in range(3):
            piece = rest.astype(bf16)
            rest = rest - piece.astype(f32)
            moved = jnp.dot(piece, order, preferred_element_type=f32)
            total = moved if total is None else total + moved
        wide_ref[k, 0:16] = edge
        wide_ref[k, 16:144] = total
        wide_ref[k, 144:160] = edge
    for d in range(4):
        at = pl.ds(pl.multiple_of(32 * ((s // 2 + d) % 4), 32), 64)
        for k in range(4):
            rest_refs[d][64 * k : 64 * k + 64] = wide_ref[k, at, :]


def pack(pos, coeffs_in, ms_image):
    def low(i, p):
        return (0, 0, jnp.maximum((p[0] % 16 + 1) // 2 - 1, 0))

    def high(i, p):
        return (0, 0, jnp.minimum((p[0] % 16 + 1) // 2, 7))

    return pl.pallas_call(
        pack_kernel,
        out_shape=(jax.ShapeDtypeStruct((256, LANES), f32),) * 4 + (jax.ShapeDtypeStruct((128, LANES), bf16),),
        grid_spec=pltpu.PrefetchScalarGridSpec(
            num_scalar_prefetch=1,
            grid=(1,),
            in_specs=[
                pl.BlockSpec((4, 128, LANES), low),
                pl.BlockSpec((4, 128, LANES), high),
                pl.BlockSpec((8, 16, LANES), low),
                pl.BlockSpec((8, 16, LANES), high),
            ],
            out_specs=(pl.BlockSpec((256, LANES), lambda i, p: (0, 0)),) * 4
            + (pl.BlockSpec((128, LANES), lambda i, p: (0, 0)),),
            scratch_shapes=[pltpu.VMEM((4, 160, LANES), f32)],
        ),
        compiler_params=pltpu.CompilerParams(vmem_limit_bytes=60 * 2**20),
        cost_estimate=pl.CostEstimate(flops=100_000_000, bytes_accessed=1_600_000, transcendentals=0),
        name="pack",
    )(pos, coeffs_in, coeffs_in, ms_image, ms_image)


def spread_kernel(hs_ref, k_ref, basis_ref, response_ref, sent_ref):
    lane = lax.broadcasted_iota(jnp.int32, (1, LANES), 1)
    hs = hs_ref[...].astype(f32)
    rows = [jnp.concatenate([hs[:, i, :], jnp.zeros((2, 256), f32)], axis=0) for i in range(4)]
    sent_ref[0, :, 128:256] = jnp.zeros((16, 128), f32)
    for a in range(9):
        sent_ref[0, 0:14, 128 + 9 * a : 137 + 9 * a] = k_ref[a]
    sent_ref[0, 0:14, 209:241] = basis_ref[...].astype(f32)
    sent_ref[0, 0:14, 241:249] = response_ref[...].astype(f32).T
    params = sent_ref[0, :, 128:256]
    for t in range(16):
        total = jnp.zeros((16, LANES), f32)
        for i in range(4):
            moved = pltpu.roll(rows[i], (24 * i + 3 - 16 * t) % 256, 1)[:, 0:128]
            total = jnp.where((lane >= 24 * i) & (lane < 24 * i + 24), moved, total)
        sent_ref[t, :, 0:128] = total
        if t:
            sent_ref[t, :, 128:256] = params


def spread(hs_image, kernels, basis, response):
    vmem = pl.BlockSpec(memory_space=pltpu.VMEM)
    return pl.pallas_call(
        spread_kernel,
        out_shape=jax.ShapeDtypeStruct((16, 16, 256), f32),
        in_specs=[vmem] * 4,
        out_specs=vmem,
        compiler_params=pltpu.CompilerParams(vmem_limit_bytes=60 * 2**20),
        cost_estimate=pl.CostEstimate(flops=1_000_000, bytes_accessed=1_000_000, transcendentals=0),
        name="spread",
    )(hs_image, kernels, basis, response)


def hand_kernel(pos_ref, r0, r1, r2, r3, mine_ref, other_ref):
    skip = 16 * (pos_ref[0] // 16 % 2)
    for d, region in enumerate((r0, r1, r2, r3)):
        for k in range(4):
            at = CROWS * (4 * d + k)
            mine_ref[at : at + CROWS] = region[pl.ds(pl.multiple_of(64 * k + skip, 16), CROWS), :]
            other_ref[at : at + CROWS] = region[pl.ds(pl.multiple_of(64 * k + 16 - skip, 16), CROWS), :]


def hand(pos, tiles):
    vmem = pl.BlockSpec(memory_space=pltpu.VMEM)
    return pl.pallas_call(
        hand_kernel,
        out_shape=(jax.ShapeDtypeStruct((16 * CROWS, LANES), f32),) * 2,
        in_specs=[pl.BlockSpec(memory_space=pltpu.SMEM)] + [vmem] * 4,
        out_specs=(vmem, vmem),
        compiler_params=pltpu.CompilerParams(vmem_limit_bytes=16 * 2**20),
        cost_estimate=pl.CostEstimate(flops=1_000_000, bytes_accessed=800_000, transcendentals=0),
        name="hand",
    )(pos, *tiles)


def encode_kernel(d_ref, out_ref):
    scales = []
    codes = []
    for k in range(4):
        part = d_ref[:, k]
        size = jnp.abs(part)
        top = jnp.max(size, axis=(0, 1, 2), keepdims=True)
        scale = rounded(jnp.maximum(top * (1 + 2**-7), 1e-30))
        code = jnp.exp2(size * (SPAN / scale) - SPAN / 2)
        codes.append(jnp.where(part < 0, -code, code))
        scales.append(jnp.broadcast_to(scale[0], (1, LANES)))
    scales = jnp.concatenate(scales + [jnp.zeros((12, LANES), f32)], axis=0).astype(bf16)
    for s in range(8):
        row = jnp.concatenate([codes[k][s] for k in range(4)], axis=0).astype(bf16)
        for t in range(16):
            out_ref[t, 32 * s : 32 * s + 32] = row
    for t in range(16):
        out_ref[t, 256:272] = scales


def encode(owned):
    vmem = pl.BlockSpec(memory_space=pltpu.VMEM)
    return pl.pallas_call(
        encode_kernel,
        out_shape=jax.ShapeDtypeStruct((16, 272, LANES), bf16),
        in_specs=[vmem],
        out_specs=vmem,
        compiler_params=pltpu.CompilerParams(vmem_limit_bytes=16 * 2**20),
        name="encode",
    )(owned)


def place_kernel(g_ref, c_ref, out_ref):
    lane = lax.broadcasted_iota(jnp.int32, (1, LANES), 1)
    low = lane < 64
    count = g_ref.shape[0] // 2
    for j in range(count):
        even, odd = [g_ref[2 * j + e, 256:272].astype(f32) * (1 / SPAN) for e in range(2)]
        scales = (jnp.where(low, even, odd), jnp.where(low, odd, even))
        columns = slice(j * LANES, j * LANES + LANES)
        for s in range(8):
            even, odd = [g_ref[2 * j + e, 32 * s : 32 * s + 32].astype(f32) for e in range(2)]
            for half, code in enumerate((jnp.where(low, even, odd), jnp.where(low, odd, even))):
                size = jnp.log2(jnp.abs(code)) + SPAN / 2
                value = jnp.where(code < 0, -size, size)
                for k in range(4):
                    part = value[8 * k : 8 * k + 8] * scales[half][k : k + 1]
                    if half:
                        part = pltpu.roll(part, 64, 1)
                    at = slice(16 * s + 8 * half, 16 * s + 8 * half + 8)
                    out_ref[k, at, columns] = c_ref[k, at, columns] + part


def place(gathered, coeffs_in):
    block = pl.BlockSpec((4, 128, 4 * LANES), lambda j: (0, 0, j))
    return pl.pallas_call(
        place_kernel,
        out_shape=jax.ShapeDtypeStruct((4, 128, 1024), f32),
        grid=(2,),
        in_specs=[pl.BlockSpec((8, 272, LANES), lambda j: (j, 0, 0)), block],
        out_specs=block,
        compiler_params=pltpu.CompilerParams(vmem_limit_bytes=32 * 2**20),
        name="place",
    )(gathered, coeffs_in)


def per_device(coeffs_in, basis, kernels, response, hs_image, ms_image):
    pos = (lax.axis_index("sub") * 16 + lax.axis_index("band")).astype(jnp.int32).reshape(1)
    sent = spread(hs_image, kernels.transpose(1, 0, 2), basis, response)
    sent, pos = lax.optimization_barrier((sent, pos))
    hp = lax.all_to_all(sent, "band", split_axis=0, concat_axis=0, tiled=True).reshape(256, 256)
    *tiles, near = pack(pos, coeffs_in, ms_image)
    tiles = [tiles[0]] + [
        lax.ppermute(tiles[d], "sub", [(i, (i + 2 * d) % 8) for i in range(8)]) for d in range(1, 4)
    ]
    hp, *tiles = lax.optimization_barrier((hp, *tiles))
    mine, other = hand(pos, tiles)
    other = lax.ppermute(other, "sub", [(i, i ^ 1) for i in range(8)])
    seen = jnp.concatenate([hp[:, 0:128].astype(bf16), near], axis=0)
    above = lax.ppermute(seen, "sub", [(i, i + 1) for i in range(7)])
    below = lax.ppermute(seen, "sub", [(i + 1, i) for i in range(7)])
    new = refine(pos, mine, other, hp, seen, above, below)
    owned = lax.all_to_all(new.reshape(8, 4, 8, LANES), "sub", split_axis=0, concat_axis=0, tiled=True)
    gathered = lax.all_to_all(encode(owned), "band", split_axis=0, concat_axis=0, tiled=True)
    return place(gathered, coeffs_in)


def solution(mesh):
    return jax.shard_map(
        per_device,
        mesh=mesh,
        in_specs=(
            P("sub", None, None),
            P("band", None),
            P("band", None, None),
            P(None, "band"),
            P("band", "sub", None),
            P(None, "sub", None),
        ),
        out_specs=P("sub", None, None),
        check_vma=False,
    )
```

```python
import functools

import jax
import jax.numpy as jnp
from jax import lax
from jax.experimental import pallas as pl
from jax.experimental.pallas import tpu as pltpu
from jax.sharding import PartitionSpec as P

STEP = 0.15
TR, TC = 16, 64
TAPS = 9
SPAN = 250.0
LANES = 128
CROWS = 48
MROWS = 32
IROWS = 10
JCOLS = 24
ROWS_LO, COLS_LO = 32, 256
f32 = jnp.float32
bf16 = jnp.bfloat16


def rounded(value):
    return value.astype(bf16).astype(f32)


def refine_kernel(pos_ref, *refs):
    mine_ref, other_ref, hp_ref, seen_ref, above_ref, below_ref, out_ref, c_ref, ms_ref, m0, m1, f0, f1, b0, b1, c1_ref, g_ref, hs0, hs1, w0, w1 = refs
    s = pos_ref[0] // 16
    b = pos_ref[0] % 16
    core = s % 2
    for d in range(4):
        chip = (s // 2 + 4 - d) % 4
        mine = pl.multiple_of((2 * chip + core) * (4 * CROWS), 4 * CROWS)
        theirs = pl.multiple_of((2 * chip + 1 - core) * (4 * CROWS), 4 * CROWS)
        c_ref[pl.ds(mine, 4 * CROWS), :] = mine_ref[d * 4 * CROWS : (d + 1) * 4 * CROWS]
        c_ref[pl.ds(theirs, 4 * CROWS), :] = other_ref[d * 4 * CROWS : (d + 1) * 4 * CROWS]
    for k in range(8):
        at = slice(256 + 16 * k, 272 + 16 * k)
        ms_ref[32 * k : 32 * k + 8, :] = above_ref[at, :].astype(f32)[8:16]
        ms_ref[32 * k + 8 : 32 * k + 24, :] = seen_ref[at, :].astype(f32)
        ms_ref[32 * k + 24 : 32 * k + 32, :] = below_ref[at, :].astype(f32)[0:8]
    bk = (b0, b1)
    m = (m0, m1)
    f = (f0, f1)
    hst = (hs0, hs1)
    w = (w0, w1)
    for h in range(2):
        at = slice(h * 128, h * 128 + 128)
        hst[h][0:72, :] = above_ref[at, :].astype(f32).T[24:96]
        hst[h][72:168, :] = hp_ref[at, 0:128].T[0:96]
        hst[h][168:240, :] = below_ref[at, :].astype(f32).T[0:72]
        w[h][...] = hp_ref[at, 128:256].T
    basis = jnp.concatenate([w0[81:113, :], w1[81:113, :]], axis=1).astype(bf16)
    response = jnp.concatenate([w0[113:121, :], w1[113:121, :]], axis=1).astype(bf16)
    combined = lax.dot_general(response, basis, (((1,), (1,)), ((), ())), preferred_element_type=f32).astype(bf16)
    lane = lax.broadcasted_iota(jnp.int32, (1, LANES), 1)
    group = lane % 32
    column = 64 * b - 16 + 4 * group + lane // 32
    in_columns = (column >= 0) & (column < 1024) & (group >= 2) & (group < 22)

    def mix(row, value, rows):
        mixed = lax.dot_general(value.astype(bf16), basis, (((0,), (0,)), ((), ())), preferred_element_type=f32)
        mixed = rounded(mixed)
        at = pl.ds(pl.multiple_of(row * LANES, LANES), rows * LANES)
        for h in range(2):
            m[h][at, :] = mixed[:, h * 128 : h * 128 + 128]

    def ms_gradient(row, block):
        predicted = jnp.dot(combined, block.astype(bf16), preferred_element_type=f32)
        seen = jnp.concatenate([ms_ref[pl.ds(row - 8 + r, 8, stride=MROWS), :] for r in range(8)], axis=1)
        misfit = (seen - predicted).astype(bf16)
        grad = lax.dot_general(combined, misfit, (((0,), (0,)), ((), ())), preferred_element_type=f32)
        for r in range(8):
            g_ref[pl.ds((row - 8 + r) * 32, 32), :] = grad[:, r * 128 : r * 128 + 128]

    def blur_row(n):
        g = lax.broadcasted_iota(jnp.int32, (JCOLS, LANES), 0)
        i_at = 4 * s + n - 3
        j_at = 16 * b + g - 3
        inside = (i_at >= 0) & (i_at < ROWS_LO) & (j_at >= 0) & (j_at < COLS_LO)
        for h in range(2):
            acc = [None, None, None]
            for a in range(TAPS):
                for q in range(4):
                    at = pl.multiple_of((4 * n + a) * LANES + 32 * q, 32)
                    x = m[h][pl.ds(at, JCOLS), :]
                    for d in range(3):
                        if 4 * d + q > 8:
                            continue
                        tap = a * 9 + 4 * d + q
                        term = w[h][tap : tap + 1, :] * x
                        acc[d] = term if acc[d] is None else acc[d] + term
            blurred = acc[0] + pltpu.roll(acc[1], JCOLS - 1, 0) + pltpu.roll(acc[2], JCOLS - 2, 0)
            seen = hst[h][pl.ds(pl.multiple_of(n * JCOLS, 8), JCOLS), :]
            f[h][pl.ds(pl.multiple_of(8 + n * JCOLS, 8), JCOLS), :] = jnp.where(inside, seen - blurred, 0.0)

    def back_rows(u):
        for h in range(2):
            win = [[f[h][pl.ds(8 + (u - t) * JCOLS - tt, JCOLS), :] for tt in range(3)] for t in range(3)]
            for p in range(4):
                for q in range(4):
                    total = None
                    for t in range(3):
                        for tt in range(3):
                            if p + 4 * t > 8 or q + 4 * tt > 8:
                                continue
                            tap = (p + 4 * t) * 9 + q + 4 * tt
                            term = w[h][tap : tap + 1, :] * win[t][tt]
                            total = term if total is None else total + term
                    at = pl.multiple_of((4 * u - 8 + p) * LANES + 32 * q, 32)
                    bk[h][pl.ds(at, JCOLS), :] = rounded(total)

    def hs_gradient(row, rows):
        at = pl.ds((row - 8) * LANES, rows * LANES)
        back = jnp.concatenate([b0[at, :].astype(bf16), b1[at, :].astype(bf16)], axis=1)
        return lax.dot_general(basis, back, (((1,), (1,)), ((), ())), preferred_element_type=f32)

    def start_row(row):
        return c_ref[pl.ds(row, 32, stride=CROWS), :]

    def loop(low, high, body):
        def step(n, _):
            body(n)
            return 0

        lax.fori_loop(low, high, step, 0)

    for block in range(CROWS // 8):
        value = jnp.concatenate([start_row(block * 8 + r) for r in range(8)], axis=1)
        mix(block * 8, value, 8)
        if 1 <= block < 5:
            ms_gradient(block * 8, value)
    loop(0, IROWS, blur_row)
    loop(2, 10, back_rows)
    for block in range(1, 5):
        grad = hs_gradient(block * 8, 8)
        values = []
        for r in range(8):
            row = block * 8 + r
            now = start_row(row)
            new = now + STEP * (grad[:, r * 128 : r * 128 + 128] + g_ref[pl.ds((row - 8) * 32, 32), :])
            row_at = 16 * s - 16 + row
            new = jnp.where(in_columns & (row_at >= 0) & (row_at < 128), new, 0.0)
            c1_ref[pl.ds((row - 8) * 32, 32), :] = new
            values.append(new)
        value = jnp.concatenate(values, axis=1)
        mix(block * 8, value, 8)
        if 2 <= block < 4:
            ms_gradient(block * 8, value)
    loop(2, 8, blur_row)
    loop(4, 8, back_rows)
    place_at = lax.broadcasted_iota(jnp.int32, (LANES, LANES), 1)
    take = lax.broadcasted_iota(jnp.int32, (LANES, LANES), 0)
    shift = 4 * (take % 32) + take // 32 - 16
    order = [(place_at == shift + 64 * ((half + b) % 2)) & (shift >= 0) & (shift < 64) for half in range(2)]
    order = [jnp.where(o, 1.0, 0.0).astype(bf16) for o in order]
    grads = [hs_gradient(16, 8), hs_gradient(24, 8)]
    for r in range(8):
        total = None
        for half in range(2):
            row = 8 + r + 8 * half
            at = pl.ds(row * 32, 32)
            value = STEP * (grads[half][:, r * 128 : r * 128 + 128] + g_ref[at, :])
            value = value + (c1_ref[at, :] - start_row(row + 8))
            rest = jnp.where((group >= 4) & (group < 20), value, 0.0)
            for _ in range(3):
                piece = rest.astype(bf16)
                rest = rest - piece.astype(f32)
                moved = jnp.dot(piece, order[half], preferred_element_type=f32)
                total = moved if total is None else total + moved
        out_ref[pl.ds(r, 32, stride=8), :] = total


def refine(pos, mine, other, hp, seen, above, below):
    vmem = pl.BlockSpec(memory_space=pltpu.VMEM)
    return pl.pallas_call(
        refine_kernel,
        out_shape=jax.ShapeDtypeStruct((32 * 8, LANES), f32),
        in_specs=[pl.BlockSpec(memory_space=pltpu.SMEM)] + [vmem] * 6,
        out_specs=vmem,
        scratch_shapes=[
            pltpu.VMEM((32 * CROWS, LANES), f32),
            pltpu.VMEM((8 * MROWS, LANES), f32),
            pltpu.VMEM((CROWS * LANES, LANES), f32),
            pltpu.VMEM((CROWS * LANES, LANES), f32),
            pltpu.VMEM((256, LANES), f32),
            pltpu.VMEM((256, LANES), f32),
            pltpu.VMEM((MROWS * LANES, LANES), f32),
            pltpu.VMEM((MROWS * LANES, LANES), f32),
            pltpu.VMEM((MROWS * 32, LANES), f32),
            pltpu.VMEM((MROWS * 32, LANES), f32),
            pltpu.VMEM((256, LANES), f32),
            pltpu.VMEM((256, LANES), f32),
            pltpu.VMEM((LANES, LANES), f32),
            pltpu.VMEM((LANES, LANES), f32),
        ],
        compiler_params=pltpu.CompilerParams(vmem_limit_bytes=40 * 2**20),
        cost_estimate=pl.CostEstimate(flops=400_000_000, bytes_accessed=2_000_000, transcendentals=0),
        name="refine",
    )(pos, mine, other, hp, seen, above, below)


def pack_kernel(pos_ref, ca_ref, cb_ref, ma_ref, mb_ref, *rest_refs):
    near_ref, wide_ref = rest_refs[4:]
    s = pos_ref[0] // 16
    b = pos_ref[0] % 16
    off = jnp.where(b % 2 == 0, 112, 48)
    lane = lax.broadcasted_iota(jnp.int32, (1, LANES), 1)
    first = lane >= off
    block = (b + 1) // 2 - jnp.where(first, 1, 0)
    keep = (block >= 0) & (block < 8)
    source = lax.broadcasted_iota(jnp.int32, (LANES, LANES), 0)
    target = lax.broadcasted_iota(jnp.int32, (LANES, LANES), 1)
    order = jnp.where(source == (4 * (target % 32) + target // 32 + off) % LANES, 1.0, 0.0).astype(bf16)
    ms = jnp.where(first, ma_ref[...].reshape(128, LANES).astype(f32), mb_ref[...].reshape(128, LANES).astype(f32))
    ms = jnp.where(keep, ms, 0.0).astype(bf16)
    ms = jnp.dot(ms, order, preferred_element_type=f32)
    near_ref[...] = ms.astype(bf16)
    edge = jnp.zeros((16, LANES), f32)
    for k in range(4):
        rest = jnp.where(keep, jnp.where(first, ca_ref[k], cb_ref[k]), 0.0)
        total = None
        for _ in range(3):
            piece = rest.astype(bf16)
            rest = rest - piece.astype(f32)
            moved = jnp.dot(piece, order, preferred_element_type=f32)
            total = moved if total is None else total + moved
        wide_ref[k, 0:16] = edge
        wide_ref[k, 16:144] = total
        wide_ref[k, 144:160] = edge
    for d in range(4):
        at = pl.ds(pl.multiple_of(32 * ((s // 2 + d) % 4), 32), 64)
        for k in range(4):
            rest_refs[d][64 * k : 64 * k + 64] = wide_ref[k, at, :]


def pack(pos, coeffs_in, ms_image):
    def low(i, p):
        return (0, 0, jnp.maximum((p[0] % 16 + 1) // 2 - 1, 0))

    def high(i, p):
        return (0, 0, jnp.minimum((p[0] % 16 + 1) // 2, 7))

    return pl.pallas_call(
        pack_kernel,
        out_shape=(jax.ShapeDtypeStruct((256, LANES), f32),) * 4 + (jax.ShapeDtypeStruct((128, LANES), bf16),),
        grid_spec=pltpu.PrefetchScalarGridSpec(
            num_scalar_prefetch=1,
            grid=(1,),
            in_specs=[
                pl.BlockSpec((4, 128, LANES), low),
                pl.BlockSpec((4, 128, LANES), high),
                pl.BlockSpec((8, 16, LANES), low),
                pl.BlockSpec((8, 16, LANES), high),
            ],
            out_specs=(pl.BlockSpec((256, LANES), lambda i, p: (0, 0)),) * 4
            + (pl.BlockSpec((128, LANES), lambda i, p: (0, 0)),),
            scratch_shapes=[pltpu.VMEM((4, 160, LANES), f32)],
        ),
        compiler_params=pltpu.CompilerParams(vmem_limit_bytes=60 * 2**20),
        cost_estimate=pl.CostEstimate(flops=100_000_000, bytes_accessed=1_600_000, transcendentals=0),
        name="pack",
    )(pos, coeffs_in, coeffs_in, ms_image, ms_image)


def spread_kernel(hs_ref, k_ref, basis_ref, response_ref, sent_ref):
    lane = lax.broadcasted_iota(jnp.int32, (1, LANES), 1)
    hs = hs_ref[...].astype(f32)
    rows = [jnp.concatenate([hs[:, i, :], jnp.zeros((2, 256), f32)], axis=0) for i in range(4)]
    sent_ref[0, :, 128:256] = jnp.zeros((16, 128), f32)
    for a in range(9):
        sent_ref[0, 0:14, 128 + 9 * a : 137 + 9 * a] = k_ref[a]
    sent_ref[0, 0:14, 209:241] = basis_ref[...].astype(f32)
    sent_ref[0, 0:14, 241:249] = response_ref[...].astype(f32).T
    params = sent_ref[0, :, 128:256]
    for t in range(16):
        total = jnp.zeros((16, LANES), f32)
        for i in range(4):
            moved = pltpu.roll(rows[i], (24 * i + 3 - 16 * t) % 256, 1)[:, 0:128]
            total = jnp.where((lane >= 24 * i) & (lane < 24 * i + 24), moved, total)
        sent_ref[t, :, 0:128] = total
        if t:
            sent_ref[t, :, 128:256] = params


def spread(hs_image, kernels, basis, response):
    vmem = pl.BlockSpec(memory_space=pltpu.VMEM)
    return pl.pallas_call(
        spread_kernel,
        out_shape=jax.ShapeDtypeStruct((16, 16, 256), f32),
        in_specs=[vmem] * 4,
        out_specs=vmem,
        compiler_params=pltpu.CompilerParams(vmem_limit_bytes=60 * 2**20),
        cost_estimate=pl.CostEstimate(flops=1_000_000, bytes_accessed=1_000_000, transcendentals=0),
        name="spread",
    )(hs_image, kernels, basis, response)


def hand_kernel(pos_ref, r0, r1, r2, r3, mine_ref, other_ref):
    skip = 16 * (pos_ref[0] // 16 % 2)
    for d, region in enumerate((r0, r1, r2, r3)):
        for k in range(4):
            at = CROWS * (4 * d + k)
            mine_ref[at : at + CROWS] = region[pl.ds(pl.multiple_of(64 * k + skip, 16), CROWS), :]
            other_ref[at : at + CROWS] = region[pl.ds(pl.multiple_of(64 * k + 16 - skip, 16), CROWS), :]


def hand(pos, tiles):
    vmem = pl.BlockSpec(memory_space=pltpu.VMEM)
    return pl.pallas_call(
        hand_kernel,
        out_shape=(jax.ShapeDtypeStruct((16 * CROWS, LANES), f32),) * 2,
        in_specs=[pl.BlockSpec(memory_space=pltpu.SMEM)] + [vmem] * 4,
        out_specs=(vmem, vmem),
        compiler_params=pltpu.CompilerParams(vmem_limit_bytes=16 * 2**20),
        cost_estimate=pl.CostEstimate(flops=1_000_000, bytes_accessed=800_000, transcendentals=0),
        name="hand",
    )(pos, *tiles)


def encode_kernel(d_ref, out_ref):
    scales = []
    codes = []
    for k in range(4):
        part = d_ref[:, k]
        size = jnp.abs(part)
        top = jnp.max(size, axis=(0, 1, 2), keepdims=True)
        scale = rounded(jnp.maximum(top * (1 + 2**-7), 1e-30))
        code = jnp.exp2(size * (SPAN / scale) - SPAN / 2)
        codes.append(jnp.where(part < 0, -code, code))
        scales.append(jnp.broadcast_to(scale[0], (1, LANES)))
    scales = jnp.concatenate(scales + [jnp.zeros((12, LANES), f32)], axis=0).astype(bf16)
    for s in range(8):
        row = jnp.concatenate([codes[k][s] for k in range(4)], axis=0).astype(bf16)
        for t in range(16):
            out_ref[t, 32 * s : 32 * s + 32] = row
    for t in range(16):
        out_ref[t, 256:272] = scales


def encode(owned):
    vmem = pl.BlockSpec(memory_space=pltpu.VMEM)
    return pl.pallas_call(
        encode_kernel,
        out_shape=jax.ShapeDtypeStruct((16, 272, LANES), bf16),
        in_specs=[vmem],
        out_specs=vmem,
        compiler_params=pltpu.CompilerParams(vmem_limit_bytes=16 * 2**20),
        name="encode",
    )(owned)


def place_kernel(g_ref, c_ref, out_ref):
    lane = lax.broadcasted_iota(jnp.int32, (1, LANES), 1)
    low = lane < 64
    count = g_ref.shape[0] // 2
    for j in range(count):
        even, odd = [g_ref[2 * j + e, 256:272].astype(f32) * (1 / SPAN) for e in range(2)]
        scales = (jnp.where(low, even, odd), jnp.where(low, odd, even))
        columns = slice(j * LANES, j * LANES + LANES)
        for s in range(8):
            even, odd = [g_ref[2 * j + e, 32 * s : 32 * s + 32].astype(f32) for e in range(2)]
            for half, code in enumerate((jnp.where(low, even, odd), jnp.where(low, odd, even))):
                size = jnp.log2(jnp.abs(code)) + SPAN / 2
                value = jnp.where(code < 0, -size, size)
                for k in range(4):
                    part = value[8 * k : 8 * k + 8] * scales[half][k : k + 1]
                    if half:
                        part = pltpu.roll(part, 64, 1)
                    at = slice(16 * s + 8 * half, 16 * s + 8 * half + 8)
                    out_ref[k, at, columns] = c_ref[k, at, columns] + part


def place(gathered, coeffs_in):
    block = pl.BlockSpec((4, 128, 4 * LANES), lambda j: (0, 0, j))
    return pl.pallas_call(
        place_kernel,
        out_shape=jax.ShapeDtypeStruct((4, 128, 1024), f32),
        grid=(2,),
        in_specs=[pl.BlockSpec((8, 272, LANES), lambda j: (j, 0, 0)), block],
        out_specs=block,
        compiler_params=pltpu.CompilerParams(vmem_limit_bytes=32 * 2**20),
        name="place",
    )(gathered, coeffs_in)


def per_device(coeffs_in, basis, kernels, response, hs_image, ms_image):
    pos = (lax.axis_index("sub") * 16 + lax.axis_index("band")).astype(jnp.int32).reshape(1)
    sent = spread(hs_image, kernels.transpose(1, 0, 2), basis, response)
    sent, pos = lax.optimization_barrier((sent, pos))
    hp = lax.all_to_all(sent, "band", split_axis=0, concat_axis=0, tiled=True).reshape(256, 256)
    *tiles, near = pack(pos, coeffs_in, ms_image)
    tiles = [tiles[0]] + [
        lax.ppermute(tiles[d], "sub", [(i, (i + 2 * d) % 8) for i in range(8)]) for d in range(1, 4)
    ]
    seen = jnp.concatenate([hp[:, 0:128].astype(bf16), near], axis=0)
    above = lax.ppermute(seen, "sub", [(i, i + 1) for i in range(7)])
    below = lax.ppermute(seen, "sub", [(i + 1, i) for i in range(7)])
    above, below, *tiles = lax.optimization_barrier((above, below, *tiles))
    mine, other = hand(pos, tiles)
    other = lax.ppermute(other, "sub", [(i, i ^ 1) for i in range(8)])
    new = refine(pos, mine, other, hp, seen, above, below)
    owned = lax.all_to_all(new.reshape(8, 4, 8, LANES), "sub", split_axis=0, concat_axis=0, tiled=True)
    gathered = lax.all_to_all(encode(owned), "band", split_axis=0, concat_axis=0, tiled=True)
    return place(gathered, coeffs_in)


def solution(mesh):
    return jax.shard_map(
        per_device,
        mesh=mesh,
        in_specs=(
            P("sub", None, None),
            P("band", None),
            P("band", None, None),
            P(None, "band"),
            P("band", "sub", None),
            P(None, "sub", None),
        ),
        out_specs=P("sub", None, None),
        check_vma=False,
    )
```

```python
import functools

import jax
import jax.numpy as jnp
from jax import lax
from jax.experimental import pallas as pl
from jax.experimental.pallas import tpu as pltpu
from jax.sharding import PartitionSpec as P

STEP = 0.15
TR, TC = 16, 64
TAPS = 9
SPAN = 250.0
LANES = 128
CROWS = 48
MROWS = 32
IROWS = 10
JCOLS = 24
ROWS_LO, COLS_LO = 32, 256
f32 = jnp.float32
bf16 = jnp.bfloat16


def rounded(value):
    return value.astype(bf16).astype(f32)


def refine_kernel(pos_ref, *refs):
    mine_ref, other_ref, hp_ref, seen_ref, cross_ref, out_ref, c_ref, ms_ref, m0, m1, f0, f1, b0, b1, c1_ref, g_ref, hs0, hs1, w0, w1 = refs
    s = pos_ref[0] // 16
    b = pos_ref[0] % 16
    core = s % 2
    for d in range(4):
        chip = (s // 2 + 4 - d) % 4
        mine = pl.multiple_of((2 * chip + core) * (4 * CROWS), 4 * CROWS)
        theirs = pl.multiple_of((2 * chip + 1 - core) * (4 * CROWS), 4 * CROWS)
        c_ref[pl.ds(mine, 4 * CROWS), :] = mine_ref[d * 4 * CROWS : (d + 1) * 4 * CROWS]
        c_ref[pl.ds(theirs, 4 * CROWS), :] = other_ref[d * 4 * CROWS : (d + 1) * 4 * CROWS]

    def neighbours(low, high):
        theirs = other_ref[16 * CROWS + low : 16 * CROWS + high]
        across = cross_ref[low:high].astype(f32)
        flag = jnp.zeros((high - low, LANES), jnp.int32) + core
        return jnp.where(flag == 0, across, theirs), jnp.where(flag == 0, theirs, across)

    ms_above, ms_below = neighbours(256, 384)
    for k in range(8):
        ms_ref[32 * k : 32 * k + 8, :] = ms_above[16 * k + 8 : 16 * k + 16]
        ms_ref[32 * k + 8 : 32 * k + 24, :] = seen_ref[256 + 16 * k : 272 + 16 * k].astype(f32)
        ms_ref[32 * k + 24 : 32 * k + 32, :] = ms_below[16 * k : 16 * k + 8]
    bk = (b0, b1)
    m = (m0, m1)
    f = (f0, f1)
    hst = (hs0, hs1)
    w = (w0, w1)
    for h in range(2):
        at = slice(h * 128, h * 128 + 128)
        above, below = neighbours(h * 128, h * 128 + 128)
        hst[h][0:72, :] = above.T[24:96]
        hst[h][72:168, :] = hp_ref[at, 0:128].T[0:96]
        hst[h][168:240, :] = below.T[0:72]
        w[h][...] = hp_ref[at, 128:256].T
    basis = jnp.concatenate([w0[81:113, :], w1[81:113, :]], axis=1).astype(bf16)
    response = jnp.concatenate([w0[113:121, :], w1[113:121, :]], axis=1).astype(bf16)
    combined = lax.dot_general(response, basis, (((1,), (1,)), ((), ())), preferred_element_type=f32).astype(bf16)
    lane = lax.broadcasted_iota(jnp.int32, (1, LANES), 1)
    group = lane % 32
    column = 64 * b - 16 + 4 * group + lane // 32
    in_columns = (column >= 0) & (column < 1024) & (group >= 2) & (group < 22)

    def mix(row, value, rows):
        mixed = lax.dot_general(value.astype(bf16), basis, (((0,), (0,)), ((), ())), preferred_element_type=f32)
        mixed = rounded(mixed)
        at = pl.ds(pl.multiple_of(row * LANES, LANES), rows * LANES)
        for h in range(2):
            m[h][at, :] = mixed[:, h * 128 : h * 128 + 128]

    def ms_gradient(row, block):
        predicted = jnp.dot(combined, block.astype(bf16), preferred_element_type=f32)
        seen = jnp.concatenate([ms_ref[pl.ds(row - 8 + r, 8, stride=MROWS), :] for r in range(8)], axis=1)
        misfit = (seen - predicted).astype(bf16)
        grad = lax.dot_general(combined, misfit, (((0,), (0,)), ((), ())), preferred_element_type=f32)
        for r in range(8):
            g_ref[pl.ds((row - 8 + r) * 32, 32), :] = grad[:, r * 128 : r * 128 + 128]

    def blur_row(n):
        g = lax.broadcasted_iota(jnp.int32, (JCOLS, LANES), 0)
        i_at = 4 * s + n - 3
        j_at = 16 * b + g - 3
        inside = (i_at >= 0) & (i_at < ROWS_LO) & (j_at >= 0) & (j_at < COLS_LO)
        for h in range(2):
            acc = [None, None, None]
            for a in range(TAPS):
                for q in range(4):
                    at = pl.multiple_of((4 * n + a) * LANES + 32 * q, 32)
                    x = m[h][pl.ds(at, JCOLS), :]
                    for d in range(3):
                        if 4 * d + q > 8:
                            continue
                        tap = a * 9 + 4 * d + q
                        term = w[h][tap : tap + 1, :] * x
                        acc[d] = term if acc[d] is None else acc[d] + term
            blurred = acc[0] + pltpu.roll(acc[1], JCOLS - 1, 0) + pltpu.roll(acc[2], JCOLS - 2, 0)
            seen = hst[h][pl.ds(pl.multiple_of(n * JCOLS, 8), JCOLS), :]
            f[h][pl.ds(pl.multiple_of(8 + n * JCOLS, 8), JCOLS), :] = jnp.where(inside, seen - blurred, 0.0)

    def back_rows(u):
        for h in range(2):
            win = [[f[h][pl.ds(8 + (u - t) * JCOLS - tt, JCOLS), :] for tt in range(3)] for t in range(3)]
            for p in range(4):
                for q in range(4):
                    total = None
                    for t in range(3):
                        for tt in range(3):
                            if p + 4 * t > 8 or q + 4 * tt > 8:
                                continue
                            tap = (p + 4 * t) * 9 + q + 4 * tt
                            term = w[h][tap : tap + 1, :] * win[t][tt]
                            total = term if total is None else total + term
                    at = pl.multiple_of((4 * u - 8 + p) * LANES + 32 * q, 32)
                    bk[h][pl.ds(at, JCOLS), :] = rounded(total)

    def hs_gradient(row, rows):
        at = pl.ds((row - 8) * LANES, rows * LANES)
        back = jnp.concatenate([b0[at, :].astype(bf16), b1[at, :].astype(bf16)], axis=1)
        return lax.dot_general(basis, back, (((1,), (1,)), ((), ())), preferred_element_type=f32)

    def start_row(row):
        return c_ref[pl.ds(row, 32, stride=CROWS), :]

    def loop(low, high, body):
        def step(n, _):
            body(n)
            return 0

        lax.fori_loop(low, high, step, 0)

    for block in range(CROWS // 8):
        value = jnp.concatenate([start_row(block * 8 + r) for r in range(8)], axis=1)
        mix(block * 8, value, 8)
        if 1 <= block < 5:
            ms_gradient(block * 8, value)
    loop(0, IROWS, blur_row)
    loop(2, 10, back_rows)
    for block in range(1, 5):
        grad = hs_gradient(block * 8, 8)
        values = []
        for r in range(8):
            row = block * 8 + r
            now = start_row(row)
            new = now + STEP * (grad[:, r * 128 : r * 128 + 128] + g_ref[pl.ds((row - 8) * 32, 32), :])
            row_at = 16 * s - 16 + row
            new = jnp.where(in_columns & (row_at >= 0) & (row_at < 128), new, 0.0)
            c1_ref[pl.ds((row - 8) * 32, 32), :] = new
            values.append(new)
        value = jnp.concatenate(values, axis=1)
        mix(block * 8, value, 8)
        if 2 <= block < 4:
            ms_gradient(block * 8, value)
    loop(2, 8, blur_row)
    loop(4, 8, back_rows)
    place_at = lax.broadcasted_iota(jnp.int32, (LANES, LANES), 1)
    take = lax.broadcasted_iota(jnp.int32, (LANES, LANES), 0)
    shift = 4 * (take % 32) + take // 32 - 16
    order = [(place_at == shift + 64 * ((half + b) % 2)) & (shift >= 0) & (shift < 64) for half in range(2)]
    order = [jnp.where(o, 1.0, 0.0).astype(bf16) for o in order]
    grads = [hs_gradient(16, 8), hs_gradient(24, 8)]
    for r in range(8):
        total = None
        for half in range(2):
            row = 8 + r + 8 * half
            at = pl.ds(row * 32, 32)
            value = STEP * (grads[half][:, r * 128 : r * 128 + 128] + g_ref[at, :])
            value = value + (c1_ref[at, :] - start_row(row + 8))
            rest = jnp.where((group >= 4) & (group < 20), value, 0.0)
            for _ in range(3):
                piece = rest.astype(bf16)
                rest = rest - piece.astype(f32)
                moved = jnp.dot(piece, order[half], preferred_element_type=f32)
                total = moved if total is None else total + moved
        out_ref[pl.ds(r, 32, stride=8), :] = total


def refine(pos, mine, other, hp, seen, cross):
    vmem = pl.BlockSpec(memory_space=pltpu.VMEM)
    return pl.pallas_call(
        refine_kernel,
        out_shape=jax.ShapeDtypeStruct((32 * 8, LANES), f32),
        in_specs=[pl.BlockSpec(memory_space=pltpu.SMEM)] + [vmem] * 5,
        out_specs=vmem,
        scratch_shapes=[
            pltpu.VMEM((32 * CROWS, LANES), f32),
            pltpu.VMEM((8 * MROWS, LANES), f32),
            pltpu.VMEM((CROWS * LANES, LANES), f32),
            pltpu.VMEM((CROWS * LANES, LANES), f32),
            pltpu.VMEM((256, LANES), f32),
            pltpu.VMEM((256, LANES), f32),
            pltpu.VMEM((MROWS * LANES, LANES), f32),
            pltpu.VMEM((MROWS * LANES, LANES), f32),
            pltpu.VMEM((MROWS * 32, LANES), f32),
            pltpu.VMEM((MROWS * 32, LANES), f32),
            pltpu.VMEM((256, LANES), f32),
            pltpu.VMEM((256, LANES), f32),
            pltpu.VMEM((LANES, LANES), f32),
            pltpu.VMEM((LANES, LANES), f32),
        ],
        compiler_params=pltpu.CompilerParams(vmem_limit_bytes=40 * 2**20),
        cost_estimate=pl.CostEstimate(flops=400_000_000, bytes_accessed=2_000_000, transcendentals=0),
        name="refine",
    )(pos, mine, other, hp, seen, cross)


def pack_kernel(pos_ref, ca_ref, cb_ref, ma_ref, mb_ref, *rest_refs):
    near_ref, wide_ref = rest_refs[4:]
    s = pos_ref[0] // 16
    b = pos_ref[0] % 16
    off = jnp.where(b % 2 == 0, 112, 48)
    lane = lax.broadcasted_iota(jnp.int32, (1, LANES), 1)
    first = lane >= off
    block = (b + 1) // 2 - jnp.where(first, 1, 0)
    keep = (block >= 0) & (block < 8)
    source = lax.broadcasted_iota(jnp.int32, (LANES, LANES), 0)
    target = lax.broadcasted_iota(jnp.int32, (LANES, LANES), 1)
    order = jnp.where(source == (4 * (target % 32) + target // 32 + off) % LANES, 1.0, 0.0).astype(bf16)
    ms = jnp.where(first, ma_ref[...].reshape(128, LANES).astype(f32), mb_ref[...].reshape(128, LANES).astype(f32))
    ms = jnp.where(keep, ms, 0.0).astype(bf16)
    ms = jnp.dot(ms, order, preferred_element_type=f32)
    near_ref[...] = ms.astype(bf16)
    edge = jnp.zeros((16, LANES), f32)
    for k in range(4):
        rest = jnp.where(keep, jnp.where(first, ca_ref[k], cb_ref[k]), 0.0)
        total = None
        for _ in range(3):
            piece = rest.astype(bf16)
            rest = rest - piece.astype(f32)
            moved = jnp.dot(piece, order, preferred_element_type=f32)
            total = moved if total is None else total + moved
        wide_ref[k, 0:16] = edge
        wide_ref[k, 16:144] = total
        wide_ref[k, 144:160] = edge
    for d in range(4):
        at = pl.ds(pl.multiple_of(32 * ((s // 2 + d) % 4), 32), 64)
        for k in range(4):
            rest_refs[d][64 * k : 64 * k + 64] = wide_ref[k, at, :]


def pack(pos, coeffs_in, ms_image):
    def low(i, p):
        return (0, 0, jnp.maximum((p[0] % 16 + 1) // 2 - 1, 0))

    def high(i, p):
        return (0, 0, jnp.minimum((p[0] % 16 + 1) // 2, 7))

    return pl.pallas_call(
        pack_kernel,
        out_shape=(jax.ShapeDtypeStruct((256, LANES), f32),) * 4 + (jax.ShapeDtypeStruct((128, LANES), bf16),),
        grid_spec=pltpu.PrefetchScalarGridSpec(
            num_scalar_prefetch=1,
            grid=(1,),
            in_specs=[
                pl.BlockSpec((4, 128, LANES), low),
                pl.BlockSpec((4, 128, LANES), high),
                pl.BlockSpec((8, 16, LANES), low),
                pl.BlockSpec((8, 16, LANES), high),
            ],
            out_specs=(pl.BlockSpec((256, LANES), lambda i, p: (0, 0)),) * 4
            + (pl.BlockSpec((128, LANES), lambda i, p: (0, 0)),),
            scratch_shapes=[pltpu.VMEM((4, 160, LANES), f32)],
        ),
        compiler_params=pltpu.CompilerParams(vmem_limit_bytes=60 * 2**20),
        cost_estimate=pl.CostEstimate(flops=100_000_000, bytes_accessed=1_600_000, transcendentals=0),
        name="pack",
    )(pos, coeffs_in, coeffs_in, ms_image, ms_image)


def spread_kernel(hs_ref, k_ref, basis_ref, response_ref, sent_ref):
    lane = lax.broadcasted_iota(jnp.int32, (1, LANES), 1)
    hs = hs_ref[...].astype(f32)
    rows = [jnp.concatenate([hs[:, i, :], jnp.zeros((2, 256), f32)], axis=0) for i in range(4)]
    sent_ref[0, :, 128:256] = jnp.zeros((16, 128), f32)
    for a in range(9):
        sent_ref[0, 0:14, 128 + 9 * a : 137 + 9 * a] = k_ref[a]
    sent_ref[0, 0:14, 209:241] = basis_ref[...].astype(f32)
    sent_ref[0, 0:14, 241:249] = response_ref[...].astype(f32).T
    params = sent_ref[0, :, 128:256]
    for t in range(16):
        total = jnp.zeros((16, LANES), f32)
        for i in range(4):
            moved = pltpu.roll(rows[i], (24 * i + 3 - 16 * t) % 256, 1)[:, 0:128]
            total = jnp.where((lane >= 24 * i) & (lane < 24 * i + 24), moved, total)
        sent_ref[t, :, 0:128] = total
        if t:
            sent_ref[t, :, 128:256] = params


def spread(hs_image, kernels, basis, response):
    vmem = pl.BlockSpec(memory_space=pltpu.VMEM)
    return pl.pallas_call(
        spread_kernel,
        out_shape=jax.ShapeDtypeStruct((16, 16, 256), f32),
        in_specs=[vmem] * 4,
        out_specs=vmem,
        compiler_params=pltpu.CompilerParams(vmem_limit_bytes=60 * 2**20),
        cost_estimate=pl.CostEstimate(flops=1_000_000, bytes_accessed=1_000_000, transcendentals=0),
        name="spread",
    )(hs_image, kernels, basis, response)


def hand_kernel(pos_ref, r0, r1, r2, r3, seen_ref, mine_ref, other_ref):
    other_ref[16 * CROWS : 16 * CROWS + 384] = seen_ref[...].astype(f32)
    skip = 16 * (pos_ref[0] // 16 % 2)
    for d, region in enumerate((r0, r1, r2, r3)):
        for k in range(4):
            at = CROWS * (4 * d + k)
            mine_ref[at : at + CROWS] = region[pl.ds(pl.multiple_of(64 * k + skip, 16), CROWS), :]
            other_ref[at : at + CROWS] = region[pl.ds(pl.multiple_of(64 * k + 16 - skip, 16), CROWS), :]


def hand(pos, tiles, seen):
    vmem = pl.BlockSpec(memory_space=pltpu.VMEM)
    return pl.pallas_call(
        hand_kernel,
        out_shape=(
            jax.ShapeDtypeStruct((16 * CROWS, LANES), f32),
            jax.ShapeDtypeStruct((16 * CROWS + 384, LANES), f32),
        ),
        in_specs=[pl.BlockSpec(memory_space=pltpu.SMEM)] + [vmem] * 5,
        out_specs=(vmem, vmem),
        compiler_params=pltpu.CompilerParams(vmem_limit_bytes=16 * 2**20),
        cost_estimate=pl.CostEstimate(flops=1_000_000, bytes_accessed=800_000, transcendentals=0),
        name="hand",
    )(pos, *tiles, seen)


def encode_kernel(d_ref, out_ref):
    scales = []
    codes = []
    for k in range(4):
        part = d_ref[:, k]
        size = jnp.abs(part)
        top = jnp.max(size, axis=(0, 1, 2), keepdims=True)
        scale = rounded(jnp.maximum(top * (1 + 2**-7), 1e-30))
        code = jnp.exp2(size * (SPAN / scale) - SPAN / 2)
        codes.append(jnp.where(part < 0, -code, code))
        scales.append(jnp.broadcast_to(scale[0], (1, LANES)))
    scales = jnp.concatenate(scales + [jnp.zeros((12, LANES), f32)], axis=0).astype(bf16)
    for s in range(8):
        row = jnp.concatenate([codes[k][s] for k in range(4)], axis=0).astype(bf16)
        for t in range(16):
            out_ref[t, 32 * s : 32 * s + 32] = row
    for t in range(16):
        out_ref[t, 256:272] = scales


def encode(owned):
    vmem = pl.BlockSpec(memory_space=pltpu.VMEM)
    return pl.pallas_call(
        encode_kernel,
        out_shape=jax.ShapeDtypeStruct((16, 272, LANES), bf16),
        in_specs=[vmem],
        out_specs=vmem,
        compiler_params=pltpu.CompilerParams(vmem_limit_bytes=16 * 2**20),
        name="encode",
    )(owned)


def place_kernel(g_ref, c_ref, out_ref):
    lane = lax.broadcasted_iota(jnp.int32, (1, LANES), 1)
    low = lane < 64
    count = g_ref.shape[0] // 2
    for j in range(count):
        even, odd = [g_ref[2 * j + e, 256:272].astype(f32) * (1 / SPAN) for e in range(2)]
        scales = (jnp.where(low, even, odd), jnp.where(low, odd, even))
        columns = slice(j * LANES, j * LANES + LANES)
        for s in range(8):
            even, odd = [g_ref[2 * j + e, 32 * s : 32 * s + 32].astype(f32) for e in range(2)]
            for half, code in enumerate((jnp.where(low, even, odd), jnp.where(low, odd, even))):
                size = jnp.log2(jnp.abs(code)) + SPAN / 2
                value = jnp.where(code < 0, -size, size)
                for k in range(4):
                    part = value[8 * k : 8 * k + 8] * scales[half][k : k + 1]
                    if half:
                        part = pltpu.roll(part, 64, 1)
                    at = slice(16 * s + 8 * half, 16 * s + 8 * half + 8)
                    out_ref[k, at, columns] = c_ref[k, at, columns] + part


def place(gathered, coeffs_in):
    block = pl.BlockSpec((4, 128, 4 * LANES), lambda j: (0, 0, j))
    return pl.pallas_call(
        place_kernel,
        out_shape=jax.ShapeDtypeStruct((4, 128, 1024), f32),
        grid=(2,),
        in_specs=[pl.BlockSpec((8, 272, LANES), lambda j: (j, 0, 0)), block],
        out_specs=block,
        compiler_params=pltpu.CompilerParams(vmem_limit_bytes=32 * 2**20),
        name="place",
    )(gathered, coeffs_in)


def per_device(coeffs_in, basis, kernels, response, hs_image, ms_image):
    pos = (lax.axis_index("sub") * 16 + lax.axis_index("band")).astype(jnp.int32).reshape(1)
    sent = spread(hs_image, kernels.transpose(1, 0, 2), basis, response)
    sent, pos = lax.optimization_barrier((sent, pos))
    hp = lax.all_to_all(sent, "band", split_axis=0, concat_axis=0, tiled=True).reshape(256, 256)
    *tiles, near = pack(pos, coeffs_in, ms_image)
    tiles = [tiles[0]] + [
        lax.ppermute(tiles[d], "sub", [(i, (i + 2 * d) % 8) for i in range(8)]) for d in range(1, 4)
    ]
    seen = jnp.concatenate([hp[:, 0:128].astype(bf16), near], axis=0)
    cross = lax.ppermute(seen, "sub", [(1, 2), (2, 1), (3, 4), (4, 3), (5, 6), (6, 5)])
    cross, *tiles = lax.optimization_barrier((cross, *tiles))
    mine, other = hand(pos, tiles, seen)
    other = lax.ppermute(other, "sub", [(i, i ^ 1) for i in range(8)])
    new = refine(pos, mine, other, hp, seen, cross)
    owned = lax.all_to_all(new.reshape(8, 4, 8, LANES), "sub", split_axis=0, concat_axis=0, tiled=True)
    gathered = lax.all_to_all(encode(owned), "band", split_axis=0, concat_axis=0, tiled=True)
    return place(gathered, coeffs_in)


def solution(mesh):
    return jax.shard_map(
        per_device,
        mesh=mesh,
        in_specs=(
            P("sub", None, None),
            P("band", None),
            P("band", None, None),
            P(None, "band"),
            P("band", "sub", None),
            P(None, "sub", None),
        ),
        out_specs=P("sub", None, None),
        check_vma=False,
    )
```

```python
import functools

import jax
import jax.numpy as jnp
from jax import lax
from jax.experimental import pallas as pl
from jax.experimental.pallas import tpu as pltpu
from jax.sharding import PartitionSpec as P

STEP = 0.15
TR, TC = 16, 64
TAPS = 9
SPAN = 250.0
LANES = 128
CROWS = 48
MROWS = 32
IROWS = 10
JCOLS = 24
ROWS_LO, COLS_LO = 32, 256
f32 = jnp.float32
bf16 = jnp.bfloat16


def rounded(value):
    return value.astype(bf16).astype(f32)


def refine_kernel(pos_ref, *refs):
    mine_ref, other_ref, hp_ref, seen_ref, cross_ref, out_ref, c_ref, ms_ref, m0, m1, f0, f1, b0, b1, c1_ref, g_ref, hs0, hs1, w0, w1 = refs
    s = pos_ref[0] // 16
    b = pos_ref[0] % 16
    core = s % 2
    for d in range(4):
        chip = (s // 2 + 4 - d) % 4
        mine = pl.multiple_of((2 * chip + core) * (4 * CROWS), 4 * CROWS)
        theirs = pl.multiple_of((2 * chip + 1 - core) * (4 * CROWS), 4 * CROWS)
        c_ref[pl.ds(mine, 4 * CROWS), :] = mine_ref[d * 4 * CROWS : (d + 1) * 4 * CROWS]
        c_ref[pl.ds(theirs, 4 * CROWS), :] = other_ref[d * 4 * CROWS : (d + 1) * 4 * CROWS]

    def neighbours(low, high):
        theirs = other_ref[16 * CROWS + low : 16 * CROWS + high]
        across = cross_ref[low:high].astype(f32)
        flag = jnp.zeros((high - low, LANES), jnp.int32) + core
        return jnp.where(flag == 0, across, theirs), jnp.where(flag == 0, theirs, across)

    ms_above, ms_below = neighbours(256, 384)
    for k in range(8):
        ms_ref[32 * k : 32 * k + 8, :] = ms_above[16 * k + 8 : 16 * k + 16]
        ms_ref[32 * k + 8 : 32 * k + 24, :] = seen_ref[256 + 16 * k : 272 + 16 * k].astype(f32)
        ms_ref[32 * k + 24 : 32 * k + 32, :] = ms_below[16 * k : 16 * k + 8]
    bk = (b0, b1)
    m = (m0, m1)
    f = (f0, f1)
    hst = (hs0, hs1)
    w = (w0, w1)
    for h in range(2):
        at = slice(h * 128, h * 128 + 128)
        above, below = neighbours(h * 128, h * 128 + 128)
        hst[h][0:72, :] = above.T[24:96]
        hst[h][72:168, :] = hp_ref[at, 0:128].T[0:96]
        hst[h][168:240, :] = below.T[0:72]
        w[h][...] = hp_ref[at, 128:256].T
    basis = jnp.concatenate([w0[81:113, :], w1[81:113, :]], axis=1).astype(bf16)
    response = jnp.concatenate([w0[113:121, :], w1[113:121, :]], axis=1).astype(bf16)
    combined = lax.dot_general(response, basis, (((1,), (1,)), ((), ())), preferred_element_type=f32).astype(bf16)
    lane = lax.broadcasted_iota(jnp.int32, (1, LANES), 1)
    group = lane % 32
    column = 64 * b - 16 + 4 * group + lane // 32
    in_columns = (column >= 0) & (column < 1024) & (group >= 2) & (group < 22)

    def mix(row, value, rows):
        mixed = lax.dot_general(value.astype(bf16), basis, (((0,), (0,)), ((), ())), preferred_element_type=f32)
        mixed = rounded(mixed)
        at = pl.ds(pl.multiple_of(row * LANES, LANES), rows * LANES)
        for h in range(2):
            m[h][at, :] = mixed[:, h * 128 : h * 128 + 128]

    def ms_gradient(row, block):
        predicted = jnp.dot(combined, block.astype(bf16), preferred_element_type=f32)
        seen = jnp.concatenate([ms_ref[pl.ds(row - 8 + r, 8, stride=MROWS), :] for r in range(8)], axis=1)
        misfit = (seen - predicted).astype(bf16)
        grad = lax.dot_general(combined, misfit, (((0,), (0,)), ((), ())), preferred_element_type=f32)
        for r in range(8):
            g_ref[pl.ds((row - 8 + r) * 32, 32), :] = grad[:, r * 128 : r * 128 + 128]

    def blur_row(n):
        g = lax.broadcasted_iota(jnp.int32, (JCOLS, LANES), 0)
        i_at = 4 * s + n - 3
        j_at = 16 * b + g - 3
        inside = (i_at >= 0) & (i_at < ROWS_LO) & (j_at >= 0) & (j_at < COLS_LO)
        for h in range(2):
            acc = [None, None, None]
            for a in range(TAPS):
                for q in range(4):
                    at = pl.multiple_of((4 * n + a) * LANES + 32 * q, 32)
                    x = m[h][pl.ds(at, JCOLS), :]
                    for d in range(3):
                        if 4 * d + q > 8:
                            continue
                        tap = a * 9 + 4 * d + q
                        term = w[h][tap : tap + 1, :] * x
                        acc[d] = term if acc[d] is None else acc[d] + term
            blurred = acc[0] + pltpu.roll(acc[1], JCOLS - 1, 0) + pltpu.roll(acc[2], JCOLS - 2, 0)
            seen = hst[h][pl.ds(pl.multiple_of(n * JCOLS, 8), JCOLS), :]
            f[h][pl.ds(pl.multiple_of(8 + n * JCOLS, 8), JCOLS), :] = jnp.where(inside, seen - blurred, 0.0)

    def back_rows(u):
        for h in range(2):
            win = [[f[h][pl.ds(8 + (u - t) * JCOLS - tt, JCOLS), :] for tt in range(3)] for t in range(3)]
            for p in range(4):
                for q in range(4):
                    total = None
                    for t in range(3):
                        for tt in range(3):
                            if p + 4 * t > 8 or q + 4 * tt > 8:
                                continue
                            tap = (p + 4 * t) * 9 + q + 4 * tt
                            term = w[h][tap : tap + 1, :] * win[t][tt]
                            total = term if total is None else total + term
                    at = pl.multiple_of((4 * u - 8 + p) * LANES + 32 * q, 32)
                    bk[h][pl.ds(at, JCOLS), :] = rounded(total)

    def hs_gradient(row, rows):
        at = pl.ds((row - 8) * LANES, rows * LANES)
        back = jnp.concatenate([b0[at, :].astype(bf16), b1[at, :].astype(bf16)], axis=1)
        return lax.dot_general(basis, back, (((1,), (1,)), ((), ())), preferred_element_type=f32)

    def start_row(row):
        return c_ref[pl.ds(row, 32, stride=CROWS), :]

    def loop(low, high, body):
        def step(n, _):
            body(n)
            return 0

        lax.fori_loop(low, high, step, 0)

    for block in range(CROWS // 8):
        value = jnp.concatenate([start_row(block * 8 + r) for r in range(8)], axis=1)
        mix(block * 8, value, 8)
        if 1 <= block < 5:
            ms_gradient(block * 8, value)
    loop(0, IROWS, blur_row)
    loop(2, 10, back_rows)
    for block in range(1, 5):
        grad = hs_gradient(block * 8, 8)
        values = []
        for r in range(8):
            row = block * 8 + r
            now = start_row(row)
            new = now + STEP * (grad[:, r * 128 : r * 128 + 128] + g_ref[pl.ds((row - 8) * 32, 32), :])
            row_at = 16 * s - 16 + row
            new = jnp.where(in_columns & (row_at >= 0) & (row_at < 128), new, 0.0)
            c1_ref[pl.ds((row - 8) * 32, 32), :] = new
            values.append(new)
        value = jnp.concatenate(values, axis=1)
        mix(block * 8, value, 8)
        if 2 <= block < 4:
            ms_gradient(block * 8, value)
    loop(2, 8, blur_row)
    loop(4, 8, back_rows)
    place_at = lax.broadcasted_iota(jnp.int32, (LANES, LANES), 1)
    take = lax.broadcasted_iota(jnp.int32, (LANES, LANES), 0)
    shift = 4 * (take % 32) + take // 32 - 16
    order = [(place_at == shift + 64 * ((half + b) % 2)) & (shift >= 0) & (shift < 64) for half in range(2)]
    order = [jnp.where(o, 1.0, 0.0).astype(bf16) for o in order]
    grads = [hs_gradient(16, 8), hs_gradient(24, 8)]
    for r in range(8):
        total = None
        for half in range(2):
            row = 8 + r + 8 * half
            at = pl.ds(row * 32, 32)
            value = STEP * (grads[half][:, r * 128 : r * 128 + 128] + g_ref[at, :])
            value = value + (c1_ref[at, :] - start_row(row + 8))
            rest = jnp.where((group >= 4) & (group < 20), value, 0.0)
            for _ in range(3):
                piece = rest.astype(bf16)
                rest = rest - piece.astype(f32)
                moved = jnp.dot(piece, order[half], preferred_element_type=f32)
                total = moved if total is None else total + moved
        out_ref[pl.ds(r, 32, stride=8), :] = total


def refine(pos, mine, other, hp, seen, cross):
    vmem = pl.BlockSpec(memory_space=pltpu.VMEM)
    return pl.pallas_call(
        refine_kernel,
        out_shape=jax.ShapeDtypeStruct((32 * 8, LANES), f32),
        in_specs=[pl.BlockSpec(memory_space=pltpu.SMEM)] + [vmem] * 5,
        out_specs=vmem,
        scratch_shapes=[
            pltpu.VMEM((32 * CROWS, LANES), f32),
            pltpu.VMEM((8 * MROWS, LANES), f32),
            pltpu.VMEM((CROWS * LANES, LANES), f32),
            pltpu.VMEM((CROWS * LANES, LANES), f32),
            pltpu.VMEM((256, LANES), f32),
            pltpu.VMEM((256, LANES), f32),
            pltpu.VMEM((MROWS * LANES, LANES), f32),
            pltpu.VMEM((MROWS * LANES, LANES), f32),
            pltpu.VMEM((MROWS * 32, LANES), f32),
            pltpu.VMEM((MROWS * 32, LANES), f32),
            pltpu.VMEM((256, LANES), f32),
            pltpu.VMEM((256, LANES), f32),
            pltpu.VMEM((LANES, LANES), f32),
            pltpu.VMEM((LANES, LANES), f32),
        ],
        compiler_params=pltpu.CompilerParams(vmem_limit_bytes=40 * 2**20),
        cost_estimate=pl.CostEstimate(flops=400_000_000, bytes_accessed=2_000_000, transcendentals=0),
        name="refine",
    )(pos, mine, other, hp, seen, cross)


def spread(hs_ref, k_ref, basis_ref, response_ref, sent_ref):
    lane = lax.broadcasted_iota(jnp.int32, (1, LANES), 1)
    hs = hs_ref[...].astype(f32)
    rows = [jnp.concatenate([hs[:, i, :], jnp.zeros((2, 256), f32)], axis=0) for i in range(4)]
    sent_ref[0, :, 128:256] = jnp.zeros((16, 128), f32)
    for a in range(9):
        sent_ref[0, 0:14, 128 + 9 * a : 137 + 9 * a] = k_ref[a]
    sent_ref[0, 0:14, 209:241] = basis_ref[...].astype(f32)
    sent_ref[0, 0:14, 241:249] = response_ref[...].astype(f32).T
    params = sent_ref[0, :, 128:256]
    for t in range(16):
        total = jnp.zeros((16, LANES), f32)
        for i in range(4):
            moved = pltpu.roll(rows[i], (24 * i + 3 - 16 * t) % 256, 1)[:, 0:128]
            total = jnp.where((lane >= 24 * i) & (lane < 24 * i + 24), moved, total)
        sent_ref[t, :, 0:128] = total
        if t:
            sent_ref[t, :, 128:256] = params


def pack_kernel(pos_ref, ca_ref, cb_ref, ma_ref, mb_ref, hs_ref, k_ref, basis_ref, response_ref, *rest_refs):
    spread(hs_ref, k_ref, basis_ref, response_ref, rest_refs[5])
    near_ref, _, wide_ref = rest_refs[4:]
    s = pos_ref[0] // 16
    b = pos_ref[0] % 16
    off = jnp.where(b % 2 == 0, 112, 48)
    lane = lax.broadcasted_iota(jnp.int32, (1, LANES), 1)
    first = lane >= off
    block = (b + 1) // 2 - jnp.where(first, 1, 0)
    keep = (block >= 0) & (block < 8)
    source = lax.broadcasted_iota(jnp.int32, (LANES, LANES), 0)
    target = lax.broadcasted_iota(jnp.int32, (LANES, LANES), 1)
    order = jnp.where(source == (4 * (target % 32) + target // 32 + off) % LANES, 1.0, 0.0).astype(bf16)
    ms = jnp.where(first, ma_ref[...].reshape(128, LANES).astype(f32), mb_ref[...].reshape(128, LANES).astype(f32))
    ms = jnp.where(keep, ms, 0.0).astype(bf16)
    ms = jnp.dot(ms, order, preferred_element_type=f32)
    near_ref[...] = ms.astype(bf16)
    edge = jnp.zeros((16, LANES), f32)
    for k in range(4):
        rest = jnp.where(keep, jnp.where(first, ca_ref[k], cb_ref[k]), 0.0)
        total = None
        for _ in range(3):
            piece = rest.astype(bf16)
            rest = rest - piece.astype(f32)
            moved = jnp.dot(piece, order, preferred_element_type=f32)
            total = moved if total is None else total + moved
        wide_ref[k, 0:16] = edge
        wide_ref[k, 16:144] = total
        wide_ref[k, 144:160] = edge
    for d in range(4):
        at = pl.ds(pl.multiple_of(32 * ((s // 2 + d) % 4), 32), 64)
        for k in range(4):
            rest_refs[d][64 * k : 64 * k + 64] = wide_ref[k, at, :]


def pack(pos, coeffs_in, ms_image, hs_image, kernels, basis, response):
    def low(i, p):
        return (0, 0, jnp.maximum((p[0] % 16 + 1) // 2 - 1, 0))

    def high(i, p):
        return (0, 0, jnp.minimum((p[0] % 16 + 1) // 2, 7))

    return pl.pallas_call(
        pack_kernel,
        out_shape=(jax.ShapeDtypeStruct((256, LANES), f32),) * 4 + (
            jax.ShapeDtypeStruct((128, LANES), bf16),
            jax.ShapeDtypeStruct((16, 16, 256), f32),
        ),
        grid_spec=pltpu.PrefetchScalarGridSpec(
            num_scalar_prefetch=1,
            grid=(1,),
            in_specs=[
                pl.BlockSpec((4, 128, LANES), low),
                pl.BlockSpec((4, 128, LANES), high),
                pl.BlockSpec((8, 16, LANES), low),
                pl.BlockSpec((8, 16, LANES), high),
                pl.BlockSpec((14, 4, 256), lambda i, p: (0, 0, 0)),
                pl.BlockSpec((9, 14, 9), lambda i, p: (0, 0, 0)),
                pl.BlockSpec((14, 32), lambda i, p: (0, 0)),
                pl.BlockSpec((8, 14), lambda i, p: (0, 0)),
            ],
            out_specs=(pl.BlockSpec((256, LANES), lambda i, p: (0, 0)),) * 4
            + (
                pl.BlockSpec((128, LANES), lambda i, p: (0, 0)),
                pl.BlockSpec((16, 16, 256), lambda i, p: (0, 0, 0)),
            ),
            scratch_shapes=[pltpu.VMEM((4, 160, LANES), f32)],
        ),
        compiler_params=pltpu.CompilerParams(vmem_limit_bytes=60 * 2**20),
        cost_estimate=pl.CostEstimate(flops=100_000_000, bytes_accessed=1_600_000, transcendentals=0),
        name="pack",
    )(pos, coeffs_in, coeffs_in, ms_image, ms_image, hs_image, kernels, basis, response)


def hand_kernel(pos_ref, r0, r1, r2, r3, seen_ref, mine_ref, other_ref):
    other_ref[16 * CROWS : 16 * CROWS + 384] = seen_ref[...].astype(f32)
    skip = 16 * (pos_ref[0] // 16 % 2)
    for d, region in enumerate((r0, r1, r2, r3)):
        for k in range(4):
            at = CROWS * (4 * d + k)
            mine_ref[at : at + CROWS] = region[pl.ds(pl.multiple_of(64 * k + skip, 16), CROWS), :]
            other_ref[at : at + CROWS] = region[pl.ds(pl.multiple_of(64 * k + 16 - skip, 16), CROWS), :]


def hand(pos, tiles, seen):
    vmem = pl.BlockSpec(memory_space=pltpu.VMEM)
    return pl.pallas_call(
        hand_kernel,
        out_shape=(
            jax.ShapeDtypeStruct((16 * CROWS, LANES), f32),
            jax.ShapeDtypeStruct((16 * CROWS + 384, LANES), f32),
        ),
        in_specs=[pl.BlockSpec(memory_space=pltpu.SMEM)] + [vmem] * 5,
        out_specs=(vmem, vmem),
        compiler_params=pltpu.CompilerParams(vmem_limit_bytes=16 * 2**20),
        cost_estimate=pl.CostEstimate(flops=1_000_000, bytes_accessed=800_000, transcendentals=0),
        name="hand",
    )(pos, *tiles, seen)


def encode_kernel(d_ref, out_ref):
    scales = []
    codes = []
    for k in range(4):
        part = d_ref[:, k]
        size = jnp.abs(part)
        top = jnp.max(size, axis=(0, 1, 2), keepdims=True)
        scale = rounded(jnp.maximum(top * (1 + 2**-7), 1e-30))
        code = jnp.exp2(size * (SPAN / scale) - SPAN / 2)
        codes.append(jnp.where(part < 0, -code, code))
        scales.append(jnp.broadcast_to(scale[0], (1, LANES)))
    scales = jnp.concatenate(scales + [jnp.zeros((12, LANES), f32)], axis=0).astype(bf16)
    for s in range(8):
        row = jnp.concatenate([codes[k][s] for k in range(4)], axis=0).astype(bf16)
        for t in range(16):
            out_ref[t, 32 * s : 32 * s + 32] = row
    for t in range(16):
        out_ref[t, 256:272] = scales


def encode(owned):
    vmem = pl.BlockSpec(memory_space=pltpu.VMEM)
    return pl.pallas_call(
        encode_kernel,
        out_shape=jax.ShapeDtypeStruct((16, 272, LANES), bf16),
        in_specs=[vmem],
        out_specs=vmem,
        compiler_params=pltpu.CompilerParams(vmem_limit_bytes=16 * 2**20),
        name="encode",
    )(owned)


def place_kernel(g_ref, c_ref, out_ref):
    lane = lax.broadcasted_iota(jnp.int32, (1, LANES), 1)
    low = lane < 64
    count = g_ref.shape[0] // 2
    for j in range(count):
        even, odd = [g_ref[2 * j + e, 256:272].astype(f32) * (1 / SPAN) for e in range(2)]
        scales = (jnp.where(low, even, odd), jnp.where(low, odd, even))
        columns = slice(j * LANES, j * LANES + LANES)
        for s in range(8):
            even, odd = [g_ref[2 * j + e, 32 * s : 32 * s + 32].astype(f32) for e in range(2)]
            for half, code in enumerate((jnp.where(low, even, odd), jnp.where(low, odd, even))):
                size = jnp.log2(jnp.abs(code)) + SPAN / 2
                value = jnp.where(code < 0, -size, size)
                for k in range(4):
                    part = value[8 * k : 8 * k + 8] * scales[half][k : k + 1]
                    if half:
                        part = pltpu.roll(part, 64, 1)
                    at = slice(16 * s + 8 * half, 16 * s + 8 * half + 8)
                    out_ref[k, at, columns] = c_ref[k, at, columns] + part


def place(gathered, coeffs_in):
    block = pl.BlockSpec((4, 128, 4 * LANES), lambda j: (0, 0, j))
    return pl.pallas_call(
        place_kernel,
        out_shape=jax.ShapeDtypeStruct((4, 128, 1024), f32),
        grid=(2,),
        in_specs=[pl.BlockSpec((8, 272, LANES), lambda j: (j, 0, 0)), block],
        out_specs=block,
        compiler_params=pltpu.CompilerParams(vmem_limit_bytes=32 * 2**20),
        name="place",
    )(gathered, coeffs_in)


def per_device(coeffs_in, basis, kernels, response, hs_image, ms_image):
    pos = (lax.axis_index("sub") * 16 + lax.axis_index("band")).astype(jnp.int32).reshape(1)
    *tiles, near, sent = pack(pos, coeffs_in, ms_image, hs_image, kernels.transpose(1, 0, 2), basis, response)
    hp = lax.all_to_all(sent, "band", split_axis=0, concat_axis=0, tiled=True).reshape(256, 256)
    tiles = [tiles[0]] + [
        lax.ppermute(tiles[d], "sub", [(i, (i + 2 * d) % 8) for i in range(8)]) for d in range(1, 4)
    ]
    seen = jnp.concatenate([hp[:, 0:128].astype(bf16), near], axis=0)
    cross = lax.ppermute(seen, "sub", [(1, 2), (2, 1), (3, 4), (4, 3), (5, 6), (6, 5)])
    cross, *tiles = lax.optimization_barrier((cross, *tiles))
    mine, other = hand(pos, tiles, seen)
    other = lax.ppermute(other, "sub", [(i, i ^ 1) for i in range(8)])
    new = refine(pos, mine, other, hp, seen, cross)
    owned = lax.all_to_all(new.reshape(8, 4, 8, LANES), "sub", split_axis=0, concat_axis=0, tiled=True)
    gathered = lax.all_to_all(encode(owned), "band", split_axis=0, concat_axis=0, tiled=True)
    return place(gathered, coeffs_in)


def solution(mesh):
    return jax.shard_map(
        per_device,
        mesh=mesh,
        in_specs=(
            P("sub", None, None),
            P("band", None),
            P("band", None, None),
            P(None, "band"),
            P("band", "sub", None),
            P(None, "sub", None),
        ),
        out_specs=P("sub", None, None),
        check_vma=False,
    )
```

```python
import functools

import jax
import jax.numpy as jnp
from jax import lax
from jax.experimental import pallas as pl
from jax.experimental.pallas import tpu as pltpu
from jax.sharding import PartitionSpec as P

STEP = 0.15
TR, TC = 16, 64
TAPS = 9
SPAN = 250.0
LANES = 128
CROWS = 48
MROWS = 32
IROWS = 10
JCOLS = 24
ROWS_LO, COLS_LO = 32, 256
f32 = jnp.float32
bf16 = jnp.bfloat16


def rounded(value):
    return value.astype(bf16).astype(f32)


def refine_kernel(pos_ref, *refs):
    mine_ref, other_ref, hp_ref, seen_ref, cross_ref, out_ref, c_ref, ms_ref, m0, m1, f0, f1, b0, b1, c1_ref, g_ref, hs0, hs1, w0, w1 = refs
    s = pos_ref[0] // 16
    b = pos_ref[0] % 16
    core = s % 2
    for d in range(4):
        chip = (s // 2 + 4 - d) % 4
        mine = pl.multiple_of((2 * chip + core) * (4 * CROWS), 4 * CROWS)
        theirs = pl.multiple_of((2 * chip + 1 - core) * (4 * CROWS), 4 * CROWS)
        c_ref[pl.ds(mine, 4 * CROWS), :] = mine_ref[d * 4 * CROWS : (d + 1) * 4 * CROWS]
        c_ref[pl.ds(theirs, 4 * CROWS), :] = other_ref[d * 4 * CROWS : (d + 1) * 4 * CROWS]

    def neighbours(low, high):
        theirs = other_ref[16 * CROWS + low : 16 * CROWS + high]
        across = cross_ref[low:high].astype(f32)
        flag = jnp.zeros((high - low, LANES), jnp.int32) + core
        return jnp.where(flag == 0, across, theirs), jnp.where(flag == 0, theirs, across)

    ms_above, ms_below = neighbours(256, 384)
    for k in range(8):
        ms_ref[32 * k : 32 * k + 8, :] = ms_above[16 * k + 8 : 16 * k + 16]
        ms_ref[32 * k + 8 : 32 * k + 24, :] = seen_ref[256 + 16 * k : 272 + 16 * k].astype(f32)
        ms_ref[32 * k + 24 : 32 * k + 32, :] = ms_below[16 * k : 16 * k + 8]
    bk = (b0, b1)
    m = (m0, m1)
    f = (f0, f1)
    hst = (hs0, hs1)
    w = (w0, w1)
    for h in range(2):
        at = slice(h * 128, h * 128 + 128)
        above, below = neighbours(h * 128, h * 128 + 128)
        hst[h][0:72, :] = above.T[24:96]
        hst[h][72:168, :] = hp_ref[at, 0:128].T[0:96]
        hst[h][168:240, :] = below.T[0:72]
        w[h][...] = hp_ref[at, 128:256].T
    basis = jnp.concatenate([w0[81:113, :], w1[81:113, :]], axis=1).astype(bf16)
    response = jnp.concatenate([w0[113:121, :], w1[113:121, :]], axis=1).astype(bf16)
    combined = lax.dot_general(response, basis, (((1,), (1,)), ((), ())), preferred_element_type=f32).astype(bf16)
    lane = lax.broadcasted_iota(jnp.int32, (1, LANES), 1)
    group = lane % 32
    column = 64 * b - 16 + 4 * group + lane // 32
    in_columns = (column >= 0) & (column < 1024) & (group >= 2) & (group < 22)

    def mix(row, value, rows):
        mixed = lax.dot_general(value.astype(bf16), basis, (((0,), (0,)), ((), ())), preferred_element_type=f32)
        mixed = rounded(mixed)
        at = pl.ds(pl.multiple_of(row * LANES, LANES), rows * LANES)
        for h in range(2):
            m[h][at, :] = mixed[:, h * 128 : h * 128 + 128]

    def ms_gradient(row, block):
        predicted = jnp.dot(combined, block.astype(bf16), preferred_element_type=f32)
        seen = jnp.concatenate([ms_ref[pl.ds(row - 8 + r, 8, stride=MROWS), :] for r in range(8)], axis=1)
        misfit = (seen - predicted).astype(bf16)
        grad = lax.dot_general(combined, misfit, (((0,), (0,)), ((), ())), preferred_element_type=f32)
        for r in range(8):
            g_ref[pl.ds((row - 8 + r) * 32, 32), :] = grad[:, r * 128 : r * 128 + 128]

    def blur_row(n):
        g = lax.broadcasted_iota(jnp.int32, (JCOLS, LANES), 0)
        i_at = 4 * s + n - 3
        j_at = 16 * b + g - 3
        inside = (i_at >= 0) & (i_at < ROWS_LO) & (j_at >= 0) & (j_at < COLS_LO)
        for h in range(2):
            acc = [None, None, None]
            for a in range(TAPS):
                for q in range(4):
                    at = pl.multiple_of((4 * n + a) * LANES + 32 * q, 32)
                    x = m[h][pl.ds(at, JCOLS), :]
                    for d in range(3):
                        if 4 * d + q > 8:
                            continue
                        tap = a * 9 + 4 * d + q
                        term = w[h][tap : tap + 1, :] * x
                        acc[d] = term if acc[d] is None else acc[d] + term
            blurred = acc[0] + pltpu.roll(acc[1], JCOLS - 1, 0) + pltpu.roll(acc[2], JCOLS - 2, 0)
            seen = hst[h][pl.ds(pl.multiple_of(n * JCOLS, 8), JCOLS), :]
            f[h][pl.ds(pl.multiple_of(8 + n * JCOLS, 8), JCOLS), :] = jnp.where(inside, seen - blurred, 0.0)

    def back_rows(u):
        for h in range(2):
            win = [[f[h][pl.ds(8 + (u - t) * JCOLS - tt, JCOLS), :] for tt in range(3)] for t in range(3)]
            for p in range(4):
                for q in range(4):
                    total = None
                    for t in range(3):
                        for tt in range(3):
                            if p + 4 * t > 8 or q + 4 * tt > 8:
                                continue
                            tap = (p + 4 * t) * 9 + q + 4 * tt
                            term = w[h][tap : tap + 1, :] * win[t][tt]
                            total = term if total is None else total + term
                    at = pl.multiple_of((4 * u - 8 + p) * LANES + 32 * q, 32)
                    bk[h][pl.ds(at, JCOLS), :] = rounded(total)

    def hs_gradient(row, rows):
        at = pl.ds((row - 8) * LANES, rows * LANES)
        back = jnp.concatenate([b0[at, :].astype(bf16), b1[at, :].astype(bf16)], axis=1)
        return lax.dot_general(basis, back, (((1,), (1,)), ((), ())), preferred_element_type=f32)

    def start_row(row):
        return c_ref[pl.ds(row, 32, stride=CROWS), :]

    def loop(low, high, body):
        def step(n, _):
            body(n)
            return 0

        lax.fori_loop(low, high, step, 0)

    for block in range(CROWS // 8):
        value = jnp.concatenate([start_row(block * 8 + r) for r in range(8)], axis=1)
        mix(block * 8, value, 8)
        if 1 <= block < 5:
            ms_gradient(block * 8, value)
    loop(0, IROWS, blur_row)
    loop(2, 10, back_rows)
    for block in range(1, 5):
        grad = hs_gradient(block * 8, 8)
        values = []
        for r in range(8):
            row = block * 8 + r
            now = start_row(row)
            new = now + STEP * (grad[:, r * 128 : r * 128 + 128] + g_ref[pl.ds((row - 8) * 32, 32), :])
            row_at = 16 * s - 16 + row
            new = jnp.where(in_columns & (row_at >= 0) & (row_at < 128), new, 0.0)
            c1_ref[pl.ds((row - 8) * 32, 32), :] = new
            values.append(new)
        value = jnp.concatenate(values, axis=1)
        mix(block * 8, value, 8)
        if 2 <= block < 4:
            ms_gradient(block * 8, value)
    loop(2, 8, blur_row)
    loop(4, 8, back_rows)
    place_at = lax.broadcasted_iota(jnp.int32, (LANES, LANES), 1)
    take = lax.broadcasted_iota(jnp.int32, (LANES, LANES), 0)
    shift = 4 * (take % 32) + take // 32 - 16
    order = [(place_at == shift + 64 * ((half + b) % 2)) & (shift >= 0) & (shift < 64) for half in range(2)]
    order = [jnp.where(o, 1.0, 0.0).astype(bf16) for o in order]
    grads = [hs_gradient(16, 8), hs_gradient(24, 8)]
    for r in range(8):
        total = None
        for half in range(2):
            row = 8 + r + 8 * half
            at = pl.ds(row * 32, 32)
            value = STEP * (grads[half][:, r * 128 : r * 128 + 128] + g_ref[at, :])
            value = value + (c1_ref[at, :] - start_row(row + 8))
            rest = jnp.where((group >= 4) & (group < 20), value, 0.0)
            for _ in range(3):
                piece = rest.astype(bf16)
                rest = rest - piece.astype(f32)
                moved = jnp.dot(piece, order[half], preferred_element_type=f32)
                total = moved if total is None else total + moved
        out_ref[pl.ds(r, 32, stride=8), :] = total


def refine(pos, mine, other, hp, seen, cross):
    vmem = pl.BlockSpec(memory_space=pltpu.VMEM)
    return pl.pallas_call(
        refine_kernel,
        out_shape=jax.ShapeDtypeStruct((32 * 8, LANES), f32),
        in_specs=[pl.BlockSpec(memory_space=pltpu.SMEM)] + [vmem] * 5,
        out_specs=vmem,
        scratch_shapes=[
            pltpu.VMEM((32 * CROWS, LANES), f32),
            pltpu.VMEM((8 * MROWS, LANES), f32),
            pltpu.VMEM((CROWS * LANES, LANES), f32),
            pltpu.VMEM((CROWS * LANES, LANES), f32),
            pltpu.VMEM((256, LANES), f32),
            pltpu.VMEM((256, LANES), f32),
            pltpu.VMEM((MROWS * LANES, LANES), f32),
            pltpu.VMEM((MROWS * LANES, LANES), f32),
            pltpu.VMEM((MROWS * 32, LANES), f32),
            pltpu.VMEM((MROWS * 32, LANES), f32),
            pltpu.VMEM((256, LANES), f32),
            pltpu.VMEM((256, LANES), f32),
            pltpu.VMEM((LANES, LANES), f32),
            pltpu.VMEM((LANES, LANES), f32),
        ],
        compiler_params=pltpu.CompilerParams(vmem_limit_bytes=40 * 2**20),
        cost_estimate=pl.CostEstimate(flops=400_000_000, bytes_accessed=2_000_000, transcendentals=0),
        name="refine",
    )(pos, mine, other, hp, seen, cross)


def spread(hs_ref, k_ref, basis_ref, response_ref, sent_ref):
    lane = lax.broadcasted_iota(jnp.int32, (1, LANES), 1)
    hs = hs_ref[...].astype(f32)
    rows = [jnp.concatenate([hs[:, i, :], jnp.zeros((2, 256), f32)], axis=0) for i in range(4)]
    sent_ref[0, :, 128:256] = jnp.zeros((16, 128), f32)
    for a in range(9):
        sent_ref[0, 0:14, 128 + 9 * a : 137 + 9 * a] = k_ref[a]
    sent_ref[0, 0:14, 209:241] = basis_ref[...].astype(f32)
    sent_ref[0, 0:14, 241:249] = response_ref[...].astype(f32).T
    params = sent_ref[0, :, 128:256]
    for t in range(16):
        total = jnp.zeros((16, LANES), f32)
        for i in range(4):
            moved = pltpu.roll(rows[i], (24 * i + 3 - 16 * t) % 256, 1)[:, 0:128]
            total = jnp.where((lane >= 24 * i) & (lane < 24 * i + 24), moved, total)
        sent_ref[t, :, 0:128] = total
        if t:
            sent_ref[t, :, 128:256] = params


def pack_kernel(pos_ref, ca_ref, cb_ref, ma_ref, mb_ref, hs_ref, k_ref, basis_ref, response_ref, *rest_refs):
    spread(hs_ref, k_ref, basis_ref, response_ref, rest_refs[5])
    near_ref, _, wide_ref = rest_refs[4:]
    s = pos_ref[0] // 16
    b = pos_ref[0] % 16
    off = jnp.where(b % 2 == 0, 112, 48)
    lane = lax.broadcasted_iota(jnp.int32, (1, LANES), 1)
    first = lane >= off
    block = (b + 1) // 2 - jnp.where(first, 1, 0)
    keep = (block >= 0) & (block < 8)
    source = lax.broadcasted_iota(jnp.int32, (LANES, LANES), 0)
    target = lax.broadcasted_iota(jnp.int32, (LANES, LANES), 1)
    order = jnp.where(source == (4 * (target % 32) + target // 32 + off) % LANES, 1.0, 0.0).astype(bf16)
    ms = jnp.where(first, ma_ref[...].reshape(128, LANES).astype(f32), mb_ref[...].reshape(128, LANES).astype(f32))
    ms = jnp.where(keep, ms, 0.0).astype(bf16)
    ms = jnp.dot(ms, order, preferred_element_type=f32)
    near_ref[...] = ms.astype(bf16)
    edge = jnp.zeros((16, LANES), f32)
    for k in range(4):
        rest = jnp.where(keep, jnp.where(first, ca_ref[k], cb_ref[k]), 0.0)
        total = None
        for _ in range(3):
            piece = rest.astype(bf16)
            rest = rest - piece.astype(f32)
            moved = jnp.dot(piece, order, preferred_element_type=f32)
            total = moved if total is None else total + moved
        wide_ref[k, 0:16] = edge
        wide_ref[k, 16:144] = total
        wide_ref[k, 144:160] = edge
    for d in range(4):
        at = pl.ds(pl.multiple_of(32 * ((s // 2 + d) % 4), 32), 64)
        for k in range(4):
            rest_refs[d][64 * k : 64 * k + 64] = wide_ref[k, at, :]


def pack(pos, coeffs_in, ms_image, hs_image, kernels, basis, response):
    def low(i, p):
        return (0, 0, jnp.maximum((p[0] % 16 + 1) // 2 - 1, 0))

    def high(i, p):
        return (0, 0, jnp.minimum((p[0] % 16 + 1) // 2, 7))

    return pl.pallas_call(
        pack_kernel,
        out_shape=(jax.ShapeDtypeStruct((256, LANES), f32),) * 4 + (
            jax.ShapeDtypeStruct((128, LANES), bf16),
            jax.ShapeDtypeStruct((16, 16, 256), f32),
        ),
        grid_spec=pltpu.PrefetchScalarGridSpec(
            num_scalar_prefetch=1,
            grid=(1,),
            in_specs=[
                pl.BlockSpec((4, 128, LANES), low),
                pl.BlockSpec((4, 128, LANES), high),
                pl.BlockSpec((8, 16, LANES), low),
                pl.BlockSpec((8, 16, LANES), high),
                pl.BlockSpec((14, 4, 256), lambda i, p: (0, 0, 0)),
                pl.BlockSpec((9, 14, 9), lambda i, p: (0, 0, 0)),
                pl.BlockSpec((14, 32), lambda i, p: (0, 0)),
                pl.BlockSpec((8, 14), lambda i, p: (0, 0)),
            ],
            out_specs=(pl.BlockSpec((256, LANES), lambda i, p: (0, 0)),) * 4
            + (
                pl.BlockSpec((128, LANES), lambda i, p: (0, 0)),
                pl.BlockSpec((16, 16, 256), lambda i, p: (0, 0, 0)),
            ),
            scratch_shapes=[pltpu.VMEM((4, 160, LANES), f32)],
        ),
        compiler_params=pltpu.CompilerParams(vmem_limit_bytes=60 * 2**20),
        cost_estimate=pl.CostEstimate(flops=100_000_000, bytes_accessed=1_600_000, transcendentals=0),
        name="pack",
    )(pos, coeffs_in, coeffs_in, ms_image, ms_image, hs_image, kernels, basis, response)


def hold_kernel(region_ref, out_ref):
    out_ref[...] = region_ref[...]


def hold(region):
    vmem = pl.BlockSpec(memory_space=pltpu.VMEM)
    return pl.pallas_call(
        hold_kernel,
        out_shape=jax.ShapeDtypeStruct(region.shape, region.dtype),
        in_specs=[vmem],
        out_specs=vmem,
        compiler_params=pltpu.CompilerParams(vmem_limit_bytes=16 * 2**20),
        name="hold",
    )(region)


def hand_kernel(pos_ref, r0, r1, r2, r3, seen_ref, mine_ref, other_ref):
    other_ref[16 * CROWS : 16 * CROWS + 384] = seen_ref[...].astype(f32)
    skip = 16 * (pos_ref[0] // 16 % 2)
    for d, region in enumerate((r0, r1, r2, r3)):
        for k in range(4):
            at = CROWS * (4 * d + k)
            mine_ref[at : at + CROWS] = region[pl.ds(pl.multiple_of(64 * k + skip, 16), CROWS), :]
            other_ref[at : at + CROWS] = region[pl.ds(pl.multiple_of(64 * k + 16 - skip, 16), CROWS), :]


def hand(pos, tiles, seen):
    vmem = pl.BlockSpec(memory_space=pltpu.VMEM)
    return pl.pallas_call(
        hand_kernel,
        out_shape=(
            jax.ShapeDtypeStruct((16 * CROWS, LANES), f32),
            jax.ShapeDtypeStruct((16 * CROWS + 384, LANES), f32),
        ),
        in_specs=[pl.BlockSpec(memory_space=pltpu.SMEM)] + [vmem] * 5,
        out_specs=(vmem, vmem),
        compiler_params=pltpu.CompilerParams(vmem_limit_bytes=16 * 2**20),
        cost_estimate=pl.CostEstimate(flops=1_000_000, bytes_accessed=800_000, transcendentals=0),
        name="hand",
    )(pos, *tiles, seen)


def encode_kernel(d_ref, out_ref):
    scales = []
    codes = []
    for k in range(4):
        part = d_ref[:, k]
        size = jnp.abs(part)
        top = jnp.max(size, axis=(0, 1, 2), keepdims=True)
        scale = rounded(jnp.maximum(top * (1 + 2**-7), 1e-30))
        code = jnp.exp2(size * (SPAN / scale) - SPAN / 2)
        codes.append(jnp.where(part < 0, -code, code))
        scales.append(jnp.broadcast_to(scale[0], (1, LANES)))
    scales = jnp.concatenate(scales + [jnp.zeros((12, LANES), f32)], axis=0).astype(bf16)
    for s in range(8):
        row = jnp.concatenate([codes[k][s] for k in range(4)], axis=0).astype(bf16)
        for t in range(16):
            out_ref[t, 32 * s : 32 * s + 32] = row
    for t in range(16):
        out_ref[t, 256:272] = scales


def encode(owned):
    vmem = pl.BlockSpec(memory_space=pltpu.VMEM)
    return pl.pallas_call(
        encode_kernel,
        out_shape=jax.ShapeDtypeStruct((16, 272, LANES), bf16),
        in_specs=[vmem],
        out_specs=vmem,
        compiler_params=pltpu.CompilerParams(vmem_limit_bytes=16 * 2**20),
        name="encode",
    )(owned)


def place_kernel(g_ref, c_ref, out_ref):
    lane = lax.broadcasted_iota(jnp.int32, (1, LANES), 1)
    low = lane < 64
    count = g_ref.shape[0] // 2
    for j in range(count):
        even, odd = [g_ref[2 * j + e, 256:272].astype(f32) * (1 / SPAN) for e in range(2)]
        scales = (jnp.where(low, even, odd), jnp.where(low, odd, even))
        columns = slice(j * LANES, j * LANES + LANES)
        for s in range(8):
            even, odd = [g_ref[2 * j + e, 32 * s : 32 * s + 32].astype(f32) for e in range(2)]
            for half, code in enumerate((jnp.where(low, even, odd), jnp.where(low, odd, even))):
                size = jnp.log2(jnp.abs(code)) + SPAN / 2
                value = jnp.where(code < 0, -size, size)
                for k in range(4):
                    part = value[8 * k : 8 * k + 8] * scales[half][k : k + 1]
                    if half:
                        part = pltpu.roll(part, 64, 1)
                    at = slice(16 * s + 8 * half, 16 * s + 8 * half + 8)
                    out_ref[k, at, columns] = c_ref[k, at, columns] + part


def place(gathered, coeffs_in):
    block = pl.BlockSpec((4, 128, 4 * LANES), lambda j: (0, 0, j))
    return pl.pallas_call(
        place_kernel,
        out_shape=jax.ShapeDtypeStruct((4, 128, 1024), f32),
        grid=(2,),
        in_specs=[pl.BlockSpec((8, 272, LANES), lambda j: (j, 0, 0)), block],
        out_specs=block,
        compiler_params=pltpu.CompilerParams(vmem_limit_bytes=32 * 2**20),
        name="place",
    )(gathered, coeffs_in)


def per_device(coeffs_in, basis, kernels, response, hs_image, ms_image):
    pos = (lax.axis_index("sub") * 16 + lax.axis_index("band")).astype(jnp.int32).reshape(1)
    *tiles, near, sent = pack(pos, coeffs_in, ms_image, hs_image, kernels.transpose(1, 0, 2), basis, response)
    hp = lax.all_to_all(sent, "band", split_axis=0, concat_axis=0, tiled=True).reshape(256, 256)
    tiles = [tiles[0]] + [
        lax.ppermute(tiles[d], "sub", [(i, (i + 2 * d) % 8) for i in range(8)]) for d in range(1, 4)
    ]
    tiles[0], near = lax.optimization_barrier((hold(tiles[0]), near))
    seen = jnp.concatenate([hp[:, 0:128].astype(bf16), near], axis=0)
    cross = lax.ppermute(seen, "sub", [(1, 2), (2, 1), (3, 4), (4, 3), (5, 6), (6, 5)])
    cross, *tiles = lax.optimization_barrier((cross, *tiles))
    mine, other = hand(pos, tiles, seen)
    other = lax.ppermute(other, "sub", [(i, i ^ 1) for i in range(8)])
    new = refine(pos, mine, other, hp, seen, cross)
    owned = lax.all_to_all(new.reshape(8, 4, 8, LANES), "sub", split_axis=0, concat_axis=0, tiled=True)
    gathered = lax.all_to_all(encode(owned), "band", split_axis=0, concat_axis=0, tiled=True)
    return place(gathered, coeffs_in)


def solution(mesh):
    return jax.shard_map(
        per_device,
        mesh=mesh,
        in_specs=(
            P("sub", None, None),
            P("band", None),
            P("band", None, None),
            P(None, "band"),
            P("band", "sub", None),
            P(None, "sub", None),
        ),
        out_specs=P("sub", None, None),
        check_vma=False,
    )
```

```python
import functools

import jax
import jax.numpy as jnp
from jax import lax
from jax.experimental import pallas as pl
from jax.experimental.pallas import tpu as pltpu
from jax.sharding import PartitionSpec as P

STEP = 0.15
TR, TC = 16, 64
TAPS = 9
SPAN = 250.0
LANES = 128
CROWS = 48
MROWS = 32
IROWS = 10
JCOLS = 24
ROWS_LO, COLS_LO = 32, 256
f32 = jnp.float32
bf16 = jnp.bfloat16


def rounded(value):
    return value.astype(bf16).astype(f32)


def refine_kernel(pos_ref, *refs):
    mine_ref, other_ref, hp_ref, seen_ref, cross_ref, out_ref, c_ref, ms_ref, m0, m1, f0, f1, b0, b1, c1_ref, g_ref, hs0, hs1, w0, w1 = refs
    s = pos_ref[0] // 16
    b = pos_ref[0] % 16
    core = s % 2
    for d in range(4):
        chip = (s // 2 + 4 - d) % 4
        mine = pl.multiple_of((2 * chip + core) * (4 * CROWS), 4 * CROWS)
        theirs = pl.multiple_of((2 * chip + 1 - core) * (4 * CROWS), 4 * CROWS)
        c_ref[pl.ds(mine, 4 * CROWS), :] = mine_ref[d * 4 * CROWS : (d + 1) * 4 * CROWS]
        c_ref[pl.ds(theirs, 4 * CROWS), :] = other_ref[d * 4 * CROWS : (d + 1) * 4 * CROWS]

    def neighbours(low, high):
        theirs = other_ref[16 * CROWS + low : 16 * CROWS + high]
        across = cross_ref[low:high].astype(f32)
        flag = jnp.zeros((high - low, LANES), jnp.int32) + core
        return jnp.where(flag == 0, across, theirs), jnp.where(flag == 0, theirs, across)

    ms_above, ms_below = neighbours(256, 384)
    for k in range(8):
        ms_ref[32 * k : 32 * k + 8, :] = ms_above[16 * k + 8 : 16 * k + 16]
        ms_ref[32 * k + 8 : 32 * k + 24, :] = seen_ref[256 + 16 * k : 272 + 16 * k].astype(f32)
        ms_ref[32 * k + 24 : 32 * k + 32, :] = ms_below[16 * k : 16 * k + 8]
    bk = (b0, b1)
    m = (m0, m1)
    f = (f0, f1)
    hst = (hs0, hs1)
    w = (w0, w1)
    for h in range(2):
        at = slice(h * 128, h * 128 + 128)
        above, below = neighbours(h * 128, h * 128 + 128)
        hst[h][0:72, :] = above.T[24:96]
        hst[h][72:168, :] = hp_ref[at, 0:128].T[0:96]
        hst[h][168:240, :] = below.T[0:72]
        w[h][...] = hp_ref[at, 128:256].T
    basis = jnp.concatenate([w0[81:113, :], w1[81:113, :]], axis=1).astype(bf16)
    response = jnp.concatenate([w0[113:121, :], w1[113:121, :]], axis=1).astype(bf16)
    combined = lax.dot_general(response, basis, (((1,), (1,)), ((), ())), preferred_element_type=f32).astype(bf16)
    lane = lax.broadcasted_iota(jnp.int32, (1, LANES), 1)
    group = lane % 32
    column = 64 * b - 16 + 4 * group + lane // 32
    in_columns = (column >= 0) & (column < 1024) & (group >= 2) & (group < 22)

    def mix(row, value, rows):
        mixed = lax.dot_general(value.astype(bf16), basis, (((0,), (0,)), ((), ())), preferred_element_type=f32)
        mixed = rounded(mixed)
        at = pl.ds(pl.multiple_of(row * LANES, LANES), rows * LANES)
        for h in range(2):
            m[h][at, :] = mixed[:, h * 128 : h * 128 + 128]

    def ms_gradient(row, block):
        predicted = jnp.dot(combined, block.astype(bf16), preferred_element_type=f32)
        seen = jnp.concatenate([ms_ref[pl.ds(row - 8 + r, 8, stride=MROWS), :] for r in range(8)], axis=1)
        misfit = (seen - predicted).astype(bf16)
        grad = lax.dot_general(combined, misfit, (((0,), (0,)), ((), ())), preferred_element_type=f32)
        for r in range(8):
            g_ref[pl.ds((row - 8 + r) * 32, 32), :] = grad[:, r * 128 : r * 128 + 128]

    def blur_row(n):
        g = lax.broadcasted_iota(jnp.int32, (JCOLS, LANES), 0)
        i_at = 4 * s + n - 3
        j_at = 16 * b + g - 3
        inside = (i_at >= 0) & (i_at < ROWS_LO) & (j_at >= 0) & (j_at < COLS_LO)
        for h in range(2):
            acc = [None, None, None]
            for a in range(TAPS):
                for q in range(4):
                    at = pl.multiple_of((4 * n + a) * LANES + 32 * q, 32)
                    x = m[h][pl.ds(at, JCOLS), :]
                    for d in range(3):
                        if 4 * d + q > 8:
                            continue
                        tap = a * 9 + 4 * d + q
                        term = w[h][tap : tap + 1, :] * x
                        acc[d] = term if acc[d] is None else acc[d] + term
            blurred = acc[0] + pltpu.roll(acc[1], JCOLS - 1, 0) + pltpu.roll(acc[2], JCOLS - 2, 0)
            seen = hst[h][pl.ds(pl.multiple_of(n * JCOLS, 8), JCOLS), :]
            f[h][pl.ds(pl.multiple_of(8 + n * JCOLS, 8), JCOLS), :] = jnp.where(inside, seen - blurred, 0.0)

    def back_rows(u):
        for h in range(2):
            win = [[f[h][pl.ds(8 + (u - t) * JCOLS - tt, JCOLS), :] for tt in range(3)] for t in range(3)]
            for p in range(4):
                for q in range(4):
                    total = None
                    for t in range(3):
                        for tt in range(3):
                            if p + 4 * t > 8 or q + 4 * tt > 8:
                                continue
                            tap = (p + 4 * t) * 9 + q + 4 * tt
                            term = w[h][tap : tap + 1, :] * win[t][tt]
                            total = term if total is None else total + term
                    at = pl.multiple_of((4 * u - 8 + p) * LANES + 32 * q, 32)
                    bk[h][pl.ds(at, JCOLS), :] = rounded(total)

    def hs_gradient(row, rows):
        at = pl.ds((row - 8) * LANES, rows * LANES)
        back = jnp.concatenate([b0[at, :].astype(bf16), b1[at, :].astype(bf16)], axis=1)
        return lax.dot_general(basis, back, (((1,), (1,)), ((), ())), preferred_element_type=f32)

    def start_row(row):
        return c_ref[pl.ds(row, 32, stride=CROWS), :]

    def loop(low, high, body):
        def step(n, _):
            body(n)
            return 0

        lax.fori_loop(low, high, step, 0)

    for block in range(CROWS // 8):
        value = jnp.concatenate([start_row(block * 8 + r) for r in range(8)], axis=1)
        mix(block * 8, value, 8)
        if 1 <= block < 5:
            ms_gradient(block * 8, value)
    loop(0, IROWS, blur_row)
    loop(2, 10, back_rows)
    for block in range(1, 5):
        grad = hs_gradient(block * 8, 8)
        values = []
        for r in range(8):
            row = block * 8 + r
            now = start_row(row)
            new = now + STEP * (grad[:, r * 128 : r * 128 + 128] + g_ref[pl.ds((row - 8) * 32, 32), :])
            row_at = 16 * s - 16 + row
            new = jnp.where(in_columns & (row_at >= 0) & (row_at < 128), new, 0.0)
            c1_ref[pl.ds((row - 8) * 32, 32), :] = new
            values.append(new)
        value = jnp.concatenate(values, axis=1)
        mix(block * 8, value, 8)
        if 2 <= block < 4:
            ms_gradient(block * 8, value)
    loop(2, 8, blur_row)
    loop(4, 8, back_rows)
    place_at = lax.broadcasted_iota(jnp.int32, (LANES, LANES), 1)
    take = lax.broadcasted_iota(jnp.int32, (LANES, LANES), 0)
    shift = 4 * (take % 32) + take // 32 - 16
    order = [(place_at == shift + 64 * ((half + b) % 2)) & (shift >= 0) & (shift < 64) for half in range(2)]
    order = [jnp.where(o, 1.0, 0.0).astype(bf16) for o in order]
    grads = [hs_gradient(16, 8), hs_gradient(24, 8)]
    for r in range(8):
        total = None
        for half in range(2):
            row = 8 + r + 8 * half
            at = pl.ds(row * 32, 32)
            value = STEP * (grads[half][:, r * 128 : r * 128 + 128] + g_ref[at, :])
            value = value + (c1_ref[at, :] - start_row(row + 8))
            rest = jnp.where((group >= 4) & (group < 20), value, 0.0)
            for _ in range(3):
                piece = rest.astype(bf16)
                rest = rest - piece.astype(f32)
                moved = jnp.dot(piece, order[half], preferred_element_type=f32)
                total = moved if total is None else total + moved
        out_ref[pl.ds(r, 32, stride=8), :] = total


def refine(pos, mine, other, hp, seen, cross):
    vmem = pl.BlockSpec(memory_space=pltpu.VMEM)
    return pl.pallas_call(
        refine_kernel,
        out_shape=jax.ShapeDtypeStruct((32 * 8, LANES), f32),
        in_specs=[pl.BlockSpec(memory_space=pltpu.SMEM)] + [vmem] * 5,
        out_specs=vmem,
        scratch_shapes=[
            pltpu.VMEM((32 * CROWS, LANES), f32),
            pltpu.VMEM((8 * MROWS, LANES), f32),
            pltpu.VMEM((CROWS * LANES, LANES), f32),
            pltpu.VMEM((CROWS * LANES, LANES), f32),
            pltpu.VMEM((256, LANES), f32),
            pltpu.VMEM((256, LANES), f32),
            pltpu.VMEM((MROWS * LANES, LANES), f32),
            pltpu.VMEM((MROWS * LANES, LANES), f32),
            pltpu.VMEM((MROWS * 32, LANES), f32),
            pltpu.VMEM((MROWS * 32, LANES), f32),
            pltpu.VMEM((256, LANES), f32),
            pltpu.VMEM((256, LANES), f32),
            pltpu.VMEM((LANES, LANES), f32),
            pltpu.VMEM((LANES, LANES), f32),
        ],
        compiler_params=pltpu.CompilerParams(vmem_limit_bytes=40 * 2**20),
        cost_estimate=pl.CostEstimate(flops=400_000_000, bytes_accessed=2_000_000, transcendentals=0),
        name="refine",
    )(pos, mine, other, hp, seen, cross)


def spread(hs_ref, k_ref, basis_ref, response_ref, sent_ref):
    lane = lax.broadcasted_iota(jnp.int32, (1, LANES), 1)
    hs = hs_ref[...].astype(f32)
    rows = [jnp.concatenate([hs[:, i, :], jnp.zeros((2, 256), f32)], axis=0) for i in range(4)]
    sent_ref[0, :, 128:256] = jnp.zeros((16, 128), f32)
    for a in range(9):
        sent_ref[0, 0:14, 128 + 9 * a : 137 + 9 * a] = k_ref[a]
    sent_ref[0, 0:14, 209:241] = basis_ref[...].astype(f32)
    sent_ref[0, 0:14, 241:249] = response_ref[...].astype(f32).T
    params = sent_ref[0, :, 128:256]
    for t in range(16):
        total = jnp.zeros((16, LANES), f32)
        for i in range(4):
            moved = pltpu.roll(rows[i], (24 * i + 3 - 16 * t) % 256, 1)[:, 0:128]
            total = jnp.where((lane >= 24 * i) & (lane < 24 * i + 24), moved, total)
        sent_ref[t, :, 0:128] = total
        if t:
            sent_ref[t, :, 128:256] = params


def pack_kernel(pos_ref, ca_ref, cb_ref, ma_ref, mb_ref, hs_ref, k_ref, basis_ref, response_ref, *rest_refs):
    spread(hs_ref, k_ref, basis_ref, response_ref, rest_refs[5])
    near_ref, _, wide_ref = rest_refs[4:]
    s = pos_ref[0] // 16
    b = pos_ref[0] % 16
    off = jnp.where(b % 2 == 0, 112, 48)
    lane = lax.broadcasted_iota(jnp.int32, (1, LANES), 1)
    first = lane >= off
    block = (b + 1) // 2 - jnp.where(first, 1, 0)
    keep = (block >= 0) & (block < 8)
    source = lax.broadcasted_iota(jnp.int32, (LANES, LANES), 0)
    target = lax.broadcasted_iota(jnp.int32, (LANES, LANES), 1)
    order = jnp.where(source == (4 * (target % 32) + target // 32 + off) % LANES, 1.0, 0.0).astype(bf16)
    ms = jnp.where(first, ma_ref[...].reshape(128, LANES).astype(f32), mb_ref[...].reshape(128, LANES).astype(f32))
    ms = jnp.where(keep, ms, 0.0).astype(bf16)
    ms = jnp.dot(ms, order, preferred_element_type=f32)
    near_ref[...] = ms.astype(bf16)
    edge = jnp.zeros((16, LANES), f32)
    for k in range(4):
        rest = jnp.where(keep, jnp.where(first, ca_ref[k], cb_ref[k]), 0.0)
        total = None
        for _ in range(3):
            piece = rest.astype(bf16)
            rest = rest - piece.astype(f32)
            moved = jnp.dot(piece, order, preferred_element_type=f32)
            total = moved if total is None else total + moved
        wide_ref[k, 0:16] = edge
        wide_ref[k, 16:144] = total
        wide_ref[k, 144:160] = edge
    for d in range(4):
        at = pl.ds(pl.multiple_of(32 * ((s // 2 + d) % 4), 32), 64)
        for k in range(4):
            rest_refs[d][64 * k : 64 * k + 64] = wide_ref[k, at, :]


def pack(pos, coeffs_in, ms_image, hs_image, kernels, basis, response):
    def low(i, p):
        return (0, 0, jnp.maximum((p[0] % 16 + 1) // 2 - 1, 0))

    def high(i, p):
        return (0, 0, jnp.minimum((p[0] % 16 + 1) // 2, 7))

    return pl.pallas_call(
        pack_kernel,
        out_shape=(jax.ShapeDtypeStruct((256, LANES), f32),) * 4 + (
            jax.ShapeDtypeStruct((128, LANES), bf16),
            jax.ShapeDtypeStruct((16, 16, 256), f32),
        ),
        grid_spec=pltpu.PrefetchScalarGridSpec(
            num_scalar_prefetch=1,
            grid=(1,),
            in_specs=[
                pl.BlockSpec((4, 128, LANES), low),
                pl.BlockSpec((4, 128, LANES), high),
                pl.BlockSpec((8, 16, LANES), low),
                pl.BlockSpec((8, 16, LANES), high),
                pl.BlockSpec((14, 4, 256), lambda i, p: (0, 0, 0)),
                pl.BlockSpec((9, 14, 9), lambda i, p: (0, 0, 0)),
                pl.BlockSpec((14, 32), lambda i, p: (0, 0)),
                pl.BlockSpec((8, 14), lambda i, p: (0, 0)),
            ],
            out_specs=(pl.BlockSpec((256, LANES), lambda i, p: (0, 0)),) * 4
            + (
                pl.BlockSpec((128, LANES), lambda i, p: (0, 0)),
                pl.BlockSpec((16, 16, 256), lambda i, p: (0, 0, 0)),
            ),
            scratch_shapes=[pltpu.VMEM((4, 160, LANES), f32)],
        ),
        compiler_params=pltpu.CompilerParams(vmem_limit_bytes=60 * 2**20),
        cost_estimate=pl.CostEstimate(flops=100_000_000, bytes_accessed=1_600_000, transcendentals=0),
        name="pack",
    )(pos, coeffs_in, coeffs_in, ms_image, ms_image, hs_image, kernels, basis, response)


def hold_kernel(region_ref, out_ref):
    out_ref[...] = region_ref[...]


def hold(region):
    vmem = pl.BlockSpec(memory_space=pltpu.VMEM)
    return pl.pallas_call(
        hold_kernel,
        out_shape=jax.ShapeDtypeStruct(region.shape, region.dtype),
        in_specs=[vmem],
        out_specs=vmem,
        compiler_params=pltpu.CompilerParams(vmem_limit_bytes=16 * 2**20),
        name="hold",
    )(region)


def hand_kernel(pos_ref, r0, r1, r2, r3, seen_ref, mine_ref, other_ref):
    other_ref[16 * CROWS : 16 * CROWS + 384] = seen_ref[...].astype(f32)
    skip = 16 * (pos_ref[0] // 16 % 2)
    for d, region in enumerate((r0, r1, r2, r3)):
        for k in range(4):
            at = CROWS * (4 * d + k)
            mine_ref[at : at + CROWS] = region[pl.ds(pl.multiple_of(64 * k + skip, 16), CROWS), :]
            other_ref[at : at + CROWS] = region[pl.ds(pl.multiple_of(64 * k + 16 - skip, 16), CROWS), :]


def hand(pos, tiles, seen):
    vmem = pl.BlockSpec(memory_space=pltpu.VMEM)
    return pl.pallas_call(
        hand_kernel,
        out_shape=(
            jax.ShapeDtypeStruct((16 * CROWS, LANES), f32),
            jax.ShapeDtypeStruct((16 * CROWS + 384, LANES), f32),
        ),
        in_specs=[pl.BlockSpec(memory_space=pltpu.SMEM)] + [vmem] * 5,
        out_specs=(vmem, vmem),
        compiler_params=pltpu.CompilerParams(vmem_limit_bytes=16 * 2**20),
        cost_estimate=pl.CostEstimate(flops=1_000_000, bytes_accessed=800_000, transcendentals=0),
        name="hand",
    )(pos, *tiles, seen)


def encode_kernel(d_ref, out_ref):
    scales = []
    codes = []
    for k in range(4):
        part = d_ref[:, k]
        size = jnp.abs(part)
        top = jnp.max(size, axis=(0, 1, 2), keepdims=True)
        scale = rounded(jnp.maximum(top * (1 + 2**-7), 1e-30))
        code = jnp.exp2(size * (SPAN / scale) - SPAN / 2)
        codes.append(jnp.where(part < 0, -code, code))
        scales.append(jnp.broadcast_to(scale[0], (1, LANES)))
    scales = jnp.concatenate(scales + [jnp.zeros((12, LANES), f32)], axis=0).astype(bf16)
    for s in range(8):
        row = jnp.concatenate([codes[k][s] for k in range(4)], axis=0).astype(bf16)
        for t in range(16):
            out_ref[t, 32 * s : 32 * s + 32] = row
    for t in range(16):
        out_ref[t, 256:272] = scales


def encode(owned):
    vmem = pl.BlockSpec(memory_space=pltpu.VMEM)
    return pl.pallas_call(
        encode_kernel,
        out_shape=jax.ShapeDtypeStruct((16, 272, LANES), bf16),
        in_specs=[vmem],
        out_specs=vmem,
        compiler_params=pltpu.CompilerParams(vmem_limit_bytes=16 * 2**20),
        name="encode",
    )(owned)


def place_kernel(g_ref, c_ref, out_ref):
    lane = lax.broadcasted_iota(jnp.int32, (1, LANES), 1)
    low = lane < 64
    count = g_ref.shape[0] // 2
    for j in range(count):
        even, odd = [g_ref[2 * j + e, 256:272].astype(f32) * (1 / SPAN) for e in range(2)]
        scales = (jnp.where(low, even, odd), jnp.where(low, odd, even))
        columns = slice(j * LANES, j * LANES + LANES)
        for s in range(8):
            even, odd = [g_ref[2 * j + e, 32 * s : 32 * s + 32].astype(f32) for e in range(2)]
            for half, code in enumerate((jnp.where(low, even, odd), jnp.where(low, odd, even))):
                size = jnp.log2(jnp.abs(code)) + SPAN / 2
                value = jnp.where(code < 0, -size, size)
                for k in range(4):
                    part = value[8 * k : 8 * k + 8] * scales[half][k : k + 1]
                    if half:
                        part = pltpu.roll(part, 64, 1)
                    at = slice(16 * s + 8 * half, 16 * s + 8 * half + 8)
                    out_ref[k, at, columns] = c_ref[k, at, columns] + part


def place(gathered, coeffs_in):
    block = pl.BlockSpec((4, 128, 4 * LANES), lambda j: (0, 0, j))
    return pl.pallas_call(
        place_kernel,
        out_shape=jax.ShapeDtypeStruct((4, 128, 1024), f32),
        grid=(2,),
        in_specs=[pl.BlockSpec((8, 272, LANES), lambda j: (j, 0, 0)), block],
        out_specs=block,
        compiler_params=pltpu.CompilerParams(vmem_limit_bytes=32 * 2**20),
        name="place",
    )(gathered, coeffs_in)


def per_device(coeffs_in, basis, kernels, response, hs_image, ms_image):
    pos = (lax.axis_index("sub") * 16 + lax.axis_index("band")).astype(jnp.int32).reshape(1)
    *tiles, near, sent = pack(pos, coeffs_in, ms_image, hs_image, kernels.transpose(1, 0, 2), basis, response)
    hp = lax.all_to_all(sent, "band", split_axis=0, concat_axis=0, tiled=True).reshape(256, 256)
    tiles = [tiles[0]] + [
        lax.ppermute(tiles[d], "sub", [(i, (i + 2 * d) % 8) for i in range(8)]) for d in range(1, 4)
    ]
    tiles[0], near = lax.optimization_barrier((hold(tiles[0]), near))
    seen = jnp.concatenate([hp[:, 0:128].astype(bf16), near], axis=0)
    cross = lax.ppermute(seen, "sub", [(1, 2), (2, 1), (3, 4), (4, 3), (5, 6), (6, 5)])
    mine, other = hand(pos, tiles, seen)
    other = lax.ppermute(other, "sub", [(i, i ^ 1) for i in range(8)])
    new = refine(pos, mine, other, hp, seen, cross)
    owned = lax.all_to_all(new.reshape(8, 4, 8, LANES), "sub", split_axis=0, concat_axis=0, tiled=True)
    gathered = lax.all_to_all(encode(owned), "band", split_axis=0, concat_axis=0, tiled=True)
    return place(gathered, coeffs_in)


def solution(mesh):
    return jax.shard_map(
        per_device,
        mesh=mesh,
        in_specs=(
            P("sub", None, None),
            P("band", None),
            P("band", None, None),
            P(None, "band"),
            P("band", "sub", None),
            P(None, "sub", None),
        ),
        out_specs=P("sub", None, None),
        check_vma=False,
    )
```

```python
import functools

import jax
import jax.numpy as jnp
from jax import lax
from jax.experimental import pallas as pl
from jax.experimental.pallas import tpu as pltpu
from jax.sharding import PartitionSpec as P

STEP = 0.15
TR, TC = 16, 64
TAPS = 9
SPAN = 250.0
LANES = 128
CROWS = 48
MROWS = 32
IROWS = 10
JCOLS = 24
ROWS_LO, COLS_LO = 32, 256
f32 = jnp.float32
bf16 = jnp.bfloat16


def rounded(value):
    return value.astype(bf16).astype(f32)


def refine_kernel(pos_ref, *refs):
    mine_ref, other_ref, w_ref, own_ref, seen_ref, cross_ref, out_ref, c_ref, ms_ref, m0, m1, f0, f1, b0, b1, c1_ref, g_ref, hs0, hs1 = refs
    s = pos_ref[0] // 16
    b = pos_ref[0] % 16
    core = s % 2
    for d in range(4):
        chip = (s // 2 + 4 - d) % 4
        mine = pl.multiple_of((2 * chip + core) * (4 * CROWS), 4 * CROWS)
        theirs = pl.multiple_of((2 * chip + 1 - core) * (4 * CROWS), 4 * CROWS)
        c_ref[pl.ds(mine, 4 * CROWS), :] = mine_ref[d * 4 * CROWS : (d + 1) * 4 * CROWS]
        c_ref[pl.ds(theirs, 4 * CROWS), :] = other_ref[d * 4 * CROWS : (d + 1) * 4 * CROWS]

    def neighbours(low, high):
        theirs = other_ref[16 * CROWS + low : 16 * CROWS + high]
        across = cross_ref[low:high].astype(f32)
        flag = jnp.zeros((high - low, LANES), jnp.int32) + core
        return jnp.where(flag == 0, across, theirs), jnp.where(flag == 0, theirs, across)

    ms_above, ms_below = neighbours(256, 384)
    for k in range(8):
        ms_ref[32 * k : 32 * k + 8, :] = ms_above[16 * k + 8 : 16 * k + 16]
        ms_ref[32 * k + 8 : 32 * k + 24, :] = seen_ref[256 + 16 * k : 272 + 16 * k].astype(f32)
        ms_ref[32 * k + 24 : 32 * k + 32, :] = ms_below[16 * k : 16 * k + 8]
    bk = (b0, b1)
    m = (m0, m1)
    f = (f0, f1)
    hst = (hs0, hs1)
    w = (w_ref.at[0], w_ref.at[1])
    for h in range(2):
        above, below = neighbours(h * 128, h * 128 + 128)
        hst[h][0:72, :] = above.T[24:96]
        hst[h][72:168, :] = own_ref[h]
        hst[h][168:240, :] = below.T[0:72]
    basis = jnp.concatenate([w_ref[0, 81:113], w_ref[1, 81:113]], axis=1).astype(bf16)
    response = jnp.concatenate([w_ref[0, 113:121], w_ref[1, 113:121]], axis=1).astype(bf16)
    combined = lax.dot_general(response, basis, (((1,), (1,)), ((), ())), preferred_element_type=f32).astype(bf16)
    lane = lax.broadcasted_iota(jnp.int32, (1, LANES), 1)
    group = lane % 32
    column = 64 * b - 16 + 4 * group + lane // 32
    in_columns = (column >= 0) & (column < 1024) & (group >= 2) & (group < 22)

    def mix(row, value, rows):
        mixed = lax.dot_general(value.astype(bf16), basis, (((0,), (0,)), ((), ())), preferred_element_type=f32)
        mixed = rounded(mixed)
        at = pl.ds(pl.multiple_of(row * LANES, LANES), rows * LANES)
        for h in range(2):
            m[h][at, :] = mixed[:, h * 128 : h * 128 + 128]

    def ms_gradient(row, block):
        predicted = jnp.dot(combined, block.astype(bf16), preferred_element_type=f32)
        seen = jnp.concatenate([ms_ref[pl.ds(row - 8 + r, 8, stride=MROWS), :] for r in range(8)], axis=1)
        misfit = (seen - predicted).astype(bf16)
        grad = lax.dot_general(combined, misfit, (((0,), (0,)), ((), ())), preferred_element_type=f32)
        for r in range(8):
            g_ref[pl.ds((row - 8 + r) * 32, 32), :] = grad[:, r * 128 : r * 128 + 128]

    def blur_row(n):
        g = lax.broadcasted_iota(jnp.int32, (JCOLS, LANES), 0)
        i_at = 4 * s + n - 3
        j_at = 16 * b + g - 3
        inside = (i_at >= 0) & (i_at < ROWS_LO) & (j_at >= 0) & (j_at < COLS_LO)
        for h in range(2):
            acc = [None, None, None]
            for a in range(TAPS):
                for q in range(4):
                    at = pl.multiple_of((4 * n + a) * LANES + 32 * q, 32)
                    x = m[h][pl.ds(at, JCOLS), :]
                    for d in range(3):
                        if 4 * d + q > 8:
                            continue
                        tap = a * 9 + 4 * d + q
                        term = w[h][tap : tap + 1, :] * x
                        acc[d] = term if acc[d] is None else acc[d] + term
            blurred = acc[0] + pltpu.roll(acc[1], JCOLS - 1, 0) + pltpu.roll(acc[2], JCOLS - 2, 0)
            seen = hst[h][pl.ds(pl.multiple_of(n * JCOLS, 8), JCOLS), :]
            f[h][pl.ds(pl.multiple_of(8 + n * JCOLS, 8), JCOLS), :] = jnp.where(inside, seen - blurred, 0.0)

    def back_rows(u):
        for h in range(2):
            win = [[f[h][pl.ds(8 + (u - t) * JCOLS - tt, JCOLS), :] for tt in range(3)] for t in range(3)]
            for p in range(4):
                for q in range(4):
                    total = None
                    for t in range(3):
                        for tt in range(3):
                            if p + 4 * t > 8 or q + 4 * tt > 8:
                                continue
                            tap = (p + 4 * t) * 9 + q + 4 * tt
                            term = w[h][tap : tap + 1, :] * win[t][tt]
                            total = term if total is None else total + term
                    at = pl.multiple_of((4 * u - 8 + p) * LANES + 32 * q, 32)
                    bk[h][pl.ds(at, JCOLS), :] = rounded(total)

    def hs_gradient(row, rows):
        at = pl.ds((row - 8) * LANES, rows * LANES)
        back = jnp.concatenate([b0[at, :].astype(bf16), b1[at, :].astype(bf16)], axis=1)
        return lax.dot_general(basis, back, (((1,), (1,)), ((), ())), preferred_element_type=f32)

    def start_row(row):
        return c_ref[pl.ds(row, 32, stride=CROWS), :]

    def loop(low, high, body):
        def step(n, _):
            body(n)
            return 0

        lax.fori_loop(low, high, step, 0)

    for block in range(CROWS // 8):
        value = jnp.concatenate([start_row(block * 8 + r) for r in range(8)], axis=1)
        mix(block * 8, value, 8)
        if 1 <= block < 5:
            ms_gradient(block * 8, value)
    loop(0, IROWS, blur_row)
    loop(2, 10, back_rows)
    for block in range(1, 5):
        grad = hs_gradient(block * 8, 8)
        values = []
        for r in range(8):
            row = block * 8 + r
            now = start_row(row)
            new = now + STEP * (grad[:, r * 128 : r * 128 + 128] + g_ref[pl.ds((row - 8) * 32, 32), :])
            row_at = 16 * s - 16 + row
            new = jnp.where(in_columns & (row_at >= 0) & (row_at < 128), new, 0.0)
            c1_ref[pl.ds((row - 8) * 32, 32), :] = new
            values.append(new)
        value = jnp.concatenate(values, axis=1)
        mix(block * 8, value, 8)
        if 2 <= block < 4:
            ms_gradient(block * 8, value)
    loop(2, 8, blur_row)
    loop(4, 8, back_rows)
    place_at = lax.broadcasted_iota(jnp.int32, (LANES, LANES), 1)
    take = lax.broadcasted_iota(jnp.int32, (LANES, LANES), 0)
    shift = 4 * (take % 32) + take // 32 - 16
    order = [(place_at == shift + 64 * ((half + b) % 2)) & (shift >= 0) & (shift < 64) for half in range(2)]
    order = [jnp.where(o, 1.0, 0.0).astype(bf16) for o in order]
    grads = [hs_gradient(16, 8), hs_gradient(24, 8)]
    for r in range(8):
        total = None
        for half in range(2):
            row = 8 + r + 8 * half
            at = pl.ds(row * 32, 32)
            value = STEP * (grads[half][:, r * 128 : r * 128 + 128] + g_ref[at, :])
            value = value + (c1_ref[at, :] - start_row(row + 8))
            rest = jnp.where((group >= 4) & (group < 20), value, 0.0)
            for _ in range(3):
                piece = rest.astype(bf16)
                rest = rest - piece.astype(f32)
                moved = jnp.dot(piece, order[half], preferred_element_type=f32)
                total = moved if total is None else total + moved
        out_ref[pl.ds(r, 32, stride=8), :] = total


def refine(pos, mine, other, w, own, seen, cross):
    vmem = pl.BlockSpec(memory_space=pltpu.VMEM)
    return pl.pallas_call(
        refine_kernel,
        out_shape=jax.ShapeDtypeStruct((32 * 8, LANES), f32),
        in_specs=[pl.BlockSpec(memory_space=pltpu.SMEM)] + [vmem] * 6,
        out_specs=vmem,
        scratch_shapes=[
            pltpu.VMEM((32 * CROWS, LANES), f32),
            pltpu.VMEM((8 * MROWS, LANES), f32),
            pltpu.VMEM((CROWS * LANES, LANES), f32),
            pltpu.VMEM((CROWS * LANES, LANES), f32),
            pltpu.VMEM((256, LANES), f32),
            pltpu.VMEM((256, LANES), f32),
            pltpu.VMEM((MROWS * LANES, LANES), f32),
            pltpu.VMEM((MROWS * LANES, LANES), f32),
            pltpu.VMEM((MROWS * 32, LANES), f32),
            pltpu.VMEM((MROWS * 32, LANES), f32),
            pltpu.VMEM((256, LANES), f32),
            pltpu.VMEM((256, LANES), f32),
        ],
        compiler_params=pltpu.CompilerParams(vmem_limit_bytes=40 * 2**20),
        cost_estimate=pl.CostEstimate(flops=400_000_000, bytes_accessed=2_000_000, transcendentals=0),
        name="refine",
    )(pos, mine, other, w, own, seen, cross)


def spread(hs_ref, k_ref, basis_ref, response_ref, sent_ref):
    lane = lax.broadcasted_iota(jnp.int32, (1, LANES), 1)
    hs = hs_ref[...].astype(f32)
    rows = [jnp.concatenate([hs[:, i, :], jnp.zeros((2, 256), f32)], axis=0) for i in range(4)]
    sent_ref[0, :, 128:256] = jnp.zeros((16, 128), f32)
    for a in range(9):
        sent_ref[0, 0:14, 128 + 9 * a : 137 + 9 * a] = k_ref[a]
    sent_ref[0, 0:14, 209:241] = basis_ref[...].astype(f32)
    sent_ref[0, 0:14, 241:249] = response_ref[...].astype(f32).T
    params = sent_ref[0, :, 128:256]
    for t in range(16):
        total = jnp.zeros((16, LANES), f32)
        for i in range(4):
            moved = pltpu.roll(rows[i], (24 * i + 3 - 16 * t) % 256, 1)[:, 0:128]
            total = jnp.where((lane >= 24 * i) & (lane < 24 * i + 24), moved, total)
        sent_ref[t, :, 0:128] = total
        if t:
            sent_ref[t, :, 128:256] = params


def pack_kernel(pos_ref, ca_ref, cb_ref, ma_ref, mb_ref, hs_ref, k_ref, basis_ref, response_ref, *rest_refs):
    spread(hs_ref, k_ref, basis_ref, response_ref, rest_refs[5])
    near_ref, _, wide_ref = rest_refs[4:]
    s = pos_ref[0] // 16
    b = pos_ref[0] % 16
    off = jnp.where(b % 2 == 0, 112, 48)
    lane = lax.broadcasted_iota(jnp.int32, (1, LANES), 1)
    first = lane >= off
    block = (b + 1) // 2 - jnp.where(first, 1, 0)
    keep = (block >= 0) & (block < 8)
    source = lax.broadcasted_iota(jnp.int32, (LANES, LANES), 0)
    target = lax.broadcasted_iota(jnp.int32, (LANES, LANES), 1)
    order = jnp.where(source == (4 * (target % 32) + target // 32 + off) % LANES, 1.0, 0.0).astype(bf16)
    ms = jnp.where(first, ma_ref[...].reshape(128, LANES).astype(f32), mb_ref[...].reshape(128, LANES).astype(f32))
    ms = jnp.where(keep, ms, 0.0).astype(bf16)
    ms = jnp.dot(ms, order, preferred_element_type=f32)
    near_ref[...] = ms.astype(bf16)
    edge = jnp.zeros((16, LANES), f32)
    for k in range(4):
        rest = jnp.where(keep, jnp.where(first, ca_ref[k], cb_ref[k]), 0.0)
        total = None
        for _ in range(3):
            piece = rest.astype(bf16)
            rest = rest - piece.astype(f32)
            moved = jnp.dot(piece, order, preferred_element_type=f32)
            total = moved if total is None else total + moved
        wide_ref[k, 0:16] = edge
        wide_ref[k, 16:144] = total
        wide_ref[k, 144:160] = edge
    for d in range(4):
        at = pl.ds(pl.multiple_of(32 * ((s // 2 + d) % 4), 32), 64)
        for k in range(4):
            rest_refs[d][64 * k : 64 * k + 64] = wide_ref[k, at, :]


def pack(pos, coeffs_in, ms_image, hs_image, kernels, basis, response):
    def low(i, p):
        return (0, 0, jnp.maximum((p[0] % 16 + 1) // 2 - 1, 0))

    def high(i, p):
        return (0, 0, jnp.minimum((p[0] % 16 + 1) // 2, 7))

    return pl.pallas_call(
        pack_kernel,
        out_shape=(jax.ShapeDtypeStruct((256, LANES), f32),) * 4 + (
            jax.ShapeDtypeStruct((128, LANES), bf16),
            jax.ShapeDtypeStruct((16, 16, 256), f32),
        ),
        grid_spec=pltpu.PrefetchScalarGridSpec(
            num_scalar_prefetch=1,
            grid=(1,),
            in_specs=[
                pl.BlockSpec((4, 128, LANES), low),
                pl.BlockSpec((4, 128, LANES), high),
                pl.BlockSpec((8, 16, LANES), low),
                pl.BlockSpec((8, 16, LANES), high),
                pl.BlockSpec((14, 4, 256), lambda i, p: (0, 0, 0)),
                pl.BlockSpec((9, 14, 9), lambda i, p: (0, 0, 0)),
                pl.BlockSpec((14, 32), lambda i, p: (0, 0)),
                pl.BlockSpec((8, 14), lambda i, p: (0, 0)),
            ],
            out_specs=(pl.BlockSpec((256, LANES), lambda i, p: (0, 0)),) * 4
            + (
                pl.BlockSpec((128, LANES), lambda i, p: (0, 0)),
                pl.BlockSpec((16, 16, 256), lambda i, p: (0, 0, 0)),
            ),
            scratch_shapes=[pltpu.VMEM((4, 160, LANES), f32)],
        ),
        compiler_params=pltpu.CompilerParams(vmem_limit_bytes=60 * 2**20),
        cost_estimate=pl.CostEstimate(flops=100_000_000, bytes_accessed=1_600_000, transcendentals=0),
        name="pack",
    )(pos, coeffs_in, coeffs_in, ms_image, ms_image, hs_image, kernels, basis, response)


def turn_kernel(hp_ref, w_ref, own_ref):
    for h in range(2):
        at = slice(h * 128, h * 128 + 128)
        w_ref[h] = hp_ref[at, 128:256].T
        own_ref[h] = hp_ref[at, 0:128].T[0:96]


def turn(hp):
    vmem = pl.BlockSpec(memory_space=pltpu.VMEM)
    return pl.pallas_call(
        turn_kernel,
        out_shape=(jax.ShapeDtypeStruct((2, 128, LANES), f32), jax.ShapeDtypeStruct((2, 96, LANES), f32)),
        in_specs=[vmem],
        out_specs=(vmem, vmem),
        compiler_params=pltpu.CompilerParams(vmem_limit_bytes=16 * 2**20),
        cost_estimate=pl.CostEstimate(flops=1_000_000, bytes_accessed=20_000_000, transcendentals=0),
        name="turn",
    )(hp)


def hold_kernel(region_ref, out_ref):
    out_ref[...] = region_ref[...]


def hold(region):
    vmem = pl.BlockSpec(memory_space=pltpu.VMEM)
    return pl.pallas_call(
        hold_kernel,
        out_shape=jax.ShapeDtypeStruct(region.shape, region.dtype),
        in_specs=[vmem],
        out_specs=vmem,
        compiler_params=pltpu.CompilerParams(vmem_limit_bytes=16 * 2**20),
        name="hold",
    )(region)


def hand_kernel(pos_ref, r0, r1, r2, r3, seen_ref, mine_ref, other_ref):
    other_ref[16 * CROWS : 16 * CROWS + 384] = seen_ref[...].astype(f32)
    skip = 16 * (pos_ref[0] // 16 % 2)
    for d, region in enumerate((r0, r1, r2, r3)):
        for k in range(4):
            at = CROWS * (4 * d + k)
            mine_ref[at : at + CROWS] = region[pl.ds(pl.multiple_of(64 * k + skip, 16), CROWS), :]
            other_ref[at : at + CROWS] = region[pl.ds(pl.multiple_of(64 * k + 16 - skip, 16), CROWS), :]


def hand(pos, tiles, seen):
    vmem = pl.BlockSpec(memory_space=pltpu.VMEM)
    return pl.pallas_call(
        hand_kernel,
        out_shape=(
            jax.ShapeDtypeStruct((16 * CROWS, LANES), f32),
            jax.ShapeDtypeStruct((16 * CROWS + 384, LANES), f32),
        ),
        in_specs=[pl.BlockSpec(memory_space=pltpu.SMEM)] + [vmem] * 5,
        out_specs=(vmem, vmem),
        compiler_params=pltpu.CompilerParams(vmem_limit_bytes=16 * 2**20),
        cost_estimate=pl.CostEstimate(flops=1_000_000, bytes_accessed=800_000, transcendentals=0),
        name="hand",
    )(pos, *tiles, seen)


def encode_kernel(d_ref, out_ref):
    scales = []
    codes = []
    for k in range(4):
        part = d_ref[:, k]
        size = jnp.abs(part)
        top = jnp.max(size, axis=(0, 1, 2), keepdims=True)
        scale = rounded(jnp.maximum(top * (1 + 2**-7), 1e-30))
        code = jnp.exp2(size * (SPAN / scale) - SPAN / 2)
        codes.append(jnp.where(part < 0, -code, code))
        scales.append(jnp.broadcast_to(scale[0], (1, LANES)))
    scales = jnp.concatenate(scales + [jnp.zeros((12, LANES), f32)], axis=0).astype(bf16)
    for s in range(8):
        row = jnp.concatenate([codes[k][s] for k in range(4)], axis=0).astype(bf16)
        for t in range(16):
            out_ref[t, 32 * s : 32 * s + 32] = row
    for t in range(16):
        out_ref[t, 256:272] = scales


def encode(owned):
    vmem = pl.BlockSpec(memory_space=pltpu.VMEM)
    return pl.pallas_call(
        encode_kernel,
        out_shape=jax.ShapeDtypeStruct((16, 272, LANES), bf16),
        in_specs=[vmem],
        out_specs=vmem,
        compiler_params=pltpu.CompilerParams(vmem_limit_bytes=16 * 2**20),
        name="encode",
    )(owned)


def place_kernel(g_ref, c_ref, out_ref):
    lane = lax.broadcasted_iota(jnp.int32, (1, LANES), 1)
    low = lane < 64
    count = g_ref.shape[0] // 2
    for j in range(count):
        even, odd = [g_ref[2 * j + e, 256:272].astype(f32) * (1 / SPAN) for e in range(2)]
        scales = (jnp.where(low, even, odd), jnp.where(low, odd, even))
        columns = slice(j * LANES, j * LANES + LANES)
        for s in range(8):
            even, odd = [g_ref[2 * j + e, 32 * s : 32 * s + 32].astype(f32) for e in range(2)]
            for half, code in enumerate((jnp.where(low, even, odd), jnp.where(low, odd, even))):
                size = jnp.log2(jnp.abs(code)) + SPAN / 2
                value = jnp.where(code < 0, -size, size)
                for k in range(4):
                    part = value[8 * k : 8 * k + 8] * scales[half][k : k + 1]
                    if half:
                        part = pltpu.roll(part, 64, 1)
                    at = slice(16 * s + 8 * half, 16 * s + 8 * half + 8)
                    out_ref[k, at, columns] = c_ref[k, at, columns] + part


def place(gathered, coeffs_in):
    block = pl.BlockSpec((4, 128, 4 * LANES), lambda j: (0, 0, j))
    return pl.pallas_call(
        place_kernel,
        out_shape=jax.ShapeDtypeStruct((4, 128, 1024), f32),
        grid=(2,),
        in_specs=[pl.BlockSpec((8, 272, LANES), lambda j: (j, 0, 0)), block],
        out_specs=block,
        compiler_params=pltpu.CompilerParams(vmem_limit_bytes=32 * 2**20),
        name="place",
    )(gathered, coeffs_in)


def per_device(coeffs_in, basis, kernels, response, hs_image, ms_image):
    pos = (lax.axis_index("sub") * 16 + lax.axis_index("band")).astype(jnp.int32).reshape(1)
    *tiles, near, sent = pack(pos, coeffs_in, ms_image, hs_image, kernels.transpose(1, 0, 2), basis, response)
    hp = lax.all_to_all(sent, "band", split_axis=0, concat_axis=0, tiled=True).reshape(256, 256)
    tiles = [tiles[0]] + [
        lax.ppermute(tiles[d], "sub", [(i, (i + 2 * d) % 8) for i in range(8)]) for d in range(1, 4)
    ]
    tiles[0], near = lax.optimization_barrier((hold(tiles[0]), near))
    seen = jnp.concatenate([hp[:, 0:128].astype(bf16), near], axis=0)
    cross = lax.ppermute(seen, "sub", [(1, 2), (2, 1), (3, 4), (4, 3), (5, 6), (6, 5)])
    cross, *tiles = lax.optimization_barrier((cross, *tiles))
    mine, other = hand(pos, tiles, seen)
    other = lax.ppermute(other, "sub", [(i, i ^ 1) for i in range(8)])
    w, own = turn(hp)
    new = refine(pos, mine, other, w, own, seen, cross)
    owned = lax.all_to_all(new.reshape(8, 4, 8, LANES), "sub", split_axis=0, concat_axis=0, tiled=True)
    gathered = lax.all_to_all(encode(owned), "band", split_axis=0, concat_axis=0, tiled=True)
    return place(gathered, coeffs_in)


def solution(mesh):
    return jax.shard_map(
        per_device,
        mesh=mesh,
        in_specs=(
            P("sub", None, None),
            P("band", None),
            P("band", None, None),
            P(None, "band"),
            P("band", "sub", None),
            P(None, "sub", None),
        ),
        out_specs=P("sub", None, None),
        check_vma=False,
    )
```

```python
import functools

import jax
import jax.numpy as jnp
from jax import lax
from jax.experimental import pallas as pl
from jax.experimental.pallas import tpu as pltpu
from jax.sharding import PartitionSpec as P

STEP = 0.15
TR, TC = 16, 64
TAPS = 9
SPAN = 250.0
LANES = 128
CROWS = 48
MROWS = 32
IROWS = 10
JCOLS = 24
ROWS_LO, COLS_LO = 32, 256
f32 = jnp.float32
bf16 = jnp.bfloat16


def rounded(value):
    return value.astype(bf16).astype(f32)


def refine_kernel(pos_ref, *refs):
    mine_ref, other_ref, hp_ref, seen_ref, cross_ref, out_ref, c_ref, ms_ref, m0, m1, f0, f1, b0, b1, c1_ref, g_ref, hs0, hs1, w0, w1 = refs
    s = pos_ref[0] // 16
    b = pos_ref[0] % 16
    core = s % 2
    for d in range(4):
        chip = (s // 2 + 4 - d) % 4
        mine = pl.multiple_of((2 * chip + core) * (4 * CROWS), 4 * CROWS)
        theirs = pl.multiple_of((2 * chip + 1 - core) * (4 * CROWS), 4 * CROWS)
        c_ref[pl.ds(mine, 4 * CROWS), :] = mine_ref[d * 4 * CROWS : (d + 1) * 4 * CROWS]
        c_ref[pl.ds(theirs, 4 * CROWS), :] = other_ref[d * 4 * CROWS : (d + 1) * 4 * CROWS]

    def neighbours(low, high):
        theirs = other_ref[16 * CROWS + low : 16 * CROWS + high]
        across = cross_ref[low:high].astype(f32)
        flag = jnp.zeros((high - low, LANES), jnp.int32) + core
        return jnp.where(flag == 0, across, theirs), jnp.where(flag == 0, theirs, across)

    ms_above, ms_below = neighbours(256, 384)
    for k in range(8):
        ms_ref[32 * k : 32 * k + 8, :] = ms_above[16 * k + 8 : 16 * k + 16]
        ms_ref[32 * k + 8 : 32 * k + 24, :] = seen_ref[256 + 16 * k : 272 + 16 * k].astype(f32)
        ms_ref[32 * k + 24 : 32 * k + 32, :] = ms_below[16 * k : 16 * k + 8]
    bk = (b0, b1)
    m = (m0, m1)
    f = (f0, f1)
    hst = (hs0, hs1)
    w = (w0, w1)
    for h in range(2):
        at = slice(h * 128, h * 128 + 128)
        above, below = neighbours(h * 128, h * 128 + 128)
        hst[h][0:72, :] = above.T[24:96]
        hst[h][72:168, :] = hp_ref[at, 0:128].T[0:96]
        hst[h][168:240, :] = below.T[0:72]
        w[h][...] = hp_ref[at, 128:256].T
    basis = jnp.concatenate([w0[81:113, :], w1[81:113, :]], axis=1).astype(bf16)
    response = jnp.concatenate([w0[113:121, :], w1[113:121, :]], axis=1).astype(bf16)
    combined = lax.dot_general(response, basis, (((1,), (1,)), ((), ())), preferred_element_type=f32).astype(bf16)
    lane = lax.broadcasted_iota(jnp.int32, (1, LANES), 1)
    group = lane % 32
    column = 64 * b - 16 + 4 * group + lane // 32
    in_columns = (column >= 0) & (column < 1024) & (group >= 2) & (group < 22)

    def mix(row, value, rows):
        mixed = lax.dot_general(value.astype(bf16), basis, (((0,), (0,)), ((), ())), preferred_element_type=f32)
        mixed = rounded(mixed)
        at = pl.ds(pl.multiple_of(row * LANES, LANES), rows * LANES)
        for h in range(2):
            m[h][at, :] = mixed[:, h * 128 : h * 128 + 128]

    def ms_gradient(row, block):
        predicted = jnp.dot(combined, block.astype(bf16), preferred_element_type=f32)
        seen = jnp.concatenate([ms_ref[pl.ds(row - 8 + r, 8, stride=MROWS), :] for r in range(8)], axis=1)
        misfit = (seen - predicted).astype(bf16)
        grad = lax.dot_general(combined, misfit, (((0,), (0,)), ((), ())), preferred_element_type=f32)
        for r in range(8):
            g_ref[pl.ds((row - 8 + r) * 32, 32), :] = grad[:, r * 128 : r * 128 + 128]

    def blur_row(n):
        g = lax.broadcasted_iota(jnp.int32, (JCOLS, LANES), 0)
        i_at = 4 * s + n - 3
        j_at = 16 * b + g - 3
        inside = (i_at >= 0) & (i_at < ROWS_LO) & (j_at >= 0) & (j_at < COLS_LO)
        for h in range(2):
            acc = [None, None, None]
            for a in range(TAPS):
                for q in range(4):
                    at = pl.multiple_of((4 * n + a) * LANES + 32 * q, 32)
                    x = m[h][pl.ds(at, JCOLS), :]
                    for d in range(3):
                        if 4 * d + q > 8:
                            continue
                        tap = a * 9 + 4 * d + q
                        term = w[h][tap : tap + 1, :] * x
                        acc[d] = term if acc[d] is None else acc[d] + term
            blurred = acc[0] + pltpu.roll(acc[1], JCOLS - 1, 0) + pltpu.roll(acc[2], JCOLS - 2, 0)
            seen = hst[h][pl.ds(pl.multiple_of(n * JCOLS, 8), JCOLS), :]
            f[h][pl.ds(pl.multiple_of(8 + n * JCOLS, 8), JCOLS), :] = jnp.where(inside, seen - blurred, 0.0)

    def back_rows(u):
        for h in range(2):
            win = [[f[h][pl.ds(8 + (u - t) * JCOLS - tt, JCOLS), :] for tt in range(3)] for t in range(3)]
            for p in range(4):
                for q in range(4):
                    total = None
                    for t in range(3):
                        for tt in range(3):
                            if p + 4 * t > 8 or q + 4 * tt > 8:
                                continue
                            tap = (p + 4 * t) * 9 + q + 4 * tt
                            term = w[h][tap : tap + 1, :] * win[t][tt]
                            total = term if total is None else total + term
                    at = pl.multiple_of((4 * u - 8 + p) * LANES + 32 * q, 32)
                    bk[h][pl.ds(at, JCOLS), :] = rounded(total)

    def hs_gradient(row, rows):
        at = pl.ds((row - 8) * LANES, rows * LANES)
        back = jnp.concatenate([b0[at, :].astype(bf16), b1[at, :].astype(bf16)], axis=1)
        return lax.dot_general(basis, back, (((1,), (1,)), ((), ())), preferred_element_type=f32)

    def start_row(row):
        return c_ref[pl.ds(row, 32, stride=CROWS), :]

    def loop(low, high, body):
        def step(n, _):
            body(n)
            return 0

        lax.fori_loop(low, high, step, 0)

    for block in range(CROWS // 8):
        value = jnp.concatenate([start_row(block * 8 + r) for r in range(8)], axis=1)
        mix(block * 8, value, 8)
        if 1 <= block < 5:
            ms_gradient(block * 8, value)
    loop(0, IROWS, blur_row)
    loop(2, 10, back_rows)
    for block in range(1, 5):
        grad = hs_gradient(block * 8, 8)
        values = []
        for r in range(8):
            row = block * 8 + r
            now = start_row(row)
            new = now + STEP * (grad[:, r * 128 : r * 128 + 128] + g_ref[pl.ds((row - 8) * 32, 32), :])
            row_at = 16 * s - 16 + row
            new = jnp.where(in_columns & (row_at >= 0) & (row_at < 128), new, 0.0)
            c1_ref[pl.ds((row - 8) * 32, 32), :] = new
            values.append(new)
        value = jnp.concatenate(values, axis=1)
        mix(block * 8, value, 8)
        if 2 <= block < 4:
            ms_gradient(block * 8, value)
    loop(2, 8, blur_row)
    loop(4, 8, back_rows)
    place_at = lax.broadcasted_iota(jnp.int32, (LANES, LANES), 1)
    take = lax.broadcasted_iota(jnp.int32, (LANES, LANES), 0)
    shift = 4 * (take % 32) + take // 32 - 16
    order = [(place_at == shift + 64 * ((half + b) % 2)) & (shift >= 0) & (shift < 64) for half in range(2)]
    order = [jnp.where(o, 1.0, 0.0).astype(bf16) for o in order]
    grads = [hs_gradient(16, 8), hs_gradient(24, 8)]
    for r in range(8):
        total = None
        for half in range(2):
            row = 8 + r + 8 * half
            at = pl.ds(row * 32, 32)
            value = STEP * (grads[half][:, r * 128 : r * 128 + 128] + g_ref[at, :])
            value = value + (c1_ref[at, :] - start_row(row + 8))
            rest = jnp.where((group >= 4) & (group < 20), value, 0.0)
            for _ in range(3):
                piece = rest.astype(bf16)
                rest = rest - piece.astype(f32)
                moved = jnp.dot(piece, order[half], preferred_element_type=f32)
                total = moved if total is None else total + moved
        out_ref[pl.ds(r, 32, stride=8), :] = total


def refine(pos, mine, other, hp, seen, cross):
    vmem = pl.BlockSpec(memory_space=pltpu.VMEM)
    return pl.pallas_call(
        refine_kernel,
        out_shape=jax.ShapeDtypeStruct((32 * 8, LANES), f32),
        in_specs=[pl.BlockSpec(memory_space=pltpu.SMEM)] + [vmem] * 5,
        out_specs=vmem,
        scratch_shapes=[
            pltpu.VMEM((32 * CROWS, LANES), f32),
            pltpu.VMEM((8 * MROWS, LANES), f32),
            pltpu.VMEM((CROWS * LANES, LANES), f32),
            pltpu.VMEM((CROWS * LANES, LANES), f32),
            pltpu.VMEM((256, LANES), f32),
            pltpu.VMEM((256, LANES), f32),
            pltpu.VMEM((MROWS * LANES, LANES), f32),
            pltpu.VMEM((MROWS * LANES, LANES), f32),
            pltpu.VMEM((MROWS * 32, LANES), f32),
            pltpu.VMEM((MROWS * 32, LANES), f32),
            pltpu.VMEM((256, LANES), f32),
            pltpu.VMEM((256, LANES), f32),
            pltpu.VMEM((LANES, LANES), f32),
            pltpu.VMEM((LANES, LANES), f32),
        ],
        compiler_params=pltpu.CompilerParams(vmem_limit_bytes=40 * 2**20),
        cost_estimate=pl.CostEstimate(flops=400_000_000, bytes_accessed=2_000_000, transcendentals=0),
        name="refine",
    )(pos, mine, other, hp, seen, cross)


def spread(hs_ref, k_ref, basis_ref, response_ref, sent_ref):
    lane = lax.broadcasted_iota(jnp.int32, (1, LANES), 1)
    hs = hs_ref[...].astype(f32)
    rows = [jnp.concatenate([hs[:, i, :], jnp.zeros((2, 256), f32)], axis=0) for i in range(4)]
    sent_ref[0, :, 128:256] = jnp.zeros((16, 128), f32)
    for a in range(9):
        sent_ref[0, 0:14, 128 + 9 * a : 137 + 9 * a] = k_ref[a]
    sent_ref[0, 0:14, 209:241] = basis_ref[...].astype(f32)
    sent_ref[0, 0:14, 241:249] = response_ref[...].astype(f32).T
    params = sent_ref[0, :, 128:256]
    for t in range(16):
        total = jnp.zeros((16, LANES), f32)
        for i in range(4):
            moved = pltpu.roll(rows[i], (24 * i + 3 - 16 * t) % 256, 1)[:, 0:128]
            total = jnp.where((lane >= 24 * i) & (lane < 24 * i + 24), moved, total)
        sent_ref[t, :, 0:128] = total
        if t:
            sent_ref[t, :, 128:256] = params


def pack_kernel(pos_ref, ca_ref, cb_ref, ma_ref, mb_ref, hs_ref, k_ref, basis_ref, response_ref, *rest_refs):
    spread(hs_ref, k_ref, basis_ref, response_ref, rest_refs[4])
    wide_ref = rest_refs[5]
    s = pos_ref[0] // 16
    b = pos_ref[0] % 16
    off = jnp.where(b % 2 == 0, 112, 48)
    lane = lax.broadcasted_iota(jnp.int32, (1, LANES), 1)
    first = lane >= off
    block = (b + 1) // 2 - jnp.where(first, 1, 0)
    keep = (block >= 0) & (block < 8)
    source = lax.broadcasted_iota(jnp.int32, (LANES, LANES), 0)
    target = lax.broadcasted_iota(jnp.int32, (LANES, LANES), 1)
    order = jnp.where(source == (4 * (target % 32) + target // 32 + off) % LANES, 1.0, 0.0).astype(bf16)
    ms = jnp.where(first, ma_ref[...].reshape(128, LANES).astype(f32), mb_ref[...].reshape(128, LANES).astype(f32))
    ms = jnp.where(keep, ms, 0.0).astype(bf16)
    ms = jnp.dot(ms, order, preferred_element_type=f32)
    rest_refs[0][256:384] = ms
    edge = jnp.zeros((16, LANES), f32)
    for k in range(4):
        rest = jnp.where(keep, jnp.where(first, ca_ref[k], cb_ref[k]), 0.0)
        total = None
        for _ in range(3):
            piece = rest.astype(bf16)
            rest = rest - piece.astype(f32)
            moved = jnp.dot(piece, order, preferred_element_type=f32)
            total = moved if total is None else total + moved
        wide_ref[k, 0:16] = edge
        wide_ref[k, 16:144] = total
        wide_ref[k, 144:160] = edge
    for d in range(4):
        at = pl.ds(pl.multiple_of(32 * ((s // 2 + d) % 4), 32), 64)
        for k in range(4):
            rest_refs[d][64 * k : 64 * k + 64] = wide_ref[k, at, :]


def pack(pos, coeffs_in, ms_image, hs_image, kernels, basis, response):
    def low(i, p):
        return (0, 0, jnp.maximum((p[0] % 16 + 1) // 2 - 1, 0))

    def high(i, p):
        return (0, 0, jnp.minimum((p[0] % 16 + 1) // 2, 7))

    return pl.pallas_call(
        pack_kernel,
        out_shape=(jax.ShapeDtypeStruct((384, LANES), f32),)
        + (jax.ShapeDtypeStruct((256, LANES), f32),) * 3
        + (jax.ShapeDtypeStruct((16, 16, 256), f32),),
        grid_spec=pltpu.PrefetchScalarGridSpec(
            num_scalar_prefetch=1,
            grid=(1,),
            in_specs=[
                pl.BlockSpec((4, 128, LANES), low),
                pl.BlockSpec((4, 128, LANES), high),
                pl.BlockSpec((8, 16, LANES), low),
                pl.BlockSpec((8, 16, LANES), high),
                pl.BlockSpec((14, 4, 256), lambda i, p: (0, 0, 0)),
                pl.BlockSpec((9, 14, 9), lambda i, p: (0, 0, 0)),
                pl.BlockSpec((14, 32), lambda i, p: (0, 0)),
                pl.BlockSpec((8, 14), lambda i, p: (0, 0)),
            ],
            out_specs=(pl.BlockSpec((384, LANES), lambda i, p: (0, 0)),)
            + (pl.BlockSpec((256, LANES), lambda i, p: (0, 0)),) * 3
            + (pl.BlockSpec((16, 16, 256), lambda i, p: (0, 0, 0)),),
            scratch_shapes=[pltpu.VMEM((4, 160, LANES), f32)],
        ),
        compiler_params=pltpu.CompilerParams(vmem_limit_bytes=60 * 2**20),
        cost_estimate=pl.CostEstimate(flops=100_000_000, bytes_accessed=1_600_000, transcendentals=0),
        name="pack",
    )(pos, coeffs_in, coeffs_in, ms_image, ms_image, hs_image, kernels, basis, response)


def hold_kernel(region_ref, out_ref, near_ref):
    out_ref[...] = region_ref[0:256]
    near_ref[...] = region_ref[256:384].astype(bf16)


def hold(region):
    vmem = pl.BlockSpec(memory_space=pltpu.VMEM)
    return pl.pallas_call(
        hold_kernel,
        out_shape=(jax.ShapeDtypeStruct((256, LANES), f32), jax.ShapeDtypeStruct((128, LANES), bf16)),
        in_specs=[vmem],
        out_specs=(vmem, vmem),
        compiler_params=pltpu.CompilerParams(vmem_limit_bytes=16 * 2**20),
        name="hold",
    )(region)


def join_kernel(hp_ref, near_ref, seen_ref):
    seen_ref[0:256] = hp_ref[:, 0:128].astype(bf16)
    seen_ref[256:384] = near_ref[...]


def join(hp, near):
    vmem = pl.BlockSpec(memory_space=pltpu.VMEM)
    return pl.pallas_call(
        join_kernel,
        out_shape=jax.ShapeDtypeStruct((384, LANES), bf16),
        in_specs=[vmem] * 2,
        out_specs=vmem,
        compiler_params=pltpu.CompilerParams(vmem_limit_bytes=16 * 2**20),
        name="join",
    )(hp, near)


def hand_kernel(pos_ref, r0, r1, r2, r3, seen_ref, mine_ref, other_ref):
    other_ref[16 * CROWS : 16 * CROWS + 384] = seen_ref[...].astype(f32)
    skip = 16 * (pos_ref[0] // 16 % 2)
    for d, region in enumerate((r0, r1, r2, r3)):
        for k in range(4):
            at = CROWS * (4 * d + k)
            mine_ref[at : at + CROWS] = region[pl.ds(pl.multiple_of(64 * k + skip, 16), CROWS), :]
            other_ref[at : at + CROWS] = region[pl.ds(pl.multiple_of(64 * k + 16 - skip, 16), CROWS), :]


def hand(pos, tiles, seen):
    vmem = pl.BlockSpec(memory_space=pltpu.VMEM)
    return pl.pallas_call(
        hand_kernel,
        out_shape=(
            jax.ShapeDtypeStruct((16 * CROWS, LANES), f32),
            jax.ShapeDtypeStruct((16 * CROWS + 384, LANES), f32),
        ),
        in_specs=[pl.BlockSpec(memory_space=pltpu.SMEM)] + [vmem] * 5,
        out_specs=(vmem, vmem),
        compiler_params=pltpu.CompilerParams(vmem_limit_bytes=16 * 2**20),
        cost_estimate=pl.CostEstimate(flops=1_000_000, bytes_accessed=800_000, transcendentals=0),
        name="hand",
    )(pos, *tiles, seen)


def encode_kernel(d_ref, out_ref):
    scales = []
    codes = []
    for k in range(4):
        part = d_ref[:, k]
        size = jnp.abs(part)
        top = jnp.max(size, axis=(0, 1, 2), keepdims=True)
        scale = rounded(jnp.maximum(top * (1 + 2**-7), 1e-30))
        code = jnp.exp2(size * (SPAN / scale) - SPAN / 2)
        codes.append(jnp.where(part < 0, -code, code))
        scales.append(jnp.broadcast_to(scale[0], (1, LANES)))
    scales = jnp.concatenate(scales + [jnp.zeros((12, LANES), f32)], axis=0).astype(bf16)
    for s in range(8):
        row = jnp.concatenate([codes[k][s] for k in range(4)], axis=0).astype(bf16)
        for t in range(16):
            out_ref[t, 32 * s : 32 * s + 32] = row
    for t in range(16):
        out_ref[t, 256:272] = scales


def encode(owned):
    vmem = pl.BlockSpec(memory_space=pltpu.VMEM)
    return pl.pallas_call(
        encode_kernel,
        out_shape=jax.ShapeDtypeStruct((16, 272, LANES), bf16),
        in_specs=[vmem],
        out_specs=vmem,
        compiler_params=pltpu.CompilerParams(vmem_limit_bytes=16 * 2**20),
        name="encode",
    )(owned)


def place_kernel(g_ref, c_ref, out_ref):
    lane = lax.broadcasted_iota(jnp.int32, (1, LANES), 1)
    low = lane < 64
    count = g_ref.shape[0] // 2
    for j in range(count):
        even, odd = [g_ref[2 * j + e, 256:272].astype(f32) * (1 / SPAN) for e in range(2)]
        scales = (jnp.where(low, even, odd), jnp.where(low, odd, even))
        columns = slice(j * LANES, j * LANES + LANES)
        for s in range(8):
            even, odd = [g_ref[2 * j + e, 32 * s : 32 * s + 32].astype(f32) for e in range(2)]
            for half, code in enumerate((jnp.where(low, even, odd), jnp.where(low, odd, even))):
                size = jnp.log2(jnp.abs(code)) + SPAN / 2
                value = jnp.where(code < 0, -size, size)
                for k in range(4):
                    part = value[8 * k : 8 * k + 8] * scales[half][k : k + 1]
                    if half:
                        part = pltpu.roll(part, 64, 1)
                    at = slice(16 * s + 8 * half, 16 * s + 8 * half + 8)
                    out_ref[k, at, columns] = c_ref[k, at, columns] + part


def place(gathered, coeffs_in):
    block = pl.BlockSpec((4, 128, 4 * LANES), lambda j: (0, 0, j))
    return pl.pallas_call(
        place_kernel,
        out_shape=jax.ShapeDtypeStruct((4, 128, 1024), f32),
        grid=(2,),
        in_specs=[pl.BlockSpec((8, 272, LANES), lambda j: (j, 0, 0)), block],
        out_specs=block,
        compiler_params=pltpu.CompilerParams(vmem_limit_bytes=32 * 2**20),
        name="place",
    )(gathered, coeffs_in)


def per_device(coeffs_in, basis, kernels, response, hs_image, ms_image):
    pos = (lax.axis_index("sub") * 16 + lax.axis_index("band")).astype(jnp.int32).reshape(1)
    *tiles, sent = pack(pos, coeffs_in, ms_image, hs_image, kernels.transpose(1, 0, 2), basis, response)
    hp = lax.all_to_all(sent, "band", split_axis=0, concat_axis=0, tiled=True).reshape(256, 256)
    tiles = [tiles[0]] + [
        lax.ppermute(tiles[d], "sub", [(i, (i + 2 * d) % 8) for i in range(8)]) for d in range(1, 4)
    ]
    tiles[0], near = hold(tiles[0])
    seen = join(hp, near)
    cross = lax.ppermute(seen, "sub", [(1, 2), (2, 1), (3, 4), (4, 3), (5, 6), (6, 5)])
    cross, *tiles = lax.optimization_barrier((cross, *tiles))
    mine, other = hand(pos, tiles, seen)
    other = lax.ppermute(other, "sub", [(i, i ^ 1) for i in range(8)])
    new = refine(pos, mine, other, hp, seen, cross)
    owned = lax.all_to_all(new.reshape(8, 4, 8, LANES), "sub", split_axis=0, concat_axis=0, tiled=True)
    gathered = lax.all_to_all(encode(owned), "band", split_axis=0, concat_axis=0, tiled=True)
    return place(gathered, coeffs_in)


def solution(mesh):
    return jax.shard_map(
        per_device,
        mesh=mesh,
        in_specs=(
            P("sub", None, None),
            P("band", None),
            P("band", None, None),
            P(None, "band"),
            P("band", "sub", None),
            P(None, "sub", None),
        ),
        out_specs=P("sub", None, None),
        check_vma=False,
    )
```

```python
import functools

import jax
import jax.numpy as jnp
from jax import lax
from jax.experimental import pallas as pl
from jax.experimental.pallas import tpu as pltpu
from jax.sharding import PartitionSpec as P

STEP = 0.15
TR, TC = 16, 64
TAPS = 9
SPAN = 250.0
LANES = 128
CROWS = 48
MROWS = 32
IROWS = 10
JCOLS = 24
ROWS_LO, COLS_LO = 32, 256
f32 = jnp.float32
bf16 = jnp.bfloat16


def rounded(value):
    return value.astype(bf16).astype(f32)


def refine_kernel(pos_ref, *refs):
    mine_ref, other_ref, hp_ref, seen_ref, cross_ref, out_ref, c_ref, ms_ref, m0, m1, f0, f1, b0, b1, c1_ref, g_ref, hs0, hs1, w0, w1 = refs
    s = pos_ref[0] // 16
    b = pos_ref[0] % 16
    core = s % 2
    for d in range(4):
        chip = (s // 2 + 4 - d) % 4
        mine = pl.multiple_of((2 * chip + core) * (4 * CROWS), 4 * CROWS)
        theirs = pl.multiple_of((2 * chip + 1 - core) * (4 * CROWS), 4 * CROWS)
        c_ref[pl.ds(mine, 4 * CROWS), :] = mine_ref[d * 4 * CROWS : (d + 1) * 4 * CROWS]
        c_ref[pl.ds(theirs, 4 * CROWS), :] = other_ref[d * 4 * CROWS : (d + 1) * 4 * CROWS]

    def neighbours(low, high):
        theirs = other_ref[16 * CROWS + low : 16 * CROWS + high]
        across = cross_ref[low:high].astype(f32)
        flag = jnp.zeros((high - low, LANES), jnp.int32) + core
        return jnp.where(flag == 0, across, theirs), jnp.where(flag == 0, theirs, across)

    ms_above, ms_below = neighbours(256, 384)
    for k in range(8):
        ms_ref[32 * k : 32 * k + 8, :] = ms_above[16 * k + 8 : 16 * k + 16]
        ms_ref[32 * k + 8 : 32 * k + 24, :] = seen_ref[256 + 16 * k : 272 + 16 * k].astype(f32)
        ms_ref[32 * k + 24 : 32 * k + 32, :] = ms_below[16 * k : 16 * k + 8]
    bk = (b0, b1)
    m = (m0, m1)
    f = (f0, f1)
    hst = (hs0, hs1)
    w = (w0, w1)
    for h in range(2):
        at = slice(h * 128, h * 128 + 128)
        above, below = neighbours(h * 128, h * 128 + 128)
        hst[h][0:72, :] = above.T[24:96]
        hst[h][72:168, :] = hp_ref[at, 0:128].T[0:96]
        hst[h][168:240, :] = below.T[0:72]
        w[h][...] = hp_ref[at, 128:256].T
    basis = jnp.concatenate([w0[81:113, :], w1[81:113, :]], axis=1).astype(bf16)
    response = jnp.concatenate([w0[113:121, :], w1[113:121, :]], axis=1).astype(bf16)
    combined = lax.dot_general(response, basis, (((1,), (1,)), ((), ())), preferred_element_type=f32).astype(bf16)
    lane = lax.broadcasted_iota(jnp.int32, (1, LANES), 1)
    group = lane % 32
    column = 64 * b - 16 + 4 * group + lane // 32
    in_columns = (column >= 0) & (column < 1024) & (group >= 2) & (group < 22)

    def mix(row, value, rows):
        mixed = lax.dot_general(value.astype(bf16), basis, (((0,), (0,)), ((), ())), preferred_element_type=f32)
        mixed = rounded(mixed)
        at = pl.ds(pl.multiple_of(row * LANES, LANES), rows * LANES)
        for h in range(2):
            m[h][at, :] = mixed[:, h * 128 : h * 128 + 128]

    def ms_gradient(row, block):
        predicted = jnp.dot(combined, block.astype(bf16), preferred_element_type=f32)
        seen = jnp.concatenate([ms_ref[pl.ds(row - 8 + r, 8, stride=MROWS), :] for r in range(8)], axis=1)
        misfit = (seen - predicted).astype(bf16)
        grad = lax.dot_general(combined, misfit, (((0,), (0,)), ((), ())), preferred_element_type=f32)
        for r in range(8):
            g_ref[pl.ds((row - 8 + r) * 32, 32), :] = grad[:, r * 128 : r * 128 + 128]

    def blur_row(n):
        g = lax.broadcasted_iota(jnp.int32, (JCOLS, LANES), 0)
        i_at = 4 * s + n - 3
        j_at = 16 * b + g - 3
        inside = (i_at >= 0) & (i_at < ROWS_LO) & (j_at >= 0) & (j_at < COLS_LO)
        for h in range(2):
            acc = [None, None, None]
            for a in range(TAPS):
                for q in range(4):
                    at = pl.multiple_of((4 * n + a) * LANES + 32 * q, 32)
                    x = m[h][pl.ds(at, JCOLS), :]
                    for d in range(3):
                        if 4 * d + q > 8:
                            continue
                        tap = a * 9 + 4 * d + q
                        term = w[h][tap : tap + 1, :] * x
                        acc[d] = term if acc[d] is None else acc[d] + term
            blurred = acc[0] + pltpu.roll(acc[1], JCOLS - 1, 0) + pltpu.roll(acc[2], JCOLS - 2, 0)
            seen = hst[h][pl.ds(pl.multiple_of(n * JCOLS, 8), JCOLS), :]
            f[h][pl.ds(pl.multiple_of(8 + n * JCOLS, 8), JCOLS), :] = jnp.where(inside, seen - blurred, 0.0)

    def back_rows(u, first=0, count=JCOLS, phases=4):
        for h in range(2):
            win = [[f[h][pl.ds(8 + (u - t) * JCOLS + first - tt, count), :] for tt in range(3)] for t in range(3)]
            for p in range(phases):
                for q in range(4):
                    total = None
                    for t in range(3):
                        for tt in range(3):
                            if p + 4 * t > 8 or q + 4 * tt > 8:
                                continue
                            tap = (p + 4 * t) * 9 + q + 4 * tt
                            term = w[h][tap : tap + 1, :] * win[t][tt]
                            total = term if total is None else total + term
                    at = (4 * u - 8 + p) * LANES + 32 * q + first
                    bk[h][pl.ds(at, count), :] = rounded(total)

    def hs_gradient(row, rows):
        at = pl.ds((row - 8) * LANES, rows * LANES)
        back = jnp.concatenate([b0[at, :].astype(bf16), b1[at, :].astype(bf16)], axis=1)
        return lax.dot_general(basis, back, (((1,), (1,)), ((), ())), preferred_element_type=f32)

    def start_row(row):
        return c_ref[pl.ds(row, 32, stride=CROWS), :]

    def loop(low, high, body):
        def step(n, _):
            body(n)
            return 0

        lax.fori_loop(low, high, step, 0)

    for block in range(CROWS // 8):
        value = jnp.concatenate([start_row(block * 8 + r) for r in range(8)], axis=1)
        mix(block * 8, value, 8)
        if 1 <= block < 5:
            ms_gradient(block * 8, value)
    loop(0, IROWS, blur_row)
    loop(2, 9, back_rows)
    back_rows(9, phases=1)
    for block in range(1, 5):
        grad = hs_gradient(block * 8, 8)
        values = []
        for r in range(8):
            row = block * 8 + r
            now = start_row(row)
            new = now + STEP * (grad[:, r * 128 : r * 128 + 128] + g_ref[pl.ds((row - 8) * 32, 32), :])
            row_at = 16 * s - 16 + row
            new = jnp.where(in_columns & (row_at >= 0) & (row_at < 128), new, 0.0)
            c1_ref[pl.ds((row - 8) * 32, 32), :] = new
            values.append(new)
        value = jnp.concatenate(values, axis=1)
        mix(block * 8, value, 8)
        if 2 <= block < 4:
            ms_gradient(block * 8, value)
    loop(2, 8, blur_row)
    loop(4, 8, lambda u: back_rows(u, 4, 16))
    place_at = lax.broadcasted_iota(jnp.int32, (LANES, LANES), 1)
    take = lax.broadcasted_iota(jnp.int32, (LANES, LANES), 0)
    shift = 4 * (take % 32) + take // 32 - 16
    order = [(place_at == shift + 64 * ((half + b) % 2)) & (shift >= 0) & (shift < 64) for half in range(2)]
    order = [jnp.where(o, 1.0, 0.0).astype(bf16) for o in order]
    grads = [hs_gradient(16, 8), hs_gradient(24, 8)]
    for r in range(8):
        total = None
        for half in range(2):
            row = 8 + r + 8 * half
            at = pl.ds(row * 32, 32)
            value = STEP * (grads[half][:, r * 128 : r * 128 + 128] + g_ref[at, :])
            value = value + (c1_ref[at, :] - start_row(row + 8))
            rest = jnp.where((group >= 4) & (group < 20), value, 0.0)
            for _ in range(3):
                piece = rest.astype(bf16)
                rest = rest - piece.astype(f32)
                moved = jnp.dot(piece, order[half], preferred_element_type=f32)
                total = moved if total is None else total + moved
        out_ref[pl.ds(r, 32, stride=8), :] = total


def refine(pos, mine, other, hp, seen, cross):
    vmem = pl.BlockSpec(memory_space=pltpu.VMEM)
    return pl.pallas_call(
        refine_kernel,
        out_shape=jax.ShapeDtypeStruct((32 * 8, LANES), f32),
        in_specs=[pl.BlockSpec(memory_space=pltpu.SMEM)] + [vmem] * 5,
        out_specs=vmem,
        scratch_shapes=[
            pltpu.VMEM((32 * CROWS, LANES), f32),
            pltpu.VMEM((8 * MROWS, LANES), f32),
            pltpu.VMEM((CROWS * LANES, LANES), f32),
            pltpu.VMEM((CROWS * LANES, LANES), f32),
            pltpu.VMEM((256, LANES), f32),
            pltpu.VMEM((256, LANES), f32),
            pltpu.VMEM((MROWS * LANES, LANES), f32),
            pltpu.VMEM((MROWS * LANES, LANES), f32),
            pltpu.VMEM((MROWS * 32, LANES), f32),
            pltpu.VMEM((MROWS * 32, LANES), f32),
            pltpu.VMEM((256, LANES), f32),
            pltpu.VMEM((256, LANES), f32),
            pltpu.VMEM((LANES, LANES), f32),
            pltpu.VMEM((LANES, LANES), f32),
        ],
        compiler_params=pltpu.CompilerParams(vmem_limit_bytes=40 * 2**20),
        cost_estimate=pl.CostEstimate(flops=400_000_000, bytes_accessed=2_000_000, transcendentals=0),
        name="refine",
    )(pos, mine, other, hp, seen, cross)


def spread(hs_ref, k_ref, basis_ref, response_ref, sent_ref):
    lane = lax.broadcasted_iota(jnp.int32, (1, LANES), 1)
    hs = hs_ref[...].astype(f32)
    rows = [jnp.concatenate([hs[:, i, :], jnp.zeros((2, 256), f32)], axis=0) for i in range(4)]
    sent_ref[0, :, 128:256] = jnp.zeros((16, 128), f32)
    for a in range(9):
        sent_ref[0, 0:14, 128 + 9 * a : 137 + 9 * a] = k_ref[a]
    sent_ref[0, 0:14, 209:241] = basis_ref[...].astype(f32)
    sent_ref[0, 0:14, 241:249] = response_ref[...].astype(f32).T
    params = sent_ref[0, :, 128:256]
    for t in range(16):
        total = jnp.zeros((16, LANES), f32)
        for i in range(4):
            moved = pltpu.roll(rows[i], (24 * i + 3 - 16 * t) % 256, 1)[:, 0:128]
            total = jnp.where((lane >= 24 * i) & (lane < 24 * i + 24), moved, total)
        sent_ref[t, :, 0:128] = total
        if t:
            sent_ref[t, :, 128:256] = params


def pack_kernel(pos_ref, ca_ref, cb_ref, ma_ref, mb_ref, hs_ref, k_ref, basis_ref, response_ref, *rest_refs):
    spread(hs_ref, k_ref, basis_ref, response_ref, rest_refs[4])
    wide_ref = rest_refs[5]
    s = pos_ref[0] // 16
    b = pos_ref[0] % 16
    off = jnp.where(b % 2 == 0, 112, 48)
    lane = lax.broadcasted_iota(jnp.int32, (1, LANES), 1)
    first = lane >= off
    block = (b + 1) // 2 - jnp.where(first, 1, 0)
    keep = (block >= 0) & (block < 8)
    source = lax.broadcasted_iota(jnp.int32, (LANES, LANES), 0)
    target = lax.broadcasted_iota(jnp.int32, (LANES, LANES), 1)
    order = jnp.where(source == (4 * (target % 32) + target // 32 + off) % LANES, 1.0, 0.0).astype(bf16)
    ms = jnp.where(first, ma_ref[...].reshape(128, LANES).astype(f32), mb_ref[...].reshape(128, LANES).astype(f32))
    ms = jnp.where(keep, ms, 0.0).astype(bf16)
    ms = jnp.dot(ms, order, preferred_element_type=f32)
    rest_refs[0][256:384] = ms
    edge = jnp.zeros((16, LANES), f32)
    for k in range(4):
        rest = jnp.where(keep, jnp.where(first, ca_ref[k], cb_ref[k]), 0.0)
        total = None
        for _ in range(3):
            piece = rest.astype(bf16)
            rest = rest - piece.astype(f32)
            moved = jnp.dot(piece, order, preferred_element_type=f32)
            total = moved if total is None else total + moved
        wide_ref[k, 0:16] = edge
        wide_ref[k, 16:144] = total
        wide_ref[k, 144:160] = edge
    for d in range(4):
        at = pl.ds(pl.multiple_of(32 * ((s // 2 + d) % 4), 32), 64)
        for k in range(4):
            rest_refs[d][64 * k : 64 * k + 64] = wide_ref[k, at, :]


def pack(pos, coeffs_in, ms_image, hs_image, kernels, basis, response):
    def low(i, p):
        return (0, 0, jnp.maximum((p[0] % 16 + 1) // 2 - 1, 0))

    def high(i, p):
        return (0, 0, jnp.minimum((p[0] % 16 + 1) // 2, 7))

    return pl.pallas_call(
        pack_kernel,
        out_shape=(jax.ShapeDtypeStruct((384, LANES), f32),)
        + (jax.ShapeDtypeStruct((256, LANES), f32),) * 3
        + (jax.ShapeDtypeStruct((16, 16, 256), f32),),
        grid_spec=pltpu.PrefetchScalarGridSpec(
            num_scalar_prefetch=1,
            grid=(1,),
            in_specs=[
                pl.BlockSpec((4, 128, LANES), low),
                pl.BlockSpec((4, 128, LANES), high),
                pl.BlockSpec((8, 16, LANES), low),
                pl.BlockSpec((8, 16, LANES), high),
                pl.BlockSpec((14, 4, 256), lambda i, p: (0, 0, 0)),
                pl.BlockSpec((9, 14, 9), lambda i, p: (0, 0, 0)),
                pl.BlockSpec((14, 32), lambda i, p: (0, 0)),
                pl.BlockSpec((8, 14), lambda i, p: (0, 0)),
            ],
            out_specs=(pl.BlockSpec((384, LANES), lambda i, p: (0, 0)),)
            + (pl.BlockSpec((256, LANES), lambda i, p: (0, 0)),) * 3
            + (pl.BlockSpec((16, 16, 256), lambda i, p: (0, 0, 0)),),
            scratch_shapes=[pltpu.VMEM((4, 160, LANES), f32)],
        ),
        compiler_params=pltpu.CompilerParams(vmem_limit_bytes=60 * 2**20),
        cost_estimate=pl.CostEstimate(flops=100_000_000, bytes_accessed=1_600_000, transcendentals=0),
        name="pack",
    )(pos, coeffs_in, coeffs_in, ms_image, ms_image, hs_image, kernels, basis, response)


def hold_kernel(region_ref, out_ref, near_ref):
    out_ref[...] = region_ref[0:256]
    near_ref[...] = region_ref[256:384].astype(bf16)


def hold(region):
    vmem = pl.BlockSpec(memory_space=pltpu.VMEM)
    return pl.pallas_call(
        hold_kernel,
        out_shape=(jax.ShapeDtypeStruct((256, LANES), f32), jax.ShapeDtypeStruct((128, LANES), bf16)),
        in_specs=[vmem],
        out_specs=(vmem, vmem),
        compiler_params=pltpu.CompilerParams(vmem_limit_bytes=16 * 2**20),
        name="hold",
    )(region)


def join_kernel(hp_ref, near_ref, seen_ref):
    seen_ref[0:256] = hp_ref[:, 0:128].astype(bf16)
    seen_ref[256:384] = near_ref[...]


def join(hp, near):
    vmem = pl.BlockSpec(memory_space=pltpu.VMEM)
    return pl.pallas_call(
        join_kernel,
        out_shape=jax.ShapeDtypeStruct((384, LANES), bf16),
        in_specs=[vmem] * 2,
        out_specs=vmem,
        compiler_params=pltpu.CompilerParams(vmem_limit_bytes=16 * 2**20),
        name="join",
    )(hp, near)


def hand_kernel(pos_ref, r0, r1, r2, r3, seen_ref, mine_ref, other_ref):
    other_ref[16 * CROWS : 16 * CROWS + 384] = seen_ref[...].astype(f32)
    skip = 16 * (pos_ref[0] // 16 % 2)
    for d, region in enumerate((r0, r1, r2, r3)):
        for k in range(4):
            at = CROWS * (4 * d + k)
            mine_ref[at : at + CROWS] = region[pl.ds(pl.multiple_of(64 * k + skip, 16), CROWS), :]
            other_ref[at : at + CROWS] = region[pl.ds(pl.multiple_of(64 * k + 16 - skip, 16), CROWS), :]


def hand(pos, tiles, seen):
    vmem = pl.BlockSpec(memory_space=pltpu.VMEM)
    return pl.pallas_call(
        hand_kernel,
        out_shape=(
            jax.ShapeDtypeStruct((16 * CROWS, LANES), f32),
            jax.ShapeDtypeStruct((16 * CROWS + 384, LANES), f32),
        ),
        in_specs=[pl.BlockSpec(memory_space=pltpu.SMEM)] + [vmem] * 5,
        out_specs=(vmem, vmem),
        compiler_params=pltpu.CompilerParams(vmem_limit_bytes=16 * 2**20),
        cost_estimate=pl.CostEstimate(flops=1_000_000, bytes_accessed=800_000, transcendentals=0),
        name="hand",
    )(pos, *tiles, seen)


def encode_kernel(d_ref, out_ref):
    scales = []
    codes = []
    for k in range(4):
        part = d_ref[:, k]
        size = jnp.abs(part)
        top = jnp.max(size, axis=(0, 1, 2), keepdims=True)
        scale = rounded(jnp.maximum(top * (1 + 2**-7), 1e-30))
        code = jnp.exp2(size * (SPAN / scale) - SPAN / 2)
        codes.append(jnp.where(part < 0, -code, code))
        scales.append(jnp.broadcast_to(scale[0], (1, LANES)))
    scales = jnp.concatenate(scales + [jnp.zeros((12, LANES), f32)], axis=0).astype(bf16)
    for s in range(8):
        row = jnp.concatenate([codes[k][s] for k in range(4)], axis=0).astype(bf16)
        for t in range(16):
            out_ref[t, 32 * s : 32 * s + 32] = row
    for t in range(16):
        out_ref[t, 256:272] = scales


def encode(owned):
    vmem = pl.BlockSpec(memory_space=pltpu.VMEM)
    return pl.pallas_call(
        encode_kernel,
        out_shape=jax.ShapeDtypeStruct((16, 272, LANES), bf16),
        in_specs=[vmem],
        out_specs=vmem,
        compiler_params=pltpu.CompilerParams(vmem_limit_bytes=16 * 2**20),
        name="encode",
    )(owned)


def place_kernel(g_ref, c_ref, out_ref):
    lane = lax.broadcasted_iota(jnp.int32, (1, LANES), 1)
    low = lane < 64
    count = g_ref.shape[0] // 2
    for j in range(count):
        even, odd = [g_ref[2 * j + e, 256:272].astype(f32) * (1 / SPAN) for e in range(2)]
        scales = (jnp.where(low, even, odd), jnp.where(low, odd, even))
        columns = slice(j * LANES, j * LANES + LANES)
        for s in range(8):
            even, odd = [g_ref[2 * j + e, 32 * s : 32 * s + 32].astype(f32) for e in range(2)]
            for half, code in enumerate((jnp.where(low, even, odd), jnp.where(low, odd, even))):
                size = jnp.log2(jnp.abs(code)) + SPAN / 2
                value = jnp.where(code < 0, -size, size)
                for k in range(4):
                    part = value[8 * k : 8 * k + 8] * scales[half][k : k + 1]
                    if half:
                        part = pltpu.roll(part, 64, 1)
                    at = slice(16 * s + 8 * half, 16 * s + 8 * half + 8)
                    out_ref[k, at, columns] = c_ref[k, at, columns] + part


def place(gathered, coeffs_in):
    block = pl.BlockSpec((4, 128, 4 * LANES), lambda j: (0, 0, j))
    return pl.pallas_call(
        place_kernel,
        out_shape=jax.ShapeDtypeStruct((4, 128, 1024), f32),
        grid=(2,),
        in_specs=[pl.BlockSpec((8, 272, LANES), lambda j: (j, 0, 0)), block],
        out_specs=block,
        compiler_params=pltpu.CompilerParams(vmem_limit_bytes=32 * 2**20),
        name="place",
    )(gathered, coeffs_in)


def per_device(coeffs_in, basis, kernels, response, hs_image, ms_image):
    pos = (lax.axis_index("sub") * 16 + lax.axis_index("band")).astype(jnp.int32).reshape(1)
    *tiles, sent = pack(pos, coeffs_in, ms_image, hs_image, kernels.transpose(1, 0, 2), basis, response)
    hp = lax.all_to_all(sent, "band", split_axis=0, concat_axis=0, tiled=True).reshape(256, 256)
    tiles = [tiles[0]] + [
        lax.ppermute(tiles[d], "sub", [(i, (i + 2 * d) % 8) for i in range(8)]) for d in range(1, 4)
    ]
    tiles[0], near = hold(tiles[0])
    seen = join(hp, near)
    cross = lax.ppermute(seen, "sub", [(1, 2), (2, 1), (3, 4), (4, 3), (5, 6), (6, 5)])
    cross, *tiles = lax.optimization_barrier((cross, *tiles))
    mine, other = hand(pos, tiles, seen)
    other = lax.ppermute(other, "sub", [(i, i ^ 1) for i in range(8)])
    new = refine(pos, mine, other, hp, seen, cross)
    owned = lax.all_to_all(new.reshape(8, 4, 8, LANES), "sub", split_axis=0, concat_axis=0, tiled=True)
    gathered = lax.all_to_all(encode(owned), "band", split_axis=0, concat_axis=0, tiled=True)
    return place(gathered, coeffs_in)


def solution(mesh):
    return jax.shard_map(
        per_device,
        mesh=mesh,
        in_specs=(
            P("sub", None, None),
            P("band", None),
            P("band", None, None),
            P(None, "band"),
            P("band", "sub", None),
            P(None, "sub", None),
        ),
        out_specs=P("sub", None, None),
        check_vma=False,
    )
```

```python
import functools

import jax
import jax.numpy as jnp
from jax import lax
from jax.experimental import pallas as pl
from jax.experimental.pallas import tpu as pltpu
from jax.sharding import PartitionSpec as P

STEP = 0.15
TR, TC = 16, 64
TAPS = 9
SPAN = 250.0
LANES = 128
CROWS = 48
MROWS = 32
IROWS = 10
JCOLS = 24
ROWS_LO, COLS_LO = 32, 256
f32 = jnp.float32
bf16 = jnp.bfloat16


def rounded(value):
    return value.astype(bf16).astype(f32)


def refine_kernel(pos_ref, *refs):
    mine_ref, other_ref, hp_ref, seen_ref, cross_ref, out_ref, c_ref, ms_ref, m0, m1, f0, f1, b0, b1, c1_ref, g_ref, hs0, hs1, w0, w1 = refs
    s = pos_ref[0] // 16
    b = pos_ref[0] % 16
    core = s % 2
    for d in range(4):
        chip = (s // 2 + 4 - d) % 4
        mine = pl.multiple_of((2 * chip + core) * (4 * CROWS), 4 * CROWS)
        theirs = pl.multiple_of((2 * chip + 1 - core) * (4 * CROWS), 4 * CROWS)
        c_ref[pl.ds(mine, 4 * CROWS), :] = mine_ref[d * 4 * CROWS : (d + 1) * 4 * CROWS]
        c_ref[pl.ds(theirs, 4 * CROWS), :] = other_ref[d * 4 * CROWS : (d + 1) * 4 * CROWS]

    def neighbours(low, high):
        theirs = other_ref[16 * CROWS + low : 16 * CROWS + high]
        across = cross_ref[low:high].astype(f32)
        flag = jnp.zeros((high - low, LANES), jnp.int32) + core
        return jnp.where(flag == 0, across, theirs), jnp.where(flag == 0, theirs, across)

    ms_above, ms_below = neighbours(256, 384)
    for k in range(8):
        ms_ref[32 * k : 32 * k + 8, :] = ms_above[16 * k + 8 : 16 * k + 16]
        ms_ref[32 * k + 8 : 32 * k + 24, :] = seen_ref[256 + 16 * k : 272 + 16 * k].astype(f32)
        ms_ref[32 * k + 24 : 32 * k + 32, :] = ms_below[16 * k : 16 * k + 8]
    bk = (b0, b1)
    m = (m0, m1)
    f = (f0, f1)
    hst = (hs0, hs1)
    w = (w0, w1)
    for h in range(2):
        at = slice(h * 128, h * 128 + 128)
        above, below = neighbours(h * 128, h * 128 + 128)
        hst[h][0:72, :] = above.T[24:96]
        hst[h][72:168, :] = hp_ref[at, 0:128].T[0:96]
        hst[h][168:240, :] = below.T[0:72]
        w[h][...] = hp_ref[at, 128:256].T
    basis = jnp.concatenate([w0[81:113, :], w1[81:113, :]], axis=1).astype(bf16)
    response = jnp.concatenate([w0[113:121, :], w1[113:121, :]], axis=1).astype(bf16)
    combined = lax.dot_general(response, basis, (((1,), (1,)), ((), ())), preferred_element_type=f32).astype(bf16)
    lane = lax.broadcasted_iota(jnp.int32, (1, LANES), 1)
    group = lane % 32
    column = 64 * b - 16 + 4 * group + lane // 32
    in_columns = (column >= 0) & (column < 1024) & (group >= 2) & (group < 22)

    def mix(row, value, rows):
        mixed = lax.dot_general(value.astype(bf16), basis, (((0,), (0,)), ((), ())), preferred_element_type=f32)
        mixed = rounded(mixed)
        at = pl.ds(pl.multiple_of(row * LANES, LANES), rows * LANES)
        for h in range(2):
            m[h][at, :] = mixed[:, h * 128 : h * 128 + 128]

    def ms_gradient(row, block):
        predicted = jnp.dot(combined, block.astype(bf16), preferred_element_type=f32)
        seen = jnp.concatenate([ms_ref[pl.ds(row - 8 + r, 8, stride=MROWS), :] for r in range(8)], axis=1)
        misfit = (seen - predicted).astype(bf16)
        grad = lax.dot_general(combined, misfit, (((0,), (0,)), ((), ())), preferred_element_type=f32)
        for r in range(8):
            g_ref[pl.ds((row - 8 + r) * 32, 32), :] = grad[:, r * 128 : r * 128 + 128]

    def blur_row(n):
        g = lax.broadcasted_iota(jnp.int32, (JCOLS, LANES), 0)
        i_at = 4 * s + n - 3
        j_at = 16 * b + g - 3
        inside = (i_at >= 0) & (i_at < ROWS_LO) & (j_at >= 0) & (j_at < COLS_LO)
        for h in range(2):
            acc = [None, None, None]
            for a in range(TAPS):
                for q in range(4):
                    at = pl.multiple_of((4 * n + a) * LANES + 32 * q, 32)
                    x = m[h][pl.ds(at, JCOLS), :]
                    for d in range(3):
                        if 4 * d + q > 8:
                            continue
                        tap = a * 9 + 4 * d + q
                        term = w[h][tap : tap + 1, :] * x
                        acc[d] = term if acc[d] is None else acc[d] + term
            blurred = acc[0] + pltpu.roll(acc[1], JCOLS - 1, 0) + pltpu.roll(acc[2], JCOLS - 2, 0)
            seen = hst[h][pl.ds(pl.multiple_of(n * JCOLS, 8), JCOLS), :]
            f[h][pl.ds(pl.multiple_of(8 + n * JCOLS, 8), JCOLS), :] = jnp.where(inside, seen - blurred, 0.0)

    def back_rows(u, first=0, count=JCOLS, phases=4):
        for h in range(2):
            win = [[f[h][pl.ds(8 + (u - t) * JCOLS + first - tt, count), :] for tt in range(3)] for t in range(3)]
            for p in range(phases):
                for q in range(4):
                    total = None
                    for t in range(3):
                        for tt in range(3):
                            if p + 4 * t > 8 or q + 4 * tt > 8:
                                continue
                            tap = (p + 4 * t) * 9 + q + 4 * tt
                            term = w[h][tap : tap + 1, :] * win[t][tt]
                            total = term if total is None else total + term
                    at = (4 * u - 8 + p) * LANES + 32 * q + first
                    bk[h][pl.ds(at, count), :] = rounded(total)

    def hs_gradient(row, rows):
        at = pl.ds((row - 8) * LANES, rows * LANES)
        back = jnp.concatenate([b0[at, :].astype(bf16), b1[at, :].astype(bf16)], axis=1)
        return lax.dot_general(basis, back, (((1,), (1,)), ((), ())), preferred_element_type=f32)

    def start_row(row):
        return c_ref[pl.ds(row, 32, stride=CROWS), :]

    def loop(low, high, body):
        def step(n, _):
            body(n)
            return 0

        lax.fori_loop(low, high, step, 0)

    for block in range(CROWS // 8):
        value = jnp.concatenate([start_row(block * 8 + r) for r in range(8)], axis=1)
        mix(block * 8, value, 8)
        if 1 <= block < 5:
            ms_gradient(block * 8, value)
    loop(0, IROWS, blur_row)
    loop(2, 9, back_rows)
    back_rows(9, phases=1)
    for block in range(1, 5):
        grad = hs_gradient(block * 8, 8)
        values = []
        for r in range(8):
            row = block * 8 + r
            now = start_row(row)
            new = now + STEP * (grad[:, r * 128 : r * 128 + 128] + g_ref[pl.ds((row - 8) * 32, 32), :])
            row_at = 16 * s - 16 + row
            new = jnp.where(in_columns & (row_at >= 0) & (row_at < 128), new, 0.0)
            c1_ref[pl.ds((row - 8) * 32, 32), :] = new
            values.append(new)
        value = jnp.concatenate(values, axis=1)
        mix(block * 8, value, 8)
        if 2 <= block < 4:
            ms_gradient(block * 8, value)
    loop(2, 8, blur_row)
    loop(4, 8, lambda u: back_rows(u, 4, 16))
    place_at = lax.broadcasted_iota(jnp.int32, (LANES, LANES), 1)
    take = lax.broadcasted_iota(jnp.int32, (LANES, LANES), 0)
    shift = 4 * (take % 32) + take // 32 - 16
    order = [(place_at == shift + 64 * ((half + b) % 2)) & (shift >= 0) & (shift < 64) for half in range(2)]
    order = [jnp.where(o, 1.0, 0.0).astype(bf16) for o in order]
    grads = [hs_gradient(16, 8), hs_gradient(24, 8)]
    for r in range(8):
        total = None
        for half in range(2):
            row = 8 + r + 8 * half
            at = pl.ds(row * 32, 32)
            value = STEP * (grads[half][:, r * 128 : r * 128 + 128] + g_ref[at, :])
            value = value + (c1_ref[at, :] - start_row(row + 8))
            rest = jnp.where((group >= 4) & (group < 20), value, 0.0)
            for _ in range(3):
                piece = rest.astype(bf16)
                rest = rest - piece.astype(f32)
                moved = jnp.dot(piece, order[half], preferred_element_type=f32)
                total = moved if total is None else total + moved
        out_ref[pl.ds(r, 32, stride=8), :] = total


def refine(pos, mine, other, hp, seen, cross):
    vmem = pl.BlockSpec(memory_space=pltpu.VMEM)
    return pl.pallas_call(
        refine_kernel,
        out_shape=jax.ShapeDtypeStruct((32 * 8, LANES), f32),
        in_specs=[pl.BlockSpec(memory_space=pltpu.SMEM)] + [vmem] * 5,
        out_specs=vmem,
        scratch_shapes=[
            pltpu.VMEM((32 * CROWS, LANES), f32),
            pltpu.VMEM((8 * MROWS, LANES), f32),
            pltpu.VMEM((CROWS * LANES, LANES), f32),
            pltpu.VMEM((CROWS * LANES, LANES), f32),
            pltpu.VMEM((256, LANES), f32),
            pltpu.VMEM((256, LANES), f32),
            pltpu.VMEM((MROWS * LANES, LANES), f32),
            pltpu.VMEM((MROWS * LANES, LANES), f32),
            pltpu.VMEM((MROWS * 32, LANES), f32),
            pltpu.VMEM((MROWS * 32, LANES), f32),
            pltpu.VMEM((256, LANES), f32),
            pltpu.VMEM((256, LANES), f32),
            pltpu.VMEM((LANES, LANES), f32),
            pltpu.VMEM((LANES, LANES), f32),
        ],
        compiler_params=pltpu.CompilerParams(vmem_limit_bytes=40 * 2**20),
        cost_estimate=pl.CostEstimate(flops=400_000_000, bytes_accessed=2_000_000, transcendentals=0),
        name="refine",
    )(pos, mine, other, hp, seen, cross)


def spread(hs_ref, k_ref, basis_ref, response_ref, sent_ref):
    lane = lax.broadcasted_iota(jnp.int32, (1, LANES), 1)
    hs = hs_ref[...].astype(f32)
    rows = [jnp.concatenate([hs[:, i, :], jnp.zeros((2, 256), f32)], axis=0) for i in range(4)]
    sent_ref[0, :, 128:256] = jnp.zeros((16, 128), f32)
    for a in range(9):
        sent_ref[0, 0:14, 128 + 9 * a : 137 + 9 * a] = k_ref[a]
    sent_ref[0, 0:14, 209:241] = basis_ref[...].astype(f32)
    sent_ref[0, 0:14, 241:249] = response_ref[...].astype(f32).T
    params = sent_ref[0, :, 128:256]
    for t in range(16):
        total = jnp.zeros((16, LANES), f32)
        for i in range(4):
            moved = pltpu.roll(rows[i], (24 * i + 3 - 16 * t) % 256, 1)[:, 0:128]
            total = jnp.where((lane >= 24 * i) & (lane < 24 * i + 24), moved, total)
        sent_ref[t, :, 0:128] = total
        if t:
            sent_ref[t, :, 128:256] = params


def pack_kernel(pos_ref, ca_ref, cb_ref, ma_ref, mb_ref, hs_ref, k_ref, basis_ref, response_ref, *rest_refs):
    spread(hs_ref, k_ref, basis_ref, response_ref, rest_refs[4])
    wide_ref = rest_refs[5]
    s = pos_ref[0] // 16
    b = pos_ref[0] % 16
    off = jnp.where(b % 2 == 0, 112, 48)
    lane = lax.broadcasted_iota(jnp.int32, (1, LANES), 1)
    first = lane >= off
    block = (b + 1) // 2 - jnp.where(first, 1, 0)
    keep = (block >= 0) & (block < 8)
    source = lax.broadcasted_iota(jnp.int32, (LANES, LANES), 0)
    target = lax.broadcasted_iota(jnp.int32, (LANES, LANES), 1)
    order = jnp.where(source == (4 * (target % 32) + target // 32 + off) % LANES, 1.0, 0.0).astype(bf16)
    ms = jnp.where(first, ma_ref[...].reshape(128, LANES).astype(f32), mb_ref[...].reshape(128, LANES).astype(f32))
    ms = jnp.where(keep, ms, 0.0).astype(bf16)
    ms = jnp.dot(ms, order, preferred_element_type=f32)
    rest_refs[0][256:384] = ms
    edge = jnp.zeros((16, LANES), f32)
    for k in range(4):
        rest = jnp.where(keep, jnp.where(first, ca_ref[k], cb_ref[k]), 0.0)
        total = None
        for _ in range(3):
            piece = rest.astype(bf16)
            rest = rest - piece.astype(f32)
            moved = jnp.dot(piece, order, preferred_element_type=f32)
            total = moved if total is None else total + moved
        wide_ref[k, 0:16] = edge
        wide_ref[k, 16:144] = total
        wide_ref[k, 144:160] = edge
    for d in range(4):
        at = pl.ds(pl.multiple_of(32 * ((s // 2 + d) % 4), 32), 64)
        for k in range(4):
            rest_refs[d][64 * k : 64 * k + 64] = wide_ref[k, at, :]


def pack(pos, coeffs_in, ms_image, hs_image, kernels, basis, response):
    def low(i, p):
        return (0, 0, jnp.maximum((p[0] % 16 + 1) // 2 - 1, 0))

    def high(i, p):
        return (0, 0, jnp.minimum((p[0] % 16 + 1) // 2, 7))

    return pl.pallas_call(
        pack_kernel,
        out_shape=(jax.ShapeDtypeStruct((384, LANES), f32),)
        + (jax.ShapeDtypeStruct((256, LANES), f32),) * 3
        + (jax.ShapeDtypeStruct((16, 16, 256), f32),),
        grid_spec=pltpu.PrefetchScalarGridSpec(
            num_scalar_prefetch=1,
            grid=(1,),
            in_specs=[
                pl.BlockSpec((4, 128, LANES), low),
                pl.BlockSpec((4, 128, LANES), high),
                pl.BlockSpec((8, 16, LANES), low),
                pl.BlockSpec((8, 16, LANES), high),
                pl.BlockSpec((14, 4, 256), lambda i, p: (0, 0, 0)),
                pl.BlockSpec((9, 14, 9), lambda i, p: (0, 0, 0)),
                pl.BlockSpec((14, 32), lambda i, p: (0, 0)),
                pl.BlockSpec((8, 14), lambda i, p: (0, 0)),
            ],
            out_specs=(pl.BlockSpec((384, LANES), lambda i, p: (0, 0)),)
            + (pl.BlockSpec((256, LANES), lambda i, p: (0, 0)),) * 3
            + (pl.BlockSpec((16, 16, 256), lambda i, p: (0, 0, 0)),),
            scratch_shapes=[pltpu.VMEM((4, 160, LANES), f32)],
        ),
        compiler_params=pltpu.CompilerParams(vmem_limit_bytes=60 * 2**20),
        cost_estimate=pl.CostEstimate(flops=100_000_000, bytes_accessed=1_600_000, transcendentals=0),
        name="pack",
    )(pos, coeffs_in, coeffs_in, ms_image, ms_image, hs_image, kernels, basis, response)


def hold_kernel(region_ref, out_ref, near_ref):
    out_ref[...] = region_ref[0:256]
    near_ref[...] = region_ref[256:384].astype(bf16)


def hold(region):
    vmem = pl.BlockSpec(memory_space=pltpu.VMEM)
    return pl.pallas_call(
        hold_kernel,
        out_shape=(jax.ShapeDtypeStruct((256, LANES), f32), jax.ShapeDtypeStruct((128, LANES), bf16)),
        in_specs=[vmem],
        out_specs=(vmem, vmem),
        compiler_params=pltpu.CompilerParams(vmem_limit_bytes=16 * 2**20),
        name="hold",
    )(region)


def join_kernel(hp_ref, near_ref, seen_ref):
    seen_ref[0:256] = hp_ref[:, 0:128].astype(bf16)
    seen_ref[256:384] = near_ref[...]


def join(hp, near):
    vmem = pl.BlockSpec(memory_space=pltpu.VMEM)
    return pl.pallas_call(
        join_kernel,
        out_shape=jax.ShapeDtypeStruct((384, LANES), bf16),
        in_specs=[vmem] * 2,
        out_specs=vmem,
        compiler_params=pltpu.CompilerParams(vmem_limit_bytes=16 * 2**20),
        name="join",
    )(hp, near)


def hand_kernel(pos_ref, r0, r2, r1, r3, seen_ref, mine_ref, other_ref):
    other_ref[16 * CROWS : 16 * CROWS + 384] = seen_ref[...].astype(f32)
    skip = 16 * (pos_ref[0] // 16 % 2)
    for d, region in enumerate((r0, r1, r2, r3)):
        for k in range(4):
            at = CROWS * (4 * d + k)
            mine_ref[at : at + CROWS] = region[pl.ds(pl.multiple_of(64 * k + skip, 16), CROWS), :]
            other_ref[at : at + CROWS] = region[pl.ds(pl.multiple_of(64 * k + 16 - skip, 16), CROWS), :]


def hand(pos, tiles, seen):
    vmem = pl.BlockSpec(memory_space=pltpu.VMEM)
    return pl.pallas_call(
        hand_kernel,
        out_shape=(
            jax.ShapeDtypeStruct((16 * CROWS, LANES), f32),
            jax.ShapeDtypeStruct((16 * CROWS + 384, LANES), f32),
        ),
        in_specs=[pl.BlockSpec(memory_space=pltpu.SMEM)] + [vmem] * 5,
        out_specs=(vmem, vmem),
        compiler_params=pltpu.CompilerParams(vmem_limit_bytes=16 * 2**20),
        cost_estimate=pl.CostEstimate(flops=1_000_000, bytes_accessed=800_000, transcendentals=0),
        name="hand",
    )(pos, tiles[0], tiles[2], tiles[1], tiles[3], seen)


def encode_kernel(d_ref, out_ref):
    scales = []
    codes = []
    for k in range(4):
        part = d_ref[:, k]
        size = jnp.abs(part)
        top = jnp.max(size, axis=(0, 1, 2), keepdims=True)
        scale = rounded(jnp.maximum(top * (1 + 2**-7), 1e-30))
        code = jnp.exp2(size * (SPAN / scale) - SPAN / 2)
        codes.append(jnp.where(part < 0, -code, code))
        scales.append(jnp.broadcast_to(scale[0], (1, LANES)))
    scales = jnp.concatenate(scales + [jnp.zeros((12, LANES), f32)], axis=0).astype(bf16)
    for s in range(8):
        row = jnp.concatenate([codes[k][s] for k in range(4)], axis=0).astype(bf16)
        for t in range(16):
            out_ref[t, 32 * s : 32 * s + 32] = row
    for t in range(16):
        out_ref[t, 256:272] = scales


def encode(owned):
    vmem = pl.BlockSpec(memory_space=pltpu.VMEM)
    return pl.pallas_call(
        encode_kernel,
        out_shape=jax.ShapeDtypeStruct((16, 272, LANES), bf16),
        in_specs=[vmem],
        out_specs=vmem,
        compiler_params=pltpu.CompilerParams(vmem_limit_bytes=16 * 2**20),
        name="encode",
    )(owned)


def place_kernel(g_ref, c_ref, out_ref):
    lane = lax.broadcasted_iota(jnp.int32, (1, LANES), 1)
    low = lane < 64
    count = g_ref.shape[0] // 2
    for j in range(count):
        even, odd = [g_ref[2 * j + e, 256:272].astype(f32) * (1 / SPAN) for e in range(2)]
        scales = (jnp.where(low, even, odd), jnp.where(low, odd, even))
        columns = slice(j * LANES, j * LANES + LANES)
        for s in range(8):
            even, odd = [g_ref[2 * j + e, 32 * s : 32 * s + 32].astype(f32) for e in range(2)]
            for half, code in enumerate((jnp.where(low, even, odd), jnp.where(low, odd, even))):
                size = jnp.log2(jnp.abs(code)) + SPAN / 2
                value = jnp.where(code < 0, -size, size)
                for k in range(4):
                    part = value[8 * k : 8 * k + 8] * scales[half][k : k + 1]
                    if half:
                        part = pltpu.roll(part, 64, 1)
                    at = slice(16 * s + 8 * half, 16 * s + 8 * half + 8)
                    out_ref[k, at, columns] = c_ref[k, at, columns] + part


def place(gathered, coeffs_in):
    block = pl.BlockSpec((4, 128, 4 * LANES), lambda j: (0, 0, j))
    return pl.pallas_call(
        place_kernel,
        out_shape=jax.ShapeDtypeStruct((4, 128, 1024), f32),
        grid=(2,),
        in_specs=[pl.BlockSpec((8, 272, LANES), lambda j: (j, 0, 0)), block],
        out_specs=block,
        compiler_params=pltpu.CompilerParams(vmem_limit_bytes=32 * 2**20),
        name="place",
    )(gathered, coeffs_in)


def per_device(coeffs_in, basis, kernels, response, hs_image, ms_image):
    pos = (lax.axis_index("sub") * 16 + lax.axis_index("band")).astype(jnp.int32).reshape(1)
    *tiles, sent = pack(pos, coeffs_in, ms_image, hs_image, kernels.transpose(1, 0, 2), basis, response)
    hp = lax.all_to_all(sent, "band", split_axis=0, concat_axis=0, tiled=True).reshape(256, 256)
    for d in (2, 1, 3):
        tiles[d] = lax.ppermute(tiles[d], "sub", [(i, (i + 2 * d) % 8) for i in range(8)])
    tiles[0], near = hold(tiles[0])
    seen = join(hp, near)
    cross = lax.ppermute(seen, "sub", [(1, 2), (2, 1), (3, 4), (4, 3), (5, 6), (6, 5)])
    cross, *tiles = lax.optimization_barrier((cross, *tiles))
    mine, other = hand(pos, tiles, seen)
    other = lax.ppermute(other, "sub", [(i, i ^ 1) for i in range(8)])
    new = refine(pos, mine, other, hp, seen, cross)
    owned = lax.all_to_all(new.reshape(8, 4, 8, LANES), "sub", split_axis=0, concat_axis=0, tiled=True)
    gathered = lax.all_to_all(encode(owned), "band", split_axis=0, concat_axis=0, tiled=True)
    return place(gathered, coeffs_in)


def solution(mesh):
    return jax.shard_map(
        per_device,
        mesh=mesh,
        in_specs=(
            P("sub", None, None),
            P("band", None),
            P("band", None, None),
            P(None, "band"),
            P("band", "sub", None),
            P(None, "sub", None),
        ),
        out_specs=P("sub", None, None),
        check_vma=False,
    )
```

```python
import functools

import jax
import jax.numpy as jnp
from jax import lax
from jax.experimental import pallas as pl
from jax.experimental.pallas import tpu as pltpu
from jax.sharding import PartitionSpec as P

STEP = 0.15
TR, TC = 16, 64
TAPS = 9
SPAN = 250.0
LANES = 128
CROWS = 48
MROWS = 32
IROWS = 10
JCOLS = 24
ROWS_LO, COLS_LO = 32, 256
f32 = jnp.float32
bf16 = jnp.bfloat16


def rounded(value):
    return value.astype(bf16).astype(f32)


def refine_kernel(pos_ref, *refs):
    mine_ref, other_ref, hp_ref, seen_ref, cross_ref, out_ref, c_ref, ms_ref, m0, m1, f0, f1, b0, b1, c1_ref, g_ref, hs0, hs1, w0, w1 = refs
    s = pos_ref[0] // 16
    b = pos_ref[0] % 16
    core = s % 2
    for d in range(4):
        chip = (s // 2 + 4 - d) % 4
        mine = pl.multiple_of((2 * chip + core) * (4 * CROWS), 4 * CROWS)
        theirs = pl.multiple_of((2 * chip + 1 - core) * (4 * CROWS), 4 * CROWS)
        c_ref[pl.ds(mine, 4 * CROWS), :] = mine_ref[d * 4 * CROWS : (d + 1) * 4 * CROWS]
        c_ref[pl.ds(theirs, 4 * CROWS), :] = other_ref[d * 4 * CROWS : (d + 1) * 4 * CROWS]

    def neighbours(low, high):
        theirs = other_ref[16 * CROWS + low : 16 * CROWS + high]
        across = cross_ref[low:high].astype(f32)
        flag = jnp.zeros((high - low, LANES), jnp.int32) + core
        return jnp.where(flag == 0, across, theirs), jnp.where(flag == 0, theirs, across)

    ms_above, ms_below = neighbours(256, 384)
    for k in range(8):
        ms_ref[32 * k : 32 * k + 8, :] = ms_above[16 * k + 8 : 16 * k + 16]
        ms_ref[32 * k + 8 : 32 * k + 24, :] = seen_ref[256 + 16 * k : 272 + 16 * k].astype(f32)
        ms_ref[32 * k + 24 : 32 * k + 32, :] = ms_below[16 * k : 16 * k + 8]
    bk = (b0, b1)
    m = (m0, m1)
    f = (f0, f1)
    hst = (hs0, hs1)
    w = (w0, w1)
    for h in range(2):
        at = slice(h * 128, h * 128 + 128)
        above, below = neighbours(h * 128, h * 128 + 128)
        hst[h][0:72, :] = above.T[24:96]
        hst[h][72:168, :] = hp_ref[at, 0:128].T[0:96]
        hst[h][168:240, :] = below.T[0:72]
        w[h][...] = hp_ref[at, 128:256].T
    basis = jnp.concatenate([w0[81:113, :], w1[81:113, :]], axis=1).astype(bf16)
    response = jnp.concatenate([w0[113:121, :], w1[113:121, :]], axis=1).astype(bf16)
    combined = lax.dot_general(response, basis, (((1,), (1,)), ((), ())), preferred_element_type=f32).astype(bf16)
    lane = lax.broadcasted_iota(jnp.int32, (1, LANES), 1)
    group = lane % 32
    column = 64 * b - 16 + 4 * group + lane // 32
    in_columns = (column >= 0) & (column < 1024) & (group >= 2) & (group < 22)

    def mix(row, value, rows):
        mixed = lax.dot_general(value.astype(bf16), basis, (((0,), (0,)), ((), ())), preferred_element_type=f32)
        mixed = rounded(mixed)
        at = pl.ds(pl.multiple_of(row * LANES, LANES), rows * LANES)
        for h in range(2):
            m[h][at, :] = mixed[:, h * 128 : h * 128 + 128]

    def ms_gradient(row, block):
        predicted = jnp.dot(combined, block.astype(bf16), preferred_element_type=f32)
        seen = jnp.concatenate([ms_ref[pl.ds(row - 8 + r, 8, stride=MROWS), :] for r in range(8)], axis=1)
        misfit = (seen - predicted).astype(bf16)
        grad = lax.dot_general(combined, misfit, (((0,), (0,)), ((), ())), preferred_element_type=f32)
        for r in range(8):
            g_ref[pl.ds((row - 8 + r) * 32, 32), :] = grad[:, r * 128 : r * 128 + 128]

    def blur_row(n):
        g = lax.broadcasted_iota(jnp.int32, (JCOLS, LANES), 0)
        i_at = 4 * s + n - 3
        j_at = 16 * b + g - 3
        inside = (i_at >= 0) & (i_at < ROWS_LO) & (j_at >= 0) & (j_at < COLS_LO)
        for h in range(2):
            acc = [None, None, None]
            for a in range(TAPS):
                for q in range(4):
                    at = pl.multiple_of((4 * n + a) * LANES + 32 * q, 32)
                    x = m[h][pl.ds(at, JCOLS), :]
                    for d in range(3):
                        if 4 * d + q > 8:
                            continue
                        tap = a * 9 + 4 * d + q
                        term = w[h][tap : tap + 1, :] * x
                        acc[d] = term if acc[d] is None else acc[d] + term
            blurred = acc[0] + pltpu.roll(acc[1], JCOLS - 1, 0) + pltpu.roll(acc[2], JCOLS - 2, 0)
            seen = hst[h][pl.ds(pl.multiple_of(n * JCOLS, 8), JCOLS), :]
            f[h][pl.ds(pl.multiple_of(8 + n * JCOLS, 8), JCOLS), :] = jnp.where(inside, seen - blurred, 0.0)

    def back_rows(u, first=0, count=JCOLS, phases=4):
        for h in range(2):
            win = [[f[h][pl.ds(8 + (u - t) * JCOLS + first - tt, count), :] for tt in range(3)] for t in range(3)]
            for p in range(phases):
                for q in range(4):
                    total = None
                    for t in range(3):
                        for tt in range(3):
                            if p + 4 * t > 8 or q + 4 * tt > 8:
                                continue
                            tap = (p + 4 * t) * 9 + q + 4 * tt
                            term = w[h][tap : tap + 1, :] * win[t][tt]
                            total = term if total is None else total + term
                    at = (4 * u - 8 + p) * LANES + 32 * q + first
                    bk[h][pl.ds(at, count), :] = rounded(total)

    def hs_gradient(row, rows):
        at = pl.ds((row - 8) * LANES, rows * LANES)
        back = jnp.concatenate([b0[at, :].astype(bf16), b1[at, :].astype(bf16)], axis=1)
        return lax.dot_general(basis, back, (((1,), (1,)), ((), ())), preferred_element_type=f32)

    def start_row(row):
        return c_ref[pl.ds(row, 32, stride=CROWS), :]

    def loop(low, high, body):
        def step(n, _):
            body(n)
            return 0

        lax.fori_loop(low, high, step, 0)

    for block in range(CROWS // 8):
        value = jnp.concatenate([start_row(block * 8 + r) for r in range(8)], axis=1)
        mix(block * 8, value, 8)
        if 1 <= block < 5:
            ms_gradient(block * 8, value)
    loop(0, IROWS, blur_row)
    loop(2, 9, back_rows)
    back_rows(9, phases=1)
    for block in range(1, 5):
        grad = hs_gradient(block * 8, 8)
        values = []
        for r in range(8):
            row = block * 8 + r
            now = start_row(row)
            new = now + STEP * (grad[:, r * 128 : r * 128 + 128] + g_ref[pl.ds((row - 8) * 32, 32), :])
            row_at = 16 * s - 16 + row
            new = jnp.where(in_columns & (row_at >= 0) & (row_at < 128), new, 0.0)
            c1_ref[pl.ds((row - 8) * 32, 32), :] = new
            values.append(new)
        value = jnp.concatenate(values, axis=1)
        mix(block * 8, value, 8)
        if 2 <= block < 4:
            ms_gradient(block * 8, value)
    loop(2, 8, blur_row)
    loop(4, 8, lambda u: back_rows(u, 4, 16))
    place_at = lax.broadcasted_iota(jnp.int32, (LANES, LANES), 1)
    take = lax.broadcasted_iota(jnp.int32, (LANES, LANES), 0)
    shift = 4 * (take % 32) + take // 32 - 16
    order = [(place_at == shift + 64 * ((half + b) % 2)) & (shift >= 0) & (shift < 64) for half in range(2)]
    order = [jnp.where(o, 1.0, 0.0).astype(bf16) for o in order]
    grads = [hs_gradient(16, 8), hs_gradient(24, 8)]
    for r in range(8):
        total = None
        for half in range(2):
            row = 8 + r + 8 * half
            at = pl.ds(row * 32, 32)
            value = STEP * (grads[half][:, r * 128 : r * 128 + 128] + g_ref[at, :])
            value = value + (c1_ref[at, :] - start_row(row + 8))
            rest = jnp.where((group >= 4) & (group < 20), value, 0.0)
            for _ in range(3):
                piece = rest.astype(bf16)
                rest = rest - piece.astype(f32)
                moved = jnp.dot(piece, order[half], preferred_element_type=f32)
                total = moved if total is None else total + moved
        out_ref[pl.ds(r, 32, stride=8), :] = total


def refine(pos, mine, other, hp, seen, cross):
    vmem = pl.BlockSpec(memory_space=pltpu.VMEM)
    return pl.pallas_call(
        refine_kernel,
        out_shape=jax.ShapeDtypeStruct((32 * 8, LANES), f32),
        in_specs=[pl.BlockSpec(memory_space=pltpu.SMEM)] + [vmem] * 5,
        out_specs=vmem,
        scratch_shapes=[
            pltpu.VMEM((32 * CROWS, LANES), f32),
            pltpu.VMEM((8 * MROWS, LANES), f32),
            pltpu.VMEM((CROWS * LANES, LANES), f32),
            pltpu.VMEM((CROWS * LANES, LANES), f32),
            pltpu.VMEM((256, LANES), f32),
            pltpu.VMEM((256, LANES), f32),
            pltpu.VMEM((MROWS * LANES, LANES), f32),
            pltpu.VMEM((MROWS * LANES, LANES), f32),
            pltpu.VMEM((MROWS * 32, LANES), f32),
            pltpu.VMEM((MROWS * 32, LANES), f32),
            pltpu.VMEM((256, LANES), f32),
            pltpu.VMEM((256, LANES), f32),
            pltpu.VMEM((LANES, LANES), f32),
            pltpu.VMEM((LANES, LANES), f32),
        ],
        compiler_params=pltpu.CompilerParams(vmem_limit_bytes=40 * 2**20),
        cost_estimate=pl.CostEstimate(flops=400_000_000, bytes_accessed=2_000_000, transcendentals=0),
        name="refine",
    )(pos, mine, other, hp, seen, cross)


def spread(hs_ref, k_ref, basis_ref, response_ref, sent_ref):
    lane = lax.broadcasted_iota(jnp.int32, (1, LANES), 1)
    hs = hs_ref[...].astype(f32)
    rows = [jnp.concatenate([hs[:, i, :], jnp.zeros((2, 256), f32)], axis=0) for i in range(4)]
    sent_ref[0, :, 128:256] = jnp.zeros((16, 128), f32)
    for a in range(9):
        sent_ref[0, 0:14, 128 + 9 * a : 137 + 9 * a] = k_ref[a]
    sent_ref[0, 0:14, 209:241] = basis_ref[...].astype(f32)
    sent_ref[0, 0:14, 241:249] = response_ref[...].astype(f32).T
    params = sent_ref[0, :, 128:256]
    for t in range(16):
        total = jnp.zeros((16, LANES), f32)
        for i in range(4):
            moved = pltpu.roll(rows[i], (24 * i + 3 - 16 * t) % 256, 1)[:, 0:128]
            total = jnp.where((lane >= 24 * i) & (lane < 24 * i + 24), moved, total)
        sent_ref[t, :, 0:128] = total
        if t:
            sent_ref[t, :, 128:256] = params


def pack_kernel(pos_ref, ca_ref, cb_ref, ma_ref, mb_ref, hs_ref, k_ref, basis_ref, response_ref, *rest_refs):
    spread(hs_ref, k_ref, basis_ref, response_ref, rest_refs[4])
    wide_ref = rest_refs[5]
    s = pos_ref[0] // 16
    b = pos_ref[0] % 16
    off = jnp.where(b % 2 == 0, 112, 48)
    lane = lax.broadcasted_iota(jnp.int32, (1, LANES), 1)
    first = lane >= off
    block = (b + 1) // 2 - jnp.where(first, 1, 0)
    keep = (block >= 0) & (block < 8)
    source = lax.broadcasted_iota(jnp.int32, (LANES, LANES), 0)
    target = lax.broadcasted_iota(jnp.int32, (LANES, LANES), 1)
    order = jnp.where(source == (4 * (target % 32) + target // 32 + off) % LANES, 1.0, 0.0).astype(bf16)
    ms = jnp.where(first, ma_ref[...].reshape(128, LANES).astype(f32), mb_ref[...].reshape(128, LANES).astype(f32))
    ms = jnp.where(keep, ms, 0.0).astype(bf16)
    ms = jnp.dot(ms, order, preferred_element_type=f32)
    rest_refs[0][256:384] = ms
    edge = jnp.zeros((16, LANES), f32)
    for k in range(4):
        rest = jnp.where(keep, jnp.where(first, ca_ref[k], cb_ref[k]), 0.0)
        total = None
        for _ in range(3):
            piece = rest.astype(bf16)
            rest = rest - piece.astype(f32)
            moved = jnp.dot(piece, order, preferred_element_type=f32)
            total = moved if total is None else total + moved
        wide_ref[k, 0:16] = edge
        wide_ref[k, 16:144] = total
        wide_ref[k, 144:160] = edge
    for d in range(4):
        at = pl.ds(pl.multiple_of(32 * ((s // 2 + d) % 4), 32), 64)
        for k in range(4):
            rest_refs[d][64 * k : 64 * k + 64] = wide_ref[k, at, :]


def pack(pos, coeffs_in, ms_image, hs_image, kernels, basis, response):
    def low(i, p):
        return (0, 0, jnp.maximum((p[0] % 16 + 1) // 2 - 1, 0))

    def high(i, p):
        return (0, 0, jnp.minimum((p[0] % 16 + 1) // 2, 7))

    return pl.pallas_call(
        pack_kernel,
        out_shape=(jax.ShapeDtypeStruct((384, LANES), f32),)
        + (jax.ShapeDtypeStruct((256, LANES), f32),) * 3
        + (jax.ShapeDtypeStruct((16, 16, 256), f32),),
        grid_spec=pltpu.PrefetchScalarGridSpec(
            num_scalar_prefetch=1,
            grid=(1,),
            in_specs=[
                pl.BlockSpec((4, 128, LANES), low),
                pl.BlockSpec((4, 128, LANES), high),
                pl.BlockSpec((8, 16, LANES), low),
                pl.BlockSpec((8, 16, LANES), high),
                pl.BlockSpec((14, 4, 256), lambda i, p: (0, 0, 0)),
                pl.BlockSpec((9, 14, 9), lambda i, p: (0, 0, 0)),
                pl.BlockSpec((14, 32), lambda i, p: (0, 0)),
                pl.BlockSpec((8, 14), lambda i, p: (0, 0)),
            ],
            out_specs=(pl.BlockSpec((384, LANES), lambda i, p: (0, 0)),)
            + (pl.BlockSpec((256, LANES), lambda i, p: (0, 0)),) * 3
            + (pl.BlockSpec((16, 16, 256), lambda i, p: (0, 0, 0)),),
            scratch_shapes=[pltpu.VMEM((4, 160, LANES), f32)],
        ),
        compiler_params=pltpu.CompilerParams(vmem_limit_bytes=60 * 2**20),
        cost_estimate=pl.CostEstimate(flops=100_000_000, bytes_accessed=1_600_000, transcendentals=0),
        name="pack",
    )(pos, coeffs_in, coeffs_in, ms_image, ms_image, hs_image, kernels, basis, response)


def hold_kernel(region_ref, out_ref, near_ref):
    out_ref[...] = region_ref[0:256]
    near_ref[...] = region_ref[256:384].astype(bf16)


def hold(region):
    vmem = pl.BlockSpec(memory_space=pltpu.VMEM)
    return pl.pallas_call(
        hold_kernel,
        out_shape=(jax.ShapeDtypeStruct((256, LANES), f32), jax.ShapeDtypeStruct((128, LANES), bf16)),
        in_specs=[vmem],
        out_specs=(vmem, vmem),
        compiler_params=pltpu.CompilerParams(vmem_limit_bytes=16 * 2**20),
        name="hold",
    )(region)


def join_kernel(hp_ref, near_ref, seen_ref):
    seen_ref[0:256] = hp_ref[:, 0:128].astype(bf16)
    seen_ref[256:384] = near_ref[...]


def join(hp, near):
    vmem = pl.BlockSpec(memory_space=pltpu.VMEM)
    return pl.pallas_call(
        join_kernel,
        out_shape=jax.ShapeDtypeStruct((384, LANES), bf16),
        in_specs=[vmem] * 2,
        out_specs=vmem,
        compiler_params=pltpu.CompilerParams(vmem_limit_bytes=16 * 2**20),
        name="join",
    )(hp, near)


def hand_kernel(pos_ref, r0, r1, r2, r3, seen_ref, mine_ref, other_ref):
    other_ref[16 * CROWS : 16 * CROWS + 384] = seen_ref[...].astype(f32)
    skip = 16 * (pos_ref[0] // 16 % 2)
    for d, region in enumerate((r0, r1, r2, r3)):
        for k in range(4):
            at = CROWS * (4 * d + k)
            mine_ref[at : at + CROWS] = region[pl.ds(pl.multiple_of(64 * k + skip, 16), CROWS), :]
            other_ref[at : at + CROWS] = region[pl.ds(pl.multiple_of(64 * k + 16 - skip, 16), CROWS), :]


def hand(pos, tiles, seen):
    vmem = pl.BlockSpec(memory_space=pltpu.VMEM)
    return pl.pallas_call(
        hand_kernel,
        out_shape=(
            jax.ShapeDtypeStruct((16 * CROWS, LANES), f32),
            jax.ShapeDtypeStruct((16 * CROWS + 384, LANES), f32),
        ),
        in_specs=[pl.BlockSpec(memory_space=pltpu.SMEM)] + [vmem] * 5,
        out_specs=(vmem, vmem),
        compiler_params=pltpu.CompilerParams(vmem_limit_bytes=16 * 2**20),
        cost_estimate=pl.CostEstimate(flops=1_000_000, bytes_accessed=800_000, transcendentals=0),
        name="hand",
    )(pos, *tiles, seen)


def encode_kernel(d_ref, out_ref):
    scales = []
    codes = []
    for k in range(4):
        part = d_ref[:, k]
        size = jnp.abs(part)
        top = jnp.max(size, axis=(0, 1, 2), keepdims=True)
        scale = rounded(jnp.maximum(top * (1 + 2**-7), 1e-30))
        code = jnp.exp2(size * (SPAN / scale) - SPAN / 2)
        codes.append(jnp.where(part < 0, -code, code))
        scales.append(jnp.broadcast_to(scale[0], (1, LANES)))
    scales = jnp.concatenate(scales + [jnp.zeros((12, LANES), f32)], axis=0).astype(bf16)
    for s in range(8):
        row = jnp.concatenate([codes[k][s] for k in range(4)], axis=0).astype(bf16)
        for t in range(16):
            out_ref[t, 32 * s : 32 * s + 32] = row
    for t in range(16):
        out_ref[t, 256:272] = scales


def encode(owned):
    vmem = pl.BlockSpec(memory_space=pltpu.VMEM)
    return pl.pallas_call(
        encode_kernel,
        out_shape=jax.ShapeDtypeStruct((16, 272, LANES), bf16),
        in_specs=[vmem],
        out_specs=vmem,
        compiler_params=pltpu.CompilerParams(vmem_limit_bytes=16 * 2**20),
        name="encode",
    )(owned)


def place_kernel(g_ref, c_ref, out_ref):
    lane = lax.broadcasted_iota(jnp.int32, (1, LANES), 1)
    low = lane < 64
    count = g_ref.shape[0] // 2
    for j in range(count):
        even, odd = [g_ref[2 * j + e, 256:272].astype(f32) * (1 / SPAN) for e in range(2)]
        scales = (jnp.where(low, even, odd), jnp.where(low, odd, even))
        columns = slice(j * LANES, j * LANES + LANES)
        for s in range(8):
            even, odd = [g_ref[2 * j + e, 32 * s : 32 * s + 32].astype(f32) for e in range(2)]
            for half, code in enumerate((jnp.where(low, even, odd), jnp.where(low, odd, even))):
                size = jnp.log2(jnp.abs(code)) + SPAN / 2
                value = jnp.where(code < 0, -size, size)
                for k in range(4):
                    part = value[8 * k : 8 * k + 8] * scales[half][k : k + 1]
                    if half:
                        part = pltpu.roll(part, 64, 1)
                    at = slice(16 * s + 8 * half, 16 * s + 8 * half + 8)
                    out_ref[k, at, columns] = c_ref[k, at, columns] + part


def place(gathered, coeffs_in):
    block = pl.BlockSpec((4, 128, 8 * LANES), lambda j: (0, 0, j))
    return pl.pallas_call(
        place_kernel,
        out_shape=jax.ShapeDtypeStruct((4, 128, 1024), f32),
        grid=(1,),
        in_specs=[pl.BlockSpec((16, 272, LANES), lambda j: (j, 0, 0)), block],
        out_specs=block,
        compiler_params=pltpu.CompilerParams(vmem_limit_bytes=32 * 2**20),
        name="place",
    )(gathered, coeffs_in)


def per_device(coeffs_in, basis, kernels, response, hs_image, ms_image):
    pos = (lax.axis_index("sub") * 16 + lax.axis_index("band")).astype(jnp.int32).reshape(1)
    *tiles, sent = pack(pos, coeffs_in, ms_image, hs_image, kernels.transpose(1, 0, 2), basis, response)
    hp = lax.all_to_all(sent, "band", split_axis=0, concat_axis=0, tiled=True).reshape(256, 256)
    tiles = [tiles[0]] + [
        lax.ppermute(tiles[d], "sub", [(i, (i + 2 * d) % 8) for i in range(8)]) for d in range(1, 4)
    ]
    tiles[0], near = hold(tiles[0])
    seen = join(hp, near)
    cross = lax.ppermute(seen, "sub", [(1, 2), (2, 1), (3, 4), (4, 3), (5, 6), (6, 5)])
    cross, *tiles = lax.optimization_barrier((cross, *tiles))
    mine, other = hand(pos, tiles, seen)
    other = lax.ppermute(other, "sub", [(i, i ^ 1) for i in range(8)])
    new = refine(pos, mine, other, hp, seen, cross)
    owned = lax.all_to_all(new.reshape(8, 4, 8, LANES), "sub", split_axis=0, concat_axis=0, tiled=True)
    gathered = lax.all_to_all(encode(owned), "band", split_axis=0, concat_axis=0, tiled=True)
    return place(gathered, coeffs_in)


def solution(mesh):
    return jax.shard_map(
        per_device,
        mesh=mesh,
        in_specs=(
            P("sub", None, None),
            P("band", None),
            P("band", None, None),
            P(None, "band"),
            P("band", "sub", None),
            P(None, "sub", None),
        ),
        out_specs=P("sub", None, None),
        check_vma=False,
    )
```

```python
import functools

import jax
import jax.numpy as jnp
from jax import lax
from jax.experimental import pallas as pl
from jax.experimental.pallas import tpu as pltpu
from jax.sharding import PartitionSpec as P

STEP = 0.15
TR, TC = 16, 64
TAPS = 9
SPAN = 250.0
LANES = 128
CROWS = 48
MROWS = 32
IROWS = 10
JCOLS = 24
ROWS_LO, COLS_LO = 32, 256
f32 = jnp.float32
bf16 = jnp.bfloat16


def rounded(value):
    return value.astype(bf16).astype(f32)


def refine_kernel(pos_ref, *refs):
    mine_ref, other_ref, hp_ref, seen_ref, cross_ref, out_ref, c_ref, ms_ref, m0, m1, f0, f1, b0, b1, c1_ref, g_ref, hs0, hs1, w0, w1 = refs
    s = pos_ref[0] // 16
    b = pos_ref[0] % 16
    core = s % 2
    for d in range(4):
        chip = (s // 2 + 4 - d) % 4
        mine = pl.multiple_of((2 * chip + core) * (4 * CROWS), 4 * CROWS)
        theirs = pl.multiple_of((2 * chip + 1 - core) * (4 * CROWS), 4 * CROWS)
        c_ref[pl.ds(mine, 4 * CROWS), :] = mine_ref[d * 4 * CROWS : (d + 1) * 4 * CROWS]
        c_ref[pl.ds(theirs, 4 * CROWS), :] = other_ref[d * 4 * CROWS : (d + 1) * 4 * CROWS]

    def neighbours(low, high):
        theirs = other_ref[16 * CROWS + low : 16 * CROWS + high]
        across = cross_ref[low:high].astype(f32)
        flag = jnp.zeros((high - low, LANES), jnp.int32) + core
        return jnp.where(flag == 0, across, theirs), jnp.where(flag == 0, theirs, across)

    ms_above, ms_below = neighbours(256, 384)
    for k in range(8):
        ms_ref[32 * k : 32 * k + 8, :] = ms_above[16 * k + 8 : 16 * k + 16]
        ms_ref[32 * k + 8 : 32 * k + 24, :] = seen_ref[256 + 16 * k : 272 + 16 * k].astype(f32)
        ms_ref[32 * k + 24 : 32 * k + 32, :] = ms_below[16 * k : 16 * k + 8]
    bk = (b0, b1)
    m = (m0, m1)
    f = (f0, f1)
    hst = (hs0, hs1)
    w = (w0, w1)
    for h in range(2):
        at = slice(h * 128, h * 128 + 128)
        above, below = neighbours(h * 128, h * 128 + 128)
        hst[h][0:72, :] = above.T[24:96]
        hst[h][72:168, :] = hp_ref[at, 0:128].T[0:96]
        hst[h][168:240, :] = below.T[0:72]
        w[h][...] = hp_ref[at, 128:256].T
    basis = jnp.concatenate([w0[81:113, :], w1[81:113, :]], axis=1).astype(bf16)
    response = jnp.concatenate([w0[113:121, :], w1[113:121, :]], axis=1).astype(bf16)
    combined = lax.dot_general(response, basis, (((1,), (1,)), ((), ())), preferred_element_type=f32).astype(bf16)
    lane = lax.broadcasted_iota(jnp.int32, (1, LANES), 1)
    group = lane % 32
    column = 64 * b - 16 + 4 * group + lane // 32
    in_columns = (column >= 0) & (column < 1024) & (group >= 2) & (group < 22)

    def mix(row, value, rows):
        mixed = lax.dot_general(value.astype(bf16), basis, (((0,), (0,)), ((), ())), preferred_element_type=f32)
        mixed = rounded(mixed)
        at = pl.ds(pl.multiple_of(row * LANES, LANES), rows * LANES)
        for h in range(2):
            m[h][at, :] = mixed[:, h * 128 : h * 128 + 128]

    def ms_gradient(row, block):
        predicted = jnp.dot(combined, block.astype(bf16), preferred_element_type=f32)
        seen = jnp.concatenate([ms_ref[pl.ds(row - 8 + r, 8, stride=MROWS), :] for r in range(8)], axis=1)
        misfit = (seen - predicted).astype(bf16)
        grad = lax.dot_general(combined, misfit, (((0,), (0,)), ((), ())), preferred_element_type=f32)
        for r in range(8):
            g_ref[pl.ds((row - 8 + r) * 32, 32), :] = grad[:, r * 128 : r * 128 + 128]

    def blur_row(n):
        g = lax.broadcasted_iota(jnp.int32, (JCOLS, LANES), 0)
        i_at = 4 * s + n - 3
        j_at = 16 * b + g - 3
        inside = (i_at >= 0) & (i_at < ROWS_LO) & (j_at >= 0) & (j_at < COLS_LO)
        for h in range(2):
            acc = [None, None, None]
            for a in range(TAPS):
                for q in range(4):
                    at = pl.multiple_of((4 * n + a) * LANES + 32 * q, 32)
                    x = m[h][pl.ds(at, JCOLS), :]
                    for d in range(3):
                        if 4 * d + q > 8:
                            continue
                        tap = a * 9 + 4 * d + q
                        term = w[h][tap : tap + 1, :] * x
                        acc[d] = term if acc[d] is None else acc[d] + term
            blurred = acc[0] + pltpu.roll(acc[1], JCOLS - 1, 0) + pltpu.roll(acc[2], JCOLS - 2, 0)
            seen = hst[h][pl.ds(pl.multiple_of(n * JCOLS, 8), JCOLS), :]
            f[h][pl.ds(pl.multiple_of(8 + n * JCOLS, 8), JCOLS), :] = jnp.where(inside, seen - blurred, 0.0)

    def back_rows(u, first=0, count=JCOLS, phases=4):
        for h in range(2):
            win = [[f[h][pl.ds(8 + (u - t) * JCOLS + first - tt, count), :] for tt in range(3)] for t in range(3)]
            for p in range(phases):
                for q in range(4):
                    total = None
                    for t in range(3):
                        for tt in range(3):
                            if p + 4 * t > 8 or q + 4 * tt > 8:
                                continue
                            tap = (p + 4 * t) * 9 + q + 4 * tt
                            term = w[h][tap : tap + 1, :] * win[t][tt]
                            total = term if total is None else total + term
                    at = (4 * u - 8 + p) * LANES + 32 * q + first
                    bk[h][pl.ds(at, count), :] = rounded(total)

    def hs_gradient(row, rows):
        at = pl.ds((row - 8) * LANES, rows * LANES)
        back = jnp.concatenate([b0[at, :].astype(bf16), b1[at, :].astype(bf16)], axis=1)
        return lax.dot_general(basis, back, (((1,), (1,)), ((), ())), preferred_element_type=f32)

    def start_row(row):
        return c_ref[pl.ds(row, 32, stride=CROWS), :]

    def loop(low, high, body):
        def step(n, _):
            body(n)
            return 0

        lax.fori_loop(low, high, step, 0)

    for block in range(CROWS // 8):
        value = jnp.concatenate([start_row(block * 8 + r) for r in range(8)], axis=1)
        mix(block * 8, value, 8)
        if 1 <= block < 5:
            ms_gradient(block * 8, value)
    loop(0, IROWS, blur_row)
    loop(2, 9, back_rows)
    back_rows(9, phases=1)
    for block in range(1, 5):
        grad = hs_gradient(block * 8, 8)
        values = []
        for r in range(8):
            row = block * 8 + r
            now = start_row(row)
            new = now + STEP * (grad[:, r * 128 : r * 128 + 128] + g_ref[pl.ds((row - 8) * 32, 32), :])
            row_at = 16 * s - 16 + row
            new = jnp.where(in_columns & (row_at >= 0) & (row_at < 128), new, 0.0)
            c1_ref[pl.ds((row - 8) * 32, 32), :] = new
            values.append(new)
        value = jnp.concatenate(values, axis=1)
        mix(block * 8, value, 8)
        if 2 <= block < 4:
            ms_gradient(block * 8, value)
    loop(2, 8, blur_row)
    loop(4, 8, lambda u: back_rows(u, 4, 16))
    place_at = lax.broadcasted_iota(jnp.int32, (LANES, LANES), 1)
    take = lax.broadcasted_iota(jnp.int32, (LANES, LANES), 0)
    shift = 4 * (take % 32) + take // 32 - 16
    order = [(place_at == shift + 64 * ((half + b) % 2)) & (shift >= 0) & (shift < 64) for half in range(2)]
    order = [jnp.where(o, 1.0, 0.0).astype(bf16) for o in order]
    grads = [hs_gradient(16, 8), hs_gradient(24, 8)]
    for r in range(8):
        total = None
        for half in range(2):
            row = 8 + r + 8 * half
            at = pl.ds(row * 32, 32)
            value = STEP * (grads[half][:, r * 128 : r * 128 + 128] + g_ref[at, :])
            value = value + (c1_ref[at, :] - start_row(row + 8))
            rest = jnp.where((group >= 4) & (group < 20), value, 0.0)
            for _ in range(3):
                piece = rest.astype(bf16)
                rest = rest - piece.astype(f32)
                moved = jnp.dot(piece, order[half], preferred_element_type=f32)
                total = moved if total is None else total + moved
        out_ref[pl.ds(r, 32, stride=8), :] = total


def refine(pos, mine, other, hp, seen, cross):
    vmem = pl.BlockSpec(memory_space=pltpu.VMEM)
    return pl.pallas_call(
        refine_kernel,
        out_shape=jax.ShapeDtypeStruct((32 * 8, LANES), f32),
        in_specs=[pl.BlockSpec(memory_space=pltpu.SMEM)] + [vmem] * 5,
        out_specs=vmem,
        scratch_shapes=[
            pltpu.VMEM((32 * CROWS, LANES), f32),
            pltpu.VMEM((8 * MROWS, LANES), f32),
            pltpu.VMEM((CROWS * LANES, LANES), f32),
            pltpu.VMEM((CROWS * LANES, LANES), f32),
            pltpu.VMEM((256, LANES), f32),
            pltpu.VMEM((256, LANES), f32),
            pltpu.VMEM((MROWS * LANES, LANES), f32),
            pltpu.VMEM((MROWS * LANES, LANES), f32),
            pltpu.VMEM((MROWS * 32, LANES), f32),
            pltpu.VMEM((MROWS * 32, LANES), f32),
            pltpu.VMEM((256, LANES), f32),
            pltpu.VMEM((256, LANES), f32),
            pltpu.VMEM((LANES, LANES), f32),
            pltpu.VMEM((LANES, LANES), f32),
        ],
        compiler_params=pltpu.CompilerParams(vmem_limit_bytes=40 * 2**20),
        cost_estimate=pl.CostEstimate(flops=400_000_000, bytes_accessed=2_000_000, transcendentals=0),
        name="refine",
    )(pos, mine, other, hp, seen, cross)


def spread(hs_ref, k_ref, basis_ref, response_ref, sent_ref):
    lane = lax.broadcasted_iota(jnp.int32, (1, LANES), 1)
    hs = hs_ref[...].astype(f32)
    rows = [jnp.concatenate([hs[:, i, :], jnp.zeros((2, 256), f32)], axis=0) for i in range(4)]
    sent_ref[0, :, 128:256] = jnp.zeros((16, 128), f32)
    for a in range(9):
        sent_ref[0, 0:14, 128 + 9 * a : 137 + 9 * a] = k_ref[a]
    sent_ref[0, 0:14, 209:241] = basis_ref[...].astype(f32)
    sent_ref[0, 0:14, 241:249] = response_ref[...].astype(f32).T
    params = sent_ref[0, :, 128:256]
    for t in range(16):
        total = jnp.zeros((16, LANES), f32)
        for i in range(4):
            moved = pltpu.roll(rows[i], (24 * i + 3 - 16 * t) % 256, 1)[:, 0:128]
            total = jnp.where((lane >= 24 * i) & (lane < 24 * i + 24), moved, total)
        sent_ref[t, :, 0:128] = total
        if t:
            sent_ref[t, :, 128:256] = params


def pack_kernel(pos_ref, ca_ref, cb_ref, ma_ref, mb_ref, hs_ref, k_ref, basis_ref, response_ref, *rest_refs):
    spread(hs_ref, k_ref, basis_ref, response_ref, rest_refs[4])
    wide_ref = rest_refs[5]
    s = pos_ref[0] // 16
    b = pos_ref[0] % 16
    off = jnp.where(b % 2 == 0, 112, 48)
    lane = lax.broadcasted_iota(jnp.int32, (1, LANES), 1)
    first = lane >= off
    block = (b + 1) // 2 - jnp.where(first, 1, 0)
    keep = (block >= 0) & (block < 8)
    source = lax.broadcasted_iota(jnp.int32, (LANES, LANES), 0)
    target = lax.broadcasted_iota(jnp.int32, (LANES, LANES), 1)
    order = jnp.where(source == (4 * (target % 32) + target // 32 + off) % LANES, 1.0, 0.0).astype(bf16)
    ms = jnp.where(first, ma_ref[...].reshape(128, LANES).astype(f32), mb_ref[...].reshape(128, LANES).astype(f32))
    ms = jnp.where(keep, ms, 0.0).astype(bf16)
    ms = jnp.dot(ms, order, preferred_element_type=f32)
    rest_refs[0][256:384] = ms
    edge = jnp.zeros((16, LANES), f32)
    for k in range(4):
        rest = jnp.where(keep, jnp.where(first, ca_ref[k], cb_ref[k]), 0.0)
        total = None
        for _ in range(3):
            piece = rest.astype(bf16)
            rest = rest - piece.astype(f32)
            moved = jnp.dot(piece, order, preferred_element_type=f32)
            total = moved if total is None else total + moved
        wide_ref[k, 0:16] = edge
        wide_ref[k, 16:144] = total
        wide_ref[k, 144:160] = edge
    for d in range(4):
        at = pl.ds(pl.multiple_of(32 * ((s // 2 + d) % 4), 32), 64)
        for k in range(4):
            rest_refs[d][64 * k : 64 * k + 64] = wide_ref[k, at, :]


def pack(pos, coeffs_in, ms_image, hs_image, kernels, basis, response):
    def low(i, p):
        return (0, 0, jnp.maximum((p[0] % 16 + 1) // 2 - 1, 0))

    def high(i, p):
        return (0, 0, jnp.minimum((p[0] % 16 + 1) // 2, 7))

    return pl.pallas_call(
        pack_kernel,
        out_shape=(jax.ShapeDtypeStruct((384, LANES), f32),)
        + (jax.ShapeDtypeStruct((256, LANES), f32),) * 3
        + (jax.ShapeDtypeStruct((16, 16, 256), f32),),
        grid_spec=pltpu.PrefetchScalarGridSpec(
            num_scalar_prefetch=1,
            grid=(1,),
            in_specs=[
                pl.BlockSpec((4, 128, LANES), low),
                pl.BlockSpec((4, 128, LANES), high),
                pl.BlockSpec((8, 16, LANES), low),
                pl.BlockSpec((8, 16, LANES), high),
                pl.BlockSpec((14, 4, 256), lambda i, p: (0, 0, 0)),
                pl.BlockSpec((9, 14, 9), lambda i, p: (0, 0, 0)),
                pl.BlockSpec((14, 32), lambda i, p: (0, 0)),
                pl.BlockSpec((8, 14), lambda i, p: (0, 0)),
            ],
            out_specs=(pl.BlockSpec((384, LANES), lambda i, p: (0, 0)),)
            + (pl.BlockSpec((256, LANES), lambda i, p: (0, 0)),) * 3
            + (pl.BlockSpec((16, 16, 256), lambda i, p: (0, 0, 0)),),
            scratch_shapes=[pltpu.VMEM((4, 160, LANES), f32)],
        ),
        compiler_params=pltpu.CompilerParams(vmem_limit_bytes=60 * 2**20),
        cost_estimate=pl.CostEstimate(flops=100_000_000, bytes_accessed=1_600_000, transcendentals=0),
        name="pack",
    )(pos, coeffs_in, coeffs_in, ms_image, ms_image, hs_image, kernels, basis, response)


def hold_kernel(region_ref, out_ref, near_ref):
    out_ref[...] = region_ref[0:256]
    near_ref[...] = region_ref[256:384].astype(bf16)


def hold(region):
    vmem = pl.BlockSpec(memory_space=pltpu.VMEM)
    return pl.pallas_call(
        hold_kernel,
        out_shape=(jax.ShapeDtypeStruct((256, LANES), f32), jax.ShapeDtypeStruct((128, LANES), bf16)),
        in_specs=[vmem],
        out_specs=(vmem, vmem),
        compiler_params=pltpu.CompilerParams(vmem_limit_bytes=16 * 2**20),
        name="hold",
    )(region)


def join_kernel(hp_ref, near_ref, seen_ref):
    seen_ref[0:256] = hp_ref[:, 0:128].astype(bf16)
    seen_ref[256:384] = near_ref[...]


def join(hp, near):
    vmem = pl.BlockSpec(memory_space=pltpu.VMEM)
    return pl.pallas_call(
        join_kernel,
        out_shape=jax.ShapeDtypeStruct((384, LANES), bf16),
        in_specs=[vmem] * 2,
        out_specs=vmem,
        compiler_params=pltpu.CompilerParams(vmem_limit_bytes=16 * 2**20),
        name="join",
    )(hp, near)


def hand_kernel(pos_ref, r0, r1, r2, r3, seen_ref, mine_ref, other_ref):
    other_ref[16 * CROWS : 16 * CROWS + 384] = seen_ref[...].astype(f32)
    skip = 16 * (pos_ref[0] // 16 % 2)
    for d, region in enumerate((r0, r1, r2, r3)):
        for k in range(4):
            at = CROWS * (4 * d + k)
            mine_ref[at : at + CROWS] = region[pl.ds(pl.multiple_of(64 * k + skip, 16), CROWS), :]
            other_ref[at : at + CROWS] = region[pl.ds(pl.multiple_of(64 * k + 16 - skip, 16), CROWS), :]


def hand(pos, tiles, seen):
    vmem = pl.BlockSpec(memory_space=pltpu.VMEM)
    return pl.pallas_call(
        hand_kernel,
        out_shape=(
            jax.ShapeDtypeStruct((16 * CROWS, LANES), f32),
            jax.ShapeDtypeStruct((16 * CROWS + 384, LANES), f32),
        ),
        in_specs=[pl.BlockSpec(memory_space=pltpu.SMEM)] + [vmem] * 5,
        out_specs=(vmem, vmem),
        compiler_params=pltpu.CompilerParams(vmem_limit_bytes=16 * 2**20),
        cost_estimate=pl.CostEstimate(flops=1_000_000, bytes_accessed=800_000, transcendentals=0),
        name="hand",
    )(pos, *tiles, seen)


def encode_kernel(d_ref, out_ref):
    scales = []
    codes = []
    for k in range(4):
        part = d_ref[:, k]
        size = jnp.abs(part)
        top = jnp.max(size, axis=(0, 1, 2), keepdims=True)
        scale = rounded(jnp.maximum(top * (1 + 2**-7), 1e-30))
        code = jnp.exp2(size * (SPAN / scale) - SPAN / 2)
        codes.append(jnp.where(part < 0, -code, code))
        scales.append(jnp.broadcast_to(scale[0], (1, LANES)))
    scales = jnp.concatenate(scales + [jnp.zeros((12, LANES), f32)], axis=0).astype(bf16)
    for s in range(8):
        row = jnp.concatenate([codes[k][s] for k in range(4)], axis=0).astype(bf16)
        for t in range(16):
            out_ref[t, 32 * s : 32 * s + 32] = row
    for t in range(16):
        out_ref[t, 256:272] = scales


def encode(owned):
    vmem = pl.BlockSpec(memory_space=pltpu.VMEM)
    return pl.pallas_call(
        encode_kernel,
        out_shape=jax.ShapeDtypeStruct((16, 272, LANES), bf16),
        in_specs=[vmem],
        out_specs=vmem,
        compiler_params=pltpu.CompilerParams(vmem_limit_bytes=16 * 2**20),
        name="encode",
    )(owned)


def place_kernel(g_ref, c_ref, out_ref):
    lane = lax.broadcasted_iota(jnp.int32, (1, LANES), 1)
    low = lane < 64
    count = g_ref.shape[0] // 2
    for j in range(count):
        even, odd = [g_ref[2 * j + e, 256:272].astype(f32) * (1 / SPAN) for e in range(2)]
        scales = (jnp.where(low, even, odd), jnp.where(low, odd, even))
        columns = slice(j * LANES, j * LANES + LANES)
        for s in range(8):
            even, odd = [g_ref[2 * j + e, 32 * s : 32 * s + 32].astype(f32) for e in range(2)]
            for half, code in enumerate((jnp.where(low, even, odd), jnp.where(low, odd, even))):
                size = jnp.log2(jnp.abs(code)) + SPAN / 2
                value = jnp.where(code < 0, -size, size)
                for k in range(4):
                    part = value[8 * k : 8 * k + 8] * scales[half][k : k + 1]
                    if half:
                        part = pltpu.roll(part, 64, 1)
                    at = slice(16 * s + 8 * half, 16 * s + 8 * half + 8)
                    out_ref[k, at, columns] = c_ref[k, at, columns] + part


def place(gathered, coeffs_in):
    block = pl.BlockSpec((4, 128, 4 * LANES), lambda j: (0, 0, j))
    return pl.pallas_call(
        place_kernel,
        out_shape=jax.ShapeDtypeStruct((4, 128, 1024), f32),
        grid=(2,),
        in_specs=[pl.BlockSpec((8, 272, LANES), lambda j: (j, 0, 0)), block],
        out_specs=block,
        compiler_params=pltpu.CompilerParams(vmem_limit_bytes=60 * 2**20),
        name="place",
    )(gathered, coeffs_in)


def per_device(coeffs_in, basis, kernels, response, hs_image, ms_image):
    pos = (lax.axis_index("sub") * 16 + lax.axis_index("band")).astype(jnp.int32).reshape(1)
    *tiles, sent = pack(pos, coeffs_in, ms_image, hs_image, kernels.transpose(1, 0, 2), basis, response)
    hp = lax.all_to_all(sent, "band", split_axis=0, concat_axis=0, tiled=True).reshape(256, 256)
    tiles = [tiles[0]] + [
        lax.ppermute(tiles[d], "sub", [(i, (i + 2 * d) % 8) for i in range(8)]) for d in range(1, 4)
    ]
    tiles[0], near = hold(tiles[0])
    seen = join(hp, near)
    cross = lax.ppermute(seen, "sub", [(1, 2), (2, 1), (3, 4), (4, 3), (5, 6), (6, 5)])
    cross, *tiles = lax.optimization_barrier((cross, *tiles))
    mine, other = hand(pos, tiles, seen)
    other = lax.ppermute(other, "sub", [(i, i ^ 1) for i in range(8)])
    new = refine(pos, mine, other, hp, seen, cross)
    owned = lax.all_to_all(new.reshape(8, 4, 8, LANES), "sub", split_axis=0, concat_axis=0, tiled=True)
    gathered = lax.all_to_all(encode(owned), "band", split_axis=0, concat_axis=0, tiled=True)
    return place(gathered, coeffs_in)


def solution(mesh):
    return jax.shard_map(
        per_device,
        mesh=mesh,
        in_specs=(
            P("sub", None, None),
            P("band", None),
            P("band", None, None),
            P(None, "band"),
            P("band", "sub", None),
            P(None, "sub", None),
        ),
        out_specs=P("sub", None, None),
        check_vma=False,
    )
```
